32 devices in a mesh: fluid: 8 (over y, x, core), wall: 4 (over z).
Axes of the slice: x: 2, y: 2, z: 4, core: 2. Of those that a mesh axis runs over, the one named last changes fastest.
Arguments:
- flow_state: float32 [4, 128, 32, 512], P(None, 'fluid', None, 'wall'), may hold values from -6 to 6
- regions: int32 [128, 32, 512], P('fluid', None, 'wall'), may hold values from 0 to 63
- obs_tiles: bfloat16 [8, 4, 32, 128, 128], P('fluid', 'wall'), may hold values from -0.5 to 0.5
- measured: bfloat16 [8, 4, 32, 3, 128], P('fluid', 'wall'), may hold values from -6 to 6
- tile_dest: int32 [8, 4, 32], P('fluid', 'wall'), may hold values from 0 to 7, as said below
- cell_list: int32 [8, 4, 8, 4], P('fluid', 'wall'), may hold values from 0 to 511
Outputs:
- velocity_next: float32 [3, 128, 32, 512], P(None, 'fluid', None, 'wall')
- adjoint: float32 [3, 128, 32, 512], P(None, 'fluid', None, 'wall')
- sensitivity: float32 [512], P(('fluid', 'wall'))
The draws below stay inside these ranges and needn't reach their ends.
Inputs may be any that keep to these rules, and one draw needn't show every extreme that they name: `tile_dest`: each device's list names every fluid block at most 4 times. In each wall column one fluid block is named exactly 4 times by the list of every device of that column.
All inputs are finite; a program needn't handle non-finite values.
Results may differ from the reference program's by a relative error of at most 0.0032.
Values may be sent and summed in bfloat16 or wider, within the bound.
No kernel may reach another device: no remote copies, remote signals or barrier semaphores. Data moves between devices by JAX's collectives and lax.ppermute only.
A program may use at most 128 MiB of HBM per device.

```python
import jax
import jax.numpy as jnp
from jax import lax

CX = 16
CY = 32
TW = 128
CAP = 4
TILE_DEV = 32
REG_DEV = 16
NX = 128
NZ = 512
N_FLUID = 8
N_WALL = 4


def draw_tile_dest(key, part):
    key_hot, key_rows = jax.random.split(jax.random.fold_in(key, 11), 2)
    hot_block = jax.random.randint(key_hot, (N_WALL,), 0, N_FLUID)
    slot_pool = jnp.arange((N_FLUID - 1) * CAP, dtype=jnp.int32) // CAP
    device_keys = jax.random.split(key_rows, N_FLUID * N_WALL)

    def draw_device(device_key, hot_here):
        key_pick, key_order = jax.random.split(device_key)
        others_rows = jax.random.permutation(key_pick, slot_pool)[:TILE_DEV - CAP]
        others_rows = others_rows + (others_rows >= hot_here).astype(jnp.int32)
        all_rows = jnp.concatenate([jnp.full((CAP,), hot_here, jnp.int32), others_rows])
        return jax.random.permutation(key_order, all_rows)
    hot_each = jnp.tile(hot_block, N_FLUID)
    drawn = jax.vmap(draw_device)(device_keys, hot_each)
    return drawn.reshape(N_FLUID, N_WALL, TILE_DEV).astype(jnp.int32)


def touch_ends(array, rng, smallest, largest):
    longest = array.shape.index(max(array.shape))
    spots = []
    for shift in (0, 1):
        where = [jax.random.randint(jax.random.fold_in(rng, axis), (), 0, length) for axis, length in enumerate(array.shape)]
        where[longest] = (where[longest] + shift) % array.shape[longest]
        spots.append(tuple(where))
    return array.at[spots[0]].set(smallest).at[spots[1]].set(largest)


def block_levels(rng, shape, shards, least, largest):
    factor_of, own = 1.0, jax.random.fold_in(rng, 6)
    for axis_at, parts in shards:
        draws = jnp.exp(jax.random.uniform(jax.random.fold_in(own, axis_at), (parts,), jnp.float32, least / len(shards), largest / len(shards)))
        factor_of = factor_of * jnp.repeat(draws, shape[axis_at] // parts).reshape([-1 if axis == axis_at else 1 for axis in range(len(shape))])
    return factor_of


def gaussian(key, shape, width, most, pieces=(), kind=jnp.bfloat16):
    result = width * jax.random.normal(key, shape, jnp.float32)
    if pieces:
        result = result * block_levels(key, shape, pieces, -0.22, 0.18)
    return jnp.clip(result, -most, most).astype(kind)


def setup_inputs(seed: int = 0) -> dict:
    splits = jax.random.split(jax.random.key(seed), 7)
    flow_state = gaussian(splits[0], (4, NX, CY, NZ), 1.0, 6.0, ((1, 8), (3, 4)), jnp.float32)
    regions = touch_ends(jax.random.randint(splits[1], (NX, CY, NZ), 0, REG_DEV * N_WALL), jax.random.fold_in(splits[1], 1), 0, (REG_DEV * N_WALL) - 1).astype(jnp.int32)
    obs_tiles = gaussian(splits[2], (N_FLUID, N_WALL, TILE_DEV, TW, TW), TW ** -0.5, 0.5, ((0, 8), (1, 4)))
    measured = gaussian(splits[3], (N_FLUID, N_WALL, TILE_DEV, 3, TW), 1.0, 6.0, ((0, 8), (1, 4)))
    tile_dest = draw_tile_dest(jax.random.fold_in(splits[6], 71), 0)
    cell_list = touch_ends(jax.random.randint(splits[5], (N_FLUID, N_WALL, N_FLUID, CAP), 0, CX * CY), jax.random.fold_in(splits[5], 1), 0, (CX * CY) - 1).astype(jnp.int32)
    return {"flow_state": flow_state, "regions": regions, "obs_tiles": obs_tiles, "measured": measured, "tile_dest": tile_dest, "cell_list": cell_list}


time_step = 0.12
nu_floor = 0.1
nu_spread = 0.9
relax_sq = 4.0
sens_scale = 0.03


def face_differences(padded, spatial):
    extent = padded.shape[spatial]
    upper_cells = lax.slice_in_dim(padded, 1, extent, axis=spatial)
    lower_cells = lax.slice_in_dim(padded, 0, extent - 1, axis=spatial)
    face_jump = upper_cells - lower_cells
    for across in (1, 2, 3):
        if across != spatial:
            face_jump = lax.slice_in_dim(face_jump, 1, face_jump.shape[across] - 1, axis=across)
    return face_jump


def viscosity(face_jump):
    shear_sq = jnp.sum(face_jump * face_jump, axis=0)
    return nu_floor + nu_spread * jnp.power(1.0 + relax_sq * shear_sq, -0.25)


def divergence(face_nus, face_jumps):
    summed = 0.0
    for spatial, nu_face, face_jump in zip((1, 2, 3), face_nus, face_jumps):
        face_flux = nu_face[None] * face_jump
        extent = face_flux.shape[spatial]
        summed = summed + lax.slice_in_dim(face_flux, 1, extent, axis=spatial) - lax.slice_in_dim(face_flux, 0, extent - 1, axis=spatial)
    return summed


def forward(padded):
    velocity = padded[:3]
    pressure = padded[3:4]
    face_jumps = [face_differences(velocity, spatial) for spatial in (1, 2, 3)]
    face_nus = [viscosity(face_jump) for face_jump in face_jumps]
    halves = []
    for spatial in (1, 2, 3):
        pressure_jump = face_differences(pressure, spatial)
        extent = pressure_jump.shape[spatial]
        halves.append(0.5 * (lax.slice_in_dim(pressure_jump, 1, extent, axis=spatial) + lax.slice_in_dim(pressure_jump, 0, extent - 1, axis=spatial)))
    gradient = jnp.concatenate(halves, axis=0)
    interior = padded[:3, 1:-1, 1:-1, 1:-1]
    velocity_next = interior + time_step * (divergence(face_nus, face_jumps) - gradient)
    return velocity_next, face_nus


def adjoint_step(padded_forcing, face_nus):
    face_jumps = [face_differences(padded_forcing, spatial) for spatial in (1, 2, 3)]
    return padded_forcing[:, 1:-1, 1:-1, 1:-1] + time_step * divergence(face_nus, face_jumps)


def reference(flow_state, regions, obs_tiles, measured, tile_dest, cell_list):
    padded = jnp.pad(flow_state, ((0, 0), (1, 1), (1, 1), (1, 1)))
    velocity_next, face_nus = forward(padded)
    obs_velocity = velocity_next.astype(jnp.bfloat16)
    block_groups = N_FLUID
    walls = N_WALL
    fluid_idx = jnp.arange(block_groups, dtype=jnp.int32)[:, None, None]
    wall_idx = jnp.arange(walls, dtype=jnp.int32)[None, :, None]
    same_target = tile_dest[..., :, None] == tile_dest[..., None, :]
    before = jnp.arange(TILE_DEV)[None, :] < jnp.arange(TILE_DEV)[:, None]
    slot_rank = jnp.sum((same_target & before).astype(jnp.int32), axis=-1)
    cell_tile = cell_list[tile_dest, wall_idx, fluid_idx, slot_rank]
    cell_x = tile_dest * CX + cell_tile // CY
    cell_y = cell_tile % CY
    wall_full = jnp.broadcast_to(wall_idx, tile_dest.shape)
    obs_grid = obs_velocity.reshape(3, block_groups * CX, CY, walls, TW)
    cell_values = obs_grid[:, cell_x, cell_y, wall_full].astype(jnp.float32)
    weights = obs_tiles.astype(jnp.float32)
    model_velocity = jnp.einsum("fwtij,cfwtj->fwtci", weights, cell_values)
    data_residual = (model_velocity - measured.astype(jnp.float32)).astype(jnp.bfloat16)
    contrib = jnp.einsum("fwtij,fwtci->cfwtj", weights, data_residual.astype(jnp.float32))
    forcing = jnp.zeros((3, block_groups * CX, CY, walls, TW), jnp.float32).at[:, cell_x, cell_y, wall_full].add(contrib)
    forcing = forcing.reshape(3, block_groups * CX, CY, walls * TW)
    padded_forcing = jnp.pad(forcing, ((0, 0), (1, 1), (1, 1), (1, 1)))
    adjoint = adjoint_step(padded_forcing, face_nus)
    product = jnp.sum(adjoint * velocity_next, axis=0)
    reg_count = REG_DEV * walls
    owner_block = (jnp.arange(block_groups * CX, dtype=jnp.int32) // CX)[:, None, None]
    segment = owner_block * reg_count + regions
    region_totals = jax.ops.segment_sum(product.reshape(-1), segment.reshape(-1), num_segments=reg_count * block_groups)
    return velocity_next, adjoint, sens_scale * region_totals
```

```python
import functools

import jax
import jax.numpy as jnp
from jax import lax
from jax.experimental import pallas as pl
from jax.experimental.pallas import tpu as pltpu
from jax.sharding import PartitionSpec as P

REG_DEV = 16

time_step = 0.12
nu_floor = 0.1
nu_spread = 0.9
relax_sq = 4.0
sens_scale = 0.03

VMEM = pl.BlockSpec(memory_space=pltpu.VMEM)
SMEM = pl.BlockSpec(memory_space=pltpu.SMEM)
ANY = pl.BlockSpec(memory_space=pl.ANY)
LIMIT = 24 * 1024 * 1024


def call(kernel, outs, ins, operands, scratch=(), flops=1, moved=1, out_specs=None):
    return pl.pallas_call(
        kernel,
        out_shape=outs,
        in_specs=ins,
        out_specs=out_specs if out_specs is not None else jax.tree.map(lambda _: VMEM, outs),
        scratch_shapes=list(scratch),
        compiler_params=pltpu.CompilerParams(vmem_limit_bytes=LIMIT),
        cost_estimate=pl.CostEstimate(flops=flops, bytes_accessed=moved, transcendentals=0),
    )(*operands)


def f32(*shape):
    return jax.ShapeDtypeStruct(shape, jnp.float32)


def bf16(*shape):
    return jax.ShapeDtypeStruct(shape, jnp.bfloat16)


def swap(block, axis, turn):
    count = lax.axis_size(axis)
    pairs = [(i, (i + 1) % count if (i + turn) % 2 == 0 else (i - 1) % count) for i in range(count)]
    return lax.ppermute(block, axis, pairs)


def cross(block, axis, mask):
    return lax.ppermute(block, axis, [(i, i ^ mask) for i in range(lax.axis_size(axis))])


def from_neighbours(index, count, first, second):
    even = index % 2 == 0
    above = jnp.where(even, first, second)
    below = jnp.where(even, second, first)
    above = jnp.where(index == count - 1, jnp.zeros_like(above), above)
    below = jnp.where(index == 0, jnp.zeros_like(below), below)
    return below, above


def pack_edges(packed, plane, m, lane):
    width = lane.shape[1]
    here = (lane == 2 * m) | (lane == (2 * m + width - 1) % width)
    return jnp.where(here, pltpu.roll(plane, 2 * m, 1), packed)


def mix_edges(below, above, lane):
    return jnp.where(lane % 2 == 0, above, pltpu.roll(below, 2, 1))


def edge_of(mixed, m):
    width = mixed.shape[1]
    return pltpu.roll(mixed, (2 * width - (2 * m + 1)) % width, 1)


def viscosity(jumps):
    shear_sq = jumps[0] * jumps[0] + jumps[1] * jumps[1] + jumps[2] * jumps[2]
    root = lax.rsqrt(1.0 + relax_sq * shear_sq)
    return nu_floor + nu_spread * (root * lax.rsqrt(root))


def iotas(rows, width):
    shape = (rows, width)
    return lax.broadcasted_iota(jnp.int32, shape, 0), lax.broadcasted_iota(jnp.int32, shape, 1)


def group_kernel(cap, dest_ref, tiles_ref, meas_ref, send_ref, count_ref, rows_ref, blank_ref, tile_sems, row_sem, blank_sem):
    count_tiles, width, _ = tiles_ref.shape
    groups = send_ref.shape[0]
    slots = groups * cap
    extra = rows_ref.shape[0] // groups

    def clear(b, carry):
        count_ref[b] = 0
        return carry

    lax.fori_loop(0, groups, clear, 0)
    _, tile_lane = iotas(8, count_tiles)

    def tile_copy(t, b, k):
        return pltpu.make_async_copy(
            tiles_ref.at[t], send_ref.at[b, pl.ds(pl.multiple_of(k * width, width), width), :], tile_sems.at[t]
        )

    def send_one(t, slot_of):
        b = dest_ref[t]
        k = count_ref[b]
        count_ref[b] = k + 1
        tile_copy(t, b, k).start()
        return jnp.where(tile_lane == t, b * cap + k, slot_of)

    slot_of = lax.fori_loop(0, count_tiles, send_one, jnp.full((8, count_tiles), -1, jnp.int32), unroll=4)

    def blank_copy(b, k):
        return pltpu.make_async_copy(
            blank_ref, send_ref.at[b, pl.ds(pl.multiple_of(k * width, width), width), :], blank_sem
        )

    if slots > count_tiles:
        blank_ref[...] = jnp.zeros_like(blank_ref)

        def blanks(b, carry):
            def one(k, inner):
                copy = blank_copy(b, k)
                copy.start()
                copy.wait()
                return inner

            return lax.fori_loop(count_ref[b], cap, one, carry)

        lax.fori_loop(0, groups, blanks, 0)

    meas = meas_ref[...].astype(jnp.float32)
    row = lax.broadcasted_iota(jnp.int32, (groups * extra, count_tiles), 0)
    within = row % extra
    row_slot = (row // extra) * cap + within // 3
    used = within < cap * 3
    total = jnp.zeros((groups * extra, width), jnp.float32)
    for c in range(3):
        pick = (row_slot == slot_of[0:1, :]) & used & (within % 3 == c)
        total += jnp.dot(
            pick.astype(jnp.float32).astype(jnp.bfloat16),
            meas[:, c, :].astype(jnp.bfloat16),
            preferred_element_type=jnp.float32,
        )
    rows_ref[...] = total.astype(jnp.bfloat16)
    for b in range(groups):
        pltpu.make_async_copy(
            rows_ref.at[pl.ds(b * extra, extra), :], send_ref.at[b, pl.ds(cap * width, extra), :], row_sem.at[b]
        ).start()

    def finish(t, carry):
        tile_copy(t, 0, 0).wait()
        return carry

    lax.fori_loop(0, count_tiles, finish, 0, unroll=4)
    for b in range(groups):
        pltpu.make_async_copy(
            rows_ref.at[pl.ds(b * extra, extra), :], send_ref.at[b, pl.ds(cap * width, extra), :], row_sem.at[b]
        ).wait()


def faces_kernel(pos_ref, flow_ref, first_ref, second_ref, edges_ref):
    fields, planes, rows, width = flow_ref.shape
    even = pos_ref[0] % 2 == 0
    _, lane = iotas(rows, width)
    for c in range(fields):
        low, high = flow_ref[c, 0], flow_ref[c, planes - 1]
        first_ref[c] = jnp.where(even, high, low)
        second_ref[c] = jnp.where(even, low, high)
    packed = jnp.zeros((rows, width), jnp.float32)
    for c in range(fields):
        for x in range(planes):
            packed = pack_edges(packed, flow_ref[c, x], c * planes + x, lane)
    edges_ref[...] = packed


def forward_kernel(
    sizes, cap, pos_ref, cells_ref, flow_ref, regions_ref, x0_ref, x1_ref, z0_ref, z1_ref,
    next_ref, nux_ref, nuyu_ref, nuyd_ref, nuzu_ref, nuzd_ref, kz_ref, kpack_ref, vpack_ref, values_ref, pick_ref,
    padded_ref, taken_ref,
):
    _, planes, rows, width = flow_ref.shape
    groups, walls = sizes
    extra = values_ref.shape[1]
    row, lane = iotas(rows, width)
    below, above = from_neighbours(pos_ref[1], walls, z0_ref[...], z1_ref[...])
    halo = mix_edges(below, above, lane)
    for c in range(4):
        low, high = from_neighbours(pos_ref[0], groups, x0_ref[c], x1_ref[c])
        padded_ref[c, 0] = low
        padded_ref[c, planes + 1] = high
        padded_ref[c, 1 : planes + 1] = flow_ref[c]
    nux_ref[0] = viscosity([padded_ref[c, 1] - padded_ref[c, 0] for c in range(3)])

    def up_y(value):
        return jnp.where(row == rows - 1, 0.0, pltpu.roll(value, rows - 1, 0))

    def down_y(value):
        return jnp.where(row == 0, 0.0, pltpu.roll(value, 1, 0))

    def plane(x, carry):
        kpack, vpack = carry
        here = [padded_ref[c, x + 1] for c in range(4)]
        over = [padded_ref[c, x + 2] for c in range(4)]
        under = [padded_ref[c, x] for c in range(4)]
        total = [None] * 3
        pressure = [None] * 3

        def add(axis, nu_up, nu_down):
            for c in range(3):
                flux = nu_up * (over[c] - here[c]) - nu_down * (here[c] - under[c])
                total[c] = flux if total[c] is None else total[c] + flux
            pressure[axis] = 0.5 * (over[3] - under[3])

        nu_up = viscosity([over[c] - here[c] for c in range(3)])
        nux_ref[x + 1] = nu_up
        add(0, nu_up, nux_ref[x])
        over = [up_y(here[c]) for c in range(4)]
        under = [down_y(here[c]) for c in range(4)]
        nu_up = viscosity([over[c] - here[c] for c in range(3)])
        nu_down = viscosity([here[c] - under[c] for c in range(3)])
        nuyu_ref[x] = nu_up
        nuyd_ref[x] = nu_down
        add(1, nu_up, nu_down)
        rim = [edge_of(halo, c * planes + x) for c in range(4)]
        over = [jnp.where(lane == width - 1, rim[c], pltpu.roll(here[c], width - 1, 1)) for c in range(4)]
        under = [jnp.where(lane == 0, rim[c], pltpu.roll(here[c], 1, 1)) for c in range(4)]
        nu_up = viscosity([over[c] - here[c] for c in range(3)])
        nu_down = viscosity([here[c] - under[c] for c in range(3)])
        nuzu_ref[x] = nu_up
        nuzd_ref[x] = nu_down
        add(2, nu_up, nu_down)
        edge_nu = time_step * jnp.where(lane == width - 1, nu_up, jnp.where(lane == 0, nu_down, 0.0))
        kz_ref[x] = edge_nu
        kpack = pack_edges(kpack, edge_nu, x, lane)
        for c in range(3):
            value = here[c] + time_step * (total[c] - pressure[c])
            next_ref[c, x] = value
            vpack = pack_edges(vpack, value, c * planes + x, lane)
        vpack = pack_edges(vpack, regions_ref[x].astype(jnp.float32), 3 * planes + x, lane)
        return kpack, vpack

    blank = jnp.zeros((rows, width), jnp.float32)
    kpack, vpack = lax.fori_loop(0, planes, plane, (blank, blank))
    kpack_ref[...] = kpack
    vpack_ref[...] = vpack

    taken_ref[...] = jnp.zeros_like(taken_ref)
    slot_rows = groups * extra
    _, slot_lane = iotas(8, slot_rows)

    def slot(s, cell_of):
        b = s // cap
        first = b * extra + (s - b * cap) * 3
        cell = cells_ref[s]
        for c in range(3):
            taken_ref[pl.ds(first + c, 1), :] = next_ref[c, cell // rows, pl.ds(cell % rows, 1), :]
        return jnp.where((slot_lane >= first) & (slot_lane < first + 3), cell, cell_of)

    cell_of = lax.fori_loop(0, groups * cap, slot, jnp.full((8, slot_rows), -1, jnp.int32), unroll=4)
    values_ref[...] = taken_ref[...].astype(jnp.bfloat16).reshape(values_ref.shape)
    lines, slot_lane = iotas(planes * rows, slot_rows)
    hit = lines == cell_of[0:1, :]
    part = (slot_lane % extra) % 3
    for c in range(3):
        pick_ref[c] = (hit & (part == c)).astype(jnp.float32).astype(jnp.bfloat16)


def forcing_kernel(cap, pos_ref, recv_ref, values_ref, pick_ref, forcing_ref, first_ref, second_ref, high_ref, low_ref):
    groups, extra, width = values_ref.shape
    _, planes, rows, _ = forcing_ref.shape
    depth = cap * width
    row, lane = iotas(extra, depth)
    own = row // 3 == lane // width
    for b in range(groups):
        weights = recv_ref[b, pl.ds(0, depth), :]
        predicted = lax.dot_general(
            values_ref[b], weights, (((1,), (1,)), ((), ())), preferred_element_type=jnp.float32
        )
        seen = recv_ref[b, pl.ds(depth, extra), :].astype(jnp.float32)
        misfit = jnp.where(own, predicted - jnp.concatenate([seen] * cap, axis=1), 0.0).astype(jnp.bfloat16)
        contrib = jnp.dot(misfit, weights, preferred_element_type=jnp.float32)
        high = contrib.astype(jnp.bfloat16)
        high_ref[pl.ds(b * extra, extra), :] = high
        low_ref[pl.ds(b * extra, extra), :] = (contrib - high.astype(jnp.float32)).astype(jnp.bfloat16)
    even = pos_ref[0] % 2 == 0
    for c in range(3):
        total = jnp.dot(pick_ref[c], high_ref[...], preferred_element_type=jnp.float32)
        total += jnp.dot(pick_ref[c], low_ref[...], preferred_element_type=jnp.float32)
        forcing_ref[c] = total.reshape(planes, rows, width)
        low, high = total[:rows], total[(planes - 1) * rows :]
        first_ref[c] = jnp.where(even, high, low)
        second_ref[c] = jnp.where(even, low, high)


def region_sums(product_ref, region_ref, sums_ref, plus_ref=None):
    count = sums_ref.shape[0]
    rows, width = product_ref.shape
    step = 32

    def group(g, carry):
        sums = [jnp.zeros((8, width), jnp.float32)] * 8
        for r in range(0, rows, step):
            values = product_ref[r : r + step, :]
            ids = region_ref[r : r + step, :] - g * 8
            for i in range(8):
                chosen = jnp.where(ids == i, values, 0.0)
                for s in range(0, step, 8):
                    sums[i] = sums[i] + chosen[s : s + 8]
        block = jnp.concatenate([jnp.sum(part, axis=0, keepdims=True) for part in sums], axis=0)
        at = pl.ds(pl.multiple_of(g * 8, 8), 8)
        sums_ref[at, :] = block if plus_ref is None else block + plus_ref[at, :]
        return carry

    lax.fori_loop(0, count // 8, group, 0)


def inner_kernel(
    walls, pos_ref, forcing_ref, next_ref, nux_ref, nuyu_ref, nuyd_ref, nuzu_ref, nuzd_ref, kpack_ref, regions_ref, v0_ref, v1_ref,
    adjoint_ref, fpack_ref, sums_ref, product_ref, ids_ref,
):
    _, planes, rows, width = forcing_ref.shape
    row, lane = iotas(rows, width)

    def plane(x, fpack):
        nus = (nux_ref[x + 1], nux_ref[x], nuyu_ref[x], nuyd_ref[x], nuzu_ref[x], nuzd_ref[x])
        next_up, next_down = jnp.minimum(x + 1, planes - 1), jnp.maximum(x - 1, 0)
        at_top, at_bottom = x == planes - 1, x == 0
        product = None
        for c in range(3):
            here = forcing_ref[c, x]
            over = jnp.where(at_top, 0.0, forcing_ref[c, next_up])
            under = jnp.where(at_bottom, 0.0, forcing_ref[c, next_down])
            total = nus[0] * (over - here) - nus[1] * (here - under)
            over = jnp.where(row == rows - 1, 0.0, pltpu.roll(here, rows - 1, 0))
            under = jnp.where(row == 0, 0.0, pltpu.roll(here, 1, 0))
            total += nus[2] * (over - here) - nus[3] * (here - under)
            over = jnp.where(lane == width - 1, 0.0, pltpu.roll(here, width - 1, 1))
            under = jnp.where(lane == 0, 0.0, pltpu.roll(here, 1, 1))
            total += nus[4] * (over - here) - nus[5] * (here - under)
            value = here + time_step * total
            adjoint_ref[c, x] = value
            part = value * next_ref[c, x]
            product = part if product is None else product + part
            fpack = pack_edges(fpack, here, c * planes + x, lane)
        at = pl.ds(pl.multiple_of(x * rows, rows), rows)
        product_ref[at, :] = product
        ids_ref[at, :] = regions_ref[x]
        return fpack

    fpack = lax.fori_loop(0, planes, plane, jnp.zeros((rows, width), jnp.float32))
    fpack_ref[...] = fpack
    below, above = from_neighbours(pos_ref[1], walls, v0_ref[...], v1_ref[...])
    mixed = mix_edges(below, above, lane)
    reach = pltpu.roll(fpack, 1, 1) * mixed
    reach = reach + pltpu.roll(reach, width - 2 * planes, 1) + pltpu.roll(reach, width - 4 * planes, 1)
    reach = jnp.where(lane < 2 * planes, reach * pltpu.roll(kpack_ref[...], 1, 1), 0.0)
    product_ref[pl.ds(planes * rows, rows), :] = reach
    ids_ref[pl.ds(planes * rows, rows), :] = pltpu.roll(mixed, (width - 6 * planes) % width, 1).astype(jnp.int32)
    region_sums(product_ref, ids_ref, sums_ref)


def edge_kernel(
    sizes, masks, pos_ref, x0_ref, x1_ref, nux_ref, next_ref, regions_ref, sums_ref, fpack_ref, *refs
):
    groups, walls = sizes
    outs, (product_ref, ids_ref, total_ref) = refs[:-3], refs[-3:]
    _, planes, rows, width = next_ref.shape
    low, high = 0.0, 0.0
    for c in range(3):
        below, above = from_neighbours(pos_ref[0], groups, x0_ref[c], x1_ref[c])
        low += below * next_ref[c, 0]
        high += above * next_ref[c, planes - 1]
    product_ref[:rows, :] = time_step * nux_ref[0] * low
    product_ref[rows:, :] = time_step * nux_ref[planes] * high
    ids_ref[:rows, :] = regions_ref[0]
    ids_ref[rows:, :] = regions_ref[planes - 1]
    region_sums(product_ref, ids_ref, total_ref, sums_ref)
    per = total_ref.shape[0] // walls
    for mask, out_ref in zip((0,) + masks, outs):
        target = pos_ref[1] ^ mask
        out_ref[:per, :] = total_ref[pl.ds(pl.multiple_of(target * per, per), per), :]
        if out_ref.shape[0] > per:
            out_ref[per:, :] = fpack_ref[...]


def final_kernel(sizes, pos_ref, inner_ref, x0_ref, x1_ref, nux_ref, kz_ref, own_ref, *refs):
    groups, walls = sizes
    arrived, adjoint_ref, sens_ref = refs[:-2], refs[-2], refs[-1]
    _, planes, rows, width = inner_ref.shape
    per = own_ref.shape[0]
    _, lane = iotas(rows, width)
    me = pos_ref[1]
    total = own_ref[...]
    below = jnp.zeros((rows, width), jnp.float32)
    above = jnp.zeros((rows, width), jnp.float32)
    for mask, ref in zip(range(1, walls), arrived):
        total = total + ref[:per, :]
        if ref.shape[0] > per:
            edges = ref[per:, :]
            above = jnp.where((me ^ mask) == me + 1, edges, above)
            below = jnp.where((me ^ mask) == me - 1, edges, below)
    sens_ref[...] = sens_scale * lax.dot_general(
        jnp.ones((8, width), jnp.float32), total, (((1,), (1,)), ((), ())),
        precision=lax.Precision.HIGHEST, preferred_element_type=jnp.float32,
    )[:1]
    mixed = mix_edges(below, above, lane)

    def plane(x, carry):
        edge_nu = kz_ref[x]
        for c in range(3):
            adjoint_ref[c, x] = inner_ref[c, x] + edge_nu * edge_of(mixed, c * planes + x)
        return carry

    lax.fori_loop(0, planes, plane, 0, unroll=4)
    for c in range(3):
        low, high = from_neighbours(pos_ref[0], groups, x0_ref[c], x1_ref[c])
        adjoint_ref[c, 0] += time_step * nux_ref[0] * low
        adjoint_ref[c, planes - 1] += time_step * nux_ref[planes] * high


def body(flow_state, regions, obs_tiles, measured, tile_dest, cell_list):
    groups, walls = lax.axis_size("fluid"), lax.axis_size("wall")
    sizes = (groups, walls)
    _, planes, rows, width = flow_state.shape
    count_tiles = obs_tiles.shape[2]
    cap = cell_list.shape[3]
    extra = -(-cap * 3 // 16) * 16
    reg_count = REG_DEV * walls
    cells = groups * cap
    grid = planes * rows * width
    pos = jnp.stack([lax.axis_index("fluid"), lax.axis_index("wall")]).astype(jnp.int32)

    send = call(
        functools.partial(group_kernel, cap),
        bf16(groups, cap * width + extra, width),
        [SMEM, ANY, VMEM],
        (tile_dest[0, 0], obs_tiles[0, 0], measured[0, 0]),
        (
            pltpu.SMEM((groups,), jnp.int32),
            pltpu.VMEM((groups * extra, width), jnp.bfloat16),
            pltpu.VMEM((width, width), jnp.bfloat16),
            pltpu.SemaphoreType.DMA((count_tiles,)),
            pltpu.SemaphoreType.DMA((groups,)),
            pltpu.SemaphoreType.DMA,
        ),
        moved=4 * count_tiles * width * width,
        out_specs=ANY,
    )
    recv = lax.all_to_all(send, "fluid", split_axis=0, concat_axis=0, tiled=True)

    xs0, xs1, zs = call(
        faces_kernel,
        (f32(4, rows, width), f32(4, rows, width), f32(rows, width)),
        [SMEM, VMEM],
        (pos, flow_state),
        moved=16 * grid,
    )
    x0, x1 = swap(xs0, "fluid", 0), swap(xs1, "fluid", 1)
    z0, z1 = swap(zs, "wall", 0), swap(zs, "wall", 1)
    velocity_next, nux, nuyu, nuyd, nuzu, nuzd, kz, kpack, vpack, values, pick = call(
        functools.partial(forward_kernel, sizes, cap),
        (f32(3, planes, rows, width), f32(planes + 1, rows, width))
        + (f32(planes, rows, width),) * 5
        + (f32(rows, width),) * 2
        + (bf16(groups, extra, width), bf16(3, planes * rows, groups * extra)),
        [SMEM, SMEM] + [VMEM] * 6,
        (pos, cell_list[0, 0].reshape(cells), flow_state, regions, x0, x1, z0, z1),
        (pltpu.VMEM((4, planes + 2, rows, width), jnp.float32), pltpu.VMEM((groups * extra, width), jnp.float32)),
        flops=200 * grid,
        moved=60 * grid,
    )
    v0, v1 = swap(vpack, "wall", 0), swap(vpack, "wall", 1)

    forcing, fs0, fs1 = call(
        functools.partial(forcing_kernel, cap),
        (f32(3, planes, rows, width), f32(3, rows, width), f32(3, rows, width)),
        [SMEM] + [VMEM] * 3,
        (pos, recv, values, pick),
        (pltpu.VMEM((groups * extra, width), jnp.bfloat16),) * 2,
        flops=4 * cells * 16 * width * width,
        moved=2 * cells * width * width + 12 * grid,
    )
    f0, f1 = swap(fs0, "fluid", 0), swap(fs1, "fluid", 1)
    inner, fpack, sums = call(
        functools.partial(inner_kernel, walls),
        (f32(3, planes, rows, width), f32(rows, width), f32(reg_count, width)),
        [SMEM] + [VMEM] * 11,
        (pos, forcing, velocity_next, nux, nuyu, nuyd, nuzu, nuzd, kpack, regions, v0, v1),
        (pltpu.VMEM(((planes + 1) * rows, width), jnp.float32), pltpu.VMEM(((planes + 1) * rows, width), jnp.int32)),
        flops=300 * grid,
        moved=60 * grid,
    )
    masks = tuple(range(1, walls))
    heights = [REG_DEV] + [REG_DEV + (rows if mask & (mask + 1) == 0 else 0) for mask in masks]
    own, *parts = call(
        functools.partial(edge_kernel, sizes, masks),
        tuple(f32(height, width) for height in heights),
        [SMEM] + [VMEM] * 7,
        (pos, f0, f1, nux, velocity_next, regions, sums, fpack),
        (
            pltpu.VMEM((2 * rows, width), jnp.float32),
            pltpu.VMEM((2 * rows, width), jnp.int32),
            pltpu.VMEM((reg_count, width), jnp.float32),
        ),
        flops=20 * grid,
        moved=4 * grid,
    )
    arrived = [cross(part, "wall", mask) for part, mask in zip(parts, masks)]
    adjoint, sens = call(
        functools.partial(final_kernel, sizes),
        (f32(3, planes, rows, width), f32(1, REG_DEV)),
        [SMEM] + [VMEM] * (6 + len(arrived)),
        (pos, inner, f0, f1, nux, kz, own, *arrived),
        flops=10 * grid,
        moved=24 * grid,
    )
    return velocity_next, adjoint, sens.reshape(REG_DEV)


def solution(mesh):
    in_specs = (
        P(None, "fluid", None, "wall"),
        P("fluid", None, "wall"),
        P("fluid", "wall", None, None, None),
        P("fluid", "wall", None, None, None),
        P("fluid", "wall", None),
        P("fluid", "wall", None, None),
    )
    out_specs = (
        P(None, "fluid", None, "wall"),
        P(None, "fluid", None, "wall"),
        P(("fluid", "wall")),
    )
    return jax.shard_map(body, mesh=mesh, in_specs=in_specs, out_specs=out_specs, check_vma=False)
```

```python
import functools

import jax
import jax.numpy as jnp
from jax import lax
from jax.experimental import pallas as pl
from jax.experimental.pallas import tpu as pltpu
from jax.sharding import PartitionSpec as P

REG_DEV = 16

time_step = 0.12
nu_floor = 0.1
nu_spread = 0.9
relax_sq = 4.0
sens_scale = 0.03

VMEM = pl.BlockSpec(memory_space=pltpu.VMEM)
SMEM = pl.BlockSpec(memory_space=pltpu.SMEM)
ANY = pl.BlockSpec(memory_space=pl.ANY)
HBM = pl.BlockSpec(memory_space=pltpu.HBM)
LIMIT = 24 * 1024 * 1024


def call(kernel, outs, ins, operands, scratch=(), flops=1, moved=1, out_specs=None, limit=LIMIT):
    return pl.pallas_call(
        kernel,
        out_shape=outs,
        in_specs=ins,
        out_specs=out_specs if out_specs is not None else jax.tree.map(lambda _: VMEM, outs),
        scratch_shapes=list(scratch),
        compiler_params=pltpu.CompilerParams(vmem_limit_bytes=limit),
        cost_estimate=pl.CostEstimate(flops=flops, bytes_accessed=moved, transcendentals=0),
    )(*operands)


def f32(*shape):
    return jax.ShapeDtypeStruct(shape, jnp.float32)


def bf16(*shape):
    return jax.ShapeDtypeStruct(shape, jnp.bfloat16)


def swap(block, axis, turn):
    count = lax.axis_size(axis)
    pairs = [(i, (i + 1) % count if (i + turn) % 2 == 0 else (i - 1) % count) for i in range(count)]
    return lax.ppermute(block, axis, pairs)


def cross(block, axis, mask):
    return lax.ppermute(block, axis, [(i, i ^ mask) for i in range(lax.axis_size(axis))])


def from_neighbours(index, count, first, second):
    even = index % 2 == 0
    above = jnp.where(even, first, second)
    below = jnp.where(even, second, first)
    above = jnp.where(index == count - 1, jnp.zeros_like(above), above)
    below = jnp.where(index == 0, jnp.zeros_like(below), below)
    return below, above


def pack_edges(packed, plane, m, lane):
    width = lane.shape[1]
    here = (lane == 2 * m) | (lane == (2 * m + width - 1) % width)
    return jnp.where(here, pltpu.roll(plane, 2 * m, 1), packed)


def mix_edges(below, above, lane):
    return jnp.where(lane % 2 == 0, above, pltpu.roll(below, 2, 1))


def edge_of(mixed, m):
    width = mixed.shape[1]
    return pltpu.roll(mixed, (2 * width - (2 * m + 1)) % width, 1)


def viscosity(jumps):
    shear_sq = jumps[0] * jumps[0] + jumps[1] * jumps[1] + jumps[2] * jumps[2]
    root = lax.rsqrt(1.0 + relax_sq * shear_sq)
    return nu_floor + nu_spread * (root * lax.rsqrt(root))


def iotas(rows, width):
    shape = (rows, width)
    return lax.broadcasted_iota(jnp.int32, shape, 0), lax.broadcasted_iota(jnp.int32, shape, 1)


def faces_kernel(flow_ref, first_ref, second_ref, sems):
    last = flow_ref.shape[1] - 1
    odd = lax.axis_index("fluid") % 2
    copies = [
        pltpu.make_async_copy(flow_ref.at[:, plane], out_ref, sems.at[i])
        for i, (plane, out_ref) in enumerate(((last - last * odd, first_ref), (last * odd, second_ref)))
    ]
    for copy in copies:
        copy.start()
    for copy in copies:
        copy.wait()


def edges_kernel(groups, flow_ref, regions_ref, x0_ref, x1_ref, edges_ref):
    fields, planes, rows, width = flow_ref.shape
    _, lane = iotas(rows, width)
    outer = jnp.zeros((rows, width), jnp.float32)
    second, beside = outer, outer
    for c in range(fields):
        for x in range(planes):
            m, plane = c * planes + x, flow_ref[c, x]
            outer = pack_edges(outer, plane, m, lane)
            second = jnp.where(lane == 2 * m, pltpu.roll(plane, (2 * m - 1) % width, 1), second)
            second = jnp.where(lane == (2 * m - 1) % width, pltpu.roll(plane, (2 * m + 1) % width, 1), second)
        for side, plane in enumerate(from_neighbours(lax.axis_index("fluid"), groups, x0_ref[c], x1_ref[c])):
            beside = pack_edges(beside, plane, 2 * c + side, lane)
    for x in range(planes):
        beside = pack_edges(beside, regions_ref[x].astype(jnp.float32), 2 * fields + x, lane)
    edges_ref[0], edges_ref[1], edges_ref[2] = outer, second, beside


def outside_edges(walls, planes, halo, second, beside, inside, rim_nu):
    rows, width = halo.shape
    row, lane = iotas(rows, width)
    x, field = (lane // 2) % planes, (lane // 2) // planes

    def spread(nu):
        nu = jnp.where(field == 0, nu, 0.0)
        return nu + pltpu.roll(nu, 2 * planes, 1) + pltpu.roll(nu, 4 * planes, 1)

    def nu_of(jump):
        return spread(viscosity([jump] + [pltpu.roll(jump, width - 2 * c * planes, 1) for c in (1, 2)]))

    over_x, under_x = pltpu.roll(halo, width - 2, 1), pltpu.roll(halo, 2, 1)
    for c in range(4):
        low = pltpu.roll(beside, (2 * c * planes - 4 * c) % width, 1)
        high = pltpu.roll(beside, (2 * (c * planes + planes - 1) - 4 * c - 2) % width, 1)
        under_x = jnp.where((x == 0) & (field == c), low, under_x)
        over_x = jnp.where((x == planes - 1) & (field == c), high, over_x)
    over_y = jnp.where(row == rows - 1, 0.0, pltpu.roll(halo, rows - 1, 0))
    under_y = jnp.where(row == 0, 0.0, pltpu.roll(halo, 1, 0))
    total = spread(rim_nu) * (inside - halo)
    for other in (over_x, under_x, over_y, under_y, second):
        total += nu_of(other - halo) * (other - halo)
    above = lane % 2 == 0
    gradient_x = pltpu.roll(0.5 * (over_x - under_x), width - 6 * planes, 1)
    gradient_y = pltpu.roll(0.5 * (over_y - under_y), width - 4 * planes, 1)
    gradient_z = pltpu.roll(0.5 * jnp.where(above, second - inside, inside - second), width - 2 * planes, 1)
    gradient = jnp.where(field == 0, gradient_x, jnp.where(field == 1, gradient_y, gradient_z))
    value = halo + time_step * (total - gradient)
    value = jnp.where(field == 3, pltpu.roll(beside, 6 * planes - 16, 1), value)
    me = lax.axis_index("wall")
    exists = jnp.where(above, jnp.where(me < walls - 1, 1, 0), jnp.where(me > 0, 1, 0)) == 1
    return jnp.where(exists & (field < 4), value, 0.0)


def group_kernel(
    cap, dest_ref, tiles_ref, meas_ref, after_ref, send_ref,
    list_ref, held_ref, seen_ref, count_ref, rows_ref, blank_ref, list_sem, seen_sem, in_sems, out_sems, row_sems, blank_sem,
):
    count_tiles, width, _ = tiles_ref.shape
    groups = send_ref.shape[0]
    slots = groups * cap
    extra = rows_ref.shape[0] // groups
    listed = pltpu.make_async_copy(dest_ref, list_ref, list_sem)
    listed.start()

    piece = count_tiles // in_sems.shape[0]

    def load(p):
        part = pl.ds(p * piece, piece)
        return pltpu.make_async_copy(tiles_ref.at[part], held_ref.at[part], in_sems.at[p])

    for p in range(in_sems.shape[0]):
        load(p).start()
    seen = pltpu.make_async_copy(meas_ref, seen_ref, seen_sem)
    seen.start()

    def clear(b, carry):
        count_ref[b] = 0
        return carry

    lax.fori_loop(0, groups, clear, 0)
    _, tile_lane = iotas(8, count_tiles)
    listed.wait()

    def store(t, b, k):
        return pltpu.make_async_copy(
            held_ref.at[t], send_ref.at[b, pl.ds(pl.multiple_of(k * width, width), width), :], out_sems.at[t]
        )

    def send_one(t, slot_of):
        b = list_ref[t]
        k = count_ref[b]
        count_ref[b] = k + 1
        store(t, b, k).start()
        return jnp.where(tile_lane == t, b * cap + k, slot_of)

    slot_of = jnp.full((8, count_tiles), -1, jnp.int32)
    for p in range(in_sems.shape[0]):
        load(p).wait()
        slot_of = lax.fori_loop(p * piece, (p + 1) * piece, send_one, slot_of, unroll=True)

    if slots > count_tiles:
        blank_ref[...] = jnp.zeros_like(blank_ref)

        def blanks(b, carry):
            def one(k, inner):
                copy = pltpu.make_async_copy(
                    blank_ref, send_ref.at[b, pl.ds(pl.multiple_of(k * width, width), width), :], blank_sem
                )
                copy.start()
                copy.wait()
                return inner

            return lax.fori_loop(count_ref[b], cap, one, carry)

        lax.fori_loop(0, groups, blanks, 0)

    seen.wait()
    row = lax.broadcasted_iota(jnp.int32, (groups * extra, count_tiles), 0)
    within = row % extra
    row_slot = (row // extra) * cap + within // 3
    used = within < cap * 3
    total = jnp.zeros((groups * extra, width), jnp.float32)
    for c in range(3):
        pick = (row_slot == slot_of[0:1, :]) & used & (within % 3 == c)
        total += jnp.dot(
            pick.astype(jnp.float32).astype(jnp.bfloat16), seen_ref[c], preferred_element_type=jnp.float32
        )
    rows_ref[...] = total.astype(jnp.bfloat16)

    def row_copy(b):
        return pltpu.make_async_copy(
            rows_ref.at[pl.ds(b * extra, extra), :], send_ref.at[b, pl.ds(cap * width, extra), :], row_sems.at[b]
        )

    for b in range(groups):
        row_copy(b).start()

    def finish(t, carry):
        store(t, 0, 0).wait()
        return carry

    lax.fori_loop(0, count_tiles, finish, 0, unroll=4)
    for b in range(groups):
        row_copy(b).wait()


def forward_kernel(
    sizes, cap, cells_ref, flow_ref, x0_ref, x1_ref, z0_ref, z1_ref, edges_ref,
    next_ref, nux_ref, nuy_ref, nuz_ref, nuy0_ref, rim_ref, outside_ref, values_ref, pick_ref,
    padded_ref, taken_ref,
):
    _, planes, rows, width = flow_ref.shape
    groups, walls = sizes
    extra = values_ref.shape[1]
    row, lane = iotas(rows, width)
    halo, second, beside = (
        mix_edges(*from_neighbours(lax.axis_index("wall"), walls, z0_ref[i], z1_ref[i]), lane) for i in range(3)
    )
    inside = pltpu.roll(edges_ref[0], 1, 1)
    jump = halo - inside
    rim_nu = viscosity([jump] + [pltpu.roll(jump, width - 2 * c * planes, 1) for c in (1, 2)])
    rim_nu = jnp.where(lane < 2 * planes, rim_nu, 0.0)
    rim_ref[...] = rim_nu
    outside_ref[...] = outside_edges(walls, planes, halo, second, beside, inside, rim_nu)
    for c in range(4):
        low, high = from_neighbours(lax.axis_index("fluid"), groups, x0_ref[c], x1_ref[c])
        padded_ref[c, 0] = low
        padded_ref[c, planes + 1] = high
        padded_ref[c, 1 : planes + 1] = flow_ref[c]
    nux_ref[0] = viscosity([padded_ref[c, 1] - padded_ref[c, 0] for c in range(3)])

    def plane(x, carry):
        here = [padded_ref[c, x + 1] for c in range(4)]
        over = [padded_ref[c, x + 2] for c in range(4)]
        under = [padded_ref[c, x] for c in range(4)]
        total = [None] * 3
        pressure = [None] * 3

        def add(axis, nu_up, nu_down):
            for c in range(3):
                flux = nu_up * (over[c] - here[c]) - nu_down * (here[c] - under[c])
                total[c] = flux if total[c] is None else total[c] + flux
            pressure[axis] = 0.5 * (over[3] - under[3])

        nu_up = viscosity([over[c] - here[c] for c in range(3)])
        nux_ref[x + 1] = nu_up
        add(0, nu_up, nux_ref[x])
        over = [jnp.where(row == rows - 1, 0.0, pltpu.roll(here[c], rows - 1, 0)) for c in range(4)]
        under = [jnp.where(row == 0, 0.0, pltpu.roll(here[c], 1, 0)) for c in range(4)]
        nu_up = viscosity([over[c] - here[c] for c in range(3)])
        nu_first = viscosity([here[c][:1] for c in range(3)])
        nuy_ref[x] = nu_up
        nuy0_ref[pl.ds(x, 1), :] = nu_first
        add(1, nu_up, jnp.where(row == 0, nu_first, pltpu.roll(nu_up, 1, 0)))
        rim = [edge_of(halo, c * planes + x) for c in range(4)]
        over = [jnp.where(lane == width - 1, rim[c], pltpu.roll(here[c], width - 1, 1)) for c in range(4)]
        under = [jnp.where(lane == 0, rim[c], pltpu.roll(here[c], 1, 1)) for c in range(4)]
        nu_up = viscosity([over[c] - here[c] for c in range(3)])
        nuz_ref[x] = nu_up
        add(2, nu_up, jnp.where(lane == 0, edge_of(rim_nu, x), pltpu.roll(nu_up, 1, 1)))
        for c in range(3):
            value = here[c] + time_step * (total[c] - pressure[c])
            next_ref[c, x] = value
        return carry

    lax.fori_loop(0, planes, plane, 0, unroll=4)

    taken_ref[...] = jnp.zeros_like(taken_ref)
    slot_rows = groups * extra
    _, slot_lane = iotas(8, slot_rows)

    def slot(s, cell_of):
        b = s // cap
        first = b * extra + (s - b * cap) * 3
        cell = cells_ref[s - b * cap, b]
        for c in range(3):
            taken_ref[pl.ds(first + c, 1), :] = next_ref[c, cell // rows, pl.ds(cell % rows, 1), :]
        return jnp.where((slot_lane >= first) & (slot_lane < first + 3), cell, cell_of)

    cell_of = lax.fori_loop(0, groups * cap, slot, jnp.full((8, slot_rows), -1, jnp.int32), unroll=4)
    values_ref[...] = taken_ref[...].astype(jnp.bfloat16).reshape(values_ref.shape)
    lines, slot_lane = iotas(planes * rows, slot_rows)
    hit = lines == cell_of[0:1, :]
    part = (slot_lane % extra) % 3
    for c in range(3):
        pick_ref[c] = (hit & (part == c)).astype(jnp.float32).astype(jnp.bfloat16)


def forcing_kernel(
    cap, recv_ref, values_ref, pick_ref, forcing_ref, first_ref, second_ref, high_ref, low_ref
):
    groups, extra, width = values_ref.shape
    _, planes, rows, _ = forcing_ref.shape
    depth = cap * width
    row, lane = iotas(extra, depth)
    own = row // 3 == lane // width
    for b in range(groups):
        weights = recv_ref[b, pl.ds(0, depth), :]
        predicted = lax.dot_general(
            values_ref[b], weights, (((1,), (1,)), ((), ())), preferred_element_type=jnp.float32
        )
        seen = recv_ref[b, pl.ds(depth, extra), :].astype(jnp.float32)
        misfit = jnp.where(own, predicted - jnp.concatenate([seen] * cap, axis=1), 0.0).astype(jnp.bfloat16)
        contrib = jnp.dot(misfit, weights, preferred_element_type=jnp.float32)
        high = contrib.astype(jnp.bfloat16)
        high_ref[pl.ds(b * extra, extra), :] = high
        low_ref[pl.ds(b * extra, extra), :] = (contrib - high.astype(jnp.float32)).astype(jnp.bfloat16)
    even = lax.axis_index("fluid") % 2 == 0
    for c in range(3):
        total = jnp.dot(pick_ref[c], high_ref[...], preferred_element_type=jnp.float32)
        total += jnp.dot(pick_ref[c], low_ref[...], preferred_element_type=jnp.float32)
        forcing_ref[c] = total.reshape(planes, rows, width)
        low, high = total[:rows], total[(planes - 1) * rows :]
        first_ref[c] = jnp.where(even, high, low)
        second_ref[c] = jnp.where(even, low, high)


def region_sums(product_ref, region_ref, sums_ref, plus_ref=None):
    count = sums_ref.shape[0]
    rows, width = product_ref.shape
    step = 32

    def group(g, carry):
        sums = [jnp.zeros((8, width), jnp.float32)] * 8
        for r in range(0, rows, step):
            values = product_ref[r : r + step, :]
            ids = region_ref[r : r + step, :] - g * 8
            for i in range(8):
                chosen = jnp.where(ids == i, values, 0.0)
                for s in range(0, step, 8):
                    sums[i] = sums[i] + chosen[s : s + 8]
        block = jnp.concatenate([jnp.sum(part, axis=0, keepdims=True) for part in sums], axis=0)
        at = pl.ds(pl.multiple_of(g * 8, 8), 8)
        sums_ref[at, :] = block if plus_ref is None else block + plus_ref[at, :]
        return carry

    lax.fori_loop(0, count // 8, group, 0)


def inner_kernel(
    forcing_ref, next_ref, nux_ref, nuy_ref, nuz_ref, nuy0_ref, rim_ref, regions_ref, outside_ref,
    adjoint_ref, fpack_ref, sums_ref, product_ref, ids_ref,
):
    _, planes, rows, width = forcing_ref.shape
    row, lane = iotas(rows, width)
    rim_nu = rim_ref[...]

    def plane(x, fpack):
        nuy, nuz = nuy_ref[x], nuz_ref[x]
        nuy_down = jnp.where(row == 0, nuy0_ref[pl.ds(x, 1), :], pltpu.roll(nuy, 1, 0))
        nuz_down = jnp.where(lane == 0, edge_of(rim_nu, x), pltpu.roll(nuz, 1, 1))
        nus = (nux_ref[x + 1], nux_ref[x], nuy, nuy_down, nuz, nuz_down)
        next_up, next_down = jnp.minimum(x + 1, planes - 1), jnp.maximum(x - 1, 0)
        at_top, at_bottom = x == planes - 1, x == 0
        product = None
        for c in range(3):
            here = forcing_ref[c, x]
            over = jnp.where(at_top, 0.0, forcing_ref[c, next_up])
            under = jnp.where(at_bottom, 0.0, forcing_ref[c, next_down])
            total = nus[0] * (over - here) - nus[1] * (here - under)
            over = jnp.where(row == rows - 1, 0.0, pltpu.roll(here, rows - 1, 0))
            under = jnp.where(row == 0, 0.0, pltpu.roll(here, 1, 0))
            total += nus[2] * (over - here) - nus[3] * (here - under)
            over = jnp.where(lane == width - 1, 0.0, pltpu.roll(here, width - 1, 1))
            under = jnp.where(lane == 0, 0.0, pltpu.roll(here, 1, 1))
            total += nus[4] * (over - here) - nus[5] * (here - under)
            value = here + time_step * total
            adjoint_ref[c, x] = value
            part = value * next_ref[c, x]
            product = part if product is None else product + part
            fpack = pack_edges(fpack, here, c * planes + x, lane)
        at = pl.ds(pl.multiple_of(x * rows, rows), rows)
        product_ref[at, :] = product
        ids_ref[at, :] = regions_ref[x]
        return fpack

    fpack = lax.fori_loop(0, planes, plane, jnp.zeros((rows, width), jnp.float32), unroll=4)
    fpack_ref[...] = fpack
    mixed = outside_ref[...]
    reach = pltpu.roll(fpack, 1, 1) * mixed
    reach = reach + pltpu.roll(reach, width - 2 * planes, 1) + pltpu.roll(reach, width - 4 * planes, 1)
    reach = time_step * reach * rim_nu
    product_ref[pl.ds(planes * rows, rows), :] = reach
    ids_ref[pl.ds(planes * rows, rows), :] = pltpu.roll(mixed, (width - 6 * planes) % width, 1).astype(jnp.int32)
    region_sums(product_ref, ids_ref, sums_ref)


def edge_kernel(
    sizes, masks, x0_ref, x1_ref, nux_ref, next_ref, regions_ref, sums_ref, fpack_ref, *refs
):
    groups, walls = sizes
    outs, (product_ref, ids_ref, total_ref) = refs[:-3], refs[-3:]
    _, planes, rows, width = next_ref.shape
    low, high = 0.0, 0.0
    for c in range(3):
        below, above = from_neighbours(lax.axis_index("fluid"), groups, x0_ref[c], x1_ref[c])
        low += below * next_ref[c, 0]
        high += above * next_ref[c, planes - 1]
    product_ref[:rows, :] = time_step * nux_ref[0] * low
    product_ref[rows:, :] = time_step * nux_ref[planes] * high
    ids_ref[:rows, :] = regions_ref[0]
    ids_ref[rows:, :] = regions_ref[planes - 1]
    region_sums(product_ref, ids_ref, total_ref, sums_ref)
    per = total_ref.shape[0] // walls
    for mask, out_ref in zip((0,) + masks, outs):
        target = lax.axis_index("wall") ^ mask
        out_ref[:per, :] = total_ref[pl.ds(pl.multiple_of(target * per, per), per), :]
        if out_ref.shape[0] > per:
            out_ref[per:, :] = fpack_ref[...]


def final_kernel(sizes, inner_ref, x0_ref, x1_ref, nux_ref, rim_ref, own_ref, *refs):
    groups, walls = sizes
    arrived, adjoint_ref, sens_ref = refs[:-2], refs[-2], refs[-1]
    _, planes, rows, width = inner_ref.shape
    per = own_ref.shape[0]
    _, lane = iotas(rows, width)
    me = lax.axis_index("wall")
    total = own_ref[...]
    below = jnp.zeros((rows, width), jnp.float32)
    above = jnp.zeros((rows, width), jnp.float32)
    for mask, ref in zip(range(1, walls), arrived):
        total = total + ref[:per, :]
        if ref.shape[0] > per:
            edges = ref[per:, :]
            above = jnp.where((me ^ mask) == me + 1, edges, above)
            below = jnp.where((me ^ mask) == me - 1, edges, below)
    sens_ref[...] = sens_scale * lax.dot_general(
        jnp.ones((8, width), jnp.float32), total, (((1,), (1,)), ((), ())),
        precision=lax.Precision.HIGHEST, preferred_element_type=jnp.float32,
    )[:1]
    mixed = mix_edges(below, above, lane)
    edge_nu = time_step * rim_ref[...]
    edge_nu = edge_nu + pltpu.roll(edge_nu, 2 * planes, 1) + pltpu.roll(edge_nu, 4 * planes, 1)
    edge_flux = mixed * edge_nu
    on_edge = (lane == 0) | (lane == width - 1)

    def plane(x, carry):
        for c in range(3):
            edge = edge_of(edge_flux, c * planes + x)
            adjoint_ref[c, x] = inner_ref[c, x] + jnp.where(on_edge, edge, 0.0)
        return carry

    lax.fori_loop(0, planes, plane, 0, unroll=4)
    for c in range(3):
        low, high = from_neighbours(lax.axis_index("fluid"), groups, x0_ref[c], x1_ref[c])
        adjoint_ref[c, 0] += time_step * nux_ref[0] * low
        adjoint_ref[c, planes - 1] += time_step * nux_ref[planes] * high


def body(flow_state, regions, obs_tiles, measured, tile_dest, cell_list):
    groups, walls = lax.axis_size("fluid"), lax.axis_size("wall")
    sizes = (groups, walls)
    _, planes, rows, width = flow_state.shape
    count_tiles = obs_tiles.shape[2]
    cap = cell_list.shape[3]
    extra = -(-cap * 3 // 16) * 16
    reg_count = REG_DEV * walls
    cells = groups * cap
    grid = planes * rows * width

    xs0, xs1 = call(
        faces_kernel,
        (f32(4, rows, width), f32(4, rows, width)),
        [HBM],
        (flow_state,),
        (pltpu.SemaphoreType.DMA((2,)),),
        limit=60 * 1024 * 1024,
    )
    x0, x1 = swap(xs0, "fluid", 0), swap(xs1, "fluid", 1)
    send = call(
        functools.partial(group_kernel, cap),
        bf16(groups, cap * width + extra, width),
        [HBM, HBM, HBM, ANY],
        (tile_dest[0, 0], obs_tiles[0, 0], jnp.transpose(measured[0, 0], (1, 0, 2)), xs1),
        (
            pltpu.SMEM((count_tiles,), jnp.int32),
            pltpu.VMEM((count_tiles, width, width), jnp.bfloat16),
            pltpu.VMEM((3, count_tiles, width), jnp.bfloat16),
            pltpu.SMEM((groups,), jnp.int32),
            pltpu.VMEM((groups * extra, width), jnp.bfloat16),
            pltpu.VMEM((width, width), jnp.bfloat16),
            pltpu.SemaphoreType.DMA,
            pltpu.SemaphoreType.DMA,
            pltpu.SemaphoreType.DMA((4,)),
            pltpu.SemaphoreType.DMA((count_tiles,)),
            pltpu.SemaphoreType.DMA((groups,)),
            pltpu.SemaphoreType.DMA,
        ),
        moved=4 * count_tiles * width * width,
        out_specs=HBM,
        limit=60 * 1024 * 1024,
    )
    send, x0, x1 = lax.optimization_barrier((send, x0, x1))
    recv = lax.all_to_all(send, "fluid", split_axis=0, concat_axis=0, tiled=True)
    zs = call(
        functools.partial(edges_kernel, groups),
        f32(3, rows, width),
        [VMEM] * 4,
        (flow_state, regions, x0, x1),
        moved=16 * grid,
    )
    z0, z1 = swap(zs, "wall", 0), swap(zs, "wall", 1)
    velocity_next, nux, nuy, nuz, nuy0, rim, outside, values, pick = call(
        functools.partial(forward_kernel, sizes, cap),
        (f32(3, planes, rows, width), f32(planes + 1, rows, width), f32(planes, rows, width), f32(planes, rows, width))
        + (f32(planes, width), f32(rows, width), f32(rows, width))
        + (bf16(groups, extra, width), bf16(3, planes * rows, groups * extra)),
        [SMEM] + [VMEM] * 6,
        (cell_list[0, 0].T, flow_state, x0, x1, z0, z1, zs),
        (pltpu.VMEM((4, planes + 2, rows, width), jnp.float32), pltpu.VMEM((groups * extra, width), jnp.float32)),
        flops=200 * grid,
        moved=60 * grid,
    )

    forcing, fs0, fs1 = call(
        functools.partial(forcing_kernel, cap),
        (f32(3, planes, rows, width), f32(3, rows, width), f32(3, rows, width)),
        [VMEM] * 3,
        (recv, values, pick),
        (pltpu.VMEM((groups * extra, width), jnp.bfloat16),) * 2,
    )
    f0, f1 = swap(fs0, "fluid", 0), swap(fs1, "fluid", 1)
    inner, fpack, sums = call(
        inner_kernel,
        (f32(3, planes, rows, width), f32(rows, width), f32(reg_count, width)),
        [VMEM] * 9,
        (forcing, velocity_next, nux, nuy, nuz, nuy0, rim, regions, outside),
        (pltpu.VMEM(((planes + 1) * rows, width), jnp.float32), pltpu.VMEM(((planes + 1) * rows, width), jnp.int32)),
    )
    masks = tuple(range(1, walls))
    heights = [REG_DEV] + [REG_DEV + (rows if mask & (mask + 1) == 0 else 0) for mask in masks]
    own, *parts = call(
        functools.partial(edge_kernel, sizes, masks),
        tuple(f32(height, width) for height in heights),
        [VMEM] * 7,
        (f0, f1, nux, velocity_next, regions, sums, fpack),
        (
            pltpu.VMEM((2 * rows, width), jnp.float32),
            pltpu.VMEM((2 * rows, width), jnp.int32),
            pltpu.VMEM((reg_count, width), jnp.float32),
        ),
        flops=20 * grid,
        moved=4 * grid,
    )
    arrived = [cross(part, "wall", mask) for part, mask in zip(parts, masks)]
    adjoint, sens = call(
        functools.partial(final_kernel, sizes),
        (f32(3, planes, rows, width), f32(1, REG_DEV)),
        [VMEM] * (6 + len(arrived)),
        (inner, f0, f1, nux, rim, own, *arrived),
        flops=10 * grid,
        moved=24 * grid,
    )
    return velocity_next, adjoint, sens.reshape(REG_DEV)


def solution(mesh):
    in_specs = (
        P(None, "fluid", None, "wall"),
        P("fluid", None, "wall"),
        P("fluid", "wall", None, None, None),
        P("fluid", "wall", None, None, None),
        P("fluid", "wall", None),
        P("fluid", "wall", None, None),
    )
    out_specs = (
        P(None, "fluid", None, "wall"),
        P(None, "fluid", None, "wall"),
        P(("fluid", "wall")),
    )
    return jax.shard_map(body, mesh=mesh, in_specs=in_specs, out_specs=out_specs, check_vma=False)
```

```python
import functools

import jax
import jax.numpy as jnp
from jax import lax
from jax.experimental import pallas as pl
from jax.experimental.pallas import tpu as pltpu
from jax.sharding import PartitionSpec as P

REG_DEV = 16

time_step = 0.12
nu_floor = 0.1
nu_spread = 0.9
relax_sq = 4.0
sens_scale = 0.03

VMEM = pl.BlockSpec(memory_space=pltpu.VMEM)
SMEM = pl.BlockSpec(memory_space=pltpu.SMEM)
ANY = pl.BlockSpec(memory_space=pl.ANY)
HBM = pl.BlockSpec(memory_space=pltpu.HBM)
LIMIT = 24 * 1024 * 1024


def call(kernel, outs, ins, operands, scratch=(), flops=1, moved=1, out_specs=None, limit=LIMIT):
    return pl.pallas_call(
        kernel,
        out_shape=outs,
        in_specs=ins,
        out_specs=out_specs if out_specs is not None else jax.tree.map(lambda _: VMEM, outs),
        scratch_shapes=list(scratch),
        compiler_params=pltpu.CompilerParams(vmem_limit_bytes=limit),
        cost_estimate=pl.CostEstimate(flops=flops, bytes_accessed=moved, transcendentals=0),
    )(*operands)


def f32(*shape):
    return jax.ShapeDtypeStruct(shape, jnp.float32)


def bf16(*shape):
    return jax.ShapeDtypeStruct(shape, jnp.bfloat16)


def swap(block, axis, turn):
    groups, walls = lax.axis_size("fluid"), lax.axis_size("wall")

    def partner(f, w):
        if axis == "fluid":
            return (f + 1 if (f + turn) % 2 == 0 else f - 1) % groups, w
        other = w + 1 if (w + turn) % 2 == 0 else w - 1
        return (f, other) if 0 <= other < walls else (f ^ 1, w)

    pairs = []
    for f in range(groups):
        for w in range(walls):
            to_f, to_w = partner(f, w)
            pairs.append((f * walls + w, to_f * walls + to_w))
    return lax.ppermute(block, ("fluid", "wall"), pairs)


def cross(block, axis, mask):
    return lax.ppermute(block, axis, [(i, i ^ mask) for i in range(lax.axis_size(axis))])


def from_neighbours(index, count, first, second):
    even = index % 2 == 0
    above = jnp.where(even, first, second)
    below = jnp.where(even, second, first)
    above = jnp.where(index == count - 1, jnp.zeros_like(above), above)
    below = jnp.where(index == 0, jnp.zeros_like(below), below)
    return below, above


def pack_edges(packed, plane, m, lane):
    width = lane.shape[1]
    here = (lane == 2 * m) | (lane == (2 * m + width - 1) % width)
    return jnp.where(here, pltpu.roll(plane, 2 * m, 1), packed)


def mix_edges(below, above, lane, shift=2):
    return jnp.where(lane % 2 == 0, above, pltpu.roll(below, shift, 1))


def edge_of(mixed, m):
    width = mixed.shape[1]
    return pltpu.roll(mixed, (2 * width - (2 * m + 1)) % width, 1)


def viscosity(jumps):
    shear_sq = jumps[0] * jumps[0] + jumps[1] * jumps[1] + jumps[2] * jumps[2]
    root = lax.rsqrt(1.0 + relax_sq * shear_sq)
    return nu_floor + nu_spread * (root * lax.rsqrt(root))


def iotas(rows, width):
    shape = (rows, width)
    return lax.broadcasted_iota(jnp.int32, shape, 0), lax.broadcasted_iota(jnp.int32, shape, 1)


def faces_kernel(flow_ref, first_ref, second_ref, sems):
    last = flow_ref.shape[1] - 1
    odd = lax.axis_index("fluid") % 2
    copies = [
        pltpu.make_async_copy(flow_ref.at[c, plane], out_ref.at[c], sems.at[i, c])
        for i, (plane, out_ref) in enumerate(((last - last * odd, first_ref), (last * odd, second_ref)))
        for c in range(flow_ref.shape[0])
    ]
    for copy in copies:
        copy.start()
    for copy in copies:
        copy.wait()


def edges_kernel(groups, flow_ref, regions_ref, x0_ref, x1_ref, edges_ref):
    fields, planes, rows, width = flow_ref.shape
    _, lane = iotas(rows, width)
    outer = jnp.zeros((rows, width), jnp.float32)
    second, beside = outer, outer
    for c in range(fields):
        for x in range(planes):
            m, plane = c * planes + x, flow_ref[c, x]
            outer = pack_edges(outer, plane, m, lane)
            here = (lane == 2 * m) | (lane == (2 * m - 3) % width)
            second = jnp.where(here, pltpu.roll(plane, (2 * m - 1) % width, 1), second)
        for side, plane in enumerate(from_neighbours(lax.axis_index("fluid"), groups, x0_ref[c], x1_ref[c])):
            beside = pack_edges(beside, plane, 2 * c + side, lane)
    for x in range(planes):
        beside = pack_edges(beside, regions_ref[x].astype(jnp.float32), 2 * fields + x, lane)
    edges_ref[0], edges_ref[1], edges_ref[2] = outer, second, beside


def outside_edges(walls, planes, halo, second, beside, inside, rim_nu):
    rows, width = halo.shape
    row, lane = iotas(rows, width)
    x, field = (lane // 2) % planes, (lane // 2) // planes

    def spread(nu):
        nu = jnp.where(field == 0, nu, 0.0)
        return nu + pltpu.roll(nu, 2 * planes, 1) + pltpu.roll(nu, 4 * planes, 1)

    def nu_of(jump):
        return spread(viscosity([jump] + [pltpu.roll(jump, width - 2 * c * planes, 1) for c in (1, 2)]))

    over_x, under_x = pltpu.roll(halo, width - 2, 1), pltpu.roll(halo, 2, 1)
    for c in range(4):
        low = pltpu.roll(beside, (2 * c * planes - 4 * c) % width, 1)
        high = pltpu.roll(beside, (2 * (c * planes + planes - 1) - 4 * c - 2) % width, 1)
        under_x = jnp.where((x == 0) & (field == c), low, under_x)
        over_x = jnp.where((x == planes - 1) & (field == c), high, over_x)
    over_y = jnp.where(row == rows - 1, 0.0, pltpu.roll(halo, rows - 1, 0))
    under_y = jnp.where(row == 0, 0.0, pltpu.roll(halo, 1, 0))
    total = spread(rim_nu) * (inside - halo)
    for other in (over_x, under_x, over_y, under_y, second):
        total += nu_of(other - halo) * (other - halo)
    above = lane % 2 == 0
    gradient_x = pltpu.roll(0.5 * (over_x - under_x), width - 6 * planes, 1)
    gradient_y = pltpu.roll(0.5 * (over_y - under_y), width - 4 * planes, 1)
    gradient_z = pltpu.roll(0.5 * jnp.where(above, second - inside, inside - second), width - 2 * planes, 1)
    gradient = jnp.where(field == 0, gradient_x, jnp.where(field == 1, gradient_y, gradient_z))
    value = halo + time_step * (total - gradient)
    value = jnp.where(field == 3, pltpu.roll(beside, 6 * planes - 16, 1), value)
    me = lax.axis_index("wall")
    exists = jnp.where(above, jnp.where(me < walls - 1, 1, 0), jnp.where(me > 0, 1, 0)) == 1
    return jnp.where(exists & (field < 4), value, 0.0)


def group_kernel(cap, dest_ref, tiles_ref, meas_ref, after_ref, *refs):
    chips = len(refs) - 12
    sends = refs[:chips]
    (list_ref, held_ref, seen_ref, count_ref, slot_ref, rows_ref, blank_ref,
     list_sem, seen_sem, in_sems, out_sems, row_sems) = refs[chips:]
    count_tiles, width, _ = tiles_ref.shape
    groups = 2 * chips
    slots = groups * cap
    extra = rows_ref.shape[0] // groups
    depth = cap * width
    me = lax.axis_index("fluid")
    listed = pltpu.make_async_copy(dest_ref, list_ref, list_sem)
    listed.start()
    piece = count_tiles // in_sems.shape[0]

    def load(p):
        part = pl.ds(p * piece, piece)
        return pltpu.make_async_copy(tiles_ref.at[part], held_ref.at[part], in_sems.at[p])

    for p in range(in_sems.shape[0]):
        load(p).start()
    seen = pltpu.make_async_copy(meas_ref, seen_ref, seen_sem)
    seen.start()

    def clear(b, carry):
        count_ref[b] = 0
        for k in range(cap):
            slot_ref[b * cap + k] = -1
        return carry

    lax.fori_loop(0, groups, clear, 0)
    if slots > count_tiles:
        blank_ref[...] = jnp.zeros_like(blank_ref)
    _, tile_lane = iotas(8, count_tiles)
    listed.wait()

    def place(t, slot_of):
        b = list_ref[t]
        k = count_ref[b]
        count_ref[b] = k + 1
        slot_ref[b * cap + k] = t
        return jnp.where(tile_lane == t, b * cap + k, slot_of)

    slot_of = lax.fori_loop(
        0, count_tiles, place, jnp.full((8, count_tiles), -1, jnp.int32), unroll=True
    )
    for p in range(in_sems.shape[0]):
        load(p).wait()

    def each(act):
        for m in list(range(1, chips)) + [0]:
            for j in range(2):
                b = me ^ (2 * m + j)
                for k in range(cap):
                    t = slot_ref[b * cap + k]
                    at = sends[m].at[j, pl.ds(k * width, width), :]
                    sem = out_sems.at[(2 * m + j) * cap + k]
                    if slots > count_tiles:

                        @pl.when(t >= 0)
                        def _():
                            act(pltpu.make_async_copy(held_ref.at[t], at, sem))

                        @pl.when(t < 0)
                        def _():
                            act(pltpu.make_async_copy(blank_ref, at, sem))

                    else:
                        act(pltpu.make_async_copy(held_ref.at[t], at, sem))

    each(lambda copy: copy.start())

    seen.wait()
    row = lax.broadcasted_iota(jnp.int32, (groups * extra, count_tiles), 0)
    within = row % extra
    row_slot = (row // extra) * cap + within // 3
    used = within < cap * 3
    total = jnp.zeros((groups * extra, width), jnp.float32)
    for c in range(3):
        pick = (row_slot == slot_of[0:1, :]) & used & (within % 3 == c)
        total += jnp.dot(
            pick.astype(jnp.float32).astype(jnp.bfloat16), seen_ref[c], preferred_element_type=jnp.float32
        )
    rows_ref[...] = total.astype(jnp.bfloat16)

    def row_copy(m, j):
        b = me ^ (2 * m + j)
        return pltpu.make_async_copy(
            rows_ref.at[pl.ds(pl.multiple_of(b * extra, extra), extra), :],
            sends[m].at[j, pl.ds(depth, extra), :],
            row_sems.at[2 * m + j],
        )

    for m in range(chips):
        for j in range(2):
            row_copy(m, j).start()
    each(lambda copy: copy.wait())
    for m in range(chips):
        for j in range(2):
            row_copy(m, j).wait()


def forward_kernel(
    sizes, cap, cells_ref, flow_ref, x0_ref, x1_ref, z0_ref, z1_ref, edges_ref,
    out_ref, next_ref, nux_ref, nuy_ref, nuz_ref, nuy0_ref, rim_ref, mine_ref, lent_ref, cells_of_ref,
    list_ref, padded_ref, taken_ref, list_sem, out_sems,
):
    _, planes, rows, width = flow_ref.shape
    groups, walls = sizes
    chips, extra, _ = mine_ref.shape
    listed = pltpu.make_async_copy(cells_ref, list_ref, list_sem)
    listed.start()
    row, lane = iotas(rows, width)
    halo = mix_edges(*from_neighbours(lax.axis_index("wall"), walls, z0_ref[0], z1_ref[0]), lane)
    inside = pltpu.roll(edges_ref[0], 1, 1)
    jump = halo - inside
    rim_nu = viscosity([jump] + [pltpu.roll(jump, width - 2 * c * planes, 1) for c in (1, 2)])
    rim_nu = jnp.where(lane < 2 * planes, rim_nu, 0.0)
    rim_ref[...] = rim_nu
    for c in range(4):
        low, high = from_neighbours(lax.axis_index("fluid"), groups, x0_ref[c], x1_ref[c])
        padded_ref[c, 0] = low
        padded_ref[c, planes + 1] = high
        padded_ref[c, 1 : planes + 1] = flow_ref[c]
    nux_ref[0] = viscosity([padded_ref[c, 1] - padded_ref[c, 0] for c in range(3)])

    def plane(x, carry):
        here = [padded_ref[c, x + 1] for c in range(4)]
        over = [padded_ref[c, x + 2] for c in range(4)]
        under = [padded_ref[c, x] for c in range(4)]
        total = [None] * 3
        pressure = [None] * 3

        def add(axis, nu_up, nu_down):
            for c in range(3):
                flux = nu_up * (over[c] - here[c]) - nu_down * (here[c] - under[c])
                total[c] = flux if total[c] is None else total[c] + flux
            pressure[axis] = 0.5 * (over[3] - under[3])

        nu_up = viscosity([over[c] - here[c] for c in range(3)])
        nux_ref[x + 1] = nu_up
        add(0, nu_up, nux_ref[x])
        over = [jnp.where(row == rows - 1, 0.0, pltpu.roll(here[c], rows - 1, 0)) for c in range(4)]
        under = [jnp.where(row == 0, 0.0, pltpu.roll(here[c], 1, 0)) for c in range(4)]
        nu_up = viscosity([over[c] - here[c] for c in range(3)])
        nu_first = viscosity([here[c][:1] for c in range(3)])
        nuy_ref[x] = nu_up
        nuy0_ref[pl.ds(x, 1), :] = nu_first
        add(1, nu_up, jnp.where(row == 0, nu_first, pltpu.roll(nu_up, 1, 0)))
        rim = [edge_of(halo, c * planes + x) for c in range(4)]
        over = [jnp.where(lane == width - 1, rim[c], pltpu.roll(here[c], width - 1, 1)) for c in range(4)]
        under = [jnp.where(lane == 0, rim[c], pltpu.roll(here[c], 1, 1)) for c in range(4)]
        nu_up = viscosity([over[c] - here[c] for c in range(3)])
        nuz_ref[x] = nu_up
        add(2, nu_up, jnp.where(lane == 0, edge_of(rim_nu, x), pltpu.roll(nu_up, 1, 1)))
        for c in range(3):
            value = here[c] + time_step * (total[c] - pressure[c])
            next_ref[c, x] = value
        return carry

    pieces = out_sems.shape[0]
    step = planes // pieces

    def store(i):
        part = pl.ds(i * step, step)
        return pltpu.make_async_copy(next_ref.at[:, part], out_ref.at[:, part], out_sems.at[i])

    for i in range(pieces):
        lax.fori_loop(i * step, (i + 1) * step, plane, 0, unroll=True)
        store(i).start()

    taken_ref[...] = jnp.zeros_like(taken_ref)
    listed.wait()
    _, slot_lane = iotas(8, groups * extra)
    cell_of = jnp.full((8, groups * extra), -1, jnp.int32)
    odd = lax.axis_index("fluid") % 2
    for b in range(groups):
        part = (odd if b % 2 == 0 else 1 - odd) * chips + b // 2
        for k in range(cap):
            cell = list_ref[k, b]
            x, y = lax.div(cell, rows), lax.rem(cell, rows)
            first = part * extra + 3 * k
            for c in range(3):
                taken_ref[pl.ds(first + c, 1), :] = next_ref[c, x, pl.ds(y, 1), :]
            cell_of = jnp.where((slot_lane >= first) & (slot_lane < first + 3), cell, cell_of)
    cells_of_ref[...] = cell_of
    taken = taken_ref[...].astype(jnp.bfloat16).reshape((2,) + mine_ref.shape)
    mine_ref[...] = taken[0]
    lent_ref[...] = taken[1]
    for i in range(pieces):
        store(i).wait()


def pick_kernel(
    sizes, cells_of_ref, z0_ref, z1_ref, edges_ref, rim_ref, outside_ref, pick_ref
):
    _, rows, width = edges_ref.shape
    groups, walls = sizes
    _, lines, slot_rows = pick_ref.shape
    planes = lines // rows
    extra = slot_rows // groups
    _, lane = iotas(rows, width)
    halo, second, beside = (
        mix_edges(*from_neighbours(lax.axis_index("wall"), walls, z0_ref[i], z1_ref[i]), lane, shift)
        for i, shift in enumerate((2, 4, 2))
    )
    inside = pltpu.roll(edges_ref[0], 1, 1)
    outside_ref[...] = outside_edges(walls, planes, halo, second, beside, inside, rim_ref[...])
    line, slot_lane = iotas(lines, slot_rows)
    hit = line == cells_of_ref[0:1, :]
    part = (slot_lane % extra) % 3
    for c in range(3):
        pick_ref[c] = (hit & (part == c)).astype(jnp.float32).astype(jnp.bfloat16)


def product_kernel(cap, block, values_ref, after_ref, *refs):
    chips, extra, width = values_ref.shape
    recvs, out_ref = refs[:chips], refs[chips]
    depth = cap * width
    row, lane = iotas(extra, depth)
    own = row // 3 == lane // width
    here = lax.axis_index("fluid") // 2
    for m, recv_ref in enumerate(recvs):
        source = here ^ m
        at = pl.ds(pl.multiple_of(source * extra, extra), extra)
        weights = recv_ref[block, pl.ds(0, depth), :]
        predicted = lax.dot_general(
            values_ref[source], weights, (((1,), (1,)), ((), ())), preferred_element_type=jnp.float32
        )
        seen = recv_ref[block, pl.ds(depth, extra), :].astype(jnp.float32)
        misfit = jnp.where(own, predicted - jnp.concatenate([seen] * cap, axis=1), 0.0).astype(jnp.bfloat16)
        contrib = jnp.dot(misfit, weights, preferred_element_type=jnp.float32)
        high = contrib.astype(jnp.bfloat16)
        out_ref[0, at, :] = high
        out_ref[1, at, :] = (contrib - high.astype(jnp.float32)).astype(jnp.bfloat16)


def forcing_kernel(mine_ref, other_ref, pick_ref, forcing_ref, first_ref, second_ref):
    _, planes, rows, width = forcing_ref.shape
    half = mine_ref.shape[1]
    even = lax.axis_index("fluid") % 2 == 0
    for c in range(3):
        total = None
        for i, part_ref in enumerate((mine_ref, other_ref)):
            pick = pick_ref[c, :, i * half : (i + 1) * half]
            for part in range(2):
                product = jnp.dot(pick, part_ref[part], preferred_element_type=jnp.float32)
                total = product if total is None else total + product
        forcing_ref[c] = total.reshape(planes, rows, width)
        low, high = total[:rows], total[(planes - 1) * rows :]
        first_ref[c] = jnp.where(even, high, low)
        second_ref[c] = jnp.where(even, low, high)


def region_sums(product_ref, region_ref, sums_ref, plus_ref=None):
    count = sums_ref.shape[0]
    rows, width = product_ref.shape
    step = 32

    def group(g, carry):
        sums = [jnp.zeros((8, width), jnp.float32)] * 8
        for r in range(0, rows, step):
            values = product_ref[r : r + step, :]
            ids = region_ref[r : r + step, :] - g * 8
            for i in range(8):
                chosen = jnp.where(ids == i, values, 0.0)
                for s in range(0, step, 8):
                    sums[i] = sums[i] + chosen[s : s + 8]
        block = jnp.concatenate([jnp.sum(part, axis=0, keepdims=True) for part in sums], axis=0)
        at = pl.ds(pl.multiple_of(g * 8, 8), 8)
        sums_ref[at, :] = block if plus_ref is None else block + plus_ref[at, :]
        return carry

    lax.fori_loop(0, count // 8, group, 0)


def inner_kernel(
    forcing_ref, next_ref, nux_ref, nuy_ref, nuz_ref, nuy0_ref, rim_ref, regions_ref, outside_ref,
    adjoint_ref, fpack_ref, sums_ref, product_ref, ids_ref,
):
    _, planes, rows, width = forcing_ref.shape
    row, lane = iotas(rows, width)
    rim_nu = rim_ref[...]

    def plane(x, fpack):
        nuy, nuz = nuy_ref[x], nuz_ref[x]
        nuy_down = jnp.where(row == 0, nuy0_ref[pl.ds(x, 1), :], pltpu.roll(nuy, 1, 0))
        nuz_down = jnp.where(lane == 0, edge_of(rim_nu, x), pltpu.roll(nuz, 1, 1))
        nus = (nux_ref[x + 1], nux_ref[x], nuy, nuy_down, nuz, nuz_down)
        next_up, next_down = jnp.minimum(x + 1, planes - 1), jnp.maximum(x - 1, 0)
        at_top, at_bottom = x == planes - 1, x == 0
        product = None
        for c in range(3):
            here = forcing_ref[c, x]
            over = jnp.where(at_top, 0.0, forcing_ref[c, next_up])
            under = jnp.where(at_bottom, 0.0, forcing_ref[c, next_down])
            total = nus[0] * (over - here) - nus[1] * (here - under)
            over = jnp.where(row == rows - 1, 0.0, pltpu.roll(here, rows - 1, 0))
            under = jnp.where(row == 0, 0.0, pltpu.roll(here, 1, 0))
            total += nus[2] * (over - here) - nus[3] * (here - under)
            over = jnp.where(lane == width - 1, 0.0, pltpu.roll(here, width - 1, 1))
            under = jnp.where(lane == 0, 0.0, pltpu.roll(here, 1, 1))
            total += nus[4] * (over - here) - nus[5] * (here - under)
            value = here + time_step * total
            adjoint_ref[c, x] = value
            part = value * next_ref[c, x]
            product = part if product is None else product + part
            fpack = pack_edges(fpack, here, c * planes + x, lane)
        at = pl.ds(pl.multiple_of(x * rows, rows), rows)
        product_ref[at, :] = product
        ids_ref[at, :] = regions_ref[x]
        return fpack

    fpack = lax.fori_loop(0, planes, plane, jnp.zeros((rows, width), jnp.float32), unroll=4)
    fpack_ref[...] = fpack
    mixed = outside_ref[...]
    reach = pltpu.roll(fpack, 1, 1) * mixed
    reach = reach + pltpu.roll(reach, width - 2 * planes, 1) + pltpu.roll(reach, width - 4 * planes, 1)
    reach = time_step * reach * rim_nu
    product_ref[pl.ds(planes * rows, rows), :] = reach
    ids_ref[pl.ds(planes * rows, rows), :] = pltpu.roll(mixed, (width - 6 * planes) % width, 1).astype(jnp.int32)
    region_sums(product_ref, ids_ref, sums_ref)


def edge_kernel(
    sizes, masks, x0_ref, x1_ref, nux_ref, next_ref, regions_ref, sums_ref, fpack_ref, *refs
):
    groups, walls = sizes
    outs, (product_ref, ids_ref, total_ref) = refs[:-3], refs[-3:]
    _, planes, rows, width = next_ref.shape
    low, high = 0.0, 0.0
    for c in range(3):
        below, above = from_neighbours(lax.axis_index("fluid"), groups, x0_ref[c], x1_ref[c])
        low += below * next_ref[c, 0]
        high += above * next_ref[c, planes - 1]
    product_ref[:rows, :] = time_step * nux_ref[0] * low
    product_ref[rows:, :] = time_step * nux_ref[planes] * high
    ids_ref[:rows, :] = regions_ref[0]
    ids_ref[rows:, :] = regions_ref[planes - 1]
    region_sums(product_ref, ids_ref, total_ref, sums_ref)
    per = total_ref.shape[0] // walls
    for mask, out_ref in zip((0,) + masks, outs):
        target = lax.axis_index("wall") ^ mask
        out_ref[:per, :] = total_ref[pl.ds(pl.multiple_of(target * per, per), per), :]
        if out_ref.shape[0] > per:
            out_ref[per:, :] = fpack_ref[...]


def final_kernel(sizes, inner_ref, x0_ref, x1_ref, nux_ref, rim_ref, own_ref, *refs):
    groups, walls = sizes
    arrived, (adjoint_ref, sens_ref, value_ref, sems) = refs[:-4], refs[-4:]
    _, planes, rows, width = inner_ref.shape
    per = own_ref.shape[0]
    _, lane = iotas(rows, width)
    me = lax.axis_index("wall")
    total = own_ref[...]
    below = jnp.zeros((rows, width), jnp.float32)
    above = jnp.zeros((rows, width), jnp.float32)
    for mask, ref in zip(range(1, walls), arrived):
        total = total + ref[:per, :]
        if ref.shape[0] > per:
            edges = ref[per:, :]
            above = jnp.where((me ^ mask) == me + 1, edges, above)
            below = jnp.where((me ^ mask) == me - 1, edges, below)
    mixed = mix_edges(below, above, lane)
    edge_nu = time_step * rim_ref[...]
    edge_nu = edge_nu + pltpu.roll(edge_nu, 2 * planes, 1) + pltpu.roll(edge_nu, 4 * planes, 1)
    edge_flux = mixed * edge_nu
    on_edge = (lane == 0) | (lane == width - 1)

    beside = [from_neighbours(lax.axis_index("fluid"), groups, x0_ref[c], x1_ref[c]) for c in range(3)]
    step = planes // sems.shape[0]

    def store(i):
        part = pl.ds(i * step, step)
        return pltpu.make_async_copy(value_ref.at[:, part], adjoint_ref.at[:, part], sems.at[i])

    for i in range(sems.shape[0]):
        for x in range(i * step, (i + 1) * step):
            for c in range(3):
                value = inner_ref[c, x] + jnp.where(on_edge, edge_of(edge_flux, c * planes + x), 0.0)
                if x == 0:
                    value += time_step * nux_ref[0] * beside[c][0]
                if x == planes - 1:
                    value += time_step * nux_ref[planes] * beside[c][1]
                value_ref[c, x] = value
        store(i).start()
    sens_ref[...] = sens_scale * lax.dot_general(
        jnp.ones((8, width), jnp.float32), total, (((1,), (1,)), ((), ())),
        precision=lax.Precision.HIGHEST, preferred_element_type=jnp.float32,
    )[:1]
    for i in range(sems.shape[0]):
        store(i).wait()


def body(flow_state, regions, obs_tiles, measured, tile_dest, cell_list):
    groups, walls = lax.axis_size("fluid"), lax.axis_size("wall")
    sizes = (groups, walls)
    _, planes, rows, width = flow_state.shape
    count_tiles = obs_tiles.shape[2]
    cap = cell_list.shape[3]
    extra = -(-cap * 3 // 16) * 16
    reg_count = REG_DEV * walls
    cells = groups * cap
    grid = planes * rows * width

    chips = groups // 2
    height = cap * width + extra
    xs0, xs1 = call(
        faces_kernel,
        (f32(4, rows, width), f32(4, rows, width)),
        [HBM],
        (flow_state,),
        (pltpu.SemaphoreType.DMA((2, 4)),),
        limit=60 * 1024 * 1024,
    )
    x0, x1 = swap(xs0, "fluid", 0), swap(xs1, "fluid", 1)
    sends = call(
        functools.partial(group_kernel, cap),
        (bf16(2, height, width),) * chips,
        [HBM] * 3 + [ANY],
        (tile_dest[0, 0], obs_tiles[0, 0], jnp.transpose(measured[0, 0], (1, 0, 2)), xs1),
        (
            pltpu.SMEM((count_tiles,), jnp.int32),
            pltpu.VMEM((count_tiles, width, width), jnp.bfloat16),
            pltpu.VMEM((3, count_tiles, width), jnp.bfloat16),
            pltpu.SMEM((groups,), jnp.int32),
            pltpu.SMEM((cells,), jnp.int32),
            pltpu.VMEM((groups * extra, width), jnp.bfloat16),
            pltpu.VMEM((width, width), jnp.bfloat16),
            pltpu.SemaphoreType.DMA,
            pltpu.SemaphoreType.DMA,
            pltpu.SemaphoreType.DMA((4,)),
            pltpu.SemaphoreType.DMA((cells,)),
            pltpu.SemaphoreType.DMA((groups,)),
        ),
        out_specs=(HBM,) * chips,
        limit=60 * 1024 * 1024,
    )
    *sends, x0, x1 = lax.optimization_barrier((*sends, x0, x1))
    recvs = [sends[0]] + [cross(sends[m], "fluid", 2 * m) for m in range(1, chips)]
    zs = call(
        functools.partial(edges_kernel, groups),
        f32(3, rows, width),
        [VMEM] * 4,
        (flow_state, regions, x0, x1),
    )
    z0, z1 = swap(zs, "wall", 0), swap(zs, "wall", 1)
    slot_rows = groups * extra
    velocity_next, velocity, nux, nuy, nuz, nuy0, rim, mine, lent, cells_of = call(
        functools.partial(forward_kernel, sizes, cap),
        (f32(3, planes, rows, width),) * 2
        + (f32(planes + 1, rows, width), f32(planes, rows, width), f32(planes, rows, width))
        + (f32(planes, width), f32(rows, width))
        + (bf16(chips, extra, width),) * 2
        + (jax.ShapeDtypeStruct((8, slot_rows), jnp.int32),),
        [ANY] + [VMEM] * 6,
        (cell_list[0, 0].T, flow_state, x0, x1, z0, z1, zs),
        (
            pltpu.SMEM((cap, groups), jnp.int32),
            pltpu.VMEM((4, planes + 2, rows, width), jnp.float32),
            pltpu.VMEM((slot_rows, width), jnp.float32),
            pltpu.SemaphoreType.DMA,
            pltpu.SemaphoreType.DMA((4,)),
        ),
        out_specs=(HBM,) + (VMEM,) * 9,
    )
    borrowed = cross(lent, "fluid", 1)
    outside, pick = call(
        functools.partial(pick_kernel, sizes),
        (f32(rows, width), bf16(3, planes * rows, slot_rows)),
        [VMEM] * 5,
        (cells_of, z0, z1, zs, rim),
    )

    def products(block, values, after):
        return call(
            functools.partial(product_kernel, cap, block),
            bf16(2, chips * extra, width),
            [VMEM, ANY] + [VMEM] * chips,
            (values, after, *recvs),
        )

    given = products(1, borrowed, pick)
    other = cross(given, "fluid", 1)
    held = products(0, mine, given)
    forcing, fs0, fs1 = call(
        forcing_kernel,
        (f32(3, planes, rows, width), f32(3, rows, width), f32(3, rows, width)),
        [VMEM] * 3,
        (held, other, pick),
    )
    f0, f1 = swap(fs0, "fluid", 0), swap(fs1, "fluid", 1)
    inner, fpack, sums = call(
        inner_kernel,
        (f32(3, planes, rows, width), f32(rows, width), f32(reg_count, width)),
        [VMEM] * 9,
        (forcing, velocity, nux, nuy, nuz, nuy0, rim, regions, outside),
        (pltpu.VMEM(((planes + 1) * rows, width), jnp.float32), pltpu.VMEM(((planes + 1) * rows, width), jnp.int32)),
    )
    masks = tuple(range(1, walls))
    heights = [REG_DEV] + [REG_DEV + (rows if mask & (mask + 1) == 0 else 0) for mask in masks]
    own, *parts = call(
        functools.partial(edge_kernel, sizes, masks),
        tuple(f32(height, width) for height in heights),
        [VMEM] * 7,
        (f0, f1, nux, velocity, regions, sums, fpack),
        (
            pltpu.VMEM((2 * rows, width), jnp.float32),
            pltpu.VMEM((2 * rows, width), jnp.int32),
            pltpu.VMEM((reg_count, width), jnp.float32),
        ),
        flops=20 * grid,
        moved=4 * grid,
    )
    arrived = [cross(part, "wall", mask) for part, mask in zip(parts, masks)]
    adjoint, sens = call(
        functools.partial(final_kernel, sizes),
        (f32(3, planes, rows, width), f32(1, REG_DEV)),
        [VMEM] * (6 + len(arrived)),
        (inner, f0, f1, nux, rim, own, *arrived),
        (pltpu.VMEM((3, planes, rows, width), jnp.float32), pltpu.SemaphoreType.DMA((4,))),
        out_specs=(HBM, VMEM),
        flops=10 * grid,
        moved=24 * grid,
    )
    return velocity_next, adjoint, sens.reshape(REG_DEV)


def solution(mesh):
    in_specs = (
        P(None, "fluid", None, "wall"),
        P("fluid", None, "wall"),
        P("fluid", "wall", None, None, None),
        P("fluid", "wall", None, None, None),
        P("fluid", "wall", None),
        P("fluid", "wall", None, None),
    )
    out_specs = (
        P(None, "fluid", None, "wall"),
        P(None, "fluid", None, "wall"),
        P(("fluid", "wall")),
    )
    return jax.shard_map(body, mesh=mesh, in_specs=in_specs, out_specs=out_specs, check_vma=False)
```

```python
import functools

import jax
import jax.numpy as jnp
from jax import lax
from jax.experimental import pallas as pl
from jax.experimental.pallas import tpu as pltpu
from jax.sharding import PartitionSpec as P

REG_DEV = 16

time_step = 0.12
nu_floor = 0.1
nu_spread = 0.9
relax_sq = 4.0
sens_scale = 0.03

VMEM = pl.BlockSpec(memory_space=pltpu.VMEM)
SMEM = pl.BlockSpec(memory_space=pltpu.SMEM)
ANY = pl.BlockSpec(memory_space=pl.ANY)
HBM = pl.BlockSpec(memory_space=pltpu.HBM)
LIMIT = 24 * 1024 * 1024


def call(kernel, outs, ins, operands, scratch=(), flops=1, moved=1, out_specs=None, limit=LIMIT):
    return pl.pallas_call(
        kernel,
        out_shape=outs,
        in_specs=ins,
        out_specs=out_specs if out_specs is not None else jax.tree.map(lambda _: VMEM, outs),
        scratch_shapes=list(scratch),
        compiler_params=pltpu.CompilerParams(vmem_limit_bytes=limit),
        cost_estimate=pl.CostEstimate(flops=flops, bytes_accessed=moved, transcendentals=0),
    )(*operands)


def f32(*shape):
    return jax.ShapeDtypeStruct(shape, jnp.float32)


def bf16(*shape):
    return jax.ShapeDtypeStruct(shape, jnp.bfloat16)


def swap(block, axis, turn):
    groups, walls = lax.axis_size("fluid"), lax.axis_size("wall")

    def partner(f, w):
        if axis == "fluid":
            return (f + 1 if (f + turn) % 2 == 0 else f - 1) % groups, w
        other = w + 1 if (w + turn) % 2 == 0 else w - 1
        return (f, other) if 0 <= other < walls else (f ^ 1, w)

    pairs = []
    for f in range(groups):
        for w in range(walls):
            to_f, to_w = partner(f, w)
            pairs.append((f * walls + w, to_f * walls + to_w))
    return lax.ppermute(block, ("fluid", "wall"), pairs)


def cross(block, axis, mask):
    return lax.ppermute(block, axis, [(i, i ^ mask) for i in range(lax.axis_size(axis))])


def from_neighbours(index, count, first, second):
    even = index % 2 == 0
    above = jnp.where(even, first, second)
    below = jnp.where(even, second, first)
    above = jnp.where(index == count - 1, jnp.zeros_like(above), above)
    below = jnp.where(index == 0, jnp.zeros_like(below), below)
    return below, above


def pack_edges(packed, plane, m, lane):
    width = lane.shape[1]
    here = (lane == 2 * m) | (lane == (2 * m + width - 1) % width)
    return jnp.where(here, pltpu.roll(plane, 2 * m, 1), packed)


def mix_edges(below, above, lane, shift=2):
    return jnp.where(lane % 2 == 0, above, pltpu.roll(below, shift, 1))


def edge_of(mixed, m):
    width = mixed.shape[1]
    return pltpu.roll(mixed, (2 * width - (2 * m + 1)) % width, 1)


def viscosity(jumps):
    shear_sq = jumps[0] * jumps[0] + jumps[1] * jumps[1] + jumps[2] * jumps[2]
    root = lax.rsqrt(1.0 + relax_sq * shear_sq)
    return nu_floor + nu_spread * (root * lax.rsqrt(root))


def iotas(rows, width):
    shape = (rows, width)
    return lax.broadcasted_iota(jnp.int32, shape, 0), lax.broadcasted_iota(jnp.int32, shape, 1)


def faces_kernel(flow_ref, first_ref, second_ref, sems):
    last = flow_ref.shape[1] - 1
    odd = lax.axis_index("fluid") % 2
    copies = [
        pltpu.make_async_copy(flow_ref.at[c, plane], out_ref.at[c], sems.at[i, c])
        for i, (plane, out_ref) in enumerate(((last - last * odd, first_ref), (last * odd, second_ref)))
        for c in range(flow_ref.shape[0])
    ]
    for copy in copies:
        copy.start()
    for copy in copies:
        copy.wait()


def edges_kernel(groups, flow_ref, regions_ref, x0_ref, x1_ref, edges_ref):
    fields, planes, rows, width = flow_ref.shape
    _, lane = iotas(rows, width)
    outer = jnp.zeros((rows, width), jnp.float32)
    second, beside = outer, outer
    for c in range(fields):
        for x in range(planes):
            m, plane = c * planes + x, flow_ref[c, x]
            outer = pack_edges(outer, plane, m, lane)
            here = (lane == 2 * m) | (lane == (2 * m - 3) % width)
            second = jnp.where(here, pltpu.roll(plane, (2 * m - 1) % width, 1), second)
        for side, plane in enumerate(from_neighbours(lax.axis_index("fluid"), groups, x0_ref[c], x1_ref[c])):
            beside = pack_edges(beside, plane, 2 * c + side, lane)
    for x in range(planes):
        beside = pack_edges(beside, regions_ref[x].astype(jnp.float32), 2 * fields + x, lane)
    edges_ref[0], edges_ref[1], edges_ref[2] = outer, second, beside


def outside_edges(walls, planes, halo, second, beside, inside, rim_nu):
    rows, width = halo.shape
    row, lane = iotas(rows, width)
    x, field = (lane // 2) % planes, (lane // 2) // planes

    def spread(nu):
        nu = jnp.where(field == 0, nu, 0.0)
        return nu + pltpu.roll(nu, 2 * planes, 1) + pltpu.roll(nu, 4 * planes, 1)

    def nu_of(jump):
        return spread(viscosity([jump] + [pltpu.roll(jump, width - 2 * c * planes, 1) for c in (1, 2)]))

    over_x, under_x = pltpu.roll(halo, width - 2, 1), pltpu.roll(halo, 2, 1)
    for c in range(4):
        low = pltpu.roll(beside, (2 * c * planes - 4 * c) % width, 1)
        high = pltpu.roll(beside, (2 * (c * planes + planes - 1) - 4 * c - 2) % width, 1)
        under_x = jnp.where((x == 0) & (field == c), low, under_x)
        over_x = jnp.where((x == planes - 1) & (field == c), high, over_x)
    over_y = jnp.where(row == rows - 1, 0.0, pltpu.roll(halo, rows - 1, 0))
    under_y = jnp.where(row == 0, 0.0, pltpu.roll(halo, 1, 0))
    total = spread(rim_nu) * (inside - halo)
    for other in (over_x, under_x, over_y, under_y, second):
        total += nu_of(other - halo) * (other - halo)
    above = lane % 2 == 0
    gradient_x = pltpu.roll(0.5 * (over_x - under_x), width - 6 * planes, 1)
    gradient_y = pltpu.roll(0.5 * (over_y - under_y), width - 4 * planes, 1)
    gradient_z = pltpu.roll(0.5 * jnp.where(above, second - inside, inside - second), width - 2 * planes, 1)
    gradient = jnp.where(field == 0, gradient_x, jnp.where(field == 1, gradient_y, gradient_z))
    value = halo + time_step * (total - gradient)
    value = jnp.where(field == 3, pltpu.roll(beside, 6 * planes - 16, 1), value)
    me = lax.axis_index("wall")
    exists = jnp.where(above, jnp.where(me < walls - 1, 1, 0), jnp.where(me > 0, 1, 0)) == 1
    return jnp.where(exists & (field < 4), value, 0.0)


def group_kernel(cap, dest_ref, tiles_ref, meas_ref, after_ref, *refs):
    chips = len(refs) - 12
    sends = refs[:chips]
    (list_ref, held_ref, seen_ref, count_ref, slot_ref, rows_ref, blank_ref,
     list_sem, seen_sem, in_sems, out_sems, row_sems) = refs[chips:]
    count_tiles, width, _ = tiles_ref.shape
    groups = 2 * chips
    slots = groups * cap
    extra = rows_ref.shape[0] // groups
    depth = cap * width
    me = lax.axis_index("fluid")
    listed = pltpu.make_async_copy(dest_ref, list_ref, list_sem)
    listed.start()
    piece = count_tiles // in_sems.shape[0]

    def load(p):
        part = pl.ds(p * piece, piece)
        return pltpu.make_async_copy(tiles_ref.at[part], held_ref.at[part], in_sems.at[p])

    for p in range(in_sems.shape[0]):
        load(p).start()
    seen = pltpu.make_async_copy(meas_ref, seen_ref, seen_sem)
    seen.start()

    def clear(b, carry):
        count_ref[b] = 0
        for k in range(cap):
            slot_ref[b * cap + k] = -1
        return carry

    lax.fori_loop(0, groups, clear, 0)
    if slots > count_tiles:
        blank_ref[...] = jnp.zeros_like(blank_ref)
    _, tile_lane = iotas(8, count_tiles)
    listed.wait()

    def place(t, slot_of):
        b = list_ref[t]
        k = count_ref[b]
        count_ref[b] = k + 1
        slot_ref[b * cap + k] = t
        return jnp.where(tile_lane == t, b * cap + k, slot_of)

    slot_of = lax.fori_loop(
        0, count_tiles, place, jnp.full((8, count_tiles), -1, jnp.int32), unroll=True
    )
    for p in range(in_sems.shape[0]):
        load(p).wait()

    def each(act):
        for m in list(range(1, chips)) + [0]:
            for j in range(2):
                b = me ^ (2 * m + j)
                for k in range(cap):
                    t = slot_ref[b * cap + k]
                    at = sends[m].at[j, pl.ds(k * width, width), :]
                    sem = out_sems.at[(2 * m + j) * cap + k]
                    if slots > count_tiles:

                        @pl.when(t >= 0)
                        def _():
                            act(pltpu.make_async_copy(held_ref.at[t], at, sem))

                        @pl.when(t < 0)
                        def _():
                            act(pltpu.make_async_copy(blank_ref, at, sem))

                    else:
                        act(pltpu.make_async_copy(held_ref.at[t], at, sem))

    each(lambda copy: copy.start())

    seen.wait()
    row = lax.broadcasted_iota(jnp.int32, (groups * extra, count_tiles), 0)
    within = row % extra
    row_slot = (row // extra) * cap + within // 3
    used = within < cap * 3
    total = jnp.zeros((groups * extra, width), jnp.float32)
    for c in range(3):
        pick = (row_slot == slot_of[0:1, :]) & used & (within % 3 == c)
        total += jnp.dot(
            pick.astype(jnp.float32).astype(jnp.bfloat16), seen_ref[c], preferred_element_type=jnp.float32
        )
    rows_ref[...] = total.astype(jnp.bfloat16)

    def row_copy(m, j):
        b = me ^ (2 * m + j)
        return pltpu.make_async_copy(
            rows_ref.at[pl.ds(pl.multiple_of(b * extra, extra), extra), :],
            sends[m].at[j, pl.ds(depth, extra), :],
            row_sems.at[2 * m + j],
        )

    for m in range(chips):
        for j in range(2):
            row_copy(m, j).start()
    each(lambda copy: copy.wait())
    for m in range(chips):
        for j in range(2):
            row_copy(m, j).wait()


def forward_kernel(
    sizes, cap, cells_ref, flow_ref, x0_ref, x1_ref, z0_ref, z1_ref, edges_ref,
    out_ref, next_ref, nux_ref, nuy_ref, nuz_ref, nuy0_ref, rim_ref, mine_ref, lent_ref, cells_of_ref,
    list_ref, padded_ref, taken_ref, list_sem, out_sems,
):
    _, planes, rows, width = flow_ref.shape
    groups, walls = sizes
    chips, extra, _ = mine_ref.shape
    listed = pltpu.make_async_copy(cells_ref, list_ref, list_sem)
    listed.start()
    row, lane = iotas(rows, width)
    halo = mix_edges(*from_neighbours(lax.axis_index("wall"), walls, z0_ref[0], z1_ref[0]), lane)
    inside = pltpu.roll(edges_ref[0], 1, 1)
    jump = halo - inside
    rim_nu = viscosity([jump] + [pltpu.roll(jump, width - 2 * c * planes, 1) for c in (1, 2)])
    rim_nu = jnp.where(lane < 2 * planes, rim_nu, 0.0)
    rim_ref[...] = rim_nu
    for c in range(4):
        low, high = from_neighbours(lax.axis_index("fluid"), groups, x0_ref[c], x1_ref[c])
        padded_ref[c, 0] = low
        padded_ref[c, planes + 1] = high
        padded_ref[c, 1 : planes + 1] = flow_ref[c]
    nux_ref[0] = viscosity([padded_ref[c, 1] - padded_ref[c, 0] for c in range(3)])

    def plane(x, carry):
        here = [padded_ref[c, x + 1] for c in range(4)]
        over = [padded_ref[c, x + 2] for c in range(4)]
        under = [padded_ref[c, x] for c in range(4)]
        total = [None] * 3
        pressure = [None] * 3

        def add(axis, nu_up, nu_down):
            for c in range(3):
                flux = nu_up * (over[c] - here[c]) - nu_down * (here[c] - under[c])
                total[c] = flux if total[c] is None else total[c] + flux
            pressure[axis] = 0.5 * (over[3] - under[3])

        nu_up = viscosity([over[c] - here[c] for c in range(3)])
        nux_ref[x + 1] = nu_up
        add(0, nu_up, nux_ref[x])
        over = [jnp.where(row == rows - 1, 0.0, pltpu.roll(here[c], rows - 1, 0)) for c in range(4)]
        under = [jnp.where(row == 0, 0.0, pltpu.roll(here[c], 1, 0)) for c in range(4)]
        nu_up = viscosity([over[c] - here[c] for c in range(3)])
        nu_first = viscosity([here[c][:1] for c in range(3)])
        nuy_ref[x] = nu_up
        nuy0_ref[pl.ds(x, 1), :] = nu_first
        add(1, nu_up, jnp.where(row == 0, nu_first, pltpu.roll(nu_up, 1, 0)))
        rim = [edge_of(halo, c * planes + x) for c in range(4)]
        over = [jnp.where(lane == width - 1, rim[c], pltpu.roll(here[c], width - 1, 1)) for c in range(4)]
        under = [jnp.where(lane == 0, rim[c], pltpu.roll(here[c], 1, 1)) for c in range(4)]
        nu_up = viscosity([over[c] - here[c] for c in range(3)])
        nuz_ref[x] = nu_up
        add(2, nu_up, jnp.where(lane == 0, edge_of(rim_nu, x), pltpu.roll(nu_up, 1, 1)))
        for c in range(3):
            value = here[c] + time_step * (total[c] - pressure[c])
            next_ref[c, x] = value
        return carry

    pieces = out_sems.shape[0]
    step = planes // pieces

    def store(i):
        part = pl.ds(i * step, step)
        return pltpu.make_async_copy(next_ref.at[:, part], out_ref.at[:, part], out_sems.at[i])

    for i in range(pieces):
        lax.fori_loop(i * step, (i + 1) * step, plane, 0, unroll=True)
        store(i).start()

    taken_ref[...] = jnp.zeros_like(taken_ref)
    listed.wait()
    _, slot_lane = iotas(8, groups * extra)
    cell_of = jnp.full((8, groups * extra), -1, jnp.int32)
    odd = lax.axis_index("fluid") % 2
    for b in range(groups):
        part = (odd if b % 2 == 0 else 1 - odd) * chips + b // 2
        for k in range(cap):
            cell = list_ref[k, b]
            x, y = lax.div(cell, rows), lax.rem(cell, rows)
            first = part * extra + 3 * k
            for c in range(3):
                taken_ref[pl.ds(first + c, 1), :] = next_ref[c, x, pl.ds(y, 1), :]
            cell_of = jnp.where((slot_lane >= first) & (slot_lane < first + 3), cell, cell_of)
    cells_of_ref[...] = cell_of
    taken = taken_ref[...].astype(jnp.bfloat16).reshape((2,) + mine_ref.shape)
    mine_ref[...] = taken[0]
    lent_ref[...] = taken[1]
    for i in range(pieces):
        store(i).wait()


def pick_kernel(
    sizes, cells_of_ref, z0_ref, z1_ref, edges_ref, rim_ref, outside_ref, pick_ref
):
    _, rows, width = edges_ref.shape
    groups, walls = sizes
    _, lines, slot_rows = pick_ref.shape
    planes = lines // rows
    extra = slot_rows // groups
    _, lane = iotas(rows, width)
    halo, second, beside = (
        mix_edges(*from_neighbours(lax.axis_index("wall"), walls, z0_ref[i], z1_ref[i]), lane, shift)
        for i, shift in enumerate((2, 4, 2))
    )
    inside = pltpu.roll(edges_ref[0], 1, 1)
    outside_ref[...] = outside_edges(walls, planes, halo, second, beside, inside, rim_ref[...])
    line, slot_lane = iotas(lines, slot_rows)
    hit = line == cells_of_ref[0:1, :]
    part = (slot_lane % extra) % 3
    for c in range(3):
        pick_ref[c] = (hit & (part == c)).astype(jnp.float32).astype(jnp.bfloat16)


def product_kernel(cap, block, values_ref, after_ref, *refs):
    chips, extra, width = values_ref.shape
    recvs, out_ref = refs[:chips], refs[chips]
    depth = cap * width
    row, lane = iotas(extra, depth)
    own = row // 3 == lane // width
    here = lax.axis_index("fluid") // 2
    for m, recv_ref in enumerate(recvs):
        source = here ^ m
        at = pl.ds(pl.multiple_of(source * extra, extra), extra)
        weights = recv_ref[block, pl.ds(0, depth), :]
        predicted = lax.dot_general(
            values_ref[source], weights, (((1,), (1,)), ((), ())), preferred_element_type=jnp.float32
        )
        seen = recv_ref[block, pl.ds(depth, extra), :].astype(jnp.float32)
        misfit = jnp.where(own, predicted - jnp.concatenate([seen] * cap, axis=1), 0.0).astype(jnp.bfloat16)
        contrib = jnp.dot(misfit, weights, preferred_element_type=jnp.float32)
        high = contrib.astype(jnp.bfloat16)
        out_ref[0, at, :] = high
        out_ref[1, at, :] = (contrib - high.astype(jnp.float32)).astype(jnp.bfloat16)


def forcing_rows(c, part, mine_ref, other_ref, pick_ref):
    half = mine_ref.shape[1]
    total = None
    for i, share_ref in enumerate((mine_ref, other_ref)):
        pick = pick_ref[c, part, i * half : (i + 1) * half]
        for share in range(2):
            product = jnp.dot(pick, share_ref[share], preferred_element_type=jnp.float32)
            total = product if total is None else total + product
    return total


def ends_kernel(mine_ref, other_ref, pick_ref, first_ref, second_ref):
    _, rows, _ = first_ref.shape
    lines = pick_ref.shape[1]
    even = lax.axis_index("fluid") % 2 == 0
    for c in range(3):
        low = forcing_rows(c, slice(0, rows), mine_ref, other_ref, pick_ref)
        high = forcing_rows(c, slice(lines - rows, lines), mine_ref, other_ref, pick_ref)
        first_ref[c] = jnp.where(even, high, low).astype(jnp.bfloat16)
        second_ref[c] = jnp.where(even, low, high).astype(jnp.bfloat16)


def forcing_kernel(mine_ref, other_ref, pick_ref, after_ref, forcing_ref):
    for c in range(3):
        forcing_ref[c] = forcing_rows(c, slice(None), mine_ref, other_ref, pick_ref).reshape(forcing_ref.shape[1:])


def region_rows(values, ids, tops):
    top, low = (ids // 8).astype(jnp.float32).astype(jnp.bfloat16), (ids % 8).astype(jnp.float32).astype(jnp.bfloat16)
    main = values.astype(jnp.bfloat16)
    rest = (values - main.astype(jnp.float32)).astype(jnp.bfloat16)
    zero = jnp.zeros_like(main)
    one = jnp.ones_like(main)
    hits = [top == jnp.bfloat16(h) for h in range(tops)]
    return (
        jnp.concatenate([jnp.where(hit, main, zero) for hit in hits], axis=0),
        jnp.concatenate([jnp.where(hit, rest, zero) for hit in hits], axis=0),
        jnp.concatenate([jnp.where(low == jnp.bfloat16(l), one, zero) for l in range(8)], axis=0),
    )


def region_sums(main, rest, ones, rows):
    over_lanes = (((1,), (1,)), ((), ()))
    total = lax.dot_general(main, ones, over_lanes, preferred_element_type=jnp.float32)
    total += lax.dot_general(rest, ones, over_lanes, preferred_element_type=jnp.float32)
    row, column = iotas(*total.shape)
    total = jnp.where(row % rows == column % rows, total, 0.0)
    return jnp.sum(total.reshape(total.shape[0] // rows, rows, total.shape[1]), axis=1)


def inner_kernel(
    forcing_ref, next_ref, nux_ref, nuy_ref, nuz_ref, nuy0_ref, rim_ref, regions_ref, outside_ref,
    adjoint_ref, fpack_ref, sums_ref, main_ref, rest_ref, ones_ref,
):
    _, planes, rows, width = forcing_ref.shape
    row, lane = iotas(rows, width)
    rim_nu = rim_ref[...]
    tops = sums_ref.shape[0]

    def add_up(x, values, ids):
        at = pl.ds(pl.multiple_of(x * width, width), width)
        for part_ref, part in zip((main_ref, rest_ref, ones_ref), region_rows(values, ids, tops)):
            part_ref[:, at] = part

    def plane(x, fpack):
        nuy, nuz = nuy_ref[x], nuz_ref[x]
        nuy_down = jnp.where(row == 0, nuy0_ref[pl.ds(x, 1), :], pltpu.roll(nuy, 1, 0))
        nuz_down = jnp.where(lane == 0, edge_of(rim_nu, x), pltpu.roll(nuz, 1, 1))
        nus = (nux_ref[x + 1], nux_ref[x], nuy, nuy_down, nuz, nuz_down)
        next_up, next_down = jnp.minimum(x + 1, planes - 1), jnp.maximum(x - 1, 0)
        at_top, at_bottom = x == planes - 1, x == 0
        product = None
        for c in range(3):
            here = forcing_ref[c, x]
            over = jnp.where(at_top, 0.0, forcing_ref[c, next_up])
            under = jnp.where(at_bottom, 0.0, forcing_ref[c, next_down])
            total = nus[0] * (over - here) - nus[1] * (here - under)
            over = jnp.where(row == rows - 1, 0.0, pltpu.roll(here, rows - 1, 0))
            under = jnp.where(row == 0, 0.0, pltpu.roll(here, 1, 0))
            total += nus[2] * (over - here) - nus[3] * (here - under)
            over = jnp.where(lane == width - 1, 0.0, pltpu.roll(here, width - 1, 1))
            under = jnp.where(lane == 0, 0.0, pltpu.roll(here, 1, 1))
            total += nus[4] * (over - here) - nus[5] * (here - under)
            value = here + time_step * total
            adjoint_ref[c, x] = value
            part = value * next_ref[c, x]
            product = part if product is None else product + part
            fpack = pack_edges(fpack, here, c * planes + x, lane)
        add_up(x, product, regions_ref[x])
        return fpack

    fpack = lax.fori_loop(0, planes, plane, jnp.zeros((rows, width), jnp.float32), unroll=4)
    fpack_ref[...] = fpack
    mixed = outside_ref[...]
    reach = pltpu.roll(fpack, 1, 1) * mixed
    reach = reach + pltpu.roll(reach, width - 2 * planes, 1) + pltpu.roll(reach, width - 4 * planes, 1)
    reach = time_step * reach * rim_nu
    add_up(planes, reach, pltpu.roll(mixed, (width - 6 * planes) % width, 1).astype(jnp.int32))
    sums_ref[...] = region_sums(main_ref[...], rest_ref[...], ones_ref[...], rows)


def edge_kernel(groups, masks, x0_ref, x1_ref, nux_ref, next_ref, regions_ref, sums_ref, fpack_ref, *outs):
    _, planes, rows, width = next_ref.shape
    tops, columns = sums_ref.shape
    low, high = 0.0, 0.0
    for c in range(3):
        below, above = beside_of(c, groups, x0_ref, x1_ref)
        low += below * next_ref[c, 0]
        high += above * next_ref[c, planes - 1]
    ends = [
        region_rows(time_step * nux_ref[0] * low, regions_ref[0], tops),
        region_rows(time_step * nux_ref[planes] * high, regions_ref[planes - 1], tops),
    ]
    total = sums_ref[...] + region_sums(*(jnp.concatenate(both, axis=1) for both in zip(*ends)), rows)
    height = tops * (columns // width)
    for mask, out_ref in zip((0,) + masks, outs):
        for i in range(columns // width):
            out_ref[i * tops : (i + 1) * tops, :] = total[:, i * width : (i + 1) * width]
        if mask:
            out_ref[height : height + rows, :] = fpack_ref[...]
            if out_ref.shape[0] > height + rows:
                out_ref[height + rows :, :] = jnp.zeros((out_ref.shape[0] - height - rows, width), jnp.float32)


def beside_of(c, groups, x0_ref, x1_ref):
    return from_neighbours(
        lax.axis_index("fluid"), groups, x0_ref[c].astype(jnp.float32), x1_ref[c].astype(jnp.float32)
    )


def final_kernel(sizes, inner_ref, x0_ref, x1_ref, nux_ref, rim_ref, own_ref, *refs):
    groups, walls = sizes
    arrived, (adjoint_ref, sens_ref, value_ref, sems) = refs[:-4], refs[-4:]
    _, planes, rows, width = inner_ref.shape
    per = own_ref.shape[0]
    _, lane = iotas(rows, width)
    me = lax.axis_index("wall")
    total = own_ref[...]
    below = jnp.zeros((rows, width), jnp.float32)
    above = jnp.zeros((rows, width), jnp.float32)
    for mask, ref in zip(range(1, walls), arrived):
        total = total + ref[:per, :]
        if mask & (mask + 1) == 0:
            edges = ref[per : per + rows, :]
            above = jnp.where((me ^ mask) == me + 1, edges, above)
            below = jnp.where((me ^ mask) == me - 1, edges, below)
    mixed = mix_edges(below, above, lane)
    edge_nu = time_step * rim_ref[...]
    edge_nu = edge_nu + pltpu.roll(edge_nu, 2 * planes, 1) + pltpu.roll(edge_nu, 4 * planes, 1)
    edge_flux = mixed * edge_nu
    on_edge = (lane == 0) | (lane == width - 1)

    beside = [beside_of(c, groups, x0_ref, x1_ref) for c in range(3)]
    step = planes // sems.shape[0]

    def store(i):
        part = pl.ds(i * step, step)
        return pltpu.make_async_copy(value_ref.at[:, part], adjoint_ref.at[:, part], sems.at[i])

    for i in range(sems.shape[0]):
        for x in range(i * step, (i + 1) * step):
            for c in range(3):
                value = inner_ref[c, x] + jnp.where(on_edge, edge_of(edge_flux, c * planes + x), 0.0)
                if x == 0:
                    value += time_step * nux_ref[0] * beside[c][0]
                if x == planes - 1:
                    value += time_step * nux_ref[planes] * beside[c][1]
                value_ref[c, x] = value
        store(i).start()
    parts = width // rows
    tops = REG_DEV * walls // 8
    owned = REG_DEV // 8
    top, _ = iotas(tops, width)
    region, lane = iotas(REG_DEV, width)
    sens = jnp.zeros((8, REG_DEV), jnp.float32)
    for i in range(8 // parts):
        for h in range(owned):
            mine = jnp.where(top == me * owned + h, total[i * tops : (i + 1) * tops], 0.0)
            gather = (region == h * 8 + i * parts + lane // rows).astype(jnp.float32)
            sens += lax.dot_general(
                jnp.broadcast_to(jnp.sum(mine, axis=0, keepdims=True), (8, width)), gather, (((1,), (1,)), ((), ())),
                precision=lax.Precision.HIGHEST, preferred_element_type=jnp.float32,
            )
    sens_ref[...] = sens_scale * sens[:1]
    for i in range(sems.shape[0]):
        store(i).wait()


def body(flow_state, regions, obs_tiles, measured, tile_dest, cell_list):
    groups, walls = lax.axis_size("fluid"), lax.axis_size("wall")
    sizes = (groups, walls)
    _, planes, rows, width = flow_state.shape
    count_tiles = obs_tiles.shape[2]
    cap = cell_list.shape[3]
    extra = -(-cap * 3 // 16) * 16
    reg_count = REG_DEV * walls
    cells = groups * cap
    grid = planes * rows * width

    chips = groups // 2
    height = cap * width + extra
    even = lax.axis_index("fluid") % 2 == 0
    low, high = flow_state[:, 0], flow_state[:, planes - 1]
    xs0, xs1 = jnp.where(even, high, low), jnp.where(even, low, high)
    x0, x1 = swap(xs0, "fluid", 0), swap(xs1, "fluid", 1)
    sends = call(
        functools.partial(group_kernel, cap),
        (bf16(2, height, width),) * chips,
        [HBM] * 3 + [ANY],
        (tile_dest[0, 0], obs_tiles[0, 0], jnp.transpose(measured[0, 0], (1, 0, 2)), xs1),
        (
            pltpu.SMEM((count_tiles,), jnp.int32),
            pltpu.VMEM((count_tiles, width, width), jnp.bfloat16),
            pltpu.VMEM((3, count_tiles, width), jnp.bfloat16),
            pltpu.SMEM((groups,), jnp.int32),
            pltpu.SMEM((cells,), jnp.int32),
            pltpu.VMEM((groups * extra, width), jnp.bfloat16),
            pltpu.VMEM((width, width), jnp.bfloat16),
            pltpu.SemaphoreType.DMA,
            pltpu.SemaphoreType.DMA,
            pltpu.SemaphoreType.DMA((4,)),
            pltpu.SemaphoreType.DMA((cells,)),
            pltpu.SemaphoreType.DMA((groups,)),
        ),
        out_specs=(HBM,) * chips,
        limit=60 * 1024 * 1024,
    )
    *sends, x0, x1 = lax.optimization_barrier((*sends, x0, x1))
    recvs = [sends[0]] + [cross(sends[m], "fluid", 2 * m) for m in range(1, chips)]
    zs = call(
        functools.partial(edges_kernel, groups),
        f32(3, rows, width),
        [VMEM] * 4,
        (flow_state, regions, x0, x1),
    )
    z0, z1 = swap(zs, "wall", 0), swap(zs, "wall", 1)
    slot_rows = groups * extra
    velocity_next, velocity, nux, nuy, nuz, nuy0, rim, mine, lent, cells_of = call(
        functools.partial(forward_kernel, sizes, cap),
        (f32(3, planes, rows, width),) * 2
        + (f32(planes + 1, rows, width), f32(planes, rows, width), f32(planes, rows, width))
        + (f32(planes, width), f32(rows, width))
        + (bf16(chips, extra, width),) * 2
        + (jax.ShapeDtypeStruct((8, slot_rows), jnp.int32),),
        [ANY] + [VMEM] * 6,
        (cell_list[0, 0].T, flow_state, x0, x1, z0, z1, zs),
        (
            pltpu.SMEM((cap, groups), jnp.int32),
            pltpu.VMEM((4, planes + 2, rows, width), jnp.float32),
            pltpu.VMEM((slot_rows, width), jnp.float32),
            pltpu.SemaphoreType.DMA,
            pltpu.SemaphoreType.DMA((4,)),
        ),
        out_specs=(HBM,) + (VMEM,) * 9,
    )
    borrowed = cross(lent, "fluid", 1)
    outside, pick = call(
        functools.partial(pick_kernel, sizes),
        (f32(rows, width), bf16(3, planes * rows, slot_rows)),
        [VMEM] * 5,
        (cells_of, z0, z1, zs, rim),
    )

    def products(block, values, after):
        return call(
            functools.partial(product_kernel, cap, block),
            bf16(2, chips * extra, width),
            [VMEM, ANY] + [VMEM] * chips,
            (values, after, *recvs),
        )

    given = products(1, borrowed, pick)
    other = cross(given, "fluid", 1)
    held = products(0, mine, given)
    fs0, fs1 = call(ends_kernel, (bf16(3, rows, width),) * 2, [VMEM] * 3, (held, other, pick))
    f0, f1 = swap(fs0, "fluid", 0), swap(fs1, "fluid", 1)
    forcing = call(forcing_kernel, f32(3, planes, rows, width), [VMEM] * 3 + [ANY], (held, other, pick, fs1))
    tops = reg_count // 8
    columns = 8 * rows
    sum_rows = tops * (columns // width)
    inner, fpack, sums = call(
        inner_kernel,
        (f32(3, planes, rows, width), f32(rows, width), f32(tops, columns)),
        [VMEM] * 9,
        (forcing, velocity, nux, nuy, nuz, nuy0, rim, regions, outside),
        (
            pltpu.VMEM((tops * rows, (planes + 1) * width), jnp.bfloat16),
            pltpu.VMEM((tops * rows, (planes + 1) * width), jnp.bfloat16),
            pltpu.VMEM((columns, (planes + 1) * width), jnp.bfloat16),
        ),
    )
    masks = tuple(range(1, walls))
    heights = [sum_rows] + [sum_rows + rows + 8 * (mask - 1) for mask in masks]
    own, *parts = call(
        functools.partial(edge_kernel, groups, masks),
        tuple(f32(height, width) for height in heights),
        [VMEM] * 7,
        (f0, f1, nux, velocity, regions, sums, fpack),
    )
    arrived = [cross(part, "wall", mask) for part, mask in zip(parts, masks)]
    adjoint, sens = call(
        functools.partial(final_kernel, sizes),
        (f32(3, planes, rows, width), f32(1, REG_DEV)),
        [VMEM] * (6 + len(arrived)),
        (inner, f0, f1, nux, rim, own, *arrived),
        (pltpu.VMEM((3, planes, rows, width), jnp.float32), pltpu.SemaphoreType.DMA((4,))),
        out_specs=(HBM, VMEM),
        flops=10 * grid,
        moved=24 * grid,
    )
    return velocity_next, adjoint, sens.reshape(REG_DEV)


def solution(mesh):
    in_specs = (
        P(None, "fluid", None, "wall"),
        P("fluid", None, "wall"),
        P("fluid", "wall", None, None, None),
        P("fluid", "wall", None, None, None),
        P("fluid", "wall", None),
        P("fluid", "wall", None, None),
    )
    out_specs = (
        P(None, "fluid", None, "wall"),
        P(None, "fluid", None, "wall"),
        P(("fluid", "wall")),
    )
    return jax.shard_map(body, mesh=mesh, in_specs=in_specs, out_specs=out_specs, check_vma=False)
```

```python
import functools

import jax
import jax.numpy as jnp
from jax import lax
from jax.experimental import pallas as pl
from jax.experimental.pallas import tpu as pltpu
from jax.sharding import PartitionSpec as P

REG_DEV = 16

time_step = 0.12
nu_floor = 0.1
nu_spread = 0.9
relax_sq = 4.0
sens_scale = 0.03

VMEM = pl.BlockSpec(memory_space=pltpu.VMEM)
SMEM = pl.BlockSpec(memory_space=pltpu.SMEM)
ANY = pl.BlockSpec(memory_space=pl.ANY)
HBM = pl.BlockSpec(memory_space=pltpu.HBM)
LIMIT = 24 * 1024 * 1024
HIDES = 100_000_000_000


def call(kernel, outs, ins, operands, scratch=(), flops=1, moved=1, out_specs=None, limit=LIMIT):
    return pl.pallas_call(
        kernel,
        out_shape=outs,
        in_specs=ins,
        out_specs=out_specs if out_specs is not None else jax.tree.map(lambda _: VMEM, outs),
        scratch_shapes=list(scratch),
        compiler_params=pltpu.CompilerParams(vmem_limit_bytes=limit),
        cost_estimate=pl.CostEstimate(flops=flops, bytes_accessed=moved, transcendentals=0),
    )(*operands)


def f32(*shape):
    return jax.ShapeDtypeStruct(shape, jnp.float32)


def bf16(*shape):
    return jax.ShapeDtypeStruct(shape, jnp.bfloat16)


def swap(block, axis, turn):
    groups, walls = lax.axis_size("fluid"), lax.axis_size("wall")

    def partner(f, w):
        at, count = (f, groups) if axis == "fluid" else (w, walls)
        other = at + 1 if (at + turn) % 2 == 0 else at - 1
        if axis == "fluid":
            return (other, w) if 0 <= other < count else (f, w ^ 1)
        return (f, other) if 0 <= other < count else (f ^ 1, w)

    pairs = []
    for f in range(groups):
        for w in range(walls):
            to_f, to_w = partner(f, w)
            pairs.append((f * walls + w, to_f * walls + to_w))
    return lax.ppermute(block, ("fluid", "wall"), pairs)


def cross(block, axis, mask):
    return lax.ppermute(block, axis, [(i, i ^ mask) for i in range(lax.axis_size(axis))])


def from_neighbours(index, count, first, second):
    even = index % 2 == 0
    above = jnp.where(even, first, second)
    below = jnp.where(even, second, first)
    above = jnp.where(index == count - 1, jnp.zeros_like(above), above)
    below = jnp.where(index == 0, jnp.zeros_like(below), below)
    return below, above


def pack_edges(packed, plane, m, lane):
    width = lane.shape[1]
    here = (lane == 2 * m) | (lane == (2 * m + width - 1) % width)
    return jnp.where(here, pltpu.roll(plane, 2 * m, 1), packed)


def mix_edges(below, above, lane, shift=2):
    return jnp.where(lane % 2 == 0, above, pltpu.roll(below, shift, 1))


def edge_of(mixed, m):
    width = mixed.shape[1]
    return pltpu.roll(mixed, (2 * width - (2 * m + 1)) % width, 1)


def viscosity(jumps):
    shear_sq = jumps[0] * jumps[0] + jumps[1] * jumps[1] + jumps[2] * jumps[2]
    root = lax.rsqrt(1.0 + relax_sq * shear_sq)
    return nu_floor + nu_spread * (root * lax.rsqrt(root))


def iotas(rows, width):
    shape = (rows, width)
    return lax.broadcasted_iota(jnp.int32, shape, 0), lax.broadcasted_iota(jnp.int32, shape, 1)


def faces_kernel(flow_ref, first_ref, second_ref, sems):
    last = flow_ref.shape[1] - 1
    odd = lax.axis_index("fluid") % 2
    copies = [
        pltpu.make_async_copy(flow_ref.at[c, plane], out_ref.at[c], sems.at[i, c])
        for i, (plane, out_ref) in enumerate(((last - last * odd, first_ref), (last * odd, second_ref)))
        for c in range(flow_ref.shape[0])
    ]
    for copy in copies:
        copy.start()
    for copy in copies:
        copy.wait()


def edges_kernel(groups, flow_ref, regions_ref, x0_ref, x1_ref, edges_ref):
    fields, planes, rows, width = flow_ref.shape
    _, lane = iotas(rows, width)
    outer = jnp.zeros((rows, width), jnp.float32)
    second, beside = outer, outer
    for c in range(fields):
        for x in range(planes):
            m, plane = c * planes + x, flow_ref[c, x]
            outer = pack_edges(outer, plane, m, lane)
            here = (lane == 2 * m) | (lane == (2 * m - 3) % width)
            second = jnp.where(here, pltpu.roll(plane, (2 * m - 1) % width, 1), second)
        for side, plane in enumerate(from_neighbours(lax.axis_index("fluid"), groups, x0_ref[c], x1_ref[c])):
            beside = pack_edges(beside, plane, 2 * c + side, lane)
    for x in range(planes):
        beside = pack_edges(beside, regions_ref[x].astype(jnp.float32), 2 * fields + x, lane)
    edges_ref[0], edges_ref[1], edges_ref[2] = outer, second, beside


def outside_edges(walls, planes, halo, second, beside, inside, rim_nu):
    rows, width = halo.shape
    row, lane = iotas(rows, width)
    x, field = (lane // 2) % planes, (lane // 2) // planes

    def spread(nu):
        nu = jnp.where(field == 0, nu, 0.0)
        return nu + pltpu.roll(nu, 2 * planes, 1) + pltpu.roll(nu, 4 * planes, 1)

    def nu_of(jump):
        return spread(viscosity([jump] + [pltpu.roll(jump, width - 2 * c * planes, 1) for c in (1, 2)]))

    over_x, under_x = pltpu.roll(halo, width - 2, 1), pltpu.roll(halo, 2, 1)
    for c in range(4):
        low = pltpu.roll(beside, (2 * c * planes - 4 * c) % width, 1)
        high = pltpu.roll(beside, (2 * (c * planes + planes - 1) - 4 * c - 2) % width, 1)
        under_x = jnp.where((x == 0) & (field == c), low, under_x)
        over_x = jnp.where((x == planes - 1) & (field == c), high, over_x)
    over_y = jnp.where(row == rows - 1, 0.0, pltpu.roll(halo, rows - 1, 0))
    under_y = jnp.where(row == 0, 0.0, pltpu.roll(halo, 1, 0))
    total = spread(rim_nu) * (inside - halo)
    for other in (over_x, under_x, over_y, under_y, second):
        total += nu_of(other - halo) * (other - halo)
    above = lane % 2 == 0
    gradient_x = pltpu.roll(0.5 * (over_x - under_x), width - 6 * planes, 1)
    gradient_y = pltpu.roll(0.5 * (over_y - under_y), width - 4 * planes, 1)
    gradient_z = pltpu.roll(0.5 * jnp.where(above, second - inside, inside - second), width - 2 * planes, 1)
    gradient = jnp.where(field == 0, gradient_x, jnp.where(field == 1, gradient_y, gradient_z))
    value = halo + time_step * (total - gradient)
    value = jnp.where(field == 3, pltpu.roll(beside, 6 * planes - 16, 1), value)
    me = lax.axis_index("wall")
    exists = jnp.where(above, jnp.where(me < walls - 1, 1, 0), jnp.where(me > 0, 1, 0)) == 1
    return jnp.where(exists & (field < 4), value, 0.0)


def group_kernel(cap, dest_ref, tiles_ref, meas_ref, after_ref, *refs):
    chips = len(refs) - 12
    sends = refs[:chips]
    (list_ref, held_ref, seen_ref, count_ref, slot_ref, rows_ref, blank_ref,
     list_sem, seen_sem, in_sems, out_sems, row_sems) = refs[chips:]
    count_tiles, width, _ = tiles_ref.shape
    groups = 2 * chips
    slots = groups * cap
    extra = rows_ref.shape[0] // groups
    depth = cap * width
    me = lax.axis_index("fluid")
    listed = pltpu.make_async_copy(dest_ref, list_ref, list_sem)
    listed.start()
    piece = count_tiles // in_sems.shape[0]

    def load(p):
        part = pl.ds(p * piece, piece)
        return pltpu.make_async_copy(tiles_ref.at[part], held_ref.at[part], in_sems.at[p])

    for p in range(in_sems.shape[0]):
        load(p).start()
    seen = pltpu.make_async_copy(meas_ref, seen_ref, seen_sem)
    seen.start()

    def clear(b, carry):
        count_ref[b] = 0
        for k in range(cap):
            slot_ref[b * cap + k] = -1
        return carry

    lax.fori_loop(0, groups, clear, 0)
    if slots > count_tiles:
        blank_ref[...] = jnp.zeros_like(blank_ref)
    _, tile_lane = iotas(8, count_tiles)
    listed.wait()

    def place(t, slot_of):
        b = list_ref[t]
        k = count_ref[b]
        count_ref[b] = k + 1
        slot_ref[b * cap + k] = t
        return jnp.where(tile_lane == t, b * cap + k, slot_of)

    slot_of = lax.fori_loop(
        0, count_tiles, place, jnp.full((8, count_tiles), -1, jnp.int32), unroll=True
    )
    for p in range(in_sems.shape[0]):
        load(p).wait()

    def each(act):
        for m in list(range(1, chips)) + [0]:
            for j in range(2):
                b = me ^ (2 * m + j)
                for k in range(cap):
                    t = slot_ref[b * cap + k]
                    at = sends[m].at[j, pl.ds(k * width, width), :]
                    sem = out_sems.at[(2 * m + j) * cap + k]
                    if slots > count_tiles:

                        @pl.when(t >= 0)
                        def _():
                            act(pltpu.make_async_copy(held_ref.at[t], at, sem))

                        @pl.when(t < 0)
                        def _():
                            act(pltpu.make_async_copy(blank_ref, at, sem))

                    else:
                        act(pltpu.make_async_copy(held_ref.at[t], at, sem))

    each(lambda copy: copy.start())

    seen.wait()
    row = lax.broadcasted_iota(jnp.int32, (groups * extra, count_tiles), 0)
    within = row % extra
    row_slot = (row // extra) * cap + within // 3
    used = within < cap * 3
    total = jnp.zeros((groups * extra, width), jnp.float32)
    for c in range(3):
        pick = (row_slot == slot_of[0:1, :]) & used & (within % 3 == c)
        total += jnp.dot(
            pick.astype(jnp.float32).astype(jnp.bfloat16), seen_ref[c], preferred_element_type=jnp.float32
        )
    rows_ref[...] = total.astype(jnp.bfloat16)

    def row_copy(m, j):
        b = me ^ (2 * m + j)
        return pltpu.make_async_copy(
            rows_ref.at[pl.ds(pl.multiple_of(b * extra, extra), extra), :],
            sends[m].at[j, pl.ds(depth, extra), :],
            row_sems.at[2 * m + j],
        )

    for m in range(chips):
        for j in range(2):
            row_copy(m, j).start()
    each(lambda copy: copy.wait())
    for m in range(chips):
        for j in range(2):
            row_copy(m, j).wait()


def forward_kernel(
    sizes, cap, cells_ref, flow_ref, x0_ref, x1_ref, z0_ref, z1_ref, edges_ref,
    out_ref, next_ref, nux_ref, nuy_ref, nuz_ref, nuy0_ref, rim_ref, mine_ref, lent_ref, cells_of_ref,
    list_ref, padded_ref, taken_ref, list_sem, out_sems,
):
    _, planes, rows, width = flow_ref.shape
    groups, walls = sizes
    chips, extra, _ = mine_ref.shape
    listed = pltpu.make_async_copy(cells_ref, list_ref, list_sem)
    listed.start()
    row, lane = iotas(rows, width)
    halo = mix_edges(*from_neighbours(lax.axis_index("wall"), walls, z0_ref[0], z1_ref[0]), lane)
    inside = pltpu.roll(edges_ref[0], 1, 1)
    jump = halo - inside
    rim_nu = viscosity([jump] + [pltpu.roll(jump, width - 2 * c * planes, 1) for c in (1, 2)])
    rim_nu = jnp.where(lane < 2 * planes, rim_nu, 0.0)
    rim_ref[...] = rim_nu
    for c in range(4):
        low, high = from_neighbours(lax.axis_index("fluid"), groups, x0_ref[c], x1_ref[c])
        padded_ref[c, 0] = low
        padded_ref[c, planes + 1] = high
        padded_ref[c, 1 : planes + 1] = flow_ref[c]
    nux_ref[0] = viscosity([padded_ref[c, 1] - padded_ref[c, 0] for c in range(3)])

    def plane(x, carry):
        here = [padded_ref[c, x + 1] for c in range(4)]
        over = [padded_ref[c, x + 2] for c in range(4)]
        under = [padded_ref[c, x] for c in range(4)]
        total = [None] * 3
        pressure = [None] * 3

        def add(axis, nu_up, nu_down):
            for c in range(3):
                flux = nu_up * (over[c] - here[c]) - nu_down * (here[c] - under[c])
                total[c] = flux if total[c] is None else total[c] + flux
            pressure[axis] = 0.5 * (over[3] - under[3])

        nu_up = viscosity([over[c] - here[c] for c in range(3)])
        nux_ref[x + 1] = nu_up
        add(0, nu_up, nux_ref[x])
        over = [jnp.where(row == rows - 1, 0.0, pltpu.roll(here[c], rows - 1, 0)) for c in range(4)]
        under = [jnp.where(row == 0, 0.0, pltpu.roll(here[c], 1, 0)) for c in range(4)]
        nu_up = viscosity([over[c] - here[c] for c in range(3)])
        nu_first = viscosity([here[c][:1] for c in range(3)])
        nuy_ref[x] = nu_up
        nuy0_ref[pl.ds(x, 1), :] = nu_first
        add(1, nu_up, jnp.where(row == 0, nu_first, pltpu.roll(nu_up, 1, 0)))
        rim = [edge_of(halo, c * planes + x) for c in range(4)]
        over = [jnp.where(lane == width - 1, rim[c], pltpu.roll(here[c], width - 1, 1)) for c in range(4)]
        under = [jnp.where(lane == 0, rim[c], pltpu.roll(here[c], 1, 1)) for c in range(4)]
        nu_up = viscosity([over[c] - here[c] for c in range(3)])
        nuz_ref[x] = nu_up
        add(2, nu_up, jnp.where(lane == 0, edge_of(rim_nu, x), pltpu.roll(nu_up, 1, 1)))
        for c in range(3):
            value = here[c] + time_step * (total[c] - pressure[c])
            next_ref[c, x] = value
        return carry

    pieces = out_sems.shape[0]
    step = planes // pieces

    def store(i):
        part = pl.ds(i * step, step)
        return pltpu.make_async_copy(next_ref.at[:, part], out_ref.at[:, part], out_sems.at[i])

    for i in range(pieces):
        lax.fori_loop(i * step, (i + 1) * step, plane, 0, unroll=True)
        store(i).start()

    taken_ref[...] = jnp.zeros_like(taken_ref)
    listed.wait()
    _, slot_lane = iotas(8, groups * extra)
    cell_of = jnp.full((8, groups * extra), -1, jnp.int32)
    odd = lax.axis_index("fluid") % 2
    for b in range(groups):
        part = (odd if b % 2 == 0 else 1 - odd) * chips + b // 2
        for k in range(cap):
            cell = list_ref[k, b]
            x, y = lax.div(cell, rows), lax.rem(cell, rows)
            first = part * extra + 3 * k
            for c in range(3):
                taken_ref[pl.ds(first + c, 1), :] = next_ref[c, x, pl.ds(y, 1), :]
            cell_of = jnp.where((slot_lane >= first) & (slot_lane < first + 3), cell, cell_of)
    cells_of_ref[...] = cell_of
    taken = taken_ref[...].astype(jnp.bfloat16).reshape((2,) + mine_ref.shape)
    mine_ref[...] = taken[0]
    lent_ref[...] = taken[1]
    for i in range(pieces):
        store(i).wait()


def pick_kernel(
    sizes, cells_of_ref, z0_ref, z1_ref, edges_ref, rim_ref, outside_ref, pick_ref
):
    _, rows, width = edges_ref.shape
    groups, walls = sizes
    _, lines, slot_rows = pick_ref.shape
    planes = lines // rows
    extra = slot_rows // groups
    _, lane = iotas(rows, width)
    halo, second, beside = (
        mix_edges(*from_neighbours(lax.axis_index("wall"), walls, z0_ref[i], z1_ref[i]), lane, shift)
        for i, shift in enumerate((2, 4, 2))
    )
    inside = pltpu.roll(edges_ref[0], 1, 1)
    outside_ref[...] = outside_edges(walls, planes, halo, second, beside, inside, rim_ref[...])
    line, slot_lane = iotas(lines, slot_rows)
    hit = line == cells_of_ref[0:1, :]
    part = (slot_lane % extra) % 3
    for c in range(3):
        pick_ref[c] = (hit & (part == c)).astype(jnp.float32).astype(jnp.bfloat16)


def product_kernel(cap, block, values_ref, after_ref, *refs):
    chips, extra, width = values_ref.shape
    recvs, out_ref = refs[:chips], refs[chips]
    depth = cap * width
    row, lane = iotas(extra, depth)
    own = row // 3 == lane // width
    here = lax.axis_index("fluid") // 2
    for m, recv_ref in enumerate(recvs):
        source = here ^ m
        at = pl.ds(pl.multiple_of(source * extra, extra), extra)
        weights = recv_ref[block, pl.ds(0, depth), :]
        predicted = lax.dot_general(
            values_ref[source], weights, (((1,), (1,)), ((), ())), preferred_element_type=jnp.float32
        )
        seen = recv_ref[block, pl.ds(depth, extra), :].astype(jnp.float32)
        misfit = jnp.where(own, predicted - jnp.concatenate([seen] * cap, axis=1), 0.0).astype(jnp.bfloat16)
        contrib = jnp.dot(misfit, weights, preferred_element_type=jnp.float32)
        high = contrib.astype(jnp.bfloat16)
        out_ref[0, at, :] = high
        out_ref[1, at, :] = (contrib - high.astype(jnp.float32)).astype(jnp.bfloat16)


def forcing_rows(c, part, mine_ref, other_ref, pick_ref):
    half = mine_ref.shape[1]
    total = None
    for i, share_ref in enumerate((mine_ref, other_ref)):
        pick = pick_ref[c, part, i * half : (i + 1) * half]
        for share in range(2):
            product = jnp.dot(pick, share_ref[share], preferred_element_type=jnp.float32)
            total = product if total is None else total + product
    return total


def ends_kernel(mine_ref, other_ref, pick_ref, first_ref, second_ref):
    _, rows, _ = first_ref.shape
    lines = pick_ref.shape[1]
    even = lax.axis_index("fluid") % 2 == 0
    for c in range(3):
        low = forcing_rows(c, slice(0, rows), mine_ref, other_ref, pick_ref)
        high = forcing_rows(c, slice(lines - rows, lines), mine_ref, other_ref, pick_ref)
        first_ref[c] = jnp.where(even, high, low).astype(jnp.bfloat16)
        second_ref[c] = jnp.where(even, low, high).astype(jnp.bfloat16)


def forcing_kernel(mine_ref, other_ref, pick_ref, after_ref, forcing_ref):
    for c in range(3):
        forcing_ref[c] = forcing_rows(c, slice(None), mine_ref, other_ref, pick_ref).reshape(forcing_ref.shape[1:])


def region_rows(values, ids, tops):
    top, low = (ids // 8).astype(jnp.float32).astype(jnp.bfloat16), (ids % 8).astype(jnp.float32).astype(jnp.bfloat16)
    main = values.astype(jnp.bfloat16)
    rest = (values - main.astype(jnp.float32)).astype(jnp.bfloat16)
    zero = jnp.zeros_like(main)
    one = jnp.ones_like(main)
    hits = [top == jnp.bfloat16(h) for h in range(tops)]
    return (
        jnp.concatenate([jnp.where(hit, main, zero) for hit in hits], axis=0),
        jnp.concatenate([jnp.where(hit, rest, zero) for hit in hits], axis=0),
        jnp.concatenate([jnp.where(low == jnp.bfloat16(l), one, zero) for l in range(8)], axis=0),
    )


def region_sums(main, rest, ones, rows):
    over_lanes = (((1,), (1,)), ((), ()))
    total = lax.dot_general(main, ones, over_lanes, preferred_element_type=jnp.float32)
    total += lax.dot_general(rest, ones, over_lanes, preferred_element_type=jnp.float32)
    row, column = iotas(*total.shape)
    total = jnp.where(row % rows == column % rows, total, 0.0)
    return jnp.sum(total.reshape(total.shape[0] // rows, rows, total.shape[1]), axis=1)


def inner_kernel(
    forcing_ref, next_ref, nux_ref, nuy_ref, nuz_ref, nuy0_ref, rim_ref, regions_ref, outside_ref,
    adjoint_ref, fpack_ref, sums_ref, main_ref, rest_ref, ones_ref,
):
    _, planes, rows, width = forcing_ref.shape
    row, lane = iotas(rows, width)
    rim_nu = rim_ref[...]
    tops = sums_ref.shape[0]

    def add_up(x, values, ids):
        at = pl.ds(pl.multiple_of(x * width, width), width)
        for part_ref, part in zip((main_ref, rest_ref, ones_ref), region_rows(values, ids, tops)):
            part_ref[:, at] = part

    def plane(x, fpack):
        nuy, nuz = nuy_ref[x], nuz_ref[x]
        nuy_down = jnp.where(row == 0, nuy0_ref[pl.ds(x, 1), :], pltpu.roll(nuy, 1, 0))
        nuz_down = jnp.where(lane == 0, edge_of(rim_nu, x), pltpu.roll(nuz, 1, 1))
        nus = (nux_ref[x + 1], nux_ref[x], nuy, nuy_down, nuz, nuz_down)
        next_up, next_down = jnp.minimum(x + 1, planes - 1), jnp.maximum(x - 1, 0)
        at_top, at_bottom = x == planes - 1, x == 0
        product = None
        for c in range(3):
            here = forcing_ref[c, x]
            over = jnp.where(at_top, 0.0, forcing_ref[c, next_up])
            under = jnp.where(at_bottom, 0.0, forcing_ref[c, next_down])
            total = nus[0] * (over - here) - nus[1] * (here - under)
            over = jnp.where(row == rows - 1, 0.0, pltpu.roll(here, rows - 1, 0))
            under = jnp.where(row == 0, 0.0, pltpu.roll(here, 1, 0))
            total += nus[2] * (over - here) - nus[3] * (here - under)
            over = jnp.where(lane == width - 1, 0.0, pltpu.roll(here, width - 1, 1))
            under = jnp.where(lane == 0, 0.0, pltpu.roll(here, 1, 1))
            total += nus[4] * (over - here) - nus[5] * (here - under)
            value = here + time_step * total
            adjoint_ref[c, x] = value
            part = value * next_ref[c, x]
            product = part if product is None else product + part
            fpack = pack_edges(fpack, here, c * planes + x, lane)
        add_up(x, product, regions_ref[x])
        return fpack

    fpack = lax.fori_loop(0, planes, plane, jnp.zeros((rows, width), jnp.float32), unroll=4)
    fpack_ref[...] = fpack
    mixed = outside_ref[...]
    reach = pltpu.roll(fpack, 1, 1) * mixed
    reach = reach + pltpu.roll(reach, width - 2 * planes, 1) + pltpu.roll(reach, width - 4 * planes, 1)
    reach = time_step * reach * rim_nu
    add_up(planes, reach, pltpu.roll(mixed, (width - 6 * planes) % width, 1).astype(jnp.int32))
    sums_ref[...] = region_sums(main_ref[...], rest_ref[...], ones_ref[...], rows)


def edge_kernel(groups, masks, x0_ref, x1_ref, nux_ref, next_ref, regions_ref, sums_ref, fpack_ref, *outs):
    _, planes, rows, width = next_ref.shape
    tops, columns = sums_ref.shape
    low, high = 0.0, 0.0
    for c in range(3):
        below, above = beside_of(c, groups, x0_ref, x1_ref)
        low += below * next_ref[c, 0]
        high += above * next_ref[c, planes - 1]
    ends = [
        region_rows(time_step * nux_ref[0] * low, regions_ref[0], tops),
        region_rows(time_step * nux_ref[planes] * high, regions_ref[planes - 1], tops),
    ]
    total = sums_ref[...] + region_sums(*(jnp.concatenate(both, axis=1) for both in zip(*ends)), rows)
    height = tops * (columns // width)
    for mask, out_ref in zip((0,) + masks, outs):
        for i in range(columns // width):
            out_ref[i * tops : (i + 1) * tops, :] = total[:, i * width : (i + 1) * width]
        if mask:
            out_ref[height : height + rows, :] = fpack_ref[...]
            if out_ref.shape[0] > height + rows:
                out_ref[height + rows :, :] = jnp.zeros((out_ref.shape[0] - height - rows, width), jnp.float32)


def beside_of(c, groups, x0_ref, x1_ref):
    return from_neighbours(
        lax.axis_index("fluid"), groups, x0_ref[c].astype(jnp.float32), x1_ref[c].astype(jnp.float32)
    )


def final_kernel(sizes, inner_ref, x0_ref, x1_ref, nux_ref, rim_ref, own_ref, *refs):
    groups, walls = sizes
    arrived, (adjoint_ref, sens_ref, value_ref, sems) = refs[:-4], refs[-4:]
    _, planes, rows, width = inner_ref.shape
    per = own_ref.shape[0]
    _, lane = iotas(rows, width)
    me = lax.axis_index("wall")
    total = own_ref[...]
    below = jnp.zeros((rows, width), jnp.float32)
    above = jnp.zeros((rows, width), jnp.float32)
    for mask, ref in zip(range(1, walls), arrived):
        total = total + ref[:per, :]
        if mask & (mask + 1) == 0:
            edges = ref[per : per + rows, :]
            above = jnp.where((me ^ mask) == me + 1, edges, above)
            below = jnp.where((me ^ mask) == me - 1, edges, below)
    mixed = mix_edges(below, above, lane)
    edge_nu = time_step * rim_ref[...]
    edge_nu = edge_nu + pltpu.roll(edge_nu, 2 * planes, 1) + pltpu.roll(edge_nu, 4 * planes, 1)
    edge_flux = mixed * edge_nu
    on_edge = (lane == 0) | (lane == width - 1)

    beside = [beside_of(c, groups, x0_ref, x1_ref) for c in range(3)]
    step = planes // sems.shape[0]

    def store(i):
        part = pl.ds(i * step, step)
        return pltpu.make_async_copy(value_ref.at[:, part], adjoint_ref.at[:, part], sems.at[i])

    for i in range(sems.shape[0]):
        for x in range(i * step, (i + 1) * step):
            for c in range(3):
                value = inner_ref[c, x] + jnp.where(on_edge, edge_of(edge_flux, c * planes + x), 0.0)
                if x == 0:
                    value += time_step * nux_ref[0] * beside[c][0]
                if x == planes - 1:
                    value += time_step * nux_ref[planes] * beside[c][1]
                value_ref[c, x] = value
        store(i).start()
    parts = width // rows
    tops = REG_DEV * walls // 8
    owned = REG_DEV // 8
    top, _ = iotas(tops, width)
    region, lane = iotas(REG_DEV, width)
    sens = jnp.zeros((8, REG_DEV), jnp.float32)
    for i in range(8 // parts):
        for h in range(owned):
            mine = jnp.where(top == me * owned + h, total[i * tops : (i + 1) * tops], 0.0)
            gather = (region == h * 8 + i * parts + lane // rows).astype(jnp.float32)
            sens += lax.dot_general(
                jnp.broadcast_to(jnp.sum(mine, axis=0, keepdims=True), (8, width)), gather, (((1,), (1,)), ((), ())),
                precision=lax.Precision.HIGHEST, preferred_element_type=jnp.float32,
            )
    sens_ref[...] = sens_scale * sens[:1]
    for i in range(sems.shape[0]):
        store(i).wait()


def body(flow_state, regions, obs_tiles, measured, tile_dest, cell_list):
    groups, walls = lax.axis_size("fluid"), lax.axis_size("wall")
    sizes = (groups, walls)
    _, planes, rows, width = flow_state.shape
    count_tiles = obs_tiles.shape[2]
    cap = cell_list.shape[3]
    extra = -(-cap * 3 // 16) * 16
    reg_count = REG_DEV * walls
    cells = groups * cap
    grid = planes * rows * width

    chips = groups // 2
    height = cap * width + extra
    even = lax.axis_index("fluid") % 2 == 0
    low, high = flow_state[:, 0], flow_state[:, planes - 1]
    xs0, xs1 = jnp.where(even, high, low), jnp.where(even, low, high)
    x0, x1 = swap(xs0, "fluid", 0), swap(xs1, "fluid", 1)
    sends = call(
        functools.partial(group_kernel, cap),
        (bf16(2, height, width),) * chips,
        [HBM] * 3 + [ANY],
        (tile_dest[0, 0], obs_tiles[0, 0], jnp.transpose(measured[0, 0], (1, 0, 2)), xs1),
        (
            pltpu.SMEM((count_tiles,), jnp.int32),
            pltpu.VMEM((count_tiles, width, width), jnp.bfloat16),
            pltpu.VMEM((3, count_tiles, width), jnp.bfloat16),
            pltpu.SMEM((groups,), jnp.int32),
            pltpu.SMEM((cells,), jnp.int32),
            pltpu.VMEM((groups * extra, width), jnp.bfloat16),
            pltpu.VMEM((width, width), jnp.bfloat16),
            pltpu.SemaphoreType.DMA,
            pltpu.SemaphoreType.DMA,
            pltpu.SemaphoreType.DMA((4,)),
            pltpu.SemaphoreType.DMA((cells,)),
            pltpu.SemaphoreType.DMA((groups,)),
        ),
        out_specs=(HBM,) * chips,
        limit=60 * 1024 * 1024,
    )
    recvs = [sends[0]] + [cross(sends[m], "fluid", 2 * m) for m in range(1, chips)]
    zs = call(
        functools.partial(edges_kernel, groups),
        f32(3, rows, width),
        [VMEM] * 4,
        (flow_state, regions, x0, x1),
        flops=HIDES,
    )
    z0, z1 = swap(zs, "wall", 0), swap(zs, "wall", 1)
    slot_rows = groups * extra
    velocity_next, velocity, nux, nuy, nuz, nuy0, rim, mine, lent, cells_of = call(
        functools.partial(forward_kernel, sizes, cap),
        (f32(3, planes, rows, width),) * 2
        + (f32(planes + 1, rows, width), f32(planes, rows, width), f32(planes, rows, width))
        + (f32(planes, width), f32(rows, width))
        + (bf16(chips, extra, width),) * 2
        + (jax.ShapeDtypeStruct((8, slot_rows), jnp.int32),),
        [ANY] + [VMEM] * 6,
        (cell_list[0, 0].T, flow_state, x0, x1, z0, z1, zs),
        (
            pltpu.SMEM((cap, groups), jnp.int32),
            pltpu.VMEM((4, planes + 2, rows, width), jnp.float32),
            pltpu.VMEM((slot_rows, width), jnp.float32),
            pltpu.SemaphoreType.DMA,
            pltpu.SemaphoreType.DMA((4,)),
        ),
        out_specs=(HBM,) + (VMEM,) * 9,
    )
    borrowed = cross(lent, "fluid", 1)
    outside, pick = call(
        functools.partial(pick_kernel, sizes),
        (f32(rows, width), bf16(3, planes * rows, slot_rows)),
        [VMEM] * 5,
        (cells_of, z0, z1, zs, rim),
    )

    def products(block, values, after):
        return call(
            functools.partial(product_kernel, cap, block),
            bf16(2, chips * extra, width),
            [VMEM, ANY] + [VMEM] * chips,
            (values, after, *recvs),
        )

    given = products(1, borrowed, pick)
    other = cross(given, "fluid", 1)
    held = products(0, mine, given)
    fs0, fs1 = call(ends_kernel, (bf16(3, rows, width),) * 2, [VMEM] * 3, (held, other, pick))
    f0, f1 = swap(fs0, "fluid", 0), swap(fs1, "fluid", 1)
    forcing = call(forcing_kernel, f32(3, planes, rows, width), [VMEM] * 3 + [ANY], (held, other, pick, fs1))
    tops = reg_count // 8
    columns = 8 * rows
    sum_rows = tops * (columns // width)
    inner, fpack, sums = call(
        inner_kernel,
        (f32(3, planes, rows, width), f32(rows, width), f32(tops, columns)),
        [VMEM] * 9,
        (forcing, velocity, nux, nuy, nuz, nuy0, rim, regions, outside),
        (
            pltpu.VMEM((tops * rows, (planes + 1) * width), jnp.bfloat16),
            pltpu.VMEM((tops * rows, (planes + 1) * width), jnp.bfloat16),
            pltpu.VMEM((columns, (planes + 1) * width), jnp.bfloat16),
        ),
    )
    masks = tuple(range(1, walls))
    heights = [sum_rows] + [sum_rows + rows + 8 * (mask - 1) for mask in masks]
    own, *parts = call(
        functools.partial(edge_kernel, groups, masks),
        tuple(f32(height, width) for height in heights),
        [VMEM] * 7,
        (f0, f1, nux, velocity, regions, sums, fpack),
    )
    arrived = [cross(part, "wall", mask) for part, mask in zip(parts, masks)]
    adjoint, sens = call(
        functools.partial(final_kernel, sizes),
        (f32(3, planes, rows, width), f32(1, REG_DEV)),
        [VMEM] * (6 + len(arrived)),
        (inner, f0, f1, nux, rim, own, *arrived),
        (pltpu.VMEM((3, planes, rows, width), jnp.float32), pltpu.SemaphoreType.DMA((4,))),
        out_specs=(HBM, VMEM),
        flops=10 * grid,
        moved=24 * grid,
    )
    return velocity_next, adjoint, sens.reshape(REG_DEV)


def solution(mesh):
    in_specs = (
        P(None, "fluid", None, "wall"),
        P("fluid", None, "wall"),
        P("fluid", "wall", None, None, None),
        P("fluid", "wall", None, None, None),
        P("fluid", "wall", None),
        P("fluid", "wall", None, None),
    )
    out_specs = (
        P(None, "fluid", None, "wall"),
        P(None, "fluid", None, "wall"),
        P(("fluid", "wall")),
    )
    return jax.shard_map(body, mesh=mesh, in_specs=in_specs, out_specs=out_specs, check_vma=False)
```

```python
import functools

import jax
import jax.numpy as jnp
from jax import lax
from jax.experimental import pallas as pl
from jax.experimental.pallas import tpu as pltpu
from jax.sharding import PartitionSpec as P

REG_DEV = 16

time_step = 0.12
nu_floor = 0.1
nu_spread = 0.9
relax_sq = 4.0
sens_scale = 0.03

VMEM = pl.BlockSpec(memory_space=pltpu.VMEM)
SMEM = pl.BlockSpec(memory_space=pltpu.SMEM)
ANY = pl.BlockSpec(memory_space=pl.ANY)
HBM = pl.BlockSpec(memory_space=pltpu.HBM)
LIMIT = 24 * 1024 * 1024
HIDES = 100_000_000_000


def call(kernel, outs, ins, operands, scratch=(), flops=1, moved=1, out_specs=None, limit=LIMIT):
    return pl.pallas_call(
        kernel,
        out_shape=outs,
        in_specs=ins,
        out_specs=out_specs if out_specs is not None else jax.tree.map(lambda _: VMEM, outs),
        scratch_shapes=list(scratch),
        compiler_params=pltpu.CompilerParams(vmem_limit_bytes=limit),
        cost_estimate=pl.CostEstimate(flops=flops, bytes_accessed=moved, transcendentals=0),
    )(*operands)


def f32(*shape):
    return jax.ShapeDtypeStruct(shape, jnp.float32)


def bf16(*shape):
    return jax.ShapeDtypeStruct(shape, jnp.bfloat16)


def swap(block, axis, turn):
    groups, walls = lax.axis_size("fluid"), lax.axis_size("wall")

    def partner(f, w):
        at, count = (f, groups) if axis == "fluid" else (w, walls)
        other = at + 1 if (at + turn) % 2 == 0 else at - 1
        if axis == "fluid":
            return (other, w) if 0 <= other < count else (f, w ^ 1)
        return (f, other) if 0 <= other < count else (f ^ 1, w)

    pairs = []
    for f in range(groups):
        for w in range(walls):
            to_f, to_w = partner(f, w)
            pairs.append((f * walls + w, to_f * walls + to_w))
    return lax.ppermute(block, ("fluid", "wall"), pairs)


def cross(block, axis, mask):
    return lax.ppermute(block, axis, [(i, i ^ mask) for i in range(lax.axis_size(axis))])


def from_neighbours(index, count, first, second):
    even = index % 2 == 0
    above = jnp.where(even, first, second)
    below = jnp.where(even, second, first)
    above = jnp.where(index == count - 1, jnp.zeros_like(above), above)
    below = jnp.where(index == 0, jnp.zeros_like(below), below)
    return below, above


def pack_edges(packed, plane, m, lane):
    width = lane.shape[1]
    here = (lane == 2 * m) | (lane == (2 * m + width - 1) % width)
    return jnp.where(here, pltpu.roll(plane, 2 * m, 1), packed)


def mix_edges(below, above, lane, shift=2):
    return jnp.where(lane % 2 == 0, above, pltpu.roll(below, shift, 1))


def edge_of(mixed, m):
    width = mixed.shape[1]
    return pltpu.roll(mixed, (2 * width - (2 * m + 1)) % width, 1)


def viscosity(jumps):
    shear_sq = jumps[0] * jumps[0] + jumps[1] * jumps[1] + jumps[2] * jumps[2]
    root = lax.rsqrt(1.0 + relax_sq * shear_sq)
    return nu_floor + nu_spread * (root * lax.rsqrt(root))


def iotas(rows, width):
    shape = (rows, width)
    return lax.broadcasted_iota(jnp.int32, shape, 0), lax.broadcasted_iota(jnp.int32, shape, 1)


def faces_kernel(flow_ref, first_ref, second_ref, sems):
    last = flow_ref.shape[1] - 1
    odd = lax.axis_index("fluid") % 2
    copies = [
        pltpu.make_async_copy(flow_ref.at[c, plane], out_ref.at[c], sems.at[i, c])
        for i, (plane, out_ref) in enumerate(((last - last * odd, first_ref), (last * odd, second_ref)))
        for c in range(flow_ref.shape[0])
    ]
    for copy in copies:
        copy.start()
    for copy in copies:
        copy.wait()


def edges_kernel(groups, flow_ref, regions_ref, x0_ref, x1_ref, edges_ref):
    fields, planes, rows, width = flow_ref.shape
    _, lane = iotas(rows, width)
    outer = jnp.zeros((rows, width), jnp.float32)
    second, beside = outer, outer
    for c in range(fields):
        for x in range(planes):
            m, plane = c * planes + x, flow_ref[c, x]
            outer = pack_edges(outer, plane, m, lane)
            here = (lane == 2 * m) | (lane == (2 * m - 3) % width)
            second = jnp.where(here, pltpu.roll(plane, (2 * m - 1) % width, 1), second)
        for side, plane in enumerate(from_neighbours(lax.axis_index("fluid"), groups, x0_ref[c], x1_ref[c])):
            beside = pack_edges(beside, plane, 2 * c + side, lane)
    for x in range(planes):
        beside = pack_edges(beside, regions_ref[x].astype(jnp.float32), 2 * fields + x, lane)
    edges_ref[0], edges_ref[1], edges_ref[2] = outer, second, beside


def outside_edges(walls, planes, halo, second, beside, inside, rim_nu):
    rows, width = halo.shape
    row, lane = iotas(rows, width)
    x, field = (lane // 2) % planes, (lane // 2) // planes

    def spread(nu):
        nu = jnp.where(field == 0, nu, 0.0)
        return nu + pltpu.roll(nu, 2 * planes, 1) + pltpu.roll(nu, 4 * planes, 1)

    def nu_of(jump):
        return spread(viscosity([jump] + [pltpu.roll(jump, width - 2 * c * planes, 1) for c in (1, 2)]))

    over_x, under_x = pltpu.roll(halo, width - 2, 1), pltpu.roll(halo, 2, 1)
    for c in range(4):
        low = pltpu.roll(beside, (2 * c * planes - 4 * c) % width, 1)
        high = pltpu.roll(beside, (2 * (c * planes + planes - 1) - 4 * c - 2) % width, 1)
        under_x = jnp.where((x == 0) & (field == c), low, under_x)
        over_x = jnp.where((x == planes - 1) & (field == c), high, over_x)
    over_y = jnp.where(row == rows - 1, 0.0, pltpu.roll(halo, rows - 1, 0))
    under_y = jnp.where(row == 0, 0.0, pltpu.roll(halo, 1, 0))
    total = spread(rim_nu) * (inside - halo)
    for other in (over_x, under_x, over_y, under_y, second):
        total += nu_of(other - halo) * (other - halo)
    above = lane % 2 == 0
    gradient_x = pltpu.roll(0.5 * (over_x - under_x), width - 6 * planes, 1)
    gradient_y = pltpu.roll(0.5 * (over_y - under_y), width - 4 * planes, 1)
    gradient_z = pltpu.roll(0.5 * jnp.where(above, second - inside, inside - second), width - 2 * planes, 1)
    gradient = jnp.where(field == 0, gradient_x, jnp.where(field == 1, gradient_y, gradient_z))
    value = halo + time_step * (total - gradient)
    value = jnp.where(field == 3, pltpu.roll(beside, 6 * planes - 16, 1), value)
    me = lax.axis_index("wall")
    exists = jnp.where(above, jnp.where(me < walls - 1, 1, 0), jnp.where(me > 0, 1, 0)) == 1
    return jnp.where(exists & (field < 4), value, 0.0)


def group_kernel(cap, dest_ref, tiles_ref, meas_ref, flow_ref, *refs):
    chips = len(refs) - 12
    sends, halo_refs = refs[:chips], refs[chips : chips + 2]
    (list_ref, held_ref, seen_ref, count_ref, slot_ref, rows_ref,
     list_sem, seen_sem, in_sems, face_sems) = refs[chips + 2 :]
    count_tiles, width, _ = tiles_ref.shape
    groups = 2 * chips
    slots = groups * cap
    extra = rows_ref.shape[0] // groups
    depth = cap * width
    me = lax.axis_index("fluid")
    listed = pltpu.make_async_copy(dest_ref, list_ref, list_sem)
    listed.start()
    piece = count_tiles // in_sems.shape[0]

    def load(p):
        part = pl.ds(p * piece, piece)
        return pltpu.make_async_copy(tiles_ref.at[part], held_ref.at[part], in_sems.at[p])

    for p in range(in_sems.shape[0]):
        load(p).start()
    seen = pltpu.make_async_copy(meas_ref, seen_ref, seen_sem)
    seen.start()
    last = flow_ref.shape[1] - 1
    fields = flow_ref.shape[0]
    faces = [
        pltpu.make_async_copy(flow_ref.at[c, plane], halo_refs[i].at[c], face_sems.at[i * fields + c])
        for i, plane in enumerate((last * (1 - me % 2), last * (me % 2)))
        for c in range(fields)
    ]
    for face in faces:
        face.start()

    def clear(b, carry):
        count_ref[b] = 0
        for k in range(cap):
            slot_ref[b * cap + k] = -1
        return carry

    lax.fori_loop(0, groups, clear, 0)
    _, tile_lane = iotas(8, count_tiles)
    listed.wait()

    def place(t, slot_of):
        b = list_ref[t]
        k = count_ref[b]
        count_ref[b] = k + 1
        slot_ref[b * cap + k] = t
        return jnp.where(tile_lane == t, b * cap + k, slot_of)

    slot_of = lax.fori_loop(
        0, count_tiles, place, jnp.full((8, count_tiles), -1, jnp.int32), unroll=True
    )
    for p in range(in_sems.shape[0]):
        load(p).wait()

    for m in list(range(1, chips)) + [0]:
        for j in range(2):
            b = me ^ (2 * m + j)
            for k in range(cap):
                t = slot_ref[b * cap + k]
                at = (j, slice(k * width, (k + 1) * width))
                if slots > count_tiles:
                    sends[m][at] = jnp.where(t >= 0, held_ref[jnp.maximum(t, 0)], jnp.zeros((width, width), jnp.bfloat16))
                else:
                    sends[m][at] = held_ref[t]
    seen.wait()
    row = lax.broadcasted_iota(jnp.int32, (groups * extra, count_tiles), 0)
    within = row % extra
    row_slot = (row // extra) * cap + within // 3
    used = within < cap * 3
    total = jnp.zeros((groups * extra, width), jnp.float32)
    for c in range(3):
        pick = (row_slot == slot_of[0:1, :]) & used & (within % 3 == c)
        total += jnp.dot(
            pick.astype(jnp.float32).astype(jnp.bfloat16), seen_ref[c], preferred_element_type=jnp.float32
        )
    rows_ref[...] = total.astype(jnp.bfloat16)

    for m in range(chips):
        for j in range(2):
            b = me ^ (2 * m + j)
            sends[m][j, depth:, :] = rows_ref[pl.ds(pl.multiple_of(b * extra, extra), extra), :]
    for face in faces:
        face.wait()


def forward_kernel(
    sizes, cap, cells_ref, flow_ref, x0_ref, x1_ref, z0_ref, z1_ref, edges_ref,
    out_ref, next_ref, nux_ref, nuy_ref, nuz_ref, nuy0_ref, rim_ref, mine_ref, lent_ref, cells_of_ref,
    list_ref, padded_ref, taken_ref, list_sem, out_sems,
):
    _, planes, rows, width = flow_ref.shape
    groups, walls = sizes
    chips, extra, _ = mine_ref.shape
    listed = pltpu.make_async_copy(cells_ref, list_ref, list_sem)
    listed.start()
    row, lane = iotas(rows, width)
    halo = mix_edges(*from_neighbours(lax.axis_index("wall"), walls, z0_ref[0], z1_ref[0]), lane)
    inside = pltpu.roll(edges_ref[0], 1, 1)
    jump = halo - inside
    rim_nu = viscosity([jump] + [pltpu.roll(jump, width - 2 * c * planes, 1) for c in (1, 2)])
    rim_nu = jnp.where(lane < 2 * planes, rim_nu, 0.0)
    rim_ref[...] = rim_nu
    for c in range(4):
        low, high = from_neighbours(lax.axis_index("fluid"), groups, x0_ref[c], x1_ref[c])
        padded_ref[c, 0] = low
        padded_ref[c, planes + 1] = high
        padded_ref[c, 1 : planes + 1] = flow_ref[c]
    nux_ref[0] = viscosity([padded_ref[c, 1] - padded_ref[c, 0] for c in range(3)])

    def plane(x, carry):
        here = [padded_ref[c, x + 1] for c in range(4)]
        over = [padded_ref[c, x + 2] for c in range(4)]
        under = [padded_ref[c, x] for c in range(4)]
        total = [None] * 3
        pressure = [None] * 3

        def add(axis, nu_up, nu_down):
            for c in range(3):
                flux = nu_up * (over[c] - here[c]) - nu_down * (here[c] - under[c])
                total[c] = flux if total[c] is None else total[c] + flux
            pressure[axis] = 0.5 * (over[3] - under[3])

        nu_up = viscosity([over[c] - here[c] for c in range(3)])
        nux_ref[x + 1] = nu_up
        add(0, nu_up, nux_ref[x])
        over = [jnp.where(row == rows - 1, 0.0, pltpu.roll(here[c], rows - 1, 0)) for c in range(4)]
        under = [jnp.where(row == 0, 0.0, pltpu.roll(here[c], 1, 0)) for c in range(4)]
        nu_up = viscosity([over[c] - here[c] for c in range(3)])
        nu_first = viscosity([here[c][:1] for c in range(3)])
        nuy_ref[x] = nu_up
        nuy0_ref[pl.ds(x, 1), :] = nu_first
        add(1, nu_up, jnp.where(row == 0, nu_first, pltpu.roll(nu_up, 1, 0)))
        rim = [edge_of(halo, c * planes + x) for c in range(4)]
        over = [jnp.where(lane == width - 1, rim[c], pltpu.roll(here[c], width - 1, 1)) for c in range(4)]
        under = [jnp.where(lane == 0, rim[c], pltpu.roll(here[c], 1, 1)) for c in range(4)]
        nu_up = viscosity([over[c] - here[c] for c in range(3)])
        nuz_ref[x] = nu_up
        add(2, nu_up, jnp.where(lane == 0, edge_of(rim_nu, x), pltpu.roll(nu_up, 1, 1)))
        for c in range(3):
            value = here[c] + time_step * (total[c] - pressure[c])
            next_ref[c, x] = value
        return carry

    pieces = out_sems.shape[0]
    step = planes // pieces

    def store(i):
        part = pl.ds(i * step, step)
        return pltpu.make_async_copy(next_ref.at[:, part], out_ref.at[:, part], out_sems.at[i])

    for i in range(pieces):
        lax.fori_loop(i * step, (i + 1) * step, plane, 0, unroll=True)
        store(i).start()

    taken_ref[...] = jnp.zeros_like(taken_ref)
    listed.wait()
    _, slot_lane = iotas(8, groups * extra)
    cell_of = jnp.full((8, groups * extra), -1, jnp.int32)
    odd = lax.axis_index("fluid") % 2
    for b in range(groups):
        part = (odd if b % 2 == 0 else 1 - odd) * chips + b // 2
        for k in range(cap):
            cell = list_ref[k, b]
            x, y = lax.div(cell, rows), lax.rem(cell, rows)
            first = part * extra + 3 * k
            for c in range(3):
                taken_ref[pl.ds(first + c, 1), :] = next_ref[c, x, pl.ds(y, 1), :]
            cell_of = jnp.where((slot_lane >= first) & (slot_lane < first + 3), cell, cell_of)
    cells_of_ref[...] = cell_of
    taken = taken_ref[...].astype(jnp.bfloat16).reshape((2,) + mine_ref.shape)
    mine_ref[...] = taken[0]
    lent_ref[...] = taken[1]
    for i in range(pieces):
        store(i).wait()


def pick_kernel(
    sizes, cells_of_ref, z0_ref, z1_ref, edges_ref, rim_ref, outside_ref, rims_ref, pick_ref
):
    _, rows, width = edges_ref.shape
    groups, walls = sizes
    _, lines, slot_rows = pick_ref.shape
    planes = lines // rows
    extra = slot_rows // groups
    _, lane = iotas(rows, width)
    halo, second, beside = (
        mix_edges(*from_neighbours(lax.axis_index("wall"), walls, z0_ref[i], z1_ref[i]), lane, shift)
        for i, shift in enumerate((2, 4, 2))
    )
    inside = pltpu.roll(edges_ref[0], 1, 1)
    rim_nu = rim_ref[...]
    outside_ref[...] = outside_edges(walls, planes, halo, second, beside, inside, rim_nu)
    rims_ref[...] = time_step * (rim_nu + pltpu.roll(rim_nu, 2 * planes, 1) + pltpu.roll(rim_nu, 4 * planes, 1))
    line, slot_lane = iotas(lines, slot_rows)
    hit = line == cells_of_ref[0:1, :]
    part = (slot_lane % extra) % 3
    for c in range(3):
        pick_ref[c] = (hit & (part == c)).astype(jnp.float32).astype(jnp.bfloat16)


def product_kernel(cap, block, values_ref, after_ref, *refs):
    chips, extra, width = values_ref.shape
    recvs, out_ref = refs[:chips], refs[chips]
    depth = cap * width
    row, lane = iotas(extra, depth)
    own = row // 3 == lane // width
    here = lax.axis_index("fluid") // 2
    for m, recv_ref in enumerate(recvs):
        source = here ^ m
        at = pl.ds(pl.multiple_of(source * extra, extra), extra)
        weights = recv_ref[block, pl.ds(0, depth), :]
        predicted = lax.dot_general(
            values_ref[source], weights, (((1,), (1,)), ((), ())), preferred_element_type=jnp.float32
        )
        seen = recv_ref[block, pl.ds(depth, extra), :].astype(jnp.float32)
        misfit = jnp.where(own, predicted - jnp.concatenate([seen] * cap, axis=1), 0.0).astype(jnp.bfloat16)
        contrib = jnp.dot(misfit, weights, preferred_element_type=jnp.float32)
        high = contrib.astype(jnp.bfloat16)
        out_ref[0, at, :] = high
        out_ref[1, at, :] = (contrib - high.astype(jnp.float32)).astype(jnp.bfloat16)


def forcing_rows(c, part, mine_ref, other_ref, pick_ref):
    half = mine_ref.shape[1]
    total = None
    for i, share_ref in enumerate((mine_ref, other_ref)):
        pick = pick_ref[c, part, i * half : (i + 1) * half]
        for share in range(2):
            product = jnp.dot(pick, share_ref[share], preferred_element_type=jnp.float32)
            total = product if total is None else total + product
    return total


def ends_kernel(mine_ref, other_ref, pick_ref, first_ref, second_ref):
    _, rows, _ = first_ref.shape
    lines = pick_ref.shape[1]
    even = lax.axis_index("fluid") % 2 == 0
    for c in range(3):
        low = forcing_rows(c, slice(0, rows), mine_ref, other_ref, pick_ref)
        high = forcing_rows(c, slice(lines - rows, lines), mine_ref, other_ref, pick_ref)
        first_ref[c] = jnp.where(even, high, low).astype(jnp.bfloat16)
        second_ref[c] = jnp.where(even, low, high).astype(jnp.bfloat16)


def forcing_kernel(mine_ref, other_ref, pick_ref, after_ref, forcing_ref):
    for c in range(3):
        forcing_ref[c] = forcing_rows(c, slice(None), mine_ref, other_ref, pick_ref).reshape(forcing_ref.shape[1:])


def region_rows(values, ids, tops):
    top, low = (ids // 8).astype(jnp.float32).astype(jnp.bfloat16), (ids % 8).astype(jnp.float32).astype(jnp.bfloat16)
    main = values.astype(jnp.bfloat16)
    rest = (values - main.astype(jnp.float32)).astype(jnp.bfloat16)
    zero = jnp.zeros_like(main)
    one = jnp.ones_like(main)
    hits = [top == jnp.bfloat16(h) for h in range(tops)]
    return (
        jnp.concatenate([jnp.where(hit, main, zero) for hit in hits], axis=0),
        jnp.concatenate([jnp.where(hit, rest, zero) for hit in hits], axis=0),
        jnp.concatenate([jnp.where(low == jnp.bfloat16(l), one, zero) for l in range(8)], axis=0),
    )


def region_sums(main, rest, ones, rows):
    over_lanes = (((1,), (1,)), ((), ()))
    total = lax.dot_general(main, ones, over_lanes, preferred_element_type=jnp.float32)
    total += lax.dot_general(rest, ones, over_lanes, preferred_element_type=jnp.float32)
    row, column = iotas(*total.shape)
    total = jnp.where(row % rows == column % rows, total, 0.0)
    return jnp.sum(total.reshape(total.shape[0] // rows, rows, total.shape[1]), axis=1)


def inner_kernel(
    forcing_ref, next_ref, nux_ref, nuy_ref, nuz_ref, nuy0_ref, rim_ref, regions_ref, outside_ref,
    adjoint_ref, fpack_ref, sums_ref, main_ref, rest_ref, ones_ref,
):
    _, planes, rows, width = forcing_ref.shape
    row, lane = iotas(rows, width)
    rim_nu = rim_ref[...]
    tops = sums_ref.shape[0]

    def add_up(x, values, ids):
        at = pl.ds(pl.multiple_of(x * width, width), width)
        for part_ref, part in zip((main_ref, rest_ref, ones_ref), region_rows(values, ids, tops)):
            part_ref[:, at] = part

    def plane(x, fpack):
        nuy, nuz = nuy_ref[x], nuz_ref[x]
        nuy_down = jnp.where(row == 0, nuy0_ref[pl.ds(x, 1), :], pltpu.roll(nuy, 1, 0))
        nuz_down = jnp.where(lane == 0, edge_of(rim_nu, x), pltpu.roll(nuz, 1, 1))
        nus = (nux_ref[x + 1], nux_ref[x], nuy, nuy_down, nuz, nuz_down)
        next_up, next_down = jnp.minimum(x + 1, planes - 1), jnp.maximum(x - 1, 0)
        at_top, at_bottom = x == planes - 1, x == 0
        product = None
        for c in range(3):
            here = forcing_ref[c, x]
            over = jnp.where(at_top, 0.0, forcing_ref[c, next_up])
            under = jnp.where(at_bottom, 0.0, forcing_ref[c, next_down])
            total = nus[0] * (over - here) - nus[1] * (here - under)
            over = jnp.where(row == rows - 1, 0.0, pltpu.roll(here, rows - 1, 0))
            under = jnp.where(row == 0, 0.0, pltpu.roll(here, 1, 0))
            total += nus[2] * (over - here) - nus[3] * (here - under)
            over = jnp.where(lane == width - 1, 0.0, pltpu.roll(here, width - 1, 1))
            under = jnp.where(lane == 0, 0.0, pltpu.roll(here, 1, 1))
            total += nus[4] * (over - here) - nus[5] * (here - under)
            value = here + time_step * total
            adjoint_ref[c, x] = value
            part = value * next_ref[c, x]
            product = part if product is None else product + part
            fpack = pack_edges(fpack, here, c * planes + x, lane)
        add_up(x, product, regions_ref[x])
        return fpack

    fpack = lax.fori_loop(0, planes, plane, jnp.zeros((rows, width), jnp.float32), unroll=4)
    fpack_ref[...] = fpack
    mixed = outside_ref[...]
    reach = pltpu.roll(fpack, 1, 1) * mixed
    reach = reach + pltpu.roll(reach, width - 2 * planes, 1) + pltpu.roll(reach, width - 4 * planes, 1)
    reach = time_step * reach * rim_nu
    add_up(planes, reach, pltpu.roll(mixed, (width - 6 * planes) % width, 1).astype(jnp.int32))
    sums_ref[...] = region_sums(main_ref[...], rest_ref[...], ones_ref[...], rows)


def edge_kernel(groups, masks, x0_ref, x1_ref, nux_ref, next_ref, regions_ref, sums_ref, fpack_ref, *outs):
    _, planes, rows, width = next_ref.shape
    tops, columns = sums_ref.shape
    low, high = 0.0, 0.0
    for c in range(3):
        below, above = beside_of(c, groups, x0_ref, x1_ref)
        low += below * next_ref[c, 0]
        high += above * next_ref[c, planes - 1]
    ends = [
        region_rows(time_step * nux_ref[0] * low, regions_ref[0], tops),
        region_rows(time_step * nux_ref[planes] * high, regions_ref[planes - 1], tops),
    ]
    total = sums_ref[...] + region_sums(*(jnp.concatenate(both, axis=1) for both in zip(*ends)), rows)
    height = tops * (columns // width)
    for mask, out_ref in zip((0,) + masks, outs):
        for i in range(columns // width):
            out_ref[i * tops : (i + 1) * tops, :] = total[:, i * width : (i + 1) * width]
        if mask:
            out_ref[height : height + rows, :] = fpack_ref[...]
            if out_ref.shape[0] > height + rows:
                out_ref[height + rows :, :] = jnp.zeros((out_ref.shape[0] - height - rows, width), jnp.float32)


def beside_of(c, groups, x0_ref, x1_ref):
    return from_neighbours(
        lax.axis_index("fluid"), groups, x0_ref[c].astype(jnp.float32), x1_ref[c].astype(jnp.float32)
    )


def final_kernel(sizes, inner_ref, x0_ref, x1_ref, nux_ref, rims_ref, own_ref, *refs):
    groups, walls = sizes
    arrived, (adjoint_ref, sens_ref, value_ref, owned_ref, sems, owned_sem) = refs[:-6], refs[-6:]
    _, planes, rows, width = inner_ref.shape
    per = own_ref.shape[0]
    _, lane = iotas(rows, width)
    me = lax.axis_index("wall")
    total = own_ref[...]
    below = jnp.zeros((rows, width), jnp.float32)
    above = jnp.zeros((rows, width), jnp.float32)
    for mask, ref in zip(range(1, walls), arrived):
        total = total + ref[:per, :]
        if mask & (mask + 1) == 0:
            edges = ref[per : per + rows, :]
            above = jnp.where((me ^ mask) == me + 1, edges, above)
            below = jnp.where((me ^ mask) == me - 1, edges, below)
    mixed = mix_edges(below, above, lane)
    edge_flux = mixed * rims_ref[...]
    on_edge = (lane == 0) | (lane == width - 1)

    beside = [beside_of(c, groups, x0_ref, x1_ref) for c in range(3)]
    step = planes // sems.shape[0]

    def store(i):
        part = pl.ds(i * step, step)
        return pltpu.make_async_copy(value_ref.at[:, part], adjoint_ref.at[:, part], sems.at[i])

    for i in range(sems.shape[0]):
        for x in range(i * step, (i + 1) * step):
            for c in range(3):
                value = inner_ref[c, x] + jnp.where(on_edge, edge_of(edge_flux, c * planes + x), 0.0)
                if x == 0:
                    value += time_step * nux_ref[0] * beside[c][0]
                if x == planes - 1:
                    value += time_step * nux_ref[planes] * beside[c][1]
                value_ref[c, x] = value
        store(i).start()
    parts = width // rows
    tops = REG_DEV * walls // 8
    owned = REG_DEV // 8
    top, _ = iotas(tops, width)
    region, lane = iotas(REG_DEV, width)
    sens = jnp.zeros((8, REG_DEV), jnp.float32)
    for i in range(8 // parts):
        for h in range(owned):
            mine = jnp.where(top == me * owned + h, total[i * tops : (i + 1) * tops], 0.0)
            gather = (region == h * 8 + i * parts + lane // rows).astype(jnp.float32)
            sens += lax.dot_general(
                jnp.broadcast_to(jnp.sum(mine, axis=0, keepdims=True), (8, width)), gather, (((1,), (1,)), ((), ())),
                precision=lax.Precision.HIGHEST, preferred_element_type=jnp.float32,
            )
    owned_ref[...] = sens_scale * sens[:1]
    owned_copy = pltpu.make_async_copy(owned_ref, sens_ref, owned_sem)
    owned_copy.start()
    for i in range(sems.shape[0]):
        store(i).wait()
    owned_copy.wait()


def body(flow_state, regions, obs_tiles, measured, tile_dest, cell_list):
    groups, walls = lax.axis_size("fluid"), lax.axis_size("wall")
    sizes = (groups, walls)
    _, planes, rows, width = flow_state.shape
    count_tiles = obs_tiles.shape[2]
    cap = cell_list.shape[3]
    extra = -(-cap * 3 // 16) * 16
    reg_count = REG_DEV * walls
    cells = groups * cap
    grid = planes * rows * width

    chips = groups // 2
    height = cap * width + extra
    *sends, xs0, xs1 = call(
        functools.partial(group_kernel, cap),
        (bf16(2, height, width),) * chips + (f32(4, rows, width),) * 2,
        [HBM] * 4,
        tuple(
            pltpu.with_memory_space_constraint(operand, pltpu.HBM)
            for operand in (tile_dest[0, 0], obs_tiles[0, 0], jnp.transpose(measured[0, 0], (1, 0, 2)), flow_state)
        ),
        (
            pltpu.SMEM((count_tiles,), jnp.int32),
            pltpu.VMEM((count_tiles, width, width), jnp.bfloat16),
            pltpu.VMEM((3, count_tiles, width), jnp.bfloat16),
            pltpu.SMEM((groups,), jnp.int32),
            pltpu.SMEM((cells,), jnp.int32),
            pltpu.VMEM((groups * extra, width), jnp.bfloat16),
            pltpu.SemaphoreType.DMA,
            pltpu.SemaphoreType.DMA,
            pltpu.SemaphoreType.DMA((4,)),
            pltpu.SemaphoreType.DMA((8,)),
        ),
        out_specs=(VMEM,) * (chips + 2),
    )
    x0, x1 = swap(xs0, "fluid", 0), swap(xs1, "fluid", 1)
    recvs = [sends[0]] + [cross(sends[m], "fluid", 2 * m) for m in range(1, chips)]
    zs = call(
        functools.partial(edges_kernel, groups),
        f32(3, rows, width),
        [VMEM] * 4,
        (flow_state, regions, x0, x1),
        flops=HIDES,
    )
    z0, z1 = swap(zs, "wall", 0), swap(zs, "wall", 1)
    slot_rows = groups * extra
    velocity_next, velocity, nux, nuy, nuz, nuy0, rim, mine, lent, cells_of = call(
        functools.partial(forward_kernel, sizes, cap),
        (f32(3, planes, rows, width),) * 2
        + (f32(planes + 1, rows, width), f32(planes, rows, width), f32(planes, rows, width))
        + (f32(planes, width), f32(rows, width))
        + (bf16(chips, extra, width),) * 2
        + (jax.ShapeDtypeStruct((8, slot_rows), jnp.int32),),
        [ANY] + [VMEM] * 6,
        (cell_list[0, 0].T, flow_state, x0, x1, z0, z1, zs),
        (
            pltpu.SMEM((cap, groups), jnp.int32),
            pltpu.VMEM((4, planes + 2, rows, width), jnp.float32),
            pltpu.VMEM((slot_rows, width), jnp.float32),
            pltpu.SemaphoreType.DMA,
            pltpu.SemaphoreType.DMA((4,)),
        ),
        out_specs=(HBM,) + (VMEM,) * 9,
    )
    borrowed = cross(lent, "fluid", 1)
    outside, rims, pick = call(
        functools.partial(pick_kernel, sizes),
        (f32(rows, width), f32(rows, width), bf16(3, planes * rows, slot_rows)),
        [VMEM] * 5,
        (cells_of, z0, z1, zs, rim),
    )

    def products(block, values, after):
        return call(
            functools.partial(product_kernel, cap, block),
            bf16(2, chips * extra, width),
            [VMEM, ANY] + [VMEM] * chips,
            (values, after, *recvs),
        )

    given = products(1, borrowed, pick)
    other = cross(given, "fluid", 1)
    held = products(0, mine, given)
    fs0, fs1 = call(ends_kernel, (bf16(3, rows, width),) * 2, [VMEM] * 3, (held, other, pick))
    f0, f1 = swap(fs0, "fluid", 0), swap(fs1, "fluid", 1)
    forcing = call(forcing_kernel, f32(3, planes, rows, width), [VMEM] * 3 + [ANY], (held, other, pick, fs1))
    tops = reg_count // 8
    columns = 8 * rows
    sum_rows = tops * (columns // width)
    inner, fpack, sums = call(
        inner_kernel,
        (f32(3, planes, rows, width), f32(rows, width), f32(tops, columns)),
        [VMEM] * 9,
        (forcing, velocity, nux, nuy, nuz, nuy0, rim, regions, outside),
        (
            pltpu.VMEM((tops * rows, (planes + 1) * width), jnp.bfloat16),
            pltpu.VMEM((tops * rows, (planes + 1) * width), jnp.bfloat16),
            pltpu.VMEM((columns, (planes + 1) * width), jnp.bfloat16),
        ),
    )
    masks = tuple(range(1, walls))
    heights = [sum_rows] + [sum_rows + rows + 8 * (mask - 1) for mask in masks]
    own, *parts = call(
        functools.partial(edge_kernel, groups, masks),
        tuple(f32(height, width) for height in heights),
        [VMEM] * 7,
        (f0, f1, nux, velocity, regions, sums, fpack),
    )
    arrived = [cross(part, "wall", mask) for part, mask in zip(parts, masks)]
    adjoint, sens = call(
        functools.partial(final_kernel, sizes),
        (f32(3, planes, rows, width), f32(1, REG_DEV)),
        [VMEM] * (6 + len(arrived)),
        (inner, f0, f1, nux, rims, own, *arrived),
        (
            pltpu.VMEM((3, planes, rows, width), jnp.float32),
            pltpu.VMEM((1, REG_DEV), jnp.float32),
            pltpu.SemaphoreType.DMA((4,)),
            pltpu.SemaphoreType.DMA,
        ),
        out_specs=(HBM, HBM),
        flops=10 * grid,
        moved=24 * grid,
    )
    return velocity_next, adjoint, sens.reshape(REG_DEV)


def solution(mesh):
    in_specs = (
        P(None, "fluid", None, "wall"),
        P("fluid", None, "wall"),
        P("fluid", "wall", None, None, None),
        P("fluid", "wall", None, None, None),
        P("fluid", "wall", None),
        P("fluid", "wall", None, None),
    )
    out_specs = (
        P(None, "fluid", None, "wall"),
        P(None, "fluid", None, "wall"),
        P(("fluid", "wall")),
    )
    return jax.shard_map(body, mesh=mesh, in_specs=in_specs, out_specs=out_specs, check_vma=False)
```

```python
import functools

import jax
import jax.numpy as jnp
from jax import lax
from jax.experimental import pallas as pl
from jax.experimental.pallas import tpu as pltpu
from jax.sharding import PartitionSpec as P

REG_DEV = 16

time_step = 0.12
nu_floor = 0.1
nu_spread = 0.9
relax_sq = 4.0
sens_scale = 0.03

VMEM = pl.BlockSpec(memory_space=pltpu.VMEM)
SMEM = pl.BlockSpec(memory_space=pltpu.SMEM)
ANY = pl.BlockSpec(memory_space=pl.ANY)
HBM = pl.BlockSpec(memory_space=pltpu.HBM)
LIMIT = 24 * 1024 * 1024
HIDES = 100_000_000_000


def call(kernel, outs, ins, operands, scratch=(), flops=1, moved=1, out_specs=None, limit=LIMIT):
    return pl.pallas_call(
        kernel,
        out_shape=outs,
        in_specs=ins,
        out_specs=out_specs if out_specs is not None else jax.tree.map(lambda _: VMEM, outs),
        scratch_shapes=list(scratch),
        compiler_params=pltpu.CompilerParams(vmem_limit_bytes=limit),
        cost_estimate=pl.CostEstimate(flops=flops, bytes_accessed=moved, transcendentals=0),
    )(*operands)


def f32(*shape):
    return jax.ShapeDtypeStruct(shape, jnp.float32)


def bf16(*shape):
    return jax.ShapeDtypeStruct(shape, jnp.bfloat16)


def swap(block, axis, turn):
    groups, walls = lax.axis_size("fluid"), lax.axis_size("wall")

    def partner(f, w):
        at, count = (f, groups) if axis == "fluid" else (w, walls)
        other = at + 1 if (at + turn) % 2 == 0 else at - 1
        if axis == "fluid":
            return (other, w) if 0 <= other < count else (f, w ^ 1)
        return (f, other) if 0 <= other < count else (f ^ 1, w)

    pairs = []
    for f in range(groups):
        for w in range(walls):
            to_f, to_w = partner(f, w)
            pairs.append((f * walls + w, to_f * walls + to_w))
    return lax.ppermute(block, ("fluid", "wall"), pairs)


def cross(block, axis, mask):
    return lax.ppermute(block, axis, [(i, i ^ mask) for i in range(lax.axis_size(axis))])


def from_neighbours(index, count, first, second):
    even = index % 2 == 0
    above = jnp.where(even, first, second)
    below = jnp.where(even, second, first)
    above = jnp.where(index == count - 1, jnp.zeros_like(above), above)
    below = jnp.where(index == 0, jnp.zeros_like(below), below)
    return below, above


def pack_edges(packed, plane, m, lane):
    width = lane.shape[1]
    here = (lane == 2 * m) | (lane == (2 * m + width - 1) % width)
    return jnp.where(here, pltpu.roll(plane, 2 * m, 1), packed)


def mix_edges(below, above, lane, shift=2):
    return jnp.where(lane % 2 == 0, above, pltpu.roll(below, shift, 1))


def edge_of(mixed, m):
    width = mixed.shape[1]
    return pltpu.roll(mixed, (2 * width - (2 * m + 1)) % width, 1)


def viscosity(jumps):
    shear_sq = jumps[0] * jumps[0] + jumps[1] * jumps[1] + jumps[2] * jumps[2]
    root = lax.rsqrt(1.0 + relax_sq * shear_sq)
    return nu_floor + nu_spread * (root * lax.rsqrt(root))


def iotas(rows, width):
    shape = (rows, width)
    return lax.broadcasted_iota(jnp.int32, shape, 0), lax.broadcasted_iota(jnp.int32, shape, 1)


def faces_kernel(flow_ref, first_ref, second_ref, sems):
    last = flow_ref.shape[1] - 1
    odd = lax.axis_index("fluid") % 2
    copies = [
        pltpu.make_async_copy(flow_ref.at[c, plane], out_ref.at[c], sems.at[i, c])
        for i, (plane, out_ref) in enumerate(((last - last * odd, first_ref), (last * odd, second_ref)))
        for c in range(flow_ref.shape[0])
    ]
    for copy in copies:
        copy.start()
    for copy in copies:
        copy.wait()


def edges_kernel(groups, flow_ref, regions_ref, x0_ref, x1_ref, edges_ref):
    fields, planes, rows, width = flow_ref.shape
    _, lane = iotas(rows, width)
    outer = jnp.zeros((rows, width), jnp.float32)
    second, beside = outer, outer
    for c in range(fields):
        for x in range(planes):
            m, plane = c * planes + x, flow_ref[c, x]
            outer = pack_edges(outer, plane, m, lane)
            here = (lane == 2 * m) | (lane == (2 * m - 3) % width)
            second = jnp.where(here, pltpu.roll(plane, (2 * m - 1) % width, 1), second)
        for side, plane in enumerate(from_neighbours(lax.axis_index("fluid"), groups, x0_ref[c], x1_ref[c])):
            beside = pack_edges(beside, plane, 2 * c + side, lane)
    for x in range(planes):
        beside = pack_edges(beside, regions_ref[x].astype(jnp.float32), 2 * fields + x, lane)
    edges_ref[0], edges_ref[1], edges_ref[2] = outer, second, beside


def outside_edges(walls, planes, halo, second, beside, inside, rim_nu):
    rows, width = halo.shape
    row, lane = iotas(rows, width)
    x, field = (lane // 2) % planes, (lane // 2) // planes

    def spread(nu):
        nu = jnp.where(field == 0, nu, 0.0)
        return nu + pltpu.roll(nu, 2 * planes, 1) + pltpu.roll(nu, 4 * planes, 1)

    def nu_of(jump):
        return spread(viscosity([jump] + [pltpu.roll(jump, width - 2 * c * planes, 1) for c in (1, 2)]))

    over_x, under_x = pltpu.roll(halo, width - 2, 1), pltpu.roll(halo, 2, 1)
    for c in range(4):
        low = pltpu.roll(beside, (2 * c * planes - 4 * c) % width, 1)
        high = pltpu.roll(beside, (2 * (c * planes + planes - 1) - 4 * c - 2) % width, 1)
        under_x = jnp.where((x == 0) & (field == c), low, under_x)
        over_x = jnp.where((x == planes - 1) & (field == c), high, over_x)
    over_y = jnp.where(row == rows - 1, 0.0, pltpu.roll(halo, rows - 1, 0))
    under_y = jnp.where(row == 0, 0.0, pltpu.roll(halo, 1, 0))
    total = spread(rim_nu) * (inside - halo)
    for other in (over_x, under_x, over_y, under_y, second):
        total += nu_of(other - halo) * (other - halo)
    above = lane % 2 == 0
    gradient_x = pltpu.roll(0.5 * (over_x - under_x), width - 6 * planes, 1)
    gradient_y = pltpu.roll(0.5 * (over_y - under_y), width - 4 * planes, 1)
    gradient_z = pltpu.roll(0.5 * jnp.where(above, second - inside, inside - second), width - 2 * planes, 1)
    gradient = jnp.where(field == 0, gradient_x, jnp.where(field == 1, gradient_y, gradient_z))
    value = halo + time_step * (total - gradient)
    value = jnp.where(field == 3, pltpu.roll(beside, 6 * planes - 16, 1), value)
    me = lax.axis_index("wall")
    exists = jnp.where(above, jnp.where(me < walls - 1, 1, 0), jnp.where(me > 0, 1, 0)) == 1
    return jnp.where(exists & (field < 4), value, 0.0)


def group_kernel(cap, dest_ref, tiles_ref, meas_ref, flow_ref, *refs):
    chips = len(refs) - 12
    sends, halo_refs = refs[:chips], refs[chips : chips + 2]
    (list_ref, held_ref, seen_ref, count_ref, slot_ref, rows_ref,
     list_sem, seen_sem, in_sems, face_sems) = refs[chips + 2 :]
    count_tiles, width, _ = tiles_ref.shape
    groups = 2 * chips
    slots = groups * cap
    extra = rows_ref.shape[0] // groups
    depth = cap * width
    me = lax.axis_index("fluid")
    listed = pltpu.make_async_copy(dest_ref, list_ref, list_sem)
    listed.start()
    piece = count_tiles // in_sems.shape[0]

    def load(p):
        part = pl.ds(p * piece, piece)
        return pltpu.make_async_copy(tiles_ref.at[part], held_ref.at[part], in_sems.at[p])

    for p in range(in_sems.shape[0]):
        load(p).start()
    seen = pltpu.make_async_copy(meas_ref, seen_ref, seen_sem)
    seen.start()
    last = flow_ref.shape[1] - 1
    fields = flow_ref.shape[0]
    faces = [
        pltpu.make_async_copy(flow_ref.at[c, plane], halo_refs[i].at[c], face_sems.at[i * fields + c])
        for i, plane in enumerate((last * (1 - me % 2), last * (me % 2)))
        for c in range(fields)
    ]
    for face in faces:
        face.start()

    def clear(b, carry):
        count_ref[b] = 0
        for k in range(cap):
            slot_ref[b * cap + k] = -1
        return carry

    lax.fori_loop(0, groups, clear, 0)
    _, tile_lane = iotas(8, count_tiles)
    listed.wait()

    def place(t, slot_of):
        b = list_ref[t]
        k = count_ref[b]
        count_ref[b] = k + 1
        slot_ref[b * cap + k] = t
        return jnp.where(tile_lane == t, b * cap + k, slot_of)

    slot_of = lax.fori_loop(
        0, count_tiles, place, jnp.full((8, count_tiles), -1, jnp.int32), unroll=True
    )
    for p in range(in_sems.shape[0]):
        load(p).wait()

    for m in list(range(1, chips)) + [0]:
        for j in range(2):
            b = me ^ (2 * m + j)
            for k in range(cap):
                t = slot_ref[b * cap + k]
                at = (j, slice(k * width, (k + 1) * width))
                if slots > count_tiles:
                    sends[m][at] = jnp.where(t >= 0, held_ref[jnp.maximum(t, 0)], jnp.zeros((width, width), jnp.bfloat16))
                else:
                    sends[m][at] = held_ref[t]
    seen.wait()
    row = lax.broadcasted_iota(jnp.int32, (groups * extra, count_tiles), 0)
    within = row % extra
    row_slot = (row // extra) * cap + within // 3
    used = within < cap * 3
    total = jnp.zeros((groups * extra, width), jnp.float32)
    for c in range(3):
        pick = (row_slot == slot_of[0:1, :]) & used & (within % 3 == c)
        total += jnp.dot(
            pick.astype(jnp.float32).astype(jnp.bfloat16), seen_ref[c], preferred_element_type=jnp.float32
        )
    rows_ref[...] = total.astype(jnp.bfloat16)

    for m in range(chips):
        for j in range(2):
            b = me ^ (2 * m + j)
            sends[m][j, depth:, :] = rows_ref[pl.ds(pl.multiple_of(b * extra, extra), extra), :]
    for face in faces:
        face.wait()


def forward_kernel(
    sizes, cap, cells_ref, flow_ref, x0_ref, x1_ref, z0_ref, z1_ref, edges_ref,
    out_ref, next_ref, nux_ref, nuy_ref, nuz_ref, nuy0_ref, rim_ref, mine_ref, lent_ref, cells_of_ref,
    list_ref, padded_ref, taken_ref, list_sem, out_sems,
):
    _, planes, rows, width = flow_ref.shape
    groups, walls = sizes
    chips, extra, _ = mine_ref.shape
    listed = pltpu.make_async_copy(cells_ref, list_ref, list_sem)
    listed.start()
    row, lane = iotas(rows, width)
    halo = mix_edges(*from_neighbours(lax.axis_index("wall"), walls, z0_ref[0], z1_ref[0]), lane)
    inside = pltpu.roll(edges_ref[0], 1, 1)
    jump = halo - inside
    rim_nu = viscosity([jump] + [pltpu.roll(jump, width - 2 * c * planes, 1) for c in (1, 2)])
    rim_nu = jnp.where(lane < 2 * planes, rim_nu, 0.0)
    rim_ref[...] = rim_nu
    for c in range(4):
        low, high = from_neighbours(lax.axis_index("fluid"), groups, x0_ref[c], x1_ref[c])
        padded_ref[c, 0] = low
        padded_ref[c, planes + 1] = high
        padded_ref[c, 1 : planes + 1] = flow_ref[c]
    nux_ref[0] = viscosity([padded_ref[c, 1] - padded_ref[c, 0] for c in range(3)])

    def plane(x, carry):
        here = [padded_ref[c, x + 1] for c in range(4)]
        over = [padded_ref[c, x + 2] for c in range(4)]
        under = [padded_ref[c, x] for c in range(4)]
        total = [None] * 3
        pressure = [None] * 3

        def add(axis, nu_up, nu_down):
            for c in range(3):
                flux = nu_up * (over[c] - here[c]) - nu_down * (here[c] - under[c])
                total[c] = flux if total[c] is None else total[c] + flux
            pressure[axis] = 0.5 * (over[3] - under[3])

        nu_up = viscosity([over[c] - here[c] for c in range(3)])
        nux_ref[x + 1] = nu_up
        add(0, nu_up, nux_ref[x])
        over = [jnp.where(row == rows - 1, 0.0, pltpu.roll(here[c], rows - 1, 0)) for c in range(4)]
        under = [jnp.where(row == 0, 0.0, pltpu.roll(here[c], 1, 0)) for c in range(4)]
        nu_up = viscosity([over[c] - here[c] for c in range(3)])
        nu_first = viscosity([here[c][:1] for c in range(3)])
        nuy_ref[x] = nu_up
        nuy0_ref[pl.ds(x, 1), :] = nu_first
        add(1, nu_up, jnp.where(row == 0, nu_first, pltpu.roll(nu_up, 1, 0)))
        rim = [edge_of(halo, c * planes + x) for c in range(4)]
        over = [jnp.where(lane == width - 1, rim[c], pltpu.roll(here[c], width - 1, 1)) for c in range(4)]
        under = [jnp.where(lane == 0, rim[c], pltpu.roll(here[c], 1, 1)) for c in range(4)]
        nu_up = viscosity([over[c] - here[c] for c in range(3)])
        nuz_ref[x] = nu_up
        add(2, nu_up, jnp.where(lane == 0, edge_of(rim_nu, x), pltpu.roll(nu_up, 1, 1)))
        for c in range(3):
            value = here[c] + time_step * (total[c] - pressure[c])
            next_ref[c, x] = value
        return carry

    pieces = out_sems.shape[0]
    step = planes // pieces

    def store(i):
        part = pl.ds(i * step, step)
        return pltpu.make_async_copy(next_ref.at[:, part], out_ref.at[:, part], out_sems.at[i])

    for i in range(pieces):
        lax.fori_loop(i * step, (i + 1) * step, plane, 0, unroll=True)
        store(i).start()

    taken_ref[...] = jnp.zeros_like(taken_ref)
    listed.wait()
    _, slot_lane = iotas(8, groups * extra)
    cell_of = jnp.full((8, groups * extra), -1, jnp.int32)
    odd = lax.axis_index("fluid") % 2
    for b in range(groups):
        part = (odd if b % 2 == 0 else 1 - odd) * chips + b // 2
        for k in range(cap):
            cell = list_ref[k, b]
            x, y = lax.div(cell, rows), lax.rem(cell, rows)
            first = part * extra + 3 * k
            for c in range(3):
                taken_ref[pl.ds(first + c, 1), :] = next_ref[c, x, pl.ds(y, 1), :]
            cell_of = jnp.where((slot_lane >= first) & (slot_lane < first + 3), cell, cell_of)
    cells_of_ref[...] = cell_of
    taken = taken_ref[...].astype(jnp.bfloat16).reshape((2,) + mine_ref.shape)
    mine_ref[...] = taken[0]
    lent_ref[...] = taken[1]
    for i in range(pieces):
        store(i).wait()


def pick_kernel(
    sizes, cells_of_ref, z0_ref, z1_ref, edges_ref, rim_ref, outside_ref, rims_ref, pick_ref
):
    _, rows, width = edges_ref.shape
    groups, walls = sizes
    _, lines, slot_rows = pick_ref.shape
    planes = lines // rows
    extra = slot_rows // groups
    _, lane = iotas(rows, width)
    halo, second, beside = (
        mix_edges(*from_neighbours(lax.axis_index("wall"), walls, z0_ref[i], z1_ref[i]), lane, shift)
        for i, shift in enumerate((2, 4, 2))
    )
    inside = pltpu.roll(edges_ref[0], 1, 1)
    rim_nu = rim_ref[...]
    outside_ref[...] = outside_edges(walls, planes, halo, second, beside, inside, rim_nu)
    rims_ref[...] = time_step * (rim_nu + pltpu.roll(rim_nu, 2 * planes, 1) + pltpu.roll(rim_nu, 4 * planes, 1))
    line, slot_lane = iotas(lines, slot_rows)
    hit = line == cells_of_ref[0:1, :]
    part = (slot_lane % extra) % 3
    for c in range(3):
        pick_ref[c] = (hit & (part == c)).astype(jnp.float32).astype(jnp.bfloat16)


def product_kernel(cap, block, values_ref, after_ref, *refs):
    chips, extra, width = values_ref.shape
    recvs, out_ref = refs[:chips], refs[chips]
    depth = cap * width
    row, lane = iotas(extra, depth)
    own = row // 3 == lane // width
    here = lax.axis_index("fluid") // 2
    for m, recv_ref in enumerate(recvs):
        source = here ^ m
        at = pl.ds(pl.multiple_of(source * extra, extra), extra)
        weights = recv_ref[block, pl.ds(0, depth), :]
        predicted = lax.dot_general(
            values_ref[source], weights, (((1,), (1,)), ((), ())), preferred_element_type=jnp.float32
        )
        seen = recv_ref[block, pl.ds(depth, extra), :].astype(jnp.float32)
        misfit = jnp.where(own, predicted - jnp.concatenate([seen] * cap, axis=1), 0.0).astype(jnp.bfloat16)
        contrib = jnp.dot(misfit, weights, preferred_element_type=jnp.float32)
        high = contrib.astype(jnp.bfloat16)
        out_ref[0, at, :] = high
        out_ref[1, at, :] = (contrib - high.astype(jnp.float32)).astype(jnp.bfloat16)


def forcing_rows(c, part, mine_ref, other_ref, pick_ref):
    half = mine_ref.shape[1]
    total = None
    for i, share_ref in enumerate((mine_ref, other_ref)):
        pick = pick_ref[c, part, i * half : (i + 1) * half]
        for share in range(2):
            product = jnp.dot(pick, share_ref[share], preferred_element_type=jnp.float32)
            total = product if total is None else total + product
    return total


def ends_kernel(mine_ref, other_ref, pick_ref, first_ref, second_ref):
    _, rows, _ = first_ref.shape
    lines = pick_ref.shape[1]
    even = lax.axis_index("fluid") % 2 == 0
    for c in range(3):
        low = forcing_rows(c, slice(0, rows), mine_ref, other_ref, pick_ref)
        high = forcing_rows(c, slice(lines - rows, lines), mine_ref, other_ref, pick_ref)
        first_ref[c] = jnp.where(even, high, low).astype(jnp.bfloat16)
        second_ref[c] = jnp.where(even, low, high).astype(jnp.bfloat16)


def forcing_kernel(mine_ref, other_ref, pick_ref, after_ref, forcing_ref):
    for c in range(3):
        forcing_ref[c] = forcing_rows(c, slice(None), mine_ref, other_ref, pick_ref).reshape(forcing_ref.shape[1:])


FOLD = 16


def region_rows(values, ids, tops):
    def folded(plane):
        return jnp.concatenate([plane[y : y + FOLD] for y in range(0, plane.shape[0], FOLD)], axis=1)

    values, ids = folded(values), folded(ids)
    top, low = (ids // 8).astype(jnp.float32).astype(jnp.bfloat16), (ids % 8).astype(jnp.float32).astype(jnp.bfloat16)
    main = values.astype(jnp.bfloat16)
    rest = (values - main.astype(jnp.float32)).astype(jnp.bfloat16)
    zero = jnp.zeros_like(main)
    one = jnp.ones_like(main)
    hits = [top == jnp.bfloat16(h) for h in range(tops)]
    return (
        jnp.concatenate([jnp.where(hit, main, zero) for hit in hits], axis=0),
        jnp.concatenate([jnp.where(hit, rest, zero) for hit in hits], axis=0),
        jnp.concatenate([jnp.where(low == jnp.bfloat16(l), one, zero) for l in range(8)], axis=0),
    )


def region_sums(main, rest, ones):
    over_lanes = (((1,), (1,)), ((), ()))
    total = lax.dot_general(main, ones, over_lanes, preferred_element_type=jnp.float32)
    total += lax.dot_general(rest, ones, over_lanes, preferred_element_type=jnp.float32)
    row, column = iotas(*total.shape)
    total = jnp.where(row % FOLD == column % FOLD, total, 0.0)
    return jnp.sum(total.reshape(total.shape[0] // FOLD, FOLD, total.shape[1]), axis=1)


def inner_kernel(
    forcing_ref, next_ref, nux_ref, nuy_ref, nuz_ref, nuy0_ref, rim_ref, regions_ref, outside_ref,
    adjoint_ref, fpack_ref, sums_ref, main_ref, rest_ref, ones_ref,
):
    _, planes, rows, width = forcing_ref.shape
    row, lane = iotas(rows, width)
    rim_nu = rim_ref[...]
    tops = sums_ref.shape[0]

    def add_up(x, values, ids):
        span = rows // FOLD * width
        at = pl.ds(pl.multiple_of(x * span, span), span)
        for part_ref, part in zip((main_ref, rest_ref, ones_ref), region_rows(values, ids, tops)):
            part_ref[:, at] = part

    def plane(x, fpack):
        nuy, nuz = nuy_ref[x], nuz_ref[x]
        nuy_down = jnp.where(row == 0, nuy0_ref[pl.ds(x, 1), :], pltpu.roll(nuy, 1, 0))
        nuz_down = jnp.where(lane == 0, edge_of(rim_nu, x), pltpu.roll(nuz, 1, 1))
        nus = (nux_ref[x + 1], nux_ref[x], nuy, nuy_down, nuz, nuz_down)
        next_up, next_down = jnp.minimum(x + 1, planes - 1), jnp.maximum(x - 1, 0)
        at_top, at_bottom = x == planes - 1, x == 0
        product = None
        for c in range(3):
            here = forcing_ref[c, x]
            over = jnp.where(at_top, 0.0, forcing_ref[c, next_up])
            under = jnp.where(at_bottom, 0.0, forcing_ref[c, next_down])
            total = nus[0] * (over - here) - nus[1] * (here - under)
            over = jnp.where(row == rows - 1, 0.0, pltpu.roll(here, rows - 1, 0))
            under = jnp.where(row == 0, 0.0, pltpu.roll(here, 1, 0))
            total += nus[2] * (over - here) - nus[3] * (here - under)
            over = jnp.where(lane == width - 1, 0.0, pltpu.roll(here, width - 1, 1))
            under = jnp.where(lane == 0, 0.0, pltpu.roll(here, 1, 1))
            total += nus[4] * (over - here) - nus[5] * (here - under)
            value = here + time_step * total
            adjoint_ref[c, x] = value
            part = value * next_ref[c, x]
            product = part if product is None else product + part
            fpack = pack_edges(fpack, here, c * planes + x, lane)
        add_up(x, product, regions_ref[x])
        return fpack

    fpack = lax.fori_loop(0, planes, plane, jnp.zeros((rows, width), jnp.float32), unroll=4)
    fpack_ref[...] = fpack
    mixed = outside_ref[...]
    reach = pltpu.roll(fpack, 1, 1) * mixed
    reach = reach + pltpu.roll(reach, width - 2 * planes, 1) + pltpu.roll(reach, width - 4 * planes, 1)
    reach = time_step * reach * rim_nu
    add_up(planes, reach, pltpu.roll(mixed, (width - 6 * planes) % width, 1).astype(jnp.int32))
    sums_ref[...] = region_sums(main_ref[...], rest_ref[...], ones_ref[...])


def edge_kernel(groups, masks, x0_ref, x1_ref, nux_ref, next_ref, regions_ref, sums_ref, fpack_ref, *outs):
    _, planes, rows, width = next_ref.shape
    tops, columns = sums_ref.shape
    low, high = 0.0, 0.0
    for c in range(3):
        below, above = beside_of(c, groups, x0_ref, x1_ref)
        low += below * next_ref[c, 0]
        high += above * next_ref[c, planes - 1]
    ends = [
        region_rows(time_step * nux_ref[0] * low, regions_ref[0], tops),
        region_rows(time_step * nux_ref[planes] * high, regions_ref[planes - 1], tops),
    ]
    total = sums_ref[...] + region_sums(*(jnp.concatenate(both, axis=1) for both in zip(*ends)))
    height = tops * (columns // width)
    for mask, out_ref in zip((0,) + masks, outs):
        for i in range(columns // width):
            out_ref[i * tops : (i + 1) * tops, :] = total[:, i * width : (i + 1) * width]
        if mask:
            out_ref[height : height + rows, :] = fpack_ref[...]
            if out_ref.shape[0] > height + rows:
                out_ref[height + rows :, :] = jnp.zeros((out_ref.shape[0] - height - rows, width), jnp.float32)


def beside_of(c, groups, x0_ref, x1_ref):
    return from_neighbours(
        lax.axis_index("fluid"), groups, x0_ref[c].astype(jnp.float32), x1_ref[c].astype(jnp.float32)
    )


def final_kernel(sizes, inner_ref, x0_ref, x1_ref, nux_ref, rims_ref, own_ref, *refs):
    groups, walls = sizes
    arrived, (adjoint_ref, sens_ref, value_ref, owned_ref, sems, owned_sem) = refs[:-6], refs[-6:]
    _, planes, rows, width = inner_ref.shape
    per = own_ref.shape[0]
    _, lane = iotas(rows, width)
    me = lax.axis_index("wall")
    total = own_ref[...]
    below = jnp.zeros((rows, width), jnp.float32)
    above = jnp.zeros((rows, width), jnp.float32)
    for mask, ref in zip(range(1, walls), arrived):
        total = total + ref[:per, :]
        if mask & (mask + 1) == 0:
            edges = ref[per : per + rows, :]
            above = jnp.where((me ^ mask) == me + 1, edges, above)
            below = jnp.where((me ^ mask) == me - 1, edges, below)
    mixed = mix_edges(below, above, lane)
    edge_flux = mixed * rims_ref[...]
    on_edge = (lane == 0) | (lane == width - 1)

    beside = [beside_of(c, groups, x0_ref, x1_ref) for c in range(3)]
    step = planes // sems.shape[0]

    def store(i):
        part = pl.ds(i * step, step)
        return pltpu.make_async_copy(value_ref.at[:, part], adjoint_ref.at[:, part], sems.at[i])

    for i in range(sems.shape[0]):
        for x in range(i * step, (i + 1) * step):
            for c in range(3):
                value = inner_ref[c, x] + jnp.where(on_edge, edge_of(edge_flux, c * planes + x), 0.0)
                if x == 0:
                    value += time_step * nux_ref[0] * beside[c][0]
                if x == planes - 1:
                    value += time_step * nux_ref[planes] * beside[c][1]
                value_ref[c, x] = value
        store(i).start()
    parts = width // FOLD
    tops = REG_DEV * walls // 8
    owned = REG_DEV // 8
    top, _ = iotas(tops, width)
    region, lane = iotas(REG_DEV, width)
    sens = jnp.zeros((8, REG_DEV), jnp.float32)
    for i in range(8 // parts):
        for h in range(owned):
            mine = jnp.where(top == me * owned + h, total[i * tops : (i + 1) * tops], 0.0)
            gather = (region == h * 8 + i * parts + lane // FOLD).astype(jnp.float32)
            sens += lax.dot_general(
                jnp.broadcast_to(jnp.sum(mine, axis=0, keepdims=True), (8, width)), gather, (((1,), (1,)), ((), ())),
                precision=lax.Precision.HIGHEST, preferred_element_type=jnp.float32,
            )
    owned_ref[...] = sens_scale * sens[:1]
    owned_copy = pltpu.make_async_copy(owned_ref, sens_ref, owned_sem)
    owned_copy.start()
    for i in range(sems.shape[0]):
        store(i).wait()
    owned_copy.wait()


def body(flow_state, regions, obs_tiles, measured, tile_dest, cell_list):
    groups, walls = lax.axis_size("fluid"), lax.axis_size("wall")
    sizes = (groups, walls)
    _, planes, rows, width = flow_state.shape
    count_tiles = obs_tiles.shape[2]
    cap = cell_list.shape[3]
    extra = -(-cap * 3 // 16) * 16
    reg_count = REG_DEV * walls
    cells = groups * cap
    grid = planes * rows * width

    chips = groups // 2
    height = cap * width + extra
    *sends, xs0, xs1 = call(
        functools.partial(group_kernel, cap),
        (bf16(2, height, width),) * chips + (f32(4, rows, width),) * 2,
        [HBM] * 4,
        tuple(
            pltpu.with_memory_space_constraint(operand, pltpu.HBM)
            for operand in (tile_dest[0, 0], obs_tiles[0, 0], jnp.transpose(measured[0, 0], (1, 0, 2)), flow_state)
        ),
        (
            pltpu.SMEM((count_tiles,), jnp.int32),
            pltpu.VMEM((count_tiles, width, width), jnp.bfloat16),
            pltpu.VMEM((3, count_tiles, width), jnp.bfloat16),
            pltpu.SMEM((groups,), jnp.int32),
            pltpu.SMEM((cells,), jnp.int32),
            pltpu.VMEM((groups * extra, width), jnp.bfloat16),
            pltpu.SemaphoreType.DMA,
            pltpu.SemaphoreType.DMA,
            pltpu.SemaphoreType.DMA((4,)),
            pltpu.SemaphoreType.DMA((8,)),
        ),
        out_specs=(VMEM,) * (chips + 2),
    )
    x0, x1 = swap(xs0, "fluid", 0), swap(xs1, "fluid", 1)
    recvs = [sends[0]] + [cross(sends[m], "fluid", 2 * m) for m in range(1, chips)]
    zs = call(
        functools.partial(edges_kernel, groups),
        f32(3, rows, width),
        [VMEM] * 4,
        (flow_state, regions, x0, x1),
        flops=HIDES,
    )
    z0, z1 = swap(zs, "wall", 0), swap(zs, "wall", 1)
    slot_rows = groups * extra
    velocity_next, velocity, nux, nuy, nuz, nuy0, rim, mine, lent, cells_of = call(
        functools.partial(forward_kernel, sizes, cap),
        (f32(3, planes, rows, width),) * 2
        + (f32(planes + 1, rows, width), f32(planes, rows, width), f32(planes, rows, width))
        + (f32(planes, width), f32(rows, width))
        + (bf16(chips, extra, width),) * 2
        + (jax.ShapeDtypeStruct((8, slot_rows), jnp.int32),),
        [ANY] + [VMEM] * 6,
        (cell_list[0, 0].T, flow_state, x0, x1, z0, z1, zs),
        (
            pltpu.SMEM((cap, groups), jnp.int32),
            pltpu.VMEM((4, planes + 2, rows, width), jnp.float32),
            pltpu.VMEM((slot_rows, width), jnp.float32),
            pltpu.SemaphoreType.DMA,
            pltpu.SemaphoreType.DMA((4,)),
        ),
        out_specs=(HBM,) + (VMEM,) * 9,
    )
    borrowed = cross(lent, "fluid", 1)
    outside, rims, pick = call(
        functools.partial(pick_kernel, sizes),
        (f32(rows, width), f32(rows, width), bf16(3, planes * rows, slot_rows)),
        [VMEM] * 5,
        (cells_of, z0, z1, zs, rim),
    )

    def products(block, values, after):
        return call(
            functools.partial(product_kernel, cap, block),
            bf16(2, chips * extra, width),
            [VMEM, ANY] + [VMEM] * chips,
            (values, after, *recvs),
        )

    given = products(1, borrowed, pick)
    other = cross(given, "fluid", 1)
    held = products(0, mine, given)
    fs0, fs1 = call(ends_kernel, (bf16(3, rows, width),) * 2, [VMEM] * 3, (held, other, pick))
    f0, f1 = swap(fs0, "fluid", 0), swap(fs1, "fluid", 1)
    forcing = call(forcing_kernel, f32(3, planes, rows, width), [VMEM] * 3 + [ANY], (held, other, pick, fs1))
    tops = reg_count // 8
    columns = 8 * FOLD
    span = (planes + 1) * rows // FOLD * width
    sum_rows = tops * (columns // width)
    inner, fpack, sums = call(
        inner_kernel,
        (f32(3, planes, rows, width), f32(rows, width), f32(tops, columns)),
        [VMEM] * 9,
        (forcing, velocity, nux, nuy, nuz, nuy0, rim, regions, outside),
        (
            pltpu.VMEM((tops * FOLD, span), jnp.bfloat16),
            pltpu.VMEM((tops * FOLD, span), jnp.bfloat16),
            pltpu.VMEM((columns, span), jnp.bfloat16),
        ),
    )
    masks = tuple(range(1, walls))
    heights = [sum_rows] + [sum_rows + rows + 8 * (mask - 1) for mask in masks]
    own, *parts = call(
        functools.partial(edge_kernel, groups, masks),
        tuple(f32(height, width) for height in heights),
        [VMEM] * 7,
        (f0, f1, nux, velocity, regions, sums, fpack),
    )
    arrived = [cross(part, "wall", mask) for part, mask in zip(parts, masks)]
    adjoint, sens = call(
        functools.partial(final_kernel, sizes),
        (f32(3, planes, rows, width), f32(1, REG_DEV)),
        [VMEM] * (6 + len(arrived)),
        (inner, f0, f1, nux, rims, own, *arrived),
        (
            pltpu.VMEM((3, planes, rows, width), jnp.float32),
            pltpu.VMEM((1, REG_DEV), jnp.float32),
            pltpu.SemaphoreType.DMA((4,)),
            pltpu.SemaphoreType.DMA,
        ),
        out_specs=(HBM, HBM),
        flops=10 * grid,
        moved=24 * grid,
    )
    return velocity_next, adjoint, sens.reshape(REG_DEV)


def solution(mesh):
    in_specs = (
        P(None, "fluid", None, "wall"),
        P("fluid", None, "wall"),
        P("fluid", "wall", None, None, None),
        P("fluid", "wall", None, None, None),
        P("fluid", "wall", None),
        P("fluid", "wall", None, None),
    )
    out_specs = (
        P(None, "fluid", None, "wall"),
        P(None, "fluid", None, "wall"),
        P(("fluid", "wall")),
    )
    return jax.shard_map(body, mesh=mesh, in_specs=in_specs, out_specs=out_specs, check_vma=False)
```

```python
import functools

import jax
import jax.numpy as jnp
from jax import lax
from jax.experimental import pallas as pl
from jax.experimental.pallas import tpu as pltpu
from jax.sharding import PartitionSpec as P

REG_DEV = 16

time_step = 0.12
nu_floor = 0.1
nu_spread = 0.9
relax_sq = 4.0
sens_scale = 0.03

VMEM = pl.BlockSpec(memory_space=pltpu.VMEM)
SMEM = pl.BlockSpec(memory_space=pltpu.SMEM)
ANY = pl.BlockSpec(memory_space=pl.ANY)
HBM = pl.BlockSpec(memory_space=pltpu.HBM)
LIMIT = 24 * 1024 * 1024
HIDES = 100_000_000_000


def call(kernel, outs, ins, operands, scratch=(), flops=1, moved=1, out_specs=None, limit=LIMIT):
    return pl.pallas_call(
        kernel,
        out_shape=outs,
        in_specs=ins,
        out_specs=out_specs if out_specs is not None else jax.tree.map(lambda _: VMEM, outs),
        scratch_shapes=list(scratch),
        compiler_params=pltpu.CompilerParams(vmem_limit_bytes=limit),
        cost_estimate=pl.CostEstimate(flops=flops, bytes_accessed=moved, transcendentals=0),
    )(*operands)


def f32(*shape):
    return jax.ShapeDtypeStruct(shape, jnp.float32)


def bf16(*shape):
    return jax.ShapeDtypeStruct(shape, jnp.bfloat16)


def swap(block, axis, turn):
    groups, walls = lax.axis_size("fluid"), lax.axis_size("wall")

    def partner(f, w):
        at, count = (f, groups) if axis == "fluid" else (w, walls)
        other = at + 1 if (at + turn) % 2 == 0 else at - 1
        if axis == "fluid":
            return (other, w) if 0 <= other < count else (f, w ^ 1)
        return (f, other) if 0 <= other < count else (f ^ 1, w)

    pairs = []
    for f in range(groups):
        for w in range(walls):
            to_f, to_w = partner(f, w)
            pairs.append((f * walls + w, to_f * walls + to_w))
    return lax.ppermute(block, ("fluid", "wall"), pairs)


def cross(block, axis, mask):
    return lax.ppermute(block, axis, [(i, i ^ mask) for i in range(lax.axis_size(axis))])


def from_neighbours(index, count, first, second):
    even = index % 2 == 0
    above = jnp.where(even, first, second)
    below = jnp.where(even, second, first)
    above = jnp.where(index == count - 1, jnp.zeros_like(above), above)
    below = jnp.where(index == 0, jnp.zeros_like(below), below)
    return below, above


def pack_edges(packed, plane, m, lane):
    width = lane.shape[1]
    here = (lane == 2 * m) | (lane == (2 * m + width - 1) % width)
    return jnp.where(here, pltpu.roll(plane, 2 * m, 1), packed)


def mix_edges(below, above, lane, shift=2):
    return jnp.where(lane % 2 == 0, above, pltpu.roll(below, shift, 1))


def edge_of(mixed, m):
    width = mixed.shape[1]
    return pltpu.roll(mixed, (2 * width - (2 * m + 1)) % width, 1)


def viscosity(jumps):
    shear_sq = jumps[0] * jumps[0] + jumps[1] * jumps[1] + jumps[2] * jumps[2]
    root = lax.rsqrt(1.0 + relax_sq * shear_sq)
    return nu_floor + nu_spread * (root * lax.rsqrt(root))


def iotas(rows, width):
    shape = (rows, width)
    return lax.broadcasted_iota(jnp.int32, shape, 0), lax.broadcasted_iota(jnp.int32, shape, 1)


def faces_kernel(flow_ref, first_ref, second_ref, sems):
    last = flow_ref.shape[1] - 1
    odd = lax.axis_index("fluid") % 2
    copies = [
        pltpu.make_async_copy(flow_ref.at[c, plane], out_ref.at[c], sems.at[i, c])
        for i, (plane, out_ref) in enumerate(((last - last * odd, first_ref), (last * odd, second_ref)))
        for c in range(flow_ref.shape[0])
    ]
    for copy in copies:
        copy.start()
    for copy in copies:
        copy.wait()


def edges_kernel(groups, flow_ref, regions_ref, x0_ref, x1_ref, edges_ref):
    fields, planes, rows, width = flow_ref.shape
    _, lane = iotas(rows, width)
    outer = jnp.zeros((rows, width), jnp.float32)
    second, beside = outer, outer
    for c in range(fields):
        for x in range(planes):
            m, plane = c * planes + x, flow_ref[c, x]
            outer = pack_edges(outer, plane, m, lane)
            here = (lane == 2 * m) | (lane == (2 * m - 3) % width)
            second = jnp.where(here, pltpu.roll(plane, (2 * m - 1) % width, 1), second)
        for side, plane in enumerate(from_neighbours(lax.axis_index("fluid"), groups, x0_ref[c], x1_ref[c])):
            beside = pack_edges(beside, plane, 2 * c + side, lane)
    for x in range(planes):
        beside = pack_edges(beside, regions_ref[x].astype(jnp.float32), 2 * fields + x, lane)
    edges_ref[0], edges_ref[1], edges_ref[2] = outer, second, beside


def outside_edges(walls, planes, halo, second, beside, inside, rim_nu):
    rows, width = halo.shape
    row, lane = iotas(rows, width)
    x, field = (lane // 2) % planes, (lane // 2) // planes

    def spread(nu):
        nu = jnp.where(field == 0, nu, 0.0)
        return nu + pltpu.roll(nu, 2 * planes, 1) + pltpu.roll(nu, 4 * planes, 1)

    def nu_of(jump):
        return spread(viscosity([jump] + [pltpu.roll(jump, width - 2 * c * planes, 1) for c in (1, 2)]))

    over_x, under_x = pltpu.roll(halo, width - 2, 1), pltpu.roll(halo, 2, 1)
    for c in range(4):
        low = pltpu.roll(beside, (2 * c * planes - 4 * c) % width, 1)
        high = pltpu.roll(beside, (2 * (c * planes + planes - 1) - 4 * c - 2) % width, 1)
        under_x = jnp.where((x == 0) & (field == c), low, under_x)
        over_x = jnp.where((x == planes - 1) & (field == c), high, over_x)
    over_y = jnp.where(row == rows - 1, 0.0, pltpu.roll(halo, rows - 1, 0))
    under_y = jnp.where(row == 0, 0.0, pltpu.roll(halo, 1, 0))
    total = spread(rim_nu) * (inside - halo)
    for other in (over_x, under_x, over_y, under_y, second):
        total += nu_of(other - halo) * (other - halo)
    above = lane % 2 == 0
    gradient_x = pltpu.roll(0.5 * (over_x - under_x), width - 6 * planes, 1)
    gradient_y = pltpu.roll(0.5 * (over_y - under_y), width - 4 * planes, 1)
    gradient_z = pltpu.roll(0.5 * jnp.where(above, second - inside, inside - second), width - 2 * planes, 1)
    gradient = jnp.where(field == 0, gradient_x, jnp.where(field == 1, gradient_y, gradient_z))
    value = halo + time_step * (total - gradient)
    value = jnp.where(field == 3, pltpu.roll(beside, 6 * planes - 16, 1), value)
    me = lax.axis_index("wall")
    exists = jnp.where(above, jnp.where(me < walls - 1, 1, 0), jnp.where(me > 0, 1, 0)) == 1
    return jnp.where(exists & (field < 4), value, 0.0)


def group_kernel(cap, dest_ref, tiles_ref, meas_ref, flow_ref, *refs):
    chips = len(refs) - 12
    sends, halo_refs = refs[:chips], refs[chips : chips + 2]
    (list_ref, held_ref, seen_ref, count_ref, slot_ref, rows_ref,
     list_sem, seen_sem, in_sems, face_sems) = refs[chips + 2 :]
    count_tiles, width, _ = tiles_ref.shape
    groups = 2 * chips
    slots = groups * cap
    extra = rows_ref.shape[0] // groups
    depth = cap * width
    me = lax.axis_index("fluid")
    listed = pltpu.make_async_copy(dest_ref, list_ref, list_sem)
    listed.start()
    piece = count_tiles // in_sems.shape[0]

    def load(p):
        part = pl.ds(p * piece, piece)
        return pltpu.make_async_copy(tiles_ref.at[part], held_ref.at[part], in_sems.at[p])

    for p in range(in_sems.shape[0]):
        load(p).start()
    seen = pltpu.make_async_copy(meas_ref, seen_ref, seen_sem)
    seen.start()
    last = flow_ref.shape[1] - 1
    fields = flow_ref.shape[0]
    faces = [
        pltpu.make_async_copy(flow_ref.at[c, plane], halo_refs[i].at[c], face_sems.at[i * fields + c])
        for i, plane in enumerate((last * (1 - me % 2), last * (me % 2)))
        for c in range(fields)
    ]
    for face in faces:
        face.start()

    def clear(b, carry):
        count_ref[b] = 0
        for k in range(cap):
            slot_ref[b * cap + k] = -1
        return carry

    lax.fori_loop(0, groups, clear, 0)
    _, tile_lane = iotas(8, count_tiles)
    listed.wait()

    def place(t, slot_of):
        b = list_ref[t]
        k = count_ref[b]
        count_ref[b] = k + 1
        slot_ref[b * cap + k] = t
        return jnp.where(tile_lane == t, b * cap + k, slot_of)

    slot_of = lax.fori_loop(
        0, count_tiles, place, jnp.full((8, count_tiles), -1, jnp.int32), unroll=True
    )
    for p in range(in_sems.shape[0]):
        load(p).wait()

    for m in list(range(1, chips)) + [0]:
        for j in range(2):
            b = me ^ (2 * m + j)
            for k in range(cap):
                t = slot_ref[b * cap + k]
                at = (j, slice(k * width, (k + 1) * width))
                if slots > count_tiles:
                    sends[m][at] = jnp.where(t >= 0, held_ref[jnp.maximum(t, 0)], jnp.zeros((width, width), jnp.bfloat16))
                else:
                    sends[m][at] = held_ref[t]
    seen.wait()
    row = lax.broadcasted_iota(jnp.int32, (groups * extra, count_tiles), 0)
    within = row % extra
    row_slot = (row // extra) * cap + within // 3
    used = within < cap * 3
    total = jnp.zeros((groups * extra, width), jnp.float32)
    for c in range(3):
        pick = (row_slot == slot_of[0:1, :]) & used & (within % 3 == c)
        total += jnp.dot(
            pick.astype(jnp.float32).astype(jnp.bfloat16), seen_ref[c], preferred_element_type=jnp.float32
        )
    rows_ref[...] = total.astype(jnp.bfloat16)

    for m in range(chips):
        for j in range(2):
            b = me ^ (2 * m + j)
            sends[m][j, depth:, :] = rows_ref[pl.ds(pl.multiple_of(b * extra, extra), extra), :]
    for face in faces:
        face.wait()


def forward_kernel(
    sizes, cap, cells_ref, flow_ref, x0_ref, x1_ref, z0_ref, z1_ref, edges_ref,
    out_ref, next_ref, nux_ref, nuy_ref, nuz_ref, nuy0_ref, rim_ref, mine_ref, lent_ref, cells_of_ref,
    list_ref, padded_ref, taken_ref, list_sem, out_sems,
):
    _, planes, rows, width = flow_ref.shape
    groups, walls = sizes
    chips, extra, _ = mine_ref.shape
    listed = pltpu.make_async_copy(cells_ref, list_ref, list_sem)
    listed.start()
    row, lane = iotas(rows, width)
    halo = mix_edges(*from_neighbours(lax.axis_index("wall"), walls, z0_ref[0], z1_ref[0]), lane)
    inside = pltpu.roll(edges_ref[0], 1, 1)
    jump = halo - inside
    rim_nu = viscosity([jump] + [pltpu.roll(jump, width - 2 * c * planes, 1) for c in (1, 2)])
    rim_nu = jnp.where(lane < 2 * planes, rim_nu, 0.0)
    rim_ref[...] = rim_nu
    for c in range(4):
        low, high = from_neighbours(lax.axis_index("fluid"), groups, x0_ref[c], x1_ref[c])
        padded_ref[c, 0] = low
        padded_ref[c, planes + 1] = high
        padded_ref[c, 1 : planes + 1] = flow_ref[c]
    nux_ref[0] = viscosity([padded_ref[c, 1] - padded_ref[c, 0] for c in range(3)])

    def plane(x, carry):
        here = [padded_ref[c, x + 1] for c in range(4)]
        over = [padded_ref[c, x + 2] for c in range(4)]
        under = [padded_ref[c, x] for c in range(4)]
        total = [None] * 3
        pressure = [None] * 3

        def add(axis, nu_up, nu_down):
            for c in range(3):
                flux = nu_up * (over[c] - here[c]) - nu_down * (here[c] - under[c])
                total[c] = flux if total[c] is None else total[c] + flux
            pressure[axis] = 0.5 * (over[3] - under[3])

        nu_up = viscosity([over[c] - here[c] for c in range(3)])
        nux_ref[x + 1] = nu_up
        add(0, nu_up, nux_ref[x])
        over = [jnp.where(row == rows - 1, 0.0, pltpu.roll(here[c], rows - 1, 0)) for c in range(4)]
        under = [jnp.where(row == 0, 0.0, pltpu.roll(here[c], 1, 0)) for c in range(4)]
        nu_up = viscosity([over[c] - here[c] for c in range(3)])
        nu_first = viscosity([here[c][:1] for c in range(3)])
        nuy_ref[x] = nu_up
        nuy0_ref[pl.ds(x, 1), :] = nu_first
        add(1, nu_up, jnp.where(row == 0, nu_first, pltpu.roll(nu_up, 1, 0)))
        rim = [edge_of(halo, c * planes + x) for c in range(4)]
        over = [jnp.where(lane == width - 1, rim[c], pltpu.roll(here[c], width - 1, 1)) for c in range(4)]
        under = [jnp.where(lane == 0, rim[c], pltpu.roll(here[c], 1, 1)) for c in range(4)]
        nu_up = viscosity([over[c] - here[c] for c in range(3)])
        nuz_ref[x] = nu_up
        add(2, nu_up, jnp.where(lane == 0, edge_of(rim_nu, x), pltpu.roll(nu_up, 1, 1)))
        for c in range(3):
            value = here[c] + time_step * (total[c] - pressure[c])
            next_ref[c, x] = value
        return carry

    pieces = out_sems.shape[0]
    step = planes // pieces

    def store(i):
        part = pl.ds(i * step, step)
        return pltpu.make_async_copy(next_ref.at[:, part], out_ref.at[:, part], out_sems.at[i])

    for i in range(pieces):
        lax.fori_loop(i * step, (i + 1) * step, plane, 0, unroll=True)
        store(i).start()

    taken_ref[...] = jnp.zeros_like(taken_ref)
    listed.wait()
    _, slot_lane = iotas(8, groups * extra)
    cell_of = jnp.full((8, groups * extra), -1, jnp.int32)
    odd = lax.axis_index("fluid") % 2
    for b in range(groups):
        part = (odd if b % 2 == 0 else 1 - odd) * chips + b // 2
        for k in range(cap):
            cell = list_ref[k, b]
            x, y = lax.div(cell, rows), lax.rem(cell, rows)
            first = part * extra + 3 * k
            for c in range(3):
                taken_ref[pl.ds(first + c, 1), :] = next_ref[c, x, pl.ds(y, 1), :]
            cell_of = jnp.where((slot_lane >= first) & (slot_lane < first + 3), cell, cell_of)
    cells_of_ref[...] = cell_of
    taken = taken_ref[...].astype(jnp.bfloat16).reshape((2,) + mine_ref.shape)
    mine_ref[...] = taken[0]
    lent_ref[...] = taken[1]
    for i in range(pieces):
        store(i).wait()


def pick_kernel(
    sizes, cells_of_ref, z0_ref, z1_ref, edges_ref, rim_ref, outside_ref, rims_ref, pick_ref
):
    _, rows, width = edges_ref.shape
    groups, walls = sizes
    _, lines, slot_rows = pick_ref.shape
    planes = lines // rows
    extra = slot_rows // groups
    _, lane = iotas(rows, width)
    halo, second, beside = (
        mix_edges(*from_neighbours(lax.axis_index("wall"), walls, z0_ref[i], z1_ref[i]), lane, shift)
        for i, shift in enumerate((2, 4, 2))
    )
    inside = pltpu.roll(edges_ref[0], 1, 1)
    rim_nu = rim_ref[...]
    outside_ref[...] = outside_edges(walls, planes, halo, second, beside, inside, rim_nu)
    rims_ref[...] = time_step * (rim_nu + pltpu.roll(rim_nu, 2 * planes, 1) + pltpu.roll(rim_nu, 4 * planes, 1))
    line, slot_lane = iotas(lines, slot_rows)
    hit = line == cells_of_ref[0:1, :]
    part = (slot_lane % extra) % 3
    for c in range(3):
        pick_ref[c] = (hit & (part == c)).astype(jnp.float32).astype(jnp.bfloat16)


def product_kernel(cap, block, masks, values_ref, before_ref, *refs):
    chips, extra, width = values_ref.shape
    recvs, out_ref = refs[:-1], refs[-1]
    depth = cap * width
    row, lane = iotas(extra, depth)
    own = row // 3 == lane // width
    here = lax.axis_index("fluid") // 2
    if before_ref.shape == out_ref.shape:
        out_ref[...] = before_ref[...]
    for m, recv_ref in zip(masks, recvs):
        source = here ^ m
        at = pl.ds(pl.multiple_of(source * extra, extra), extra)
        weights = recv_ref[block, pl.ds(0, depth), :]
        predicted = lax.dot_general(
            values_ref[source], weights, (((1,), (1,)), ((), ())), preferred_element_type=jnp.float32
        )
        seen = recv_ref[block, pl.ds(depth, extra), :].astype(jnp.float32)
        misfit = jnp.where(own, predicted - jnp.concatenate([seen] * cap, axis=1), 0.0).astype(jnp.bfloat16)
        contrib = jnp.dot(misfit, weights, preferred_element_type=jnp.float32)
        high = contrib.astype(jnp.bfloat16)
        out_ref[0, at, :] = high
        out_ref[1, at, :] = (contrib - high.astype(jnp.float32)).astype(jnp.bfloat16)


def shares(mine_ref, other_ref):
    return jnp.concatenate([ref[part] for part in range(2) for ref in (mine_ref, other_ref)], axis=0)


def forcing_rows(c, part, pick_ref, rows):
    pick = pick_ref[c, part, :]
    return jnp.dot(jnp.concatenate([pick, pick], axis=1), rows, preferred_element_type=jnp.float32)


def ends_kernel(mine_ref, other_ref, pick_ref, first_ref, second_ref):
    _, rows, _ = first_ref.shape
    lines = pick_ref.shape[1]
    even = lax.axis_index("fluid") % 2 == 0
    both = shares(mine_ref, other_ref)
    for c in range(3):
        low = forcing_rows(c, slice(0, rows), pick_ref, both)
        high = forcing_rows(c, slice(lines - rows, lines), pick_ref, both)
        first_ref[c] = jnp.where(even, high, low).astype(jnp.bfloat16)
        second_ref[c] = jnp.where(even, low, high).astype(jnp.bfloat16)


def forcing_kernel(mine_ref, other_ref, pick_ref, after_ref, forcing_ref):
    both = shares(mine_ref, other_ref)
    for c in range(3):
        forcing_ref[c] = forcing_rows(c, slice(None), pick_ref, both).reshape(forcing_ref.shape[1:])


FOLD = 16


def region_rows(values, ids, tops):
    def folded(plane):
        return jnp.concatenate([plane[y : y + FOLD] for y in range(0, plane.shape[0], FOLD)], axis=1)

    values, ids = folded(values), folded(ids)
    top, low = (ids // 8).astype(jnp.float32).astype(jnp.bfloat16), (ids % 8).astype(jnp.float32).astype(jnp.bfloat16)
    main = values.astype(jnp.bfloat16)
    rest = (values - main.astype(jnp.float32)).astype(jnp.bfloat16)
    zero = jnp.zeros_like(main)
    one = jnp.ones_like(main)
    hits = [top == jnp.bfloat16(h) for h in range(tops)]
    return (
        jnp.concatenate([jnp.where(hit, main, zero) for hit in hits], axis=0),
        jnp.concatenate([jnp.where(hit, rest, zero) for hit in hits], axis=0),
        jnp.concatenate([jnp.where(low == jnp.bfloat16(l), one, zero) for l in range(8)], axis=0),
    )


def region_sums(main, rest, ones):
    over_lanes = (((1,), (1,)), ((), ()))
    total = lax.dot_general(main, ones, over_lanes, preferred_element_type=jnp.float32)
    total += lax.dot_general(rest, ones, over_lanes, preferred_element_type=jnp.float32)
    row, column = iotas(*total.shape)
    total = jnp.where(row % FOLD == column % FOLD, total, 0.0)
    return jnp.sum(total.reshape(total.shape[0] // FOLD, FOLD, total.shape[1]), axis=1)


def inner_kernel(
    forcing_ref, next_ref, nux_ref, nuy_ref, nuz_ref, nuy0_ref, rim_ref, regions_ref, outside_ref,
    adjoint_ref, fpack_ref, sums_ref, main_ref, rest_ref, ones_ref,
):
    _, planes, rows, width = forcing_ref.shape
    row, lane = iotas(rows, width)
    rim_nu = rim_ref[...]
    tops = sums_ref.shape[0]

    def add_up(x, values, ids):
        span = rows // FOLD * width
        at = pl.ds(pl.multiple_of(x * span, span), span)
        for part_ref, part in zip((main_ref, rest_ref, ones_ref), region_rows(values, ids, tops)):
            part_ref[:, at] = part

    def plane(x, fpack):
        nuy, nuz = nuy_ref[x], nuz_ref[x]
        nuy_down = jnp.where(row == 0, nuy0_ref[pl.ds(x, 1), :], pltpu.roll(nuy, 1, 0))
        nuz_down = jnp.where(lane == 0, edge_of(rim_nu, x), pltpu.roll(nuz, 1, 1))
        nus = (nux_ref[x + 1], nux_ref[x], nuy, nuy_down, nuz, nuz_down)
        next_up, next_down = jnp.minimum(x + 1, planes - 1), jnp.maximum(x - 1, 0)
        at_top, at_bottom = x == planes - 1, x == 0
        product = None
        for c in range(3):
            here = forcing_ref[c, x]
            over = jnp.where(at_top, 0.0, forcing_ref[c, next_up])
            under = jnp.where(at_bottom, 0.0, forcing_ref[c, next_down])
            total = nus[0] * (over - here) - nus[1] * (here - under)
            over = jnp.where(row == rows - 1, 0.0, pltpu.roll(here, rows - 1, 0))
            under = jnp.where(row == 0, 0.0, pltpu.roll(here, 1, 0))
            total += nus[2] * (over - here) - nus[3] * (here - under)
            over = jnp.where(lane == width - 1, 0.0, pltpu.roll(here, width - 1, 1))
            under = jnp.where(lane == 0, 0.0, pltpu.roll(here, 1, 1))
            total += nus[4] * (over - here) - nus[5] * (here - under)
            value = here + time_step * total
            adjoint_ref[c, x] = value
            part = value * next_ref[c, x]
            product = part if product is None else product + part
            fpack = pack_edges(fpack, here, c * planes + x, lane)
        add_up(x, product, regions_ref[x])
        return fpack

    fpack = lax.fori_loop(0, planes, plane, jnp.zeros((rows, width), jnp.float32), unroll=4)
    fpack_ref[...] = fpack
    mixed = outside_ref[...]
    reach = pltpu.roll(fpack, 1, 1) * mixed
    reach = reach + pltpu.roll(reach, width - 2 * planes, 1) + pltpu.roll(reach, width - 4 * planes, 1)
    reach = time_step * reach * rim_nu
    add_up(planes, reach, pltpu.roll(mixed, (width - 6 * planes) % width, 1).astype(jnp.int32))
    sums_ref[...] = region_sums(main_ref[...], rest_ref[...], ones_ref[...])


def edge_kernel(groups, masks, x0_ref, x1_ref, nux_ref, next_ref, regions_ref, sums_ref, fpack_ref, *outs):
    _, planes, rows, width = next_ref.shape
    tops, columns = sums_ref.shape
    low, high = 0.0, 0.0
    for c in range(3):
        below, above = beside_of(c, groups, x0_ref, x1_ref)
        low += below * next_ref[c, 0]
        high += above * next_ref[c, planes - 1]
    ends = [
        region_rows(time_step * nux_ref[0] * low, regions_ref[0], tops),
        region_rows(time_step * nux_ref[planes] * high, regions_ref[planes - 1], tops),
    ]
    total = sums_ref[...] + region_sums(*(jnp.concatenate(both, axis=1) for both in zip(*ends)))
    height = tops * (columns // width)
    for mask, out_ref in zip((0,) + masks, outs):
        for i in range(columns // width):
            out_ref[i * tops : (i + 1) * tops, :] = total[:, i * width : (i + 1) * width]
        if mask:
            out_ref[height : height + rows, :] = fpack_ref[...]
            if out_ref.shape[0] > height + rows:
                out_ref[height + rows :, :] = jnp.zeros((out_ref.shape[0] - height - rows, width), jnp.float32)


def beside_of(c, groups, x0_ref, x1_ref):
    return from_neighbours(
        lax.axis_index("fluid"), groups, x0_ref[c].astype(jnp.float32), x1_ref[c].astype(jnp.float32)
    )


def final_kernel(sizes, inner_ref, x0_ref, x1_ref, nux_ref, rims_ref, own_ref, *refs):
    groups, walls = sizes
    arrived, (adjoint_ref, sens_ref, value_ref, owned_ref, sems, owned_sem) = refs[:-6], refs[-6:]
    _, planes, rows, width = inner_ref.shape
    per = own_ref.shape[0]
    _, lane = iotas(rows, width)
    me = lax.axis_index("wall")
    total = own_ref[...]
    below = jnp.zeros((rows, width), jnp.float32)
    above = jnp.zeros((rows, width), jnp.float32)
    for mask, ref in zip(range(1, walls), arrived):
        total = total + ref[:per, :]
        if mask & (mask + 1) == 0:
            edges = ref[per : per + rows, :]
            above = jnp.where((me ^ mask) == me + 1, edges, above)
            below = jnp.where((me ^ mask) == me - 1, edges, below)
    mixed = mix_edges(below, above, lane)
    edge_flux = mixed * rims_ref[...]
    on_edge = (lane == 0) | (lane == width - 1)

    beside = [beside_of(c, groups, x0_ref, x1_ref) for c in range(3)]
    step = planes // sems.shape[0]

    def store(i):
        part = pl.ds(i * step, step)
        return pltpu.make_async_copy(value_ref.at[:, part], adjoint_ref.at[:, part], sems.at[i])

    for i in range(sems.shape[0]):
        for x in range(i * step, (i + 1) * step):
            for c in range(3):
                value = inner_ref[c, x] + jnp.where(on_edge, edge_of(edge_flux, c * planes + x), 0.0)
                if x == 0:
                    value += time_step * nux_ref[0] * beside[c][0]
                if x == planes - 1:
                    value += time_step * nux_ref[planes] * beside[c][1]
                value_ref[c, x] = value
        store(i).start()
    parts = width // FOLD
    tops = REG_DEV * walls // 8
    owned = REG_DEV // 8
    top, _ = iotas(tops, width)
    region, lane = iotas(REG_DEV, width)
    sens = jnp.zeros((8, REG_DEV), jnp.float32)
    for i in range(8 // parts):
        for h in range(owned):
            mine = jnp.where(top == me * owned + h, total[i * tops : (i + 1) * tops], 0.0)
            gather = (region == h * 8 + i * parts + lane // FOLD).astype(jnp.float32)
            sens += lax.dot_general(
                jnp.broadcast_to(jnp.sum(mine, axis=0, keepdims=True), (8, width)), gather, (((1,), (1,)), ((), ())),
                precision=lax.Precision.HIGHEST, preferred_element_type=jnp.float32,
            )
    owned_ref[...] = sens_scale * sens[:1]
    owned_copy = pltpu.make_async_copy(owned_ref, sens_ref, owned_sem)
    owned_copy.start()
    for i in range(sems.shape[0]):
        store(i).wait()
    owned_copy.wait()


def body(flow_state, regions, obs_tiles, measured, tile_dest, cell_list):
    groups, walls = lax.axis_size("fluid"), lax.axis_size("wall")
    sizes = (groups, walls)
    _, planes, rows, width = flow_state.shape
    count_tiles = obs_tiles.shape[2]
    cap = cell_list.shape[3]
    extra = -(-cap * 3 // 16) * 16
    reg_count = REG_DEV * walls
    cells = groups * cap
    grid = planes * rows * width

    chips = groups // 2
    height = cap * width + extra
    *sends, xs0, xs1 = call(
        functools.partial(group_kernel, cap),
        (bf16(2, height, width),) * chips + (f32(4, rows, width),) * 2,
        [HBM] * 4,
        tuple(
            pltpu.with_memory_space_constraint(operand, pltpu.HBM)
            for operand in (tile_dest[0, 0], obs_tiles[0, 0], jnp.transpose(measured[0, 0], (1, 0, 2)), flow_state)
        ),
        (
            pltpu.SMEM((count_tiles,), jnp.int32),
            pltpu.VMEM((count_tiles, width, width), jnp.bfloat16),
            pltpu.VMEM((3, count_tiles, width), jnp.bfloat16),
            pltpu.SMEM((groups,), jnp.int32),
            pltpu.SMEM((cells,), jnp.int32),
            pltpu.VMEM((groups * extra, width), jnp.bfloat16),
            pltpu.SemaphoreType.DMA,
            pltpu.SemaphoreType.DMA,
            pltpu.SemaphoreType.DMA((4,)),
            pltpu.SemaphoreType.DMA((8,)),
        ),
        out_specs=(VMEM,) * (chips + 2),
    )
    x0, x1 = swap(xs0, "fluid", 0), swap(xs1, "fluid", 1)
    recvs = [sends[0]] + [cross(sends[m], "fluid", 2 * m) for m in range(1, chips)]
    zs = call(
        functools.partial(edges_kernel, groups),
        f32(3, rows, width),
        [VMEM] * 4,
        (flow_state, regions, x0, x1),
        flops=HIDES,
    )
    z0, z1 = swap(zs, "wall", 0), swap(zs, "wall", 1)
    slot_rows = groups * extra
    velocity_next, velocity, nux, nuy, nuz, nuy0, rim, mine, lent, cells_of = call(
        functools.partial(forward_kernel, sizes, cap),
        (f32(3, planes, rows, width),) * 2
        + (f32(planes + 1, rows, width), f32(planes, rows, width), f32(planes, rows, width))
        + (f32(planes, width), f32(rows, width))
        + (bf16(chips, extra, width),) * 2
        + (jax.ShapeDtypeStruct((8, slot_rows), jnp.int32),),
        [ANY] + [VMEM] * 6,
        (cell_list[0, 0].T, flow_state, x0, x1, z0, z1, zs),
        (
            pltpu.SMEM((cap, groups), jnp.int32),
            pltpu.VMEM((4, planes + 2, rows, width), jnp.float32),
            pltpu.VMEM((slot_rows, width), jnp.float32),
            pltpu.SemaphoreType.DMA,
            pltpu.SemaphoreType.DMA((4,)),
        ),
        out_specs=(HBM,) + (VMEM,) * 9,
    )
    borrowed = cross(lent, "fluid", 1)
    outside, rims, pick = call(
        functools.partial(pick_kernel, sizes),
        (f32(rows, width), f32(rows, width), bf16(3, planes * rows, slot_rows)),
        [VMEM] * 5,
        (cells_of, z0, z1, zs, rim),
    )

    def products(block, masks, values, before):
        whole = (2, chips * extra, width)
        return call(
            functools.partial(product_kernel, cap, block, masks),
            bf16(*whole),
            [VMEM, VMEM if before.shape == whole else ANY] + [VMEM] * len(masks),
            (values, before, *(recvs[m] for m in masks)),
        )

    given = products(1, tuple(range(chips // 2)), borrowed, pick)
    given = products(1, tuple(range(chips // 2, chips)), borrowed, given)
    other = cross(given, "fluid", 1)
    held = products(0, tuple(range(chips)), mine, outside)
    fs0, fs1 = call(ends_kernel, (bf16(3, rows, width),) * 2, [VMEM] * 3, (held, other, pick))
    f0, f1 = swap(fs0, "fluid", 0), swap(fs1, "fluid", 1)
    forcing = call(forcing_kernel, f32(3, planes, rows, width), [VMEM] * 3 + [ANY], (held, other, pick, fs1))
    tops = reg_count // 8
    columns = 8 * FOLD
    span = (planes + 1) * rows // FOLD * width
    sum_rows = tops * (columns // width)
    inner, fpack, sums = call(
        inner_kernel,
        (f32(3, planes, rows, width), f32(rows, width), f32(tops, columns)),
        [VMEM] * 9,
        (forcing, velocity, nux, nuy, nuz, nuy0, rim, regions, outside),
        (
            pltpu.VMEM((tops * FOLD, span), jnp.bfloat16),
            pltpu.VMEM((tops * FOLD, span), jnp.bfloat16),
            pltpu.VMEM((columns, span), jnp.bfloat16),
        ),
    )
    masks = tuple(range(1, walls))
    heights = [sum_rows] + [sum_rows + rows + 8 * (mask - 1) for mask in masks]
    own, *parts = call(
        functools.partial(edge_kernel, groups, masks),
        tuple(f32(height, width) for height in heights),
        [VMEM] * 7,
        (f0, f1, nux, velocity, regions, sums, fpack),
    )
    arrived = [cross(part, "wall", mask) for part, mask in zip(parts, masks)]
    adjoint, sens = call(
        functools.partial(final_kernel, sizes),
        (f32(3, planes, rows, width), f32(1, REG_DEV)),
        [VMEM] * (6 + len(arrived)),
        (inner, f0, f1, nux, rims, own, *arrived),
        (
            pltpu.VMEM((3, planes, rows, width), jnp.float32),
            pltpu.VMEM((1, REG_DEV), jnp.float32),
            pltpu.SemaphoreType.DMA((4,)),
            pltpu.SemaphoreType.DMA,
        ),
        out_specs=(HBM, HBM),
        flops=10 * grid,
        moved=24 * grid,
    )
    return velocity_next, adjoint, sens.reshape(REG_DEV)


def solution(mesh):
    in_specs = (
        P(None, "fluid", None, "wall"),
        P("fluid", None, "wall"),
        P("fluid", "wall", None, None, None),
        P("fluid", "wall", None, None, None),
        P("fluid", "wall", None),
        P("fluid", "wall", None, None),
    )
    out_specs = (
        P(None, "fluid", None, "wall"),
        P(None, "fluid", None, "wall"),
        P(("fluid", "wall")),
    )
    return jax.shard_map(body, mesh=mesh, in_specs=in_specs, out_specs=out_specs, check_vma=False)
```

```python
import functools

import jax
import jax.numpy as jnp
from jax import lax
from jax.experimental import pallas as pl
from jax.experimental.pallas import tpu as pltpu
from jax.sharding import PartitionSpec as P

REG_DEV = 16

time_step = 0.12
nu_floor = 0.1
nu_spread = 0.9
relax_sq = 4.0
sens_scale = 0.03

VMEM = pl.BlockSpec(memory_space=pltpu.VMEM)
SMEM = pl.BlockSpec(memory_space=pltpu.SMEM)
ANY = pl.BlockSpec(memory_space=pl.ANY)
HBM = pl.BlockSpec(memory_space=pltpu.HBM)
LIMIT = 24 * 1024 * 1024
HIDES = 100_000_000_000


def call(kernel, outs, ins, operands, scratch=(), flops=1, moved=1, out_specs=None, limit=LIMIT):
    return pl.pallas_call(
        kernel,
        out_shape=outs,
        in_specs=ins,
        out_specs=out_specs if out_specs is not None else jax.tree.map(lambda _: VMEM, outs),
        scratch_shapes=list(scratch),
        compiler_params=pltpu.CompilerParams(vmem_limit_bytes=limit),
        cost_estimate=pl.CostEstimate(flops=flops, bytes_accessed=moved, transcendentals=0),
    )(*operands)


def f32(*shape):
    return jax.ShapeDtypeStruct(shape, jnp.float32)


def bf16(*shape):
    return jax.ShapeDtypeStruct(shape, jnp.bfloat16)


def swap(block, axis, turn):
    groups, walls = lax.axis_size("fluid"), lax.axis_size("wall")

    def partner(f, w):
        at, count = (f, groups) if axis == "fluid" else (w, walls)
        other = at + 1 if (at + turn) % 2 == 0 else at - 1
        if axis == "fluid":
            return (other, w) if 0 <= other < count else (f, w ^ 1)
        return (f, other) if 0 <= other < count else (f ^ 1, w)

    pairs = []
    for f in range(groups):
        for w in range(walls):
            to_f, to_w = partner(f, w)
            pairs.append((f * walls + w, to_f * walls + to_w))
    return lax.ppermute(block, ("fluid", "wall"), pairs)


def cross(block, axis, mask):
    return lax.ppermute(block, axis, [(i, i ^ mask) for i in range(lax.axis_size(axis))])


def from_neighbours(index, count, first, second):
    even = index % 2 == 0
    above = jnp.where(even, first, second)
    below = jnp.where(even, second, first)
    above = jnp.where(index == count - 1, jnp.zeros_like(above), above)
    below = jnp.where(index == 0, jnp.zeros_like(below), below)
    return below, above


def pack_edges(packed, plane, m, lane):
    width = lane.shape[1]
    here = (lane == 2 * m) | (lane == (2 * m + width - 1) % width)
    return jnp.where(here, pltpu.roll(plane, 2 * m, 1), packed)


def mix_edges(below, above, lane, shift=2):
    return jnp.where(lane % 2 == 0, above, pltpu.roll(below, shift, 1))


def edge_of(mixed, m):
    width = mixed.shape[1]
    return pltpu.roll(mixed, (2 * width - (2 * m + 1)) % width, 1)


def viscosity(jumps):
    shear_sq = jumps[0] * jumps[0] + jumps[1] * jumps[1] + jumps[2] * jumps[2]
    root = lax.rsqrt(1.0 + relax_sq * shear_sq)
    return nu_floor + nu_spread * (root * lax.rsqrt(root))


def iotas(rows, width):
    shape = (rows, width)
    return lax.broadcasted_iota(jnp.int32, shape, 0), lax.broadcasted_iota(jnp.int32, shape, 1)


def faces_kernel(flow_ref, first_ref, second_ref, sems):
    last = flow_ref.shape[1] - 1
    odd = lax.axis_index("fluid") % 2
    copies = [
        pltpu.make_async_copy(flow_ref.at[c, plane], out_ref.at[c], sems.at[i, c])
        for i, (plane, out_ref) in enumerate(((last - last * odd, first_ref), (last * odd, second_ref)))
        for c in range(flow_ref.shape[0])
    ]
    for copy in copies:
        copy.start()
    for copy in copies:
        copy.wait()


def edges_kernel(groups, flow_ref, regions_ref, x0_ref, x1_ref, edges_ref):
    fields, planes, rows, width = flow_ref.shape
    _, lane = iotas(rows, width)
    outer = jnp.zeros((rows, width), jnp.float32)
    second, beside = outer, outer
    for c in range(fields):
        for x in range(planes):
            m, plane = c * planes + x, flow_ref[c, x]
            outer = pack_edges(outer, plane, m, lane)
            here = (lane == 2 * m) | (lane == (2 * m - 3) % width)
            second = jnp.where(here, pltpu.roll(plane, (2 * m - 1) % width, 1), second)
        for side, plane in enumerate(from_neighbours(lax.axis_index("fluid"), groups, x0_ref[c], x1_ref[c])):
            beside = pack_edges(beside, plane, 2 * c + side, lane)
    for x in range(planes):
        beside = pack_edges(beside, regions_ref[x].astype(jnp.float32), 2 * fields + x, lane)
    edges_ref[0], edges_ref[1], edges_ref[2] = outer, second, beside


def outside_edges(walls, planes, halo, second, beside, inside, rim_nu):
    rows, width = halo.shape
    row, lane = iotas(rows, width)
    x, field = (lane // 2) % planes, (lane // 2) // planes

    def spread(nu):
        nu = jnp.where(field == 0, nu, 0.0)
        return nu + pltpu.roll(nu, 2 * planes, 1) + pltpu.roll(nu, 4 * planes, 1)

    def nu_of(jump):
        return spread(viscosity([jump] + [pltpu.roll(jump, width - 2 * c * planes, 1) for c in (1, 2)]))

    over_x, under_x = pltpu.roll(halo, width - 2, 1), pltpu.roll(halo, 2, 1)
    for c in range(4):
        low = pltpu.roll(beside, (2 * c * planes - 4 * c) % width, 1)
        high = pltpu.roll(beside, (2 * (c * planes + planes - 1) - 4 * c - 2) % width, 1)
        under_x = jnp.where((x == 0) & (field == c), low, under_x)
        over_x = jnp.where((x == planes - 1) & (field == c), high, over_x)
    over_y = jnp.where(row == rows - 1, 0.0, pltpu.roll(halo, rows - 1, 0))
    under_y = jnp.where(row == 0, 0.0, pltpu.roll(halo, 1, 0))
    total = spread(rim_nu) * (inside - halo)
    for other in (over_x, under_x, over_y, under_y, second):
        total += nu_of(other - halo) * (other - halo)
    above = lane % 2 == 0
    gradient_x = pltpu.roll(0.5 * (over_x - under_x), width - 6 * planes, 1)
    gradient_y = pltpu.roll(0.5 * (over_y - under_y), width - 4 * planes, 1)
    gradient_z = pltpu.roll(0.5 * jnp.where(above, second - inside, inside - second), width - 2 * planes, 1)
    gradient = jnp.where(field == 0, gradient_x, jnp.where(field == 1, gradient_y, gradient_z))
    value = halo + time_step * (total - gradient)
    value = jnp.where(field == 3, pltpu.roll(beside, 6 * planes - 16, 1), value)
    me = lax.axis_index("wall")
    exists = jnp.where(above, jnp.where(me < walls - 1, 1, 0), jnp.where(me > 0, 1, 0)) == 1
    return jnp.where(exists & (field < 4), value, 0.0)


def group_kernel(cap, dest_ref, tiles_ref, meas_ref, flow_ref, *refs):
    chips = len(refs) - 12
    sends, halo_refs = refs[:chips], refs[chips : chips + 2]
    (list_ref, held_ref, seen_ref, count_ref, slot_ref, rows_ref,
     list_sem, seen_sem, in_sems, face_sems) = refs[chips + 2 :]
    count_tiles, width, _ = tiles_ref.shape
    groups = 2 * chips
    slots = groups * cap
    extra = rows_ref.shape[0] // groups
    depth = cap * width
    me = lax.axis_index("fluid")
    listed = pltpu.make_async_copy(dest_ref, list_ref, list_sem)
    listed.start()
    piece = count_tiles // in_sems.shape[0]

    def load(p):
        part = pl.ds(p * piece, piece)
        return pltpu.make_async_copy(tiles_ref.at[part], held_ref.at[part], in_sems.at[p])

    for p in range(in_sems.shape[0]):
        load(p).start()
    seen = pltpu.make_async_copy(meas_ref, seen_ref, seen_sem)
    seen.start()
    last = flow_ref.shape[1] - 1
    fields = flow_ref.shape[0]
    faces = [
        pltpu.make_async_copy(flow_ref.at[c, plane], halo_refs[i].at[c], face_sems.at[i * fields + c])
        for i, plane in enumerate((last * (1 - me % 2), last * (me % 2)))
        for c in range(fields)
    ]
    for face in faces:
        face.start()

    def clear(b, carry):
        count_ref[b] = 0
        for k in range(cap):
            slot_ref[b * cap + k] = -1
        return carry

    lax.fori_loop(0, groups, clear, 0)
    _, tile_lane = iotas(8, count_tiles)
    listed.wait()

    def place(t, slot_of):
        b = list_ref[t]
        k = count_ref[b]
        count_ref[b] = k + 1
        slot_ref[b * cap + k] = t
        return jnp.where(tile_lane == t, b * cap + k, slot_of)

    slot_of = lax.fori_loop(
        0, count_tiles, place, jnp.full((8, count_tiles), -1, jnp.int32), unroll=True
    )
    seen.wait()
    row = lax.broadcasted_iota(jnp.int32, (groups * extra, count_tiles), 0)
    within = row % extra
    row_slot = (row // extra) * cap + within // 3
    used = within < cap * 3
    total = jnp.zeros((groups * extra, width), jnp.float32)
    for c in range(3):
        pick = (row_slot == slot_of[0:1, :]) & used & (within % 3 == c)
        total += jnp.dot(
            pick.astype(jnp.float32).astype(jnp.bfloat16), seen_ref[c], preferred_element_type=jnp.float32
        )
    rows_ref[...] = total.astype(jnp.bfloat16)

    for p in range(in_sems.shape[0]):
        load(p).wait()

    for m in list(range(1, chips)) + [0]:
        for j in range(2):
            b = me ^ (2 * m + j)
            for k in range(cap):
                t = slot_ref[b * cap + k]
                at = (j, slice(k * width, (k + 1) * width))
                if slots > count_tiles:
                    sends[m][at] = jnp.where(t >= 0, held_ref[jnp.maximum(t, 0)], jnp.zeros((width, width), jnp.bfloat16))
                else:
                    sends[m][at] = held_ref[t]
    for m in range(chips):
        for j in range(2):
            b = me ^ (2 * m + j)
            sends[m][j, depth:, :] = rows_ref[pl.ds(pl.multiple_of(b * extra, extra), extra), :]
    for face in faces:
        face.wait()


def forward_kernel(
    sizes, cap, cells_ref, flow_ref, x0_ref, x1_ref, z0_ref, z1_ref, edges_ref,
    out_ref, next_ref, nux_ref, nuy_ref, nuz_ref, nuy0_ref, rim_ref, mine_ref, lent_ref, cells_of_ref,
    list_ref, padded_ref, taken_ref, list_sem, out_sems,
):
    _, planes, rows, width = flow_ref.shape
    groups, walls = sizes
    chips, extra, _ = mine_ref.shape
    listed = pltpu.make_async_copy(cells_ref, list_ref, list_sem)
    listed.start()
    row, lane = iotas(rows, width)
    halo = mix_edges(*from_neighbours(lax.axis_index("wall"), walls, z0_ref[0], z1_ref[0]), lane)
    inside = pltpu.roll(edges_ref[0], 1, 1)
    jump = halo - inside
    rim_nu = viscosity([jump] + [pltpu.roll(jump, width - 2 * c * planes, 1) for c in (1, 2)])
    rim_nu = jnp.where(lane < 2 * planes, rim_nu, 0.0)
    rim_ref[...] = rim_nu
    for c in range(4):
        low, high = from_neighbours(lax.axis_index("fluid"), groups, x0_ref[c], x1_ref[c])
        padded_ref[c, 0] = low
        padded_ref[c, planes + 1] = high
        padded_ref[c, 1 : planes + 1] = flow_ref[c]
    nux_ref[0] = viscosity([padded_ref[c, 1] - padded_ref[c, 0] for c in range(3)])

    def plane(x, carry):
        here = [padded_ref[c, x + 1] for c in range(4)]
        over = [padded_ref[c, x + 2] for c in range(4)]
        under = [padded_ref[c, x] for c in range(4)]
        total = [None] * 3
        pressure = [None] * 3

        def add(axis, nu_up, nu_down):
            for c in range(3):
                flux = nu_up * (over[c] - here[c]) - nu_down * (here[c] - under[c])
                total[c] = flux if total[c] is None else total[c] + flux
            pressure[axis] = 0.5 * (over[3] - under[3])

        nu_up = viscosity([over[c] - here[c] for c in range(3)])
        nux_ref[x + 1] = nu_up
        add(0, nu_up, nux_ref[x])
        over = [jnp.where(row == rows - 1, 0.0, pltpu.roll(here[c], rows - 1, 0)) for c in range(4)]
        under = [jnp.where(row == 0, 0.0, pltpu.roll(here[c], 1, 0)) for c in range(4)]
        nu_up = viscosity([over[c] - here[c] for c in range(3)])
        nu_first = viscosity([here[c][:1] for c in range(3)])
        nuy_ref[x] = nu_up
        nuy0_ref[pl.ds(x, 1), :] = nu_first
        add(1, nu_up, jnp.where(row == 0, nu_first, pltpu.roll(nu_up, 1, 0)))
        rim = [edge_of(halo, c * planes + x) for c in range(4)]
        over = [jnp.where(lane == width - 1, rim[c], pltpu.roll(here[c], width - 1, 1)) for c in range(4)]
        under = [jnp.where(lane == 0, rim[c], pltpu.roll(here[c], 1, 1)) for c in range(4)]
        nu_up = viscosity([over[c] - here[c] for c in range(3)])
        nuz_ref[x] = nu_up
        add(2, nu_up, jnp.where(lane == 0, edge_of(rim_nu, x), pltpu.roll(nu_up, 1, 1)))
        for c in range(3):
            value = here[c] + time_step * (total[c] - pressure[c])
            next_ref[c, x] = value
        return carry

    pieces = out_sems.shape[0]
    step = planes // pieces

    def store(i):
        part = pl.ds(i * step, step)
        return pltpu.make_async_copy(next_ref.at[:, part], out_ref.at[:, part], out_sems.at[i])

    for i in range(pieces):
        lax.fori_loop(i * step, (i + 1) * step, plane, 0, unroll=True)
        store(i).start()

    taken_ref[...] = jnp.zeros_like(taken_ref)
    listed.wait()
    _, slot_lane = iotas(8, groups * extra)
    cell_of = jnp.full((8, groups * extra), -1, jnp.int32)
    odd = lax.axis_index("fluid") % 2
    for b in range(groups):
        part = (odd if b % 2 == 0 else 1 - odd) * chips + b // 2
        for k in range(cap):
            cell = list_ref[k, b]
            x, y = lax.div(cell, rows), lax.rem(cell, rows)
            first = part * extra + 3 * k
            for c in range(3):
                taken_ref[pl.ds(first + c, 1), :] = next_ref[c, x, pl.ds(y, 1), :]
            cell_of = jnp.where((slot_lane >= first) & (slot_lane < first + 3), cell, cell_of)
    cells_of_ref[...] = cell_of
    taken = taken_ref[...].astype(jnp.bfloat16).reshape((2,) + mine_ref.shape)
    mine_ref[...] = taken[0]
    lent_ref[...] = taken[1]
    for i in range(pieces):
        store(i).wait()


def pick_kernel(
    sizes, cells_of_ref, z0_ref, z1_ref, edges_ref, rim_ref, nuy_ref, nuz_ref, nuy0_ref,
    outside_ref, rims_ref, pick_ref, nuyd_ref, nuzd_ref,
):
    _, rows, width = edges_ref.shape
    groups, walls = sizes
    _, lines, slot_rows = pick_ref.shape
    planes = lines // rows
    extra = slot_rows // groups
    _, lane = iotas(rows, width)
    halo, second, beside = (
        mix_edges(*from_neighbours(lax.axis_index("wall"), walls, z0_ref[i], z1_ref[i]), lane, shift)
        for i, shift in enumerate((2, 4, 2))
    )
    inside = pltpu.roll(edges_ref[0], 1, 1)
    rim_nu = rim_ref[...]
    outside_ref[...] = outside_edges(walls, planes, halo, second, beside, inside, rim_nu)
    rims_ref[...] = time_step * (rim_nu + pltpu.roll(rim_nu, 2 * planes, 1) + pltpu.roll(rim_nu, 4 * planes, 1))
    line, slot_lane = iotas(lines, slot_rows)
    hit = line == cells_of_ref[0:1, :]
    part = (slot_lane % extra) % 3
    for c in range(3):
        pick_ref[c] = (hit & (part == c)).astype(jnp.float32).astype(jnp.bfloat16)
    row, _ = iotas(rows, width)
    for x in range(planes):
        nuyd_ref[x] = jnp.where(row == 0, nuy0_ref[x : x + 1, :], pltpu.roll(nuy_ref[x], 1, 0))
        nuzd_ref[x] = jnp.where(lane == 0, edge_of(rim_nu, x), pltpu.roll(nuz_ref[x], 1, 1))


def product_kernel(cap, block, masks, values_ref, before_ref, *refs):
    chips, extra, width = values_ref.shape
    recvs, out_ref = refs[:-1], refs[-1]
    depth = cap * width
    row, lane = iotas(extra, depth)
    own = row // 3 == lane // width
    here = lax.axis_index("fluid") // 2
    if before_ref.shape == out_ref.shape:
        out_ref[...] = before_ref[...]
    for m, recv_ref in zip(masks, recvs):
        source = here ^ m
        at = pl.ds(pl.multiple_of(source * extra, extra), extra)
        weights = recv_ref[block, pl.ds(0, depth), :]
        predicted = lax.dot_general(
            values_ref[source], weights, (((1,), (1,)), ((), ())), preferred_element_type=jnp.float32
        )
        seen = recv_ref[block, pl.ds(depth, extra), :].astype(jnp.float32)
        misfit = jnp.where(own, predicted - jnp.concatenate([seen] * cap, axis=1), 0.0).astype(jnp.bfloat16)
        contrib = jnp.dot(misfit, weights, preferred_element_type=jnp.float32)
        high = contrib.astype(jnp.bfloat16)
        out_ref[0, at, :] = high
        out_ref[1, at, :] = (contrib - high.astype(jnp.float32)).astype(jnp.bfloat16)


def shares(mine_ref, other_ref):
    return jnp.concatenate([ref[part] for part in range(2) for ref in (mine_ref, other_ref)], axis=0)


def forcing_rows(c, part, pick_ref, rows):
    pick = pick_ref[c, part, :]
    return jnp.dot(jnp.concatenate([pick, pick], axis=1), rows, preferred_element_type=jnp.float32)


def ends_kernel(mine_ref, other_ref, pick_ref, first_ref, second_ref):
    _, rows, _ = first_ref.shape
    lines = pick_ref.shape[1]
    even = lax.axis_index("fluid") % 2 == 0
    both = shares(mine_ref, other_ref)
    for c in range(3):
        low = forcing_rows(c, slice(0, rows), pick_ref, both)
        high = forcing_rows(c, slice(lines - rows, lines), pick_ref, both)
        first_ref[c] = jnp.where(even, high, low).astype(jnp.bfloat16)
        second_ref[c] = jnp.where(even, low, high).astype(jnp.bfloat16)


def forcing_kernel(mine_ref, other_ref, pick_ref, after_ref, forcing_ref):
    both = shares(mine_ref, other_ref)
    for c in range(3):
        forcing_ref[c] = forcing_rows(c, slice(None), pick_ref, both).reshape(forcing_ref.shape[1:])


FOLD = 16


def region_rows(values, ids, tops):
    def folded(plane):
        return jnp.concatenate([plane[y : y + FOLD] for y in range(0, plane.shape[0], FOLD)], axis=1)

    values, ids = folded(values), folded(ids)
    top, low = (ids // 8).astype(jnp.float32).astype(jnp.bfloat16), (ids % 8).astype(jnp.float32).astype(jnp.bfloat16)
    main = values.astype(jnp.bfloat16)
    rest = (values - main.astype(jnp.float32)).astype(jnp.bfloat16)
    zero = jnp.zeros_like(main)
    one = jnp.ones_like(main)
    hits = [top == jnp.bfloat16(h) for h in range(tops)]
    return (
        jnp.concatenate([jnp.where(hit, main, zero) for hit in hits], axis=0),
        jnp.concatenate([jnp.where(hit, rest, zero) for hit in hits], axis=0),
        jnp.concatenate([jnp.where(low == jnp.bfloat16(l), one, zero) for l in range(8)], axis=0),
    )


def region_sums(main, rest, ones):
    over_lanes = (((1,), (1,)), ((), ()))
    total = lax.dot_general(main, ones, over_lanes, preferred_element_type=jnp.float32)
    total += lax.dot_general(rest, ones, over_lanes, preferred_element_type=jnp.float32)
    row, column = iotas(*total.shape)
    total = jnp.where(row % FOLD == column % FOLD, total, 0.0)
    return jnp.sum(total.reshape(total.shape[0] // FOLD, FOLD, total.shape[1]), axis=1)


def inner_kernel(
    forcing_ref, next_ref, nux_ref, nuy_ref, nuyd_ref, nuz_ref, nuzd_ref, rim_ref, regions_ref, outside_ref,
    adjoint_ref, fpack_ref, sums_ref, main_ref, rest_ref, ones_ref,
):
    _, planes, rows, width = forcing_ref.shape
    row, lane = iotas(rows, width)
    rim_nu = rim_ref[...]
    tops = sums_ref.shape[0]

    def add_up(x, values, ids):
        span = rows // FOLD * width
        at = pl.ds(pl.multiple_of(x * span, span), span)
        for part_ref, part in zip((main_ref, rest_ref, ones_ref), region_rows(values, ids, tops)):
            part_ref[:, at] = part

    def plane(x, fpack):
        nus = (nux_ref[x + 1], nux_ref[x], nuy_ref[x], nuyd_ref[x], nuz_ref[x], nuzd_ref[x])
        next_up, next_down = jnp.minimum(x + 1, planes - 1), jnp.maximum(x - 1, 0)
        at_top, at_bottom = x == planes - 1, x == 0
        product = None
        for c in range(3):
            here = forcing_ref[c, x]
            over = jnp.where(at_top, 0.0, forcing_ref[c, next_up])
            under = jnp.where(at_bottom, 0.0, forcing_ref[c, next_down])
            total = nus[0] * (over - here) - nus[1] * (here - under)
            over = jnp.where(row == rows - 1, 0.0, pltpu.roll(here, rows - 1, 0))
            under = jnp.where(row == 0, 0.0, pltpu.roll(here, 1, 0))
            total += nus[2] * (over - here) - nus[3] * (here - under)
            over = jnp.where(lane == width - 1, 0.0, pltpu.roll(here, width - 1, 1))
            under = jnp.where(lane == 0, 0.0, pltpu.roll(here, 1, 1))
            total += nus[4] * (over - here) - nus[5] * (here - under)
            value = here + time_step * total
            adjoint_ref[c, x] = value
            part = value * next_ref[c, x]
            product = part if product is None else product + part
            fpack = pack_edges(fpack, here, c * planes + x, lane)
        add_up(x, product, regions_ref[x])
        return fpack

    fpack = lax.fori_loop(0, planes, plane, jnp.zeros((rows, width), jnp.float32), unroll=4)
    fpack_ref[...] = fpack
    mixed = outside_ref[...]
    reach = pltpu.roll(fpack, 1, 1) * mixed
    reach = reach + pltpu.roll(reach, width - 2 * planes, 1) + pltpu.roll(reach, width - 4 * planes, 1)
    reach = time_step * reach * rim_nu
    add_up(planes, reach, pltpu.roll(mixed, (width - 6 * planes) % width, 1).astype(jnp.int32))
    sums_ref[...] = region_sums(main_ref[...], rest_ref[...], ones_ref[...])


def edge_kernel(groups, masks, x0_ref, x1_ref, nux_ref, next_ref, regions_ref, sums_ref, fpack_ref, *outs):
    _, planes, rows, width = next_ref.shape
    tops, columns = sums_ref.shape
    low, high = 0.0, 0.0
    for c in range(3):
        below, above = beside_of(c, groups, x0_ref, x1_ref)
        low += below * next_ref[c, 0]
        high += above * next_ref[c, planes - 1]
    ends = [
        region_rows(time_step * nux_ref[0] * low, regions_ref[0], tops),
        region_rows(time_step * nux_ref[planes] * high, regions_ref[planes - 1], tops),
    ]
    total = sums_ref[...] + region_sums(*(jnp.concatenate(both, axis=1) for both in zip(*ends)))
    height = tops * (columns // width)
    for mask, out_ref in zip((0,) + masks, outs):
        for i in range(columns // width):
            out_ref[i * tops : (i + 1) * tops, :] = total[:, i * width : (i + 1) * width]
        if mask:
            out_ref[height : height + rows, :] = fpack_ref[...]
            if out_ref.shape[0] > height + rows:
                out_ref[height + rows :, :] = jnp.zeros((out_ref.shape[0] - height - rows, width), jnp.float32)


def beside_of(c, groups, x0_ref, x1_ref):
    return from_neighbours(
        lax.axis_index("fluid"), groups, x0_ref[c].astype(jnp.float32), x1_ref[c].astype(jnp.float32)
    )


def final_kernel(sizes, inner_ref, x0_ref, x1_ref, nux_ref, rims_ref, own_ref, *refs):
    groups, walls = sizes
    arrived, (adjoint_ref, sens_ref, value_ref, owned_ref, sems, owned_sem) = refs[:-6], refs[-6:]
    _, planes, rows, width = inner_ref.shape
    per = own_ref.shape[0]
    _, lane = iotas(rows, width)
    me = lax.axis_index("wall")
    total = own_ref[...]
    below = jnp.zeros((rows, width), jnp.float32)
    above = jnp.zeros((rows, width), jnp.float32)
    for mask, ref in zip(range(1, walls), arrived):
        total = total + ref[:per, :]
        if mask & (mask + 1) == 0:
            edges = ref[per : per + rows, :]
            above = jnp.where((me ^ mask) == me + 1, edges, above)
            below = jnp.where((me ^ mask) == me - 1, edges, below)
    mixed = mix_edges(below, above, lane)
    edge_flux = mixed * rims_ref[...]
    on_edge = (lane == 0) | (lane == width - 1)

    beside = [beside_of(c, groups, x0_ref, x1_ref) for c in range(3)]
    step = planes // sems.shape[0]

    def store(i):
        part = pl.ds(i * step, step)
        return pltpu.make_async_copy(value_ref.at[:, part], adjoint_ref.at[:, part], sems.at[i])

    for i in range(sems.shape[0]):
        for x in range(i * step, (i + 1) * step):
            for c in range(3):
                value = inner_ref[c, x] + jnp.where(on_edge, edge_of(edge_flux, c * planes + x), 0.0)
                if x == 0:
                    value += time_step * nux_ref[0] * beside[c][0]
                if x == planes - 1:
                    value += time_step * nux_ref[planes] * beside[c][1]
                value_ref[c, x] = value
        store(i).start()
    parts = width // FOLD
    tops = REG_DEV * walls // 8
    owned = REG_DEV // 8
    top, _ = iotas(tops, width)
    region, lane = iotas(REG_DEV, width)
    sens = jnp.zeros((8, REG_DEV), jnp.float32)
    for i in range(8 // parts):
        for h in range(owned):
            mine = jnp.where(top == me * owned + h, total[i * tops : (i + 1) * tops], 0.0)
            gather = (region == h * 8 + i * parts + lane // FOLD).astype(jnp.float32)
            sens += lax.dot_general(
                jnp.broadcast_to(jnp.sum(mine, axis=0, keepdims=True), (8, width)), gather, (((1,), (1,)), ((), ())),
                precision=lax.Precision.HIGHEST, preferred_element_type=jnp.float32,
            )
    owned_ref[...] = sens_scale * sens[:1]
    owned_copy = pltpu.make_async_copy(owned_ref, sens_ref, owned_sem)
    owned_copy.start()
    for i in range(sems.shape[0]):
        store(i).wait()
    owned_copy.wait()


def body(flow_state, regions, obs_tiles, measured, tile_dest, cell_list):
    groups, walls = lax.axis_size("fluid"), lax.axis_size("wall")
    sizes = (groups, walls)
    _, planes, rows, width = flow_state.shape
    count_tiles = obs_tiles.shape[2]
    cap = cell_list.shape[3]
    extra = -(-cap * 3 // 16) * 16
    reg_count = REG_DEV * walls
    cells = groups * cap
    grid = planes * rows * width

    chips = groups // 2
    height = cap * width + extra
    *sends, xs0, xs1 = call(
        functools.partial(group_kernel, cap),
        (bf16(2, height, width),) * chips + (f32(4, rows, width),) * 2,
        [HBM] * 4,
        tuple(
            pltpu.with_memory_space_constraint(operand, pltpu.HBM)
            for operand in (tile_dest[0, 0], obs_tiles[0, 0], jnp.transpose(measured[0, 0], (1, 0, 2)), flow_state)
        ),
        (
            pltpu.SMEM((count_tiles,), jnp.int32),
            pltpu.VMEM((count_tiles, width, width), jnp.bfloat16),
            pltpu.VMEM((3, count_tiles, width), jnp.bfloat16),
            pltpu.SMEM((groups,), jnp.int32),
            pltpu.SMEM((cells,), jnp.int32),
            pltpu.VMEM((groups * extra, width), jnp.bfloat16),
            pltpu.SemaphoreType.DMA,
            pltpu.SemaphoreType.DMA,
            pltpu.SemaphoreType.DMA((4,)),
            pltpu.SemaphoreType.DMA((8,)),
        ),
        out_specs=(VMEM,) * (chips + 2),
    )
    x0, x1 = swap(xs0, "fluid", 0), swap(xs1, "fluid", 1)
    recvs = [sends[0]] + [cross(sends[m], "fluid", 2 * m) for m in range(1, chips)]
    zs = call(
        functools.partial(edges_kernel, groups),
        f32(3, rows, width),
        [VMEM] * 4,
        (flow_state, regions, x0, x1),
        flops=HIDES,
    )
    z0, z1 = swap(zs, "wall", 0), swap(zs, "wall", 1)
    slot_rows = groups * extra
    velocity_next, velocity, nux, nuy, nuz, nuy0, rim, mine, lent, cells_of = call(
        functools.partial(forward_kernel, sizes, cap),
        (f32(3, planes, rows, width),) * 2
        + (f32(planes + 1, rows, width), f32(planes, rows, width), f32(planes, rows, width))
        + (f32(planes, width), f32(rows, width))
        + (bf16(chips, extra, width),) * 2
        + (jax.ShapeDtypeStruct((8, slot_rows), jnp.int32),),
        [ANY] + [VMEM] * 6,
        (cell_list[0, 0].T, flow_state, x0, x1, z0, z1, zs),
        (
            pltpu.SMEM((cap, groups), jnp.int32),
            pltpu.VMEM((4, planes + 2, rows, width), jnp.float32),
            pltpu.VMEM((slot_rows, width), jnp.float32),
            pltpu.SemaphoreType.DMA,
            pltpu.SemaphoreType.DMA((4,)),
        ),
        out_specs=(HBM,) + (VMEM,) * 9,
    )
    borrowed = cross(lent, "fluid", 1)
    outside, rims, pick, nuyd, nuzd = call(
        functools.partial(pick_kernel, sizes),
        (f32(rows, width), f32(rows, width), bf16(3, planes * rows, slot_rows)) + (f32(planes, rows, width),) * 2,
        [VMEM] * 8,
        (cells_of, z0, z1, zs, rim, nuy, nuz, nuy0),
    )

    def products(block, masks, values, before):
        whole = (2, chips * extra, width)
        return call(
            functools.partial(product_kernel, cap, block, masks),
            bf16(*whole),
            [VMEM, VMEM if before.shape == whole else ANY] + [VMEM] * len(masks),
            (values, before, *(recvs[m] for m in masks)),
        )

    given = products(1, tuple(range(chips // 2)), borrowed, pick)
    given = products(1, tuple(range(chips // 2, chips)), borrowed, given)
    other = cross(given, "fluid", 1)
    held = products(0, tuple(range(chips)), mine, outside)
    fs0, fs1 = call(ends_kernel, (bf16(3, rows, width),) * 2, [VMEM] * 3, (held, other, pick))
    f0, f1 = swap(fs0, "fluid", 0), swap(fs1, "fluid", 1)
    forcing = call(forcing_kernel, f32(3, planes, rows, width), [VMEM] * 3 + [ANY], (held, other, pick, fs1))
    tops = reg_count // 8
    columns = 8 * FOLD
    span = (planes + 1) * rows // FOLD * width
    sum_rows = tops * (columns // width)
    inner, fpack, sums = call(
        inner_kernel,
        (f32(3, planes, rows, width), f32(rows, width), f32(tops, columns)),
        [VMEM] * 10,
        (forcing, velocity, nux, nuy, nuyd, nuz, nuzd, rim, regions, outside),
        (
            pltpu.VMEM((tops * FOLD, span), jnp.bfloat16),
            pltpu.VMEM((tops * FOLD, span), jnp.bfloat16),
            pltpu.VMEM((columns, span), jnp.bfloat16),
        ),
    )
    masks = tuple(range(1, walls))
    heights = [sum_rows] + [sum_rows + rows + 8 * (mask - 1) for mask in masks]
    own, *parts = call(
        functools.partial(edge_kernel, groups, masks),
        tuple(f32(height, width) for height in heights),
        [VMEM] * 7,
        (f0, f1, nux, velocity, regions, sums, fpack),
    )
    arrived = [cross(part, "wall", mask) for part, mask in zip(parts, masks)]
    adjoint, sens = call(
        functools.partial(final_kernel, sizes),
        (f32(3, planes, rows, width), f32(1, REG_DEV)),
        [VMEM] * (6 + len(arrived)),
        (inner, f0, f1, nux, rims, own, *arrived),
        (
            pltpu.VMEM((3, planes, rows, width), jnp.float32),
            pltpu.VMEM((1, REG_DEV), jnp.float32),
            pltpu.SemaphoreType.DMA((4,)),
            pltpu.SemaphoreType.DMA,
        ),
        out_specs=(HBM, HBM),
        flops=10 * grid,
        moved=24 * grid,
    )
    return velocity_next, adjoint, sens.reshape(REG_DEV)


def solution(mesh):
    in_specs = (
        P(None, "fluid", None, "wall"),
        P("fluid", None, "wall"),
        P("fluid", "wall", None, None, None),
        P("fluid", "wall", None, None, None),
        P("fluid", "wall", None),
        P("fluid", "wall", None, None),
    )
    out_specs = (
        P(None, "fluid", None, "wall"),
        P(None, "fluid", None, "wall"),
        P(("fluid", "wall")),
    )
    return jax.shard_map(body, mesh=mesh, in_specs=in_specs, out_specs=out_specs, check_vma=False)
```

```python
import functools

import jax
import jax.numpy as jnp
from jax import lax
from jax.experimental import pallas as pl
from jax.experimental.pallas import tpu as pltpu
from jax.sharding import PartitionSpec as P

REG_DEV = 16

time_step = 0.12
nu_floor = 0.1
nu_spread = 0.9
relax_sq = 4.0
sens_scale = 0.03

VMEM = pl.BlockSpec(memory_space=pltpu.VMEM)
SMEM = pl.BlockSpec(memory_space=pltpu.SMEM)
ANY = pl.BlockSpec(memory_space=pl.ANY)
HBM = pl.BlockSpec(memory_space=pltpu.HBM)
LIMIT = 24 * 1024 * 1024
HIDES = 100_000_000_000


def call(kernel, outs, ins, operands, scratch=(), flops=1, moved=1, out_specs=None, limit=LIMIT):
    return pl.pallas_call(
        kernel,
        out_shape=outs,
        in_specs=ins,
        out_specs=out_specs if out_specs is not None else jax.tree.map(lambda _: VMEM, outs),
        scratch_shapes=list(scratch),
        compiler_params=pltpu.CompilerParams(vmem_limit_bytes=limit),
        cost_estimate=pl.CostEstimate(flops=flops, bytes_accessed=moved, transcendentals=0),
    )(*operands)


def f32(*shape):
    return jax.ShapeDtypeStruct(shape, jnp.float32)


def bf16(*shape):
    return jax.ShapeDtypeStruct(shape, jnp.bfloat16)


def swap(block, axis, turn):
    groups, walls = lax.axis_size("fluid"), lax.axis_size("wall")

    def partner(f, w):
        at, count = (f, groups) if axis == "fluid" else (w, walls)
        other = at + 1 if (at + turn) % 2 == 0 else at - 1
        if axis == "fluid":
            return (other, w) if 0 <= other < count else (f, w ^ 1)
        return (f, other) if 0 <= other < count else (f ^ 1, w)

    pairs = []
    for f in range(groups):
        for w in range(walls):
            to_f, to_w = partner(f, w)
            pairs.append((f * walls + w, to_f * walls + to_w))
    return lax.ppermute(block, ("fluid", "wall"), pairs)


def cross(block, axis, mask):
    return lax.ppermute(block, axis, [(i, i ^ mask) for i in range(lax.axis_size(axis))])


def from_neighbours(index, count, first, second):
    even = index % 2 == 0
    above = jnp.where(even, first, second)
    below = jnp.where(even, second, first)
    above = jnp.where(index == count - 1, jnp.zeros_like(above), above)
    below = jnp.where(index == 0, jnp.zeros_like(below), below)
    return below, above


def pack_edges(packed, plane, m, lane):
    width = lane.shape[1]
    here = (lane == 2 * m) | (lane == (2 * m + width - 1) % width)
    return jnp.where(here, pltpu.roll(plane, 2 * m, 1), packed)


def mix_edges(below, above, lane, shift=2):
    return jnp.where(lane % 2 == 0, above, pltpu.roll(below, shift, 1))


def edge_of(mixed, m):
    width = mixed.shape[1]
    return pltpu.roll(mixed, (2 * width - (2 * m + 1)) % width, 1)


def viscosity(jumps):
    shear_sq = jumps[0] * jumps[0] + jumps[1] * jumps[1] + jumps[2] * jumps[2]
    root = lax.rsqrt(1.0 + relax_sq * shear_sq)
    return nu_floor + nu_spread * (root * lax.rsqrt(root))


def iotas(rows, width):
    shape = (rows, width)
    return lax.broadcasted_iota(jnp.int32, shape, 0), lax.broadcasted_iota(jnp.int32, shape, 1)


def faces_kernel(flow_ref, first_ref, second_ref, sems):
    last = flow_ref.shape[1] - 1
    odd = lax.axis_index("fluid") % 2
    copies = [
        pltpu.make_async_copy(flow_ref.at[c, plane], out_ref.at[c], sems.at[i, c])
        for i, (plane, out_ref) in enumerate(((last - last * odd, first_ref), (last * odd, second_ref)))
        for c in range(flow_ref.shape[0])
    ]
    for copy in copies:
        copy.start()
    for copy in copies:
        copy.wait()


def edges_kernel(groups, flow_ref, regions_ref, x0_ref, x1_ref, edges_ref):
    fields, planes, rows, width = flow_ref.shape
    _, lane = iotas(rows, width)
    outer = jnp.zeros((rows, width), jnp.float32)
    second, beside = outer, outer
    for c in range(fields):
        for x in range(planes):
            m, plane = c * planes + x, flow_ref[c, x]
            outer = pack_edges(outer, plane, m, lane)
            here = (lane == 2 * m) | (lane == (2 * m - 3) % width)
            second = jnp.where(here, pltpu.roll(plane, (2 * m - 1) % width, 1), second)
        for side, plane in enumerate(from_neighbours(lax.axis_index("fluid"), groups, x0_ref[c], x1_ref[c])):
            beside = pack_edges(beside, plane, 2 * c + side, lane)
    for x in range(planes):
        beside = pack_edges(beside, regions_ref[x].astype(jnp.float32), 2 * fields + x, lane)
    edges_ref[0], edges_ref[1], edges_ref[2] = outer, second, beside


def outside_edges(walls, planes, halo, second, beside, inside, rim_nu):
    rows, width = halo.shape
    row, lane = iotas(rows, width)
    x, field = (lane // 2) % planes, (lane // 2) // planes

    def spread(nu):
        nu = jnp.where(field == 0, nu, 0.0)
        return nu + pltpu.roll(nu, 2 * planes, 1) + pltpu.roll(nu, 4 * planes, 1)

    def nu_of(jump):
        return spread(viscosity([jump] + [pltpu.roll(jump, width - 2 * c * planes, 1) for c in (1, 2)]))

    over_x, under_x = pltpu.roll(halo, width - 2, 1), pltpu.roll(halo, 2, 1)
    for c in range(4):
        low = pltpu.roll(beside, (2 * c * planes - 4 * c) % width, 1)
        high = pltpu.roll(beside, (2 * (c * planes + planes - 1) - 4 * c - 2) % width, 1)
        under_x = jnp.where((x == 0) & (field == c), low, under_x)
        over_x = jnp.where((x == planes - 1) & (field == c), high, over_x)
    over_y = jnp.where(row == rows - 1, 0.0, pltpu.roll(halo, rows - 1, 0))
    under_y = jnp.where(row == 0, 0.0, pltpu.roll(halo, 1, 0))
    total = spread(rim_nu) * (inside - halo)
    for other in (over_x, under_x, over_y, under_y, second):
        total += nu_of(other - halo) * (other - halo)
    above = lane % 2 == 0
    gradient_x = pltpu.roll(0.5 * (over_x - under_x), width - 6 * planes, 1)
    gradient_y = pltpu.roll(0.5 * (over_y - under_y), width - 4 * planes, 1)
    gradient_z = pltpu.roll(0.5 * jnp.where(above, second - inside, inside - second), width - 2 * planes, 1)
    gradient = jnp.where(field == 0, gradient_x, jnp.where(field == 1, gradient_y, gradient_z))
    value = halo + time_step * (total - gradient)
    value = jnp.where(field == 3, pltpu.roll(beside, 6 * planes - 16, 1), value)
    me = lax.axis_index("wall")
    exists = jnp.where(above, jnp.where(me < walls - 1, 1, 0), jnp.where(me > 0, 1, 0)) == 1
    return jnp.where(exists & (field < 4), value, 0.0)


def group_kernel(cap, dest_ref, tiles_ref, meas_ref, flow_ref, *refs):
    chips = len(refs) - 12
    sends, halo_refs = refs[:chips], refs[chips : chips + 2]
    (list_ref, held_ref, seen_ref, count_ref, slot_ref, rows_ref,
     list_sem, seen_sem, in_sems, face_sems) = refs[chips + 2 :]
    count_tiles, width, _ = tiles_ref.shape
    groups = 2 * chips
    slots = groups * cap
    extra = rows_ref.shape[0] // groups
    depth = cap * width
    me = lax.axis_index("fluid")
    listed = pltpu.make_async_copy(dest_ref, list_ref, list_sem)
    listed.start()
    piece = count_tiles // in_sems.shape[0]

    def load(p):
        part = pl.ds(p * piece, piece)
        return pltpu.make_async_copy(tiles_ref.at[part], held_ref.at[part], in_sems.at[p])

    for p in range(in_sems.shape[0]):
        load(p).start()
    seen = pltpu.make_async_copy(meas_ref, seen_ref, seen_sem)
    seen.start()
    last = flow_ref.shape[1] - 1
    fields = flow_ref.shape[0]
    faces = [
        pltpu.make_async_copy(flow_ref.at[c, plane], halo_refs[i].at[c], face_sems.at[i * fields + c])
        for i, plane in enumerate((last * (1 - me % 2), last * (me % 2)))
        for c in range(fields)
    ]
    for face in faces:
        face.start()

    def clear(b, carry):
        count_ref[b] = 0
        for k in range(cap):
            slot_ref[b * cap + k] = -1
        return carry

    lax.fori_loop(0, groups, clear, 0)
    _, tile_lane = iotas(8, count_tiles)
    listed.wait()

    def place(t, slot_of):
        b = list_ref[t]
        k = count_ref[b]
        count_ref[b] = k + 1
        slot_ref[b * cap + k] = t
        return jnp.where(tile_lane == t, b * cap + k, slot_of)

    slot_of = lax.fori_loop(
        0, count_tiles, place, jnp.full((8, count_tiles), -1, jnp.int32), unroll=True
    )
    seen.wait()
    row = lax.broadcasted_iota(jnp.int32, (groups * extra, count_tiles), 0)
    within = row % extra
    row_slot = (row // extra) * cap + within // 3
    used = within < cap * 3
    total = jnp.zeros((groups * extra, width), jnp.float32)
    for c in range(3):
        pick = (row_slot == slot_of[0:1, :]) & used & (within % 3 == c)
        total += jnp.dot(
            pick.astype(jnp.float32).astype(jnp.bfloat16), seen_ref[c], preferred_element_type=jnp.float32
        )
    rows_ref[...] = total.astype(jnp.bfloat16)

    for p in range(in_sems.shape[0]):
        load(p).wait()

    for m in list(range(1, chips)) + [0]:
        for j in range(2):
            b = me ^ (2 * m + j)
            for k in range(cap):
                t = slot_ref[b * cap + k]
                at = (j, slice(k * width, (k + 1) * width))
                if slots > count_tiles:
                    sends[m][at] = jnp.where(t >= 0, held_ref[jnp.maximum(t, 0)], jnp.zeros((width, width), jnp.bfloat16))
                else:
                    sends[m][at] = held_ref[t]
    for m in range(chips):
        for j in range(2):
            b = me ^ (2 * m + j)
            sends[m][j, depth:, :] = rows_ref[pl.ds(pl.multiple_of(b * extra, extra), extra), :]
    for face in faces:
        face.wait()


def forward_kernel(
    sizes, cap, cells_ref, flow_ref, x0_ref, x1_ref, z0_ref, z1_ref, edges_ref,
    out_ref, next_ref, nux_ref, nuy_ref, nuz_ref, nuy0_ref, rim_ref, mine_ref, lent_ref, cells_of_ref,
    list_ref, padded_ref, taken_ref, list_sem, out_sems,
):
    _, planes, rows, width = flow_ref.shape
    groups, walls = sizes
    chips, extra, _ = mine_ref.shape
    listed = pltpu.make_async_copy(cells_ref, list_ref, list_sem)
    listed.start()
    row, lane = iotas(rows, width)
    halo = mix_edges(*from_neighbours(lax.axis_index("wall"), walls, z0_ref[0], z1_ref[0]), lane)
    inside = pltpu.roll(edges_ref[0], 1, 1)
    jump = halo - inside
    rim_nu = viscosity([jump] + [pltpu.roll(jump, width - 2 * c * planes, 1) for c in (1, 2)])
    rim_nu = jnp.where(lane < 2 * planes, rim_nu, 0.0)
    rim_ref[...] = rim_nu
    for c in range(4):
        low, high = from_neighbours(lax.axis_index("fluid"), groups, x0_ref[c], x1_ref[c])
        padded_ref[c, 0] = low
        padded_ref[c, planes + 1] = high
        padded_ref[c, 1 : planes + 1] = flow_ref[c]
    nux_ref[0] = viscosity([padded_ref[c, 1] - padded_ref[c, 0] for c in range(3)])

    def plane(x, carry):
        here = [padded_ref[c, x + 1] for c in range(4)]
        over = [padded_ref[c, x + 2] for c in range(4)]
        under = [padded_ref[c, x] for c in range(4)]
        total = [None] * 3
        pressure = [None] * 3

        def add(axis, nu_up, nu_down):
            for c in range(3):
                flux = nu_up * (over[c] - here[c]) - nu_down * (here[c] - under[c])
                total[c] = flux if total[c] is None else total[c] + flux
            pressure[axis] = 0.5 * (over[3] - under[3])

        nu_up = viscosity([over[c] - here[c] for c in range(3)])
        nux_ref[x + 1] = nu_up
        add(0, nu_up, nux_ref[x])
        over = [jnp.where(row == rows - 1, 0.0, pltpu.roll(here[c], rows - 1, 0)) for c in range(4)]
        under = [jnp.where(row == 0, 0.0, pltpu.roll(here[c], 1, 0)) for c in range(4)]
        nu_up = viscosity([over[c] - here[c] for c in range(3)])
        nu_first = viscosity([here[c][:1] for c in range(3)])
        nuy_ref[x] = nu_up
        nuy0_ref[pl.ds(x, 1), :] = nu_first
        add(1, nu_up, jnp.where(row == 0, nu_first, pltpu.roll(nu_up, 1, 0)))
        rim = [edge_of(halo, c * planes + x) for c in range(4)]
        over = [jnp.where(lane == width - 1, rim[c], pltpu.roll(here[c], width - 1, 1)) for c in range(4)]
        under = [jnp.where(lane == 0, rim[c], pltpu.roll(here[c], 1, 1)) for c in range(4)]
        nu_up = viscosity([over[c] - here[c] for c in range(3)])
        nuz_ref[x] = nu_up
        add(2, nu_up, jnp.where(lane == 0, edge_of(rim_nu, x), pltpu.roll(nu_up, 1, 1)))
        for c in range(3):
            value = here[c] + time_step * (total[c] - pressure[c])
            next_ref[c, x] = value
        return carry

    pieces = out_sems.shape[0]
    step = planes // pieces

    def store(i):
        part = pl.ds(i * step, step)
        return pltpu.make_async_copy(next_ref.at[:, part], out_ref.at[:, part], out_sems.at[i])

    for i in range(pieces):
        lax.fori_loop(i * step, (i + 1) * step, plane, 0, unroll=True)
        store(i).start()

    taken_ref[...] = jnp.zeros_like(taken_ref)
    listed.wait()
    _, slot_lane = iotas(8, groups * extra)
    cell_of = jnp.full((8, groups * extra), -1, jnp.int32)
    odd = lax.axis_index("fluid") % 2
    for b in range(groups):
        part = (odd if b % 2 == 0 else 1 - odd) * chips + b // 2
        for k in range(cap):
            cell = list_ref[k, b]
            x, y = lax.div(cell, rows), lax.rem(cell, rows)
            first = part * extra + 3 * k
            for c in range(3):
                taken_ref[pl.ds(first + c, 1), :] = next_ref[c, x, pl.ds(y, 1), :]
            cell_of = jnp.where((slot_lane >= first) & (slot_lane < first + 3), cell, cell_of)
    cells_of_ref[...] = cell_of
    taken = taken_ref[...].astype(jnp.bfloat16).reshape((2,) + mine_ref.shape)
    mine_ref[...] = taken[0]
    lent_ref[...] = taken[1]
    for i in range(pieces):
        store(i).wait()


def pick_kernel(
    sizes, cells_of_ref, z0_ref, z1_ref, edges_ref, rim_ref, nuy_ref, nuz_ref, nuy0_ref,
    outside_ref, rims_ref, pick_ref, nuyd_ref, nuzd_ref,
):
    _, rows, width = edges_ref.shape
    groups, walls = sizes
    _, lines, slot_rows = pick_ref.shape
    planes = lines // rows
    extra = slot_rows // groups
    _, lane = iotas(rows, width)
    halo, second, beside = (
        mix_edges(*from_neighbours(lax.axis_index("wall"), walls, z0_ref[i], z1_ref[i]), lane, shift)
        for i, shift in enumerate((2, 4, 2))
    )
    inside = pltpu.roll(edges_ref[0], 1, 1)
    rim_nu = rim_ref[...]
    outside_ref[...] = outside_edges(walls, planes, halo, second, beside, inside, rim_nu)
    rims_ref[...] = time_step * (rim_nu + pltpu.roll(rim_nu, 2 * planes, 1) + pltpu.roll(rim_nu, 4 * planes, 1))
    line, slot_lane = iotas(lines, slot_rows)
    hit = line == cells_of_ref[0:1, :]
    part = (slot_lane % extra) % 3
    for c in range(3):
        pick_ref[c] = (hit & (part == c)).astype(jnp.float32).astype(jnp.bfloat16)
    row, _ = iotas(rows, width)
    for x in range(planes):
        nuyd_ref[x] = jnp.where(row == 0, nuy0_ref[x : x + 1, :], pltpu.roll(nuy_ref[x], 1, 0))
        nuzd_ref[x] = jnp.where(lane == 0, edge_of(rim_nu, x), pltpu.roll(nuz_ref[x], 1, 1))


def product_kernel(cap, block, masks, more, values_ref, before_ref, *refs):
    chips, extra, width = values_ref.shape
    recvs, out_ref = refs[:-1], refs[-1]
    depth = cap * width
    row, lane = iotas(extra, depth)
    own = row // 3 == lane // width
    here = lax.axis_index("fluid") // 2
    if more:
        out_ref[...] = before_ref[...]
    for m, recv_ref in zip(masks, recvs):
        source = here ^ m
        at = pl.ds(pl.multiple_of(source * extra, extra), extra)
        weights = recv_ref[block, pl.ds(0, depth), :]
        predicted = lax.dot_general(
            values_ref[source], weights, (((1,), (1,)), ((), ())), preferred_element_type=jnp.float32
        )
        seen = recv_ref[block, pl.ds(depth, extra), :].astype(jnp.float32)
        misfit = jnp.where(own, predicted - jnp.concatenate([seen] * cap, axis=1), 0.0).astype(jnp.bfloat16)
        contrib = jnp.dot(misfit, weights, preferred_element_type=jnp.float32)
        high = contrib.astype(jnp.bfloat16)
        out_ref[0, at, :] = high
        out_ref[1, at, :] = (contrib - high.astype(jnp.float32)).astype(jnp.bfloat16)


def shares(mine_ref, other_ref):
    return jnp.concatenate([ref[part] for part in range(2) for ref in (mine_ref, other_ref)], axis=0)


def forcing_rows(c, part, pick_ref, rows):
    pick = pick_ref[c, part, :]
    return jnp.dot(jnp.concatenate([pick, pick], axis=1), rows, preferred_element_type=jnp.float32)


def ends_kernel(mine_ref, other_ref, pick_ref, first_ref, second_ref):
    _, rows, _ = first_ref.shape
    lines = pick_ref.shape[1]
    even = lax.axis_index("fluid") % 2 == 0
    both = shares(mine_ref, other_ref)
    for c in range(3):
        low = forcing_rows(c, slice(0, rows), pick_ref, both)
        high = forcing_rows(c, slice(lines - rows, lines), pick_ref, both)
        first_ref[c] = jnp.where(even, high, low).astype(jnp.bfloat16)
        second_ref[c] = jnp.where(even, low, high).astype(jnp.bfloat16)


def forcing_kernel(mine_ref, other_ref, pick_ref, after_ref, forcing_ref):
    both = shares(mine_ref, other_ref)
    for c in range(3):
        forcing_ref[c] = forcing_rows(c, slice(None), pick_ref, both).reshape(forcing_ref.shape[1:])


FOLD = 16


def region_rows(values, ids, tops):
    def folded(plane):
        return jnp.concatenate([plane[y : y + FOLD] for y in range(0, plane.shape[0], FOLD)], axis=1)

    values, ids = folded(values), folded(ids)
    top, low = (ids // 8).astype(jnp.float32).astype(jnp.bfloat16), (ids % 8).astype(jnp.float32).astype(jnp.bfloat16)
    main = values.astype(jnp.bfloat16)
    rest = (values - main.astype(jnp.float32)).astype(jnp.bfloat16)
    zero = jnp.zeros_like(main)
    one = jnp.ones_like(main)
    hits = [top == jnp.bfloat16(h) for h in range(tops)]
    return (
        jnp.concatenate([jnp.where(hit, main, zero) for hit in hits], axis=0),
        jnp.concatenate([jnp.where(hit, rest, zero) for hit in hits], axis=0),
        jnp.concatenate([jnp.where(low == jnp.bfloat16(l), one, zero) for l in range(8)], axis=0),
    )


def region_sums(main, rest, ones):
    over_lanes = (((1,), (1,)), ((), ()))
    total = lax.dot_general(main, ones, over_lanes, preferred_element_type=jnp.float32)
    total += lax.dot_general(rest, ones, over_lanes, preferred_element_type=jnp.float32)
    row, column = iotas(*total.shape)
    total = jnp.where(row % FOLD == column % FOLD, total, 0.0)
    return jnp.sum(total.reshape(total.shape[0] // FOLD, FOLD, total.shape[1]), axis=1)


def inner_kernel(
    forcing_ref, next_ref, nux_ref, nuy_ref, nuyd_ref, nuz_ref, nuzd_ref, rim_ref, regions_ref, outside_ref,
    adjoint_ref, fpack_ref, sums_ref, main_ref, rest_ref, ones_ref,
):
    _, planes, rows, width = forcing_ref.shape
    row, lane = iotas(rows, width)
    rim_nu = rim_ref[...]
    tops = sums_ref.shape[0]

    def add_up(x, values, ids):
        span = rows // FOLD * width
        at = pl.ds(pl.multiple_of(x * span, span), span)
        for part_ref, part in zip((main_ref, rest_ref, ones_ref), region_rows(values, ids, tops)):
            part_ref[:, at] = part

    def plane(x, fpack):
        nus = (nux_ref[x + 1], nux_ref[x], nuy_ref[x], nuyd_ref[x], nuz_ref[x], nuzd_ref[x])
        next_up, next_down = jnp.minimum(x + 1, planes - 1), jnp.maximum(x - 1, 0)
        at_top, at_bottom = x == planes - 1, x == 0
        product = None
        for c in range(3):
            here = forcing_ref[c, x]
            over = jnp.where(at_top, 0.0, forcing_ref[c, next_up])
            under = jnp.where(at_bottom, 0.0, forcing_ref[c, next_down])
            total = nus[0] * (over - here) - nus[1] * (here - under)
            over = jnp.where(row == rows - 1, 0.0, pltpu.roll(here, rows - 1, 0))
            under = jnp.where(row == 0, 0.0, pltpu.roll(here, 1, 0))
            total += nus[2] * (over - here) - nus[3] * (here - under)
            over = jnp.where(lane == width - 1, 0.0, pltpu.roll(here, width - 1, 1))
            under = jnp.where(lane == 0, 0.0, pltpu.roll(here, 1, 1))
            total += nus[4] * (over - here) - nus[5] * (here - under)
            value = here + time_step * total
            adjoint_ref[c, x] = value
            part = value * next_ref[c, x]
            product = part if product is None else product + part
            fpack = pack_edges(fpack, here, c * planes + x, lane)
        add_up(x, product, regions_ref[x])
        return fpack

    fpack = lax.fori_loop(0, planes, plane, jnp.zeros((rows, width), jnp.float32), unroll=4)
    fpack_ref[...] = fpack
    mixed = outside_ref[...]
    reach = pltpu.roll(fpack, 1, 1) * mixed
    reach = reach + pltpu.roll(reach, width - 2 * planes, 1) + pltpu.roll(reach, width - 4 * planes, 1)
    reach = time_step * reach * rim_nu
    add_up(planes, reach, pltpu.roll(mixed, (width - 6 * planes) % width, 1).astype(jnp.int32))
    sums_ref[...] = region_sums(main_ref[...], rest_ref[...], ones_ref[...])


def edge_kernel(groups, masks, x0_ref, x1_ref, nux_ref, next_ref, regions_ref, sums_ref, fpack_ref, *outs):
    _, planes, rows, width = next_ref.shape
    tops, columns = sums_ref.shape
    low, high = 0.0, 0.0
    for c in range(3):
        below, above = beside_of(c, groups, x0_ref, x1_ref)
        low += below * next_ref[c, 0]
        high += above * next_ref[c, planes - 1]
    ends = [
        region_rows(time_step * nux_ref[0] * low, regions_ref[0], tops),
        region_rows(time_step * nux_ref[planes] * high, regions_ref[planes - 1], tops),
    ]
    total = sums_ref[...] + region_sums(*(jnp.concatenate(both, axis=1) for both in zip(*ends)))
    height = tops * (columns // width)
    for mask, out_ref in zip((0,) + masks, outs):
        for i in range(columns // width):
            out_ref[i * tops : (i + 1) * tops, :] = total[:, i * width : (i + 1) * width]
        if mask:
            out_ref[height : height + rows, :] = fpack_ref[...]
            if out_ref.shape[0] > height + rows:
                out_ref[height + rows :, :] = jnp.zeros((out_ref.shape[0] - height - rows, width), jnp.float32)


def beside_of(c, groups, x0_ref, x1_ref):
    return from_neighbours(
        lax.axis_index("fluid"), groups, x0_ref[c].astype(jnp.float32), x1_ref[c].astype(jnp.float32)
    )


def final_kernel(sizes, inner_ref, x0_ref, x1_ref, nux_ref, rims_ref, own_ref, *refs):
    groups, walls = sizes
    arrived, (adjoint_ref, sens_ref, value_ref, owned_ref, sems, owned_sem) = refs[:-6], refs[-6:]
    _, planes, rows, width = inner_ref.shape
    per = own_ref.shape[0]
    _, lane = iotas(rows, width)
    me = lax.axis_index("wall")
    total = own_ref[...]
    below = jnp.zeros((rows, width), jnp.float32)
    above = jnp.zeros((rows, width), jnp.float32)
    for mask, ref in zip(range(1, walls), arrived):
        total = total + ref[:per, :]
        if mask & (mask + 1) == 0:
            edges = ref[per : per + rows, :]
            above = jnp.where((me ^ mask) == me + 1, edges, above)
            below = jnp.where((me ^ mask) == me - 1, edges, below)
    mixed = mix_edges(below, above, lane)
    edge_flux = mixed * rims_ref[...]
    on_edge = (lane == 0) | (lane == width - 1)

    beside = [beside_of(c, groups, x0_ref, x1_ref) for c in range(3)]
    step = planes // sems.shape[0]

    def store(i):
        part = pl.ds(i * step, step)
        return pltpu.make_async_copy(value_ref.at[:, part], adjoint_ref.at[:, part], sems.at[i])

    for i in range(sems.shape[0]):
        for x in range(i * step, (i + 1) * step):
            for c in range(3):
                value = inner_ref[c, x] + jnp.where(on_edge, edge_of(edge_flux, c * planes + x), 0.0)
                if x == 0:
                    value += time_step * nux_ref[0] * beside[c][0]
                if x == planes - 1:
                    value += time_step * nux_ref[planes] * beside[c][1]
                value_ref[c, x] = value
        store(i).start()
    parts = width // FOLD
    tops = REG_DEV * walls // 8
    owned = REG_DEV // 8
    top, _ = iotas(tops, width)
    region, lane = iotas(REG_DEV, width)
    sens = jnp.zeros((8, REG_DEV), jnp.float32)
    for i in range(8 // parts):
        for h in range(owned):
            mine = jnp.where(top == me * owned + h, total[i * tops : (i + 1) * tops], 0.0)
            gather = (region == h * 8 + i * parts + lane // FOLD).astype(jnp.float32)
            sens += lax.dot_general(
                jnp.broadcast_to(jnp.sum(mine, axis=0, keepdims=True), (8, width)), gather, (((1,), (1,)), ((), ())),
                precision=lax.Precision.HIGHEST, preferred_element_type=jnp.float32,
            )
    owned_ref[...] = sens_scale * sens[:1]
    owned_copy = pltpu.make_async_copy(owned_ref, sens_ref, owned_sem)
    owned_copy.start()
    for i in range(sems.shape[0]):
        store(i).wait()
    owned_copy.wait()


def body(flow_state, regions, obs_tiles, measured, tile_dest, cell_list):
    groups, walls = lax.axis_size("fluid"), lax.axis_size("wall")
    sizes = (groups, walls)
    _, planes, rows, width = flow_state.shape
    count_tiles = obs_tiles.shape[2]
    cap = cell_list.shape[3]
    extra = -(-cap * 3 // 16) * 16
    reg_count = REG_DEV * walls
    cells = groups * cap
    grid = planes * rows * width

    chips = groups // 2
    height = cap * width + extra
    *sends, xs0, xs1 = call(
        functools.partial(group_kernel, cap),
        (bf16(2, height, width),) * chips + (f32(4, rows, width),) * 2,
        [HBM] * 4,
        tuple(
            pltpu.with_memory_space_constraint(operand, pltpu.HBM)
            for operand in (tile_dest[0, 0], obs_tiles[0, 0], jnp.transpose(measured[0, 0], (1, 0, 2)), flow_state)
        ),
        (
            pltpu.SMEM((count_tiles,), jnp.int32),
            pltpu.VMEM((count_tiles, width, width), jnp.bfloat16),
            pltpu.VMEM((3, count_tiles, width), jnp.bfloat16),
            pltpu.SMEM((groups,), jnp.int32),
            pltpu.SMEM((cells,), jnp.int32),
            pltpu.VMEM((groups * extra, width), jnp.bfloat16),
            pltpu.SemaphoreType.DMA,
            pltpu.SemaphoreType.DMA,
            pltpu.SemaphoreType.DMA((4,)),
            pltpu.SemaphoreType.DMA((8,)),
        ),
        out_specs=(VMEM,) * (chips + 2),
    )
    x0, x1 = swap(xs0, "fluid", 0), swap(xs1, "fluid", 1)
    recvs = [sends[0]] + [cross(sends[m], "fluid", 2 * m) for m in range(1, chips)]
    zs = call(
        functools.partial(edges_kernel, groups),
        f32(3, rows, width),
        [VMEM] * 4,
        (flow_state, regions, x0, x1),
        flops=HIDES,
    )
    z0, z1 = swap(zs, "wall", 0), swap(zs, "wall", 1)
    slot_rows = groups * extra
    velocity_next, velocity, nux, nuy, nuz, nuy0, rim, mine, lent, cells_of = call(
        functools.partial(forward_kernel, sizes, cap),
        (f32(3, planes, rows, width),) * 2
        + (f32(planes + 1, rows, width), f32(planes, rows, width), f32(planes, rows, width))
        + (f32(planes, width), f32(rows, width))
        + (bf16(chips, extra, width),) * 2
        + (jax.ShapeDtypeStruct((8, slot_rows), jnp.int32),),
        [ANY] + [VMEM] * 6,
        (cell_list[0, 0].T, flow_state, x0, x1, z0, z1, zs),
        (
            pltpu.SMEM((cap, groups), jnp.int32),
            pltpu.VMEM((4, planes + 2, rows, width), jnp.float32),
            pltpu.VMEM((slot_rows, width), jnp.float32),
            pltpu.SemaphoreType.DMA,
            pltpu.SemaphoreType.DMA((4,)),
        ),
        out_specs=(HBM,) + (VMEM,) * 9,
    )
    borrowed = cross(lent, "fluid", 1)
    outside, rims, pick, nuyd, nuzd = call(
        functools.partial(pick_kernel, sizes),
        (f32(rows, width), f32(rows, width), bf16(3, planes * rows, slot_rows)) + (f32(planes, rows, width),) * 2,
        [VMEM] * 8,
        (cells_of, z0, z1, zs, rim, nuy, nuz, nuy0),
    )

    def products(block, masks, values, before, more=False):
        whole = (2, chips * extra, width)
        return call(
            functools.partial(product_kernel, cap, block, masks, more),
            bf16(*whole),
            [VMEM, VMEM if more else ANY] + [VMEM] * len(masks),
            (values, before, *(recvs[m] for m in masks)),
        )

    held = products(0, tuple(range(chips // 2)), mine, pick)
    given = products(1, tuple(range(chips // 2)), borrowed, held)
    given = products(1, tuple(range(chips // 2, chips)), borrowed, given, True)
    other = cross(given, "fluid", 1)
    held = products(0, tuple(range(chips // 2, chips)), mine, held, True)
    fs0, fs1 = call(ends_kernel, (bf16(3, rows, width),) * 2, [VMEM] * 3, (held, other, pick))
    f0, f1 = swap(fs0, "fluid", 0), swap(fs1, "fluid", 1)
    forcing = call(forcing_kernel, f32(3, planes, rows, width), [VMEM] * 3 + [ANY], (held, other, pick, fs1))
    tops = reg_count // 8
    columns = 8 * FOLD
    span = (planes + 1) * rows // FOLD * width
    sum_rows = tops * (columns // width)
    inner, fpack, sums = call(
        inner_kernel,
        (f32(3, planes, rows, width), f32(rows, width), f32(tops, columns)),
        [VMEM] * 10,
        (forcing, velocity, nux, nuy, nuyd, nuz, nuzd, rim, regions, outside),
        (
            pltpu.VMEM((tops * FOLD, span), jnp.bfloat16),
            pltpu.VMEM((tops * FOLD, span), jnp.bfloat16),
            pltpu.VMEM((columns, span), jnp.bfloat16),
        ),
    )
    masks = tuple(range(1, walls))
    heights = [sum_rows] + [sum_rows + rows + 8 * (mask - 1) for mask in masks]
    own, *parts = call(
        functools.partial(edge_kernel, groups, masks),
        tuple(f32(height, width) for height in heights),
        [VMEM] * 7,
        (f0, f1, nux, velocity, regions, sums, fpack),
    )
    arrived = [cross(part, "wall", mask) for part, mask in zip(parts, masks)]
    adjoint, sens = call(
        functools.partial(final_kernel, sizes),
        (f32(3, planes, rows, width), f32(1, REG_DEV)),
        [VMEM] * (6 + len(arrived)),
        (inner, f0, f1, nux, rims, own, *arrived),
        (
            pltpu.VMEM((3, planes, rows, width), jnp.float32),
            pltpu.VMEM((1, REG_DEV), jnp.float32),
            pltpu.SemaphoreType.DMA((4,)),
            pltpu.SemaphoreType.DMA,
        ),
        out_specs=(HBM, HBM),
        flops=10 * grid,
        moved=24 * grid,
    )
    return velocity_next, adjoint, sens.reshape(REG_DEV)


def solution(mesh):
    in_specs = (
        P(None, "fluid", None, "wall"),
        P("fluid", None, "wall"),
        P("fluid", "wall", None, None, None),
        P("fluid", "wall", None, None, None),
        P("fluid", "wall", None),
        P("fluid", "wall", None, None),
    )
    out_specs = (
        P(None, "fluid", None, "wall"),
        P(None, "fluid", None, "wall"),
        P(("fluid", "wall")),
    )
    return jax.shard_map(body, mesh=mesh, in_specs=in_specs, out_specs=out_specs, check_vma=False)
```

```python
import functools

import jax
import jax.numpy as jnp
from jax import lax
from jax.experimental import pallas as pl
from jax.experimental.pallas import tpu as pltpu
from jax.sharding import PartitionSpec as P

REG_DEV = 16

time_step = 0.12
nu_floor = 0.1
nu_spread = 0.9
relax_sq = 4.0
sens_scale = 0.03

VMEM = pl.BlockSpec(memory_space=pltpu.VMEM)
SMEM = pl.BlockSpec(memory_space=pltpu.SMEM)
ANY = pl.BlockSpec(memory_space=pl.ANY)
HBM = pl.BlockSpec(memory_space=pltpu.HBM)
LIMIT = 24 * 1024 * 1024
HIDES = 100_000_000_000


def call(kernel, outs, ins, operands, scratch=(), flops=1, moved=1, out_specs=None, limit=LIMIT):
    return pl.pallas_call(
        kernel,
        out_shape=outs,
        in_specs=ins,
        out_specs=out_specs if out_specs is not None else jax.tree.map(lambda _: VMEM, outs),
        scratch_shapes=list(scratch),
        compiler_params=pltpu.CompilerParams(vmem_limit_bytes=limit),
        cost_estimate=pl.CostEstimate(flops=flops, bytes_accessed=moved, transcendentals=0),
    )(*operands)


def f32(*shape):
    return jax.ShapeDtypeStruct(shape, jnp.float32)


def bf16(*shape):
    return jax.ShapeDtypeStruct(shape, jnp.bfloat16)


def swap(block, axis, turn):
    groups, walls = lax.axis_size("fluid"), lax.axis_size("wall")

    def partner(f, w):
        at, count = (f, groups) if axis == "fluid" else (w, walls)
        other = at + 1 if (at + turn) % 2 == 0 else at - 1
        if axis == "fluid":
            return (other, w) if 0 <= other < count else (f, w ^ 1)
        return (f, other) if 0 <= other < count else (f ^ 1, w)

    pairs = []
    for f in range(groups):
        for w in range(walls):
            to_f, to_w = partner(f, w)
            pairs.append((f * walls + w, to_f * walls + to_w))
    return lax.ppermute(block, ("fluid", "wall"), pairs)


def cross(block, axis, mask):
    return lax.ppermute(block, axis, [(i, i ^ mask) for i in range(lax.axis_size(axis))])


def from_neighbours(index, count, first, second):
    even = index % 2 == 0
    above = jnp.where(even, first, second)
    below = jnp.where(even, second, first)
    above = jnp.where(index == count - 1, jnp.zeros_like(above), above)
    below = jnp.where(index == 0, jnp.zeros_like(below), below)
    return below, above


def pack_edges(packed, plane, m, lane):
    width = lane.shape[1]
    here = (lane == 2 * m) | (lane == (2 * m + width - 1) % width)
    return jnp.where(here, pltpu.roll(plane, 2 * m, 1), packed)


def mix_edges(below, above, lane, shift=2):
    return jnp.where(lane % 2 == 0, above, pltpu.roll(below, shift, 1))


def edge_of(mixed, m):
    width = mixed.shape[1]
    return pltpu.roll(mixed, (2 * width - (2 * m + 1)) % width, 1)


def viscosity(jumps):
    shear_sq = jumps[0] * jumps[0] + jumps[1] * jumps[1] + jumps[2] * jumps[2]
    root = lax.rsqrt(1.0 + relax_sq * shear_sq)
    return nu_floor + nu_spread * (root * lax.rsqrt(root))


def iotas(rows, width):
    shape = (rows, width)
    return lax.broadcasted_iota(jnp.int32, shape, 0), lax.broadcasted_iota(jnp.int32, shape, 1)


def faces_kernel(flow_ref, first_ref, second_ref, sems):
    last = flow_ref.shape[1] - 1
    odd = lax.axis_index("fluid") % 2
    copies = [
        pltpu.make_async_copy(flow_ref.at[c, plane], out_ref.at[c], sems.at[i, c])
        for i, (plane, out_ref) in enumerate(((last - last * odd, first_ref), (last * odd, second_ref)))
        for c in range(flow_ref.shape[0])
    ]
    for copy in copies:
        copy.start()
    for copy in copies:
        copy.wait()


def edges_kernel(groups, flow_ref, regions_ref, x0_ref, x1_ref, edges_ref):
    fields, planes, rows, width = flow_ref.shape
    _, lane = iotas(rows, width)
    outer = jnp.zeros((rows, width), jnp.float32)
    second, beside = outer, outer
    for c in range(fields):
        for x in range(planes):
            m, plane = c * planes + x, flow_ref[c, x]
            outer = pack_edges(outer, plane, m, lane)
            here = (lane == 2 * m) | (lane == (2 * m - 3) % width)
            second = jnp.where(here, pltpu.roll(plane, (2 * m - 1) % width, 1), second)
        for side, plane in enumerate(from_neighbours(lax.axis_index("fluid"), groups, x0_ref[c], x1_ref[c])):
            beside = pack_edges(beside, plane, 2 * c + side, lane)
    for x in range(planes):
        beside = pack_edges(beside, regions_ref[x].astype(jnp.float32), 2 * fields + x, lane)
    edges_ref[0], edges_ref[1], edges_ref[2] = outer, second, beside


def outside_edges(walls, planes, halo, second, beside, inside, rim_nu):
    rows, width = halo.shape
    row, lane = iotas(rows, width)
    x, field = (lane // 2) % planes, (lane // 2) // planes

    def spread(nu):
        nu = jnp.where(field == 0, nu, 0.0)
        return nu + pltpu.roll(nu, 2 * planes, 1) + pltpu.roll(nu, 4 * planes, 1)

    def nu_of(jump):
        return spread(viscosity([jump] + [pltpu.roll(jump, width - 2 * c * planes, 1) for c in (1, 2)]))

    over_x, under_x = pltpu.roll(halo, width - 2, 1), pltpu.roll(halo, 2, 1)
    for c in range(4):
        low = pltpu.roll(beside, (2 * c * planes - 4 * c) % width, 1)
        high = pltpu.roll(beside, (2 * (c * planes + planes - 1) - 4 * c - 2) % width, 1)
        under_x = jnp.where((x == 0) & (field == c), low, under_x)
        over_x = jnp.where((x == planes - 1) & (field == c), high, over_x)
    over_y = jnp.where(row == rows - 1, 0.0, pltpu.roll(halo, rows - 1, 0))
    under_y = jnp.where(row == 0, 0.0, pltpu.roll(halo, 1, 0))
    total = spread(rim_nu) * (inside - halo)
    for other in (over_x, under_x, over_y, under_y, second):
        total += nu_of(other - halo) * (other - halo)
    above = lane % 2 == 0
    gradient_x = pltpu.roll(0.5 * (over_x - under_x), width - 6 * planes, 1)
    gradient_y = pltpu.roll(0.5 * (over_y - under_y), width - 4 * planes, 1)
    gradient_z = pltpu.roll(0.5 * jnp.where(above, second - inside, inside - second), width - 2 * planes, 1)
    gradient = jnp.where(field == 0, gradient_x, jnp.where(field == 1, gradient_y, gradient_z))
    value = halo + time_step * (total - gradient)
    value = jnp.where(field == 3, pltpu.roll(beside, 6 * planes - 16, 1), value)
    me = lax.axis_index("wall")
    exists = jnp.where(above, jnp.where(me < walls - 1, 1, 0), jnp.where(me > 0, 1, 0)) == 1
    return jnp.where(exists & (field < 4), value, 0.0)


def group_kernel(cap, dest_ref, tiles_ref, meas_ref, flow_ref, *refs):
    chips = len(refs) - 12
    sends, halo_refs = refs[:chips], refs[chips : chips + 2]
    (list_ref, held_ref, seen_ref, count_ref, slot_ref, rows_ref,
     list_sem, seen_sem, in_sems, face_sems) = refs[chips + 2 :]
    count_tiles, width, _ = tiles_ref.shape
    groups = 2 * chips
    slots = groups * cap
    extra = rows_ref.shape[0] // groups
    depth = cap * width
    me = lax.axis_index("fluid")
    listed = pltpu.make_async_copy(dest_ref, list_ref, list_sem)
    listed.start()
    piece = count_tiles // in_sems.shape[0]

    def load(p):
        part = pl.ds(p * piece, piece)
        return pltpu.make_async_copy(tiles_ref.at[part], held_ref.at[part], in_sems.at[p])

    for p in range(in_sems.shape[0]):
        load(p).start()
    seen = pltpu.make_async_copy(meas_ref, seen_ref, seen_sem)
    seen.start()
    last = flow_ref.shape[1] - 1
    fields = flow_ref.shape[0]
    faces = [
        pltpu.make_async_copy(flow_ref.at[c, plane], halo_refs[i].at[c], face_sems.at[i * fields + c])
        for i, plane in enumerate((last * (1 - me % 2), last * (me % 2)))
        for c in range(fields)
    ]
    for face in faces:
        face.start()

    def clear(b, carry):
        count_ref[b] = 0
        for k in range(cap):
            slot_ref[b * cap + k] = -1
        return carry

    lax.fori_loop(0, groups, clear, 0)
    _, tile_lane = iotas(8, count_tiles)
    listed.wait()

    def place(t, slot_of):
        b = list_ref[t]
        k = count_ref[b]
        count_ref[b] = k + 1
        slot_ref[b * cap + k] = t
        return jnp.where(tile_lane == t, b * cap + k, slot_of)

    slot_of = lax.fori_loop(
        0, count_tiles, place, jnp.full((8, count_tiles), -1, jnp.int32), unroll=True
    )
    seen.wait()
    row = lax.broadcasted_iota(jnp.int32, (groups * extra, count_tiles), 0)
    within = row % extra
    row_slot = (row // extra) * cap + within // 3
    used = within < cap * 3
    total = jnp.zeros((groups * extra, width), jnp.float32)
    for c in range(3):
        pick = (row_slot == slot_of[0:1, :]) & used & (within % 3 == c)
        total += jnp.dot(
            pick.astype(jnp.float32).astype(jnp.bfloat16), seen_ref[c], preferred_element_type=jnp.float32
        )
    rows_ref[...] = total.astype(jnp.bfloat16)

    for p in range(in_sems.shape[0]):
        load(p).wait()

    for m in list(range(1, chips)) + [0]:
        for j in range(2):
            b = me ^ (2 * m + j)
            for k in range(cap):
                t = slot_ref[b * cap + k]
                at = (j, slice(k * width, (k + 1) * width))
                if slots > count_tiles:
                    sends[m][at] = jnp.where(t >= 0, held_ref[jnp.maximum(t, 0)], jnp.zeros((width, width), jnp.bfloat16))
                else:
                    sends[m][at] = held_ref[t]
    for m in range(chips):
        for j in range(2):
            b = me ^ (2 * m + j)
            sends[m][j, depth:, :] = rows_ref[pl.ds(pl.multiple_of(b * extra, extra), extra), :]
    for face in faces:
        face.wait()


def forward_kernel(
    sizes, cap, cells_ref, flow_ref, x0_ref, x1_ref, z0_ref, z1_ref, edges_ref,
    out_ref, next_ref, nux_ref, nuy_ref, nuz_ref, nuy0_ref, rim_ref, mine_ref, lent_ref, cells_of_ref,
    list_ref, padded_ref, taken_ref, list_sem, out_sems,
):
    _, planes, rows, width = flow_ref.shape
    groups, walls = sizes
    chips, extra, _ = mine_ref.shape
    listed = pltpu.make_async_copy(cells_ref, list_ref, list_sem)
    listed.start()
    row, lane = iotas(rows, width)
    halo = mix_edges(*from_neighbours(lax.axis_index("wall"), walls, z0_ref[0], z1_ref[0]), lane)
    inside = pltpu.roll(edges_ref[0], 1, 1)
    jump = halo - inside
    rim_nu = viscosity([jump] + [pltpu.roll(jump, width - 2 * c * planes, 1) for c in (1, 2)])
    rim_nu = jnp.where(lane < 2 * planes, rim_nu, 0.0)
    rim_ref[...] = rim_nu
    for c in range(4):
        low, high = from_neighbours(lax.axis_index("fluid"), groups, x0_ref[c], x1_ref[c])
        padded_ref[c, 0] = low
        padded_ref[c, planes + 1] = high
        padded_ref[c, 1 : planes + 1] = flow_ref[c]
    nux_ref[0] = viscosity([padded_ref[c, 1] - padded_ref[c, 0] for c in range(3)])

    def plane(x, carry):
        here = [padded_ref[c, x + 1] for c in range(4)]
        over = [padded_ref[c, x + 2] for c in range(4)]
        under = [padded_ref[c, x] for c in range(4)]
        total = [None] * 3
        pressure = [None] * 3

        def add(axis, nu_up, nu_down):
            for c in range(3):
                flux = nu_up * (over[c] - here[c]) - nu_down * (here[c] - under[c])
                total[c] = flux if total[c] is None else total[c] + flux
            pressure[axis] = 0.5 * (over[3] - under[3])

        nu_up = viscosity([over[c] - here[c] for c in range(3)])
        nux_ref[x + 1] = nu_up
        add(0, nu_up, nux_ref[x])
        over = [jnp.where(row == rows - 1, 0.0, pltpu.roll(here[c], rows - 1, 0)) for c in range(4)]
        under = [jnp.where(row == 0, 0.0, pltpu.roll(here[c], 1, 0)) for c in range(4)]
        nu_up = viscosity([over[c] - here[c] for c in range(3)])
        nu_first = viscosity([here[c][:1] for c in range(3)])
        nuy_ref[x] = nu_up
        nuy0_ref[pl.ds(x, 1), :] = nu_first
        add(1, nu_up, jnp.where(row == 0, nu_first, pltpu.roll(nu_up, 1, 0)))
        rim = [edge_of(halo, c * planes + x) for c in range(4)]
        over = [jnp.where(lane == width - 1, rim[c], pltpu.roll(here[c], width - 1, 1)) for c in range(4)]
        under = [jnp.where(lane == 0, rim[c], pltpu.roll(here[c], 1, 1)) for c in range(4)]
        nu_up = viscosity([over[c] - here[c] for c in range(3)])
        nuz_ref[x] = nu_up
        add(2, nu_up, jnp.where(lane == 0, edge_of(rim_nu, x), pltpu.roll(nu_up, 1, 1)))
        for c in range(3):
            value = here[c] + time_step * (total[c] - pressure[c])
            next_ref[c, x] = value
        return carry

    pieces = out_sems.shape[0]
    step = planes // pieces

    def store(i):
        part = pl.ds(i * step, step)
        return pltpu.make_async_copy(next_ref.at[:, part], out_ref.at[:, part], out_sems.at[i])

    for i in range(pieces):
        lax.fori_loop(i * step, (i + 1) * step, plane, 0, unroll=True)
        store(i).start()

    taken_ref[...] = jnp.zeros_like(taken_ref)
    listed.wait()
    _, slot_lane = iotas(8, groups * extra)
    cell_of = jnp.full((8, groups * extra), -1, jnp.int32)
    odd = lax.axis_index("fluid") % 2
    for b in range(groups):
        part = (odd if b % 2 == 0 else 1 - odd) * chips + b // 2
        for k in range(cap):
            cell = list_ref[k, b]
            x, y = lax.div(cell, rows), lax.rem(cell, rows)
            first = part * extra + 3 * k
            for c in range(3):
                taken_ref[pl.ds(first + c, 1), :] = next_ref[c, x, pl.ds(y, 1), :]
            cell_of = jnp.where((slot_lane >= first) & (slot_lane < first + 3), cell, cell_of)
    cells_of_ref[...] = cell_of
    taken = taken_ref[...].astype(jnp.bfloat16).reshape((2,) + mine_ref.shape)
    mine_ref[...] = taken[0]
    lent_ref[...] = taken[1]
    for i in range(pieces):
        store(i).wait()


def pick_kernel(
    sizes, cells_of_ref, z0_ref, z1_ref, edges_ref, rim_ref, nuy_ref, nuz_ref, nuy0_ref,
    outside_ref, rims_ref, pick_ref, nuyd_ref, nuzd_ref,
):
    _, rows, width = edges_ref.shape
    groups, walls = sizes
    _, lines, slot_rows = pick_ref.shape
    planes = lines // rows
    extra = slot_rows // groups
    _, lane = iotas(rows, width)
    halo, second, beside = (
        mix_edges(*from_neighbours(lax.axis_index("wall"), walls, z0_ref[i], z1_ref[i]), lane, shift)
        for i, shift in enumerate((2, 4, 2))
    )
    inside = pltpu.roll(edges_ref[0], 1, 1)
    rim_nu = rim_ref[...]
    outside_ref[...] = outside_edges(walls, planes, halo, second, beside, inside, rim_nu)
    rims_ref[...] = time_step * (rim_nu + pltpu.roll(rim_nu, 2 * planes, 1) + pltpu.roll(rim_nu, 4 * planes, 1))
    line, slot_lane = iotas(lines, slot_rows)
    hit = line == cells_of_ref[0:1, :]
    part = (slot_lane % extra) % 3
    for c in range(3):
        pick_ref[c] = (hit & (part == c)).astype(jnp.float32).astype(jnp.bfloat16)
    row, _ = iotas(rows, width)
    for x in range(planes):
        nuyd_ref[x] = jnp.where(row == 0, nuy0_ref[x : x + 1, :], pltpu.roll(nuy_ref[x], 1, 0))
        nuzd_ref[x] = jnp.where(lane == 0, edge_of(rim_nu, x), pltpu.roll(nuz_ref[x], 1, 1))


def product_kernel(cap, block, masks, values_ref, before_ref, *refs):
    chips, extra, width = values_ref.shape
    recvs, out_ref = refs[:-1], refs[-1]
    depth = cap * width
    row, lane = iotas(extra, depth)
    own = row // 3 == lane // width
    here = lax.axis_index("fluid") // 2
    if before_ref.shape == out_ref.shape:
        out_ref[...] = before_ref[...]
    for m, recv_ref in zip(masks, recvs):
        source = here ^ m
        at = pl.ds(pl.multiple_of(source * extra, extra), extra)
        weights = recv_ref[block, pl.ds(0, depth), :]
        predicted = lax.dot_general(
            values_ref[source], weights, (((1,), (1,)), ((), ())), preferred_element_type=jnp.float32
        )
        seen = recv_ref[block, pl.ds(depth, extra), :].astype(jnp.float32)
        misfit = jnp.where(own, predicted - jnp.concatenate([seen] * cap, axis=1), 0.0).astype(jnp.bfloat16)
        contrib = jnp.dot(misfit, weights, preferred_element_type=jnp.float32)
        high = contrib.astype(jnp.bfloat16)
        out_ref[0, at, :] = high
        out_ref[1, at, :] = (contrib - high.astype(jnp.float32)).astype(jnp.bfloat16)


def shares(mine_ref, other_ref):
    return jnp.concatenate([ref[part] for part in range(2) for ref in (mine_ref, other_ref)], axis=0)


def forcing_rows(c, part, pick_ref, rows):
    pick = pick_ref[c, part, :]
    return jnp.dot(jnp.concatenate([pick, pick], axis=1), rows, preferred_element_type=jnp.float32)


def ends_kernel(mine_ref, other_ref, pick_ref, first_ref, second_ref):
    _, rows, _ = first_ref.shape
    lines = pick_ref.shape[1]
    even = lax.axis_index("fluid") % 2 == 0
    both = shares(mine_ref, other_ref)
    for c in range(3):
        low = forcing_rows(c, slice(0, rows), pick_ref, both)
        high = forcing_rows(c, slice(lines - rows, lines), pick_ref, both)
        first_ref[c] = jnp.where(even, high, low).astype(jnp.bfloat16)
        second_ref[c] = jnp.where(even, low, high).astype(jnp.bfloat16)


def forcing_kernel(mine_ref, other_ref, pick_ref, after_ref, forcing_ref):
    both = shares(mine_ref, other_ref)
    for c in range(3):
        forcing_ref[c] = forcing_rows(c, slice(None), pick_ref, both).reshape(forcing_ref.shape[1:])


FOLD = 16


def region_rows(values, ids, tops):
    def folded(plane):
        return jnp.concatenate([plane[y : y + FOLD] for y in range(0, plane.shape[0], FOLD)], axis=1)

    values, ids = folded(values), folded(ids)
    top, low = (ids // 8).astype(jnp.float32).astype(jnp.bfloat16), (ids % 8).astype(jnp.float32).astype(jnp.bfloat16)
    main = values.astype(jnp.bfloat16)
    rest = (values - main.astype(jnp.float32)).astype(jnp.bfloat16)
    zero = jnp.zeros_like(main)
    one = jnp.ones_like(main)
    hits = [top == jnp.bfloat16(h) for h in range(tops)]
    return (
        jnp.concatenate([jnp.where(hit, main, zero) for hit in hits], axis=0),
        jnp.concatenate([jnp.where(hit, rest, zero) for hit in hits], axis=0),
        jnp.concatenate([jnp.where(low == jnp.bfloat16(l), one, zero) for l in range(8)], axis=0),
    )


def region_sums(main, rest, ones):
    over_lanes = (((1,), (1,)), ((), ()))
    total = lax.dot_general(main, ones, over_lanes, preferred_element_type=jnp.float32)
    total += lax.dot_general(rest, ones, over_lanes, preferred_element_type=jnp.float32)
    row, column = iotas(*total.shape)
    total = jnp.where(row % FOLD == column % FOLD, total, 0.0)
    return jnp.sum(total.reshape(total.shape[0] // FOLD, FOLD, total.shape[1]), axis=1)


def inner_kernel(
    forcing_ref, next_ref, nux_ref, nuy_ref, nuyd_ref, nuz_ref, nuzd_ref, rim_ref, regions_ref, outside_ref,
    adjoint_ref, fpack_ref, sums_ref, main_ref, rest_ref, ones_ref,
):
    _, planes, rows, width = forcing_ref.shape
    row, lane = iotas(rows, width)
    rim_nu = rim_ref[...]
    tops = sums_ref.shape[0]

    def add_up(x, values, ids):
        span = rows // FOLD * width
        at = pl.ds(pl.multiple_of(x * span, span), span)
        for part_ref, part in zip((main_ref, rest_ref, ones_ref), region_rows(values, ids, tops)):
            part_ref[:, at] = part

    def plane(x, fpack):
        nus = (nux_ref[x + 1], nux_ref[x], nuy_ref[x], nuyd_ref[x], nuz_ref[x], nuzd_ref[x])
        next_up, next_down = jnp.minimum(x + 1, planes - 1), jnp.maximum(x - 1, 0)
        at_top, at_bottom = x == planes - 1, x == 0
        product = None
        for c in range(3):
            here = forcing_ref[c, x]
            over = jnp.where(at_top, 0.0, forcing_ref[c, next_up])
            under = jnp.where(at_bottom, 0.0, forcing_ref[c, next_down])
            total = nus[0] * (over - here) - nus[1] * (here - under)
            over = jnp.where(row == rows - 1, 0.0, pltpu.roll(here, rows - 1, 0))
            under = jnp.where(row == 0, 0.0, pltpu.roll(here, 1, 0))
            total += nus[2] * (over - here) - nus[3] * (here - under)
            over = jnp.where(lane == width - 1, 0.0, pltpu.roll(here, width - 1, 1))
            under = jnp.where(lane == 0, 0.0, pltpu.roll(here, 1, 1))
            total += nus[4] * (over - here) - nus[5] * (here - under)
            value = here + time_step * total
            adjoint_ref[c, x] = value
            part = value * next_ref[c, x]
            product = part if product is None else product + part
            fpack = pack_edges(fpack, here, c * planes + x, lane)
        add_up(x, product, regions_ref[x])
        return fpack

    fpack = lax.fori_loop(0, planes, plane, jnp.zeros((rows, width), jnp.float32), unroll=4)
    fpack_ref[...] = fpack
    mixed = outside_ref[...]
    reach = pltpu.roll(fpack, 1, 1) * mixed
    reach = reach + pltpu.roll(reach, width - 2 * planes, 1) + pltpu.roll(reach, width - 4 * planes, 1)
    reach = time_step * reach * rim_nu
    add_up(planes, reach, pltpu.roll(mixed, (width - 6 * planes) % width, 1).astype(jnp.int32))
    sums_ref[...] = region_sums(main_ref[...], rest_ref[...], ones_ref[...])


def edge_kernel(groups, masks, x0_ref, x1_ref, nux_ref, next_ref, regions_ref, sums_ref, fpack_ref, *outs):
    _, planes, rows, width = next_ref.shape
    tops, columns = sums_ref.shape
    low, high = 0.0, 0.0
    for c in range(3):
        below, above = beside_of(c, groups, x0_ref, x1_ref)
        low += below * next_ref[c, 0]
        high += above * next_ref[c, planes - 1]
    ends = [
        region_rows(time_step * nux_ref[0] * low, regions_ref[0], tops),
        region_rows(time_step * nux_ref[planes] * high, regions_ref[planes - 1], tops),
    ]
    total = sums_ref[...] + region_sums(*(jnp.concatenate(both, axis=1) for both in zip(*ends)))
    total = jnp.concatenate([total[:, at : at + width] for at in range(0, columns, width)], axis=0)
    high = total.astype(jnp.bfloat16)
    total = jnp.concatenate([high, (total - high.astype(jnp.float32)).astype(jnp.bfloat16)], axis=0)
    height = total.shape[0]
    for mask, out_ref in zip((0,) + masks, outs):
        out_ref[:height, :] = total
        if mask:
            out_ref[height : height + rows, :] = fpack_ref[...].astype(jnp.bfloat16)
            if out_ref.shape[0] > height + rows:
                out_ref[height + rows :, :] = jnp.zeros((out_ref.shape[0] - height - rows, width), jnp.bfloat16)


def beside_of(c, groups, x0_ref, x1_ref):
    return from_neighbours(
        lax.axis_index("fluid"), groups, x0_ref[c].astype(jnp.float32), x1_ref[c].astype(jnp.float32)
    )


def final_kernel(sizes, inner_ref, x0_ref, x1_ref, nux_ref, rims_ref, own_ref, *refs):
    groups, walls = sizes
    arrived, (adjoint_ref, sens_ref, value_ref, owned_ref, sems, owned_sem) = refs[:-6], refs[-6:]
    _, planes, rows, width = inner_ref.shape
    per = own_ref.shape[0]
    _, lane = iotas(rows, width)
    me = lax.axis_index("wall")

    def sums_of(ref):
        parts = ref[:per, :].astype(jnp.float32)
        return parts[: per // 2] + parts[per // 2 :]

    total = sums_of(own_ref)
    below = jnp.zeros((rows, width), jnp.float32)
    above = jnp.zeros((rows, width), jnp.float32)
    for mask, ref in zip(range(1, walls), arrived):
        total = total + sums_of(ref)
        if mask & (mask + 1) == 0:
            edges = ref[per : per + rows, :].astype(jnp.float32)
            above = jnp.where((me ^ mask) == me + 1, edges, above)
            below = jnp.where((me ^ mask) == me - 1, edges, below)
    mixed = mix_edges(below, above, lane)
    edge_flux = mixed * rims_ref[...]
    on_edge = (lane == 0) | (lane == width - 1)

    beside = [beside_of(c, groups, x0_ref, x1_ref) for c in range(3)]
    step = planes // sems.shape[0]

    def store(i):
        part = pl.ds(i * step, step)
        return pltpu.make_async_copy(value_ref.at[:, part], adjoint_ref.at[:, part], sems.at[i])

    for i in range(sems.shape[0]):
        for x in range(i * step, (i + 1) * step):
            for c in range(3):
                value = inner_ref[c, x] + jnp.where(on_edge, edge_of(edge_flux, c * planes + x), 0.0)
                if x == 0:
                    value += time_step * nux_ref[0] * beside[c][0]
                if x == planes - 1:
                    value += time_step * nux_ref[planes] * beside[c][1]
                value_ref[c, x] = value
        store(i).start()
    parts = width // FOLD
    tops = REG_DEV * walls // 8
    owned = REG_DEV // 8
    top, _ = iotas(tops, width)
    region, lane = iotas(REG_DEV, width)
    sens = jnp.zeros((8, REG_DEV), jnp.float32)
    for i in range(8 // parts):
        for h in range(owned):
            mine = jnp.where(top == me * owned + h, total[i * tops : (i + 1) * tops], 0.0)
            gather = (region == h * 8 + i * parts + lane // FOLD).astype(jnp.float32)
            sens += lax.dot_general(
                jnp.broadcast_to(jnp.sum(mine, axis=0, keepdims=True), (8, width)), gather, (((1,), (1,)), ((), ())),
                precision=lax.Precision.HIGHEST, preferred_element_type=jnp.float32,
            )
    owned_ref[...] = sens_scale * sens[:1]
    owned_copy = pltpu.make_async_copy(owned_ref, sens_ref, owned_sem)
    owned_copy.start()
    for i in range(sems.shape[0]):
        store(i).wait()
    owned_copy.wait()


def body(flow_state, regions, obs_tiles, measured, tile_dest, cell_list):
    groups, walls = lax.axis_size("fluid"), lax.axis_size("wall")
    sizes = (groups, walls)
    _, planes, rows, width = flow_state.shape
    count_tiles = obs_tiles.shape[2]
    cap = cell_list.shape[3]
    extra = -(-cap * 3 // 16) * 16
    reg_count = REG_DEV * walls
    cells = groups * cap
    grid = planes * rows * width

    chips = groups // 2
    height = cap * width + extra
    *sends, xs0, xs1 = call(
        functools.partial(group_kernel, cap),
        (bf16(2, height, width),) * chips + (f32(4, rows, width),) * 2,
        [HBM] * 4,
        tuple(
            pltpu.with_memory_space_constraint(operand, pltpu.HBM)
            for operand in (tile_dest[0, 0], obs_tiles[0, 0], jnp.transpose(measured[0, 0], (1, 0, 2)), flow_state)
        ),
        (
            pltpu.SMEM((count_tiles,), jnp.int32),
            pltpu.VMEM((count_tiles, width, width), jnp.bfloat16),
            pltpu.VMEM((3, count_tiles, width), jnp.bfloat16),
            pltpu.SMEM((groups,), jnp.int32),
            pltpu.SMEM((cells,), jnp.int32),
            pltpu.VMEM((groups * extra, width), jnp.bfloat16),
            pltpu.SemaphoreType.DMA,
            pltpu.SemaphoreType.DMA,
            pltpu.SemaphoreType.DMA((4,)),
            pltpu.SemaphoreType.DMA((8,)),
        ),
        out_specs=(VMEM,) * (chips + 2),
    )
    x0, x1 = swap(xs0, "fluid", 0), swap(xs1, "fluid", 1)
    recvs = [sends[0]] + [cross(sends[m], "fluid", 2 * m) for m in range(1, chips)]
    zs = call(
        functools.partial(edges_kernel, groups),
        f32(3, rows, width),
        [VMEM] * 4,
        (flow_state, regions, x0, x1),
        flops=HIDES,
    )
    z0, z1 = swap(zs, "wall", 0), swap(zs, "wall", 1)
    slot_rows = groups * extra
    velocity_next, velocity, nux, nuy, nuz, nuy0, rim, mine, lent, cells_of = call(
        functools.partial(forward_kernel, sizes, cap),
        (f32(3, planes, rows, width),) * 2
        + (f32(planes + 1, rows, width), f32(planes, rows, width), f32(planes, rows, width))
        + (f32(planes, width), f32(rows, width))
        + (bf16(chips, extra, width),) * 2
        + (jax.ShapeDtypeStruct((8, slot_rows), jnp.int32),),
        [ANY] + [VMEM] * 6,
        (cell_list[0, 0].T, flow_state, x0, x1, z0, z1, zs),
        (
            pltpu.SMEM((cap, groups), jnp.int32),
            pltpu.VMEM((4, planes + 2, rows, width), jnp.float32),
            pltpu.VMEM((slot_rows, width), jnp.float32),
            pltpu.SemaphoreType.DMA,
            pltpu.SemaphoreType.DMA((4,)),
        ),
        out_specs=(HBM,) + (VMEM,) * 9,
    )
    borrowed = cross(lent, "fluid", 1)
    outside, rims, pick, nuyd, nuzd = call(
        functools.partial(pick_kernel, sizes),
        (f32(rows, width), f32(rows, width), bf16(3, planes * rows, slot_rows)) + (f32(planes, rows, width),) * 2,
        [VMEM] * 8,
        (cells_of, z0, z1, zs, rim, nuy, nuz, nuy0),
    )

    def products(block, masks, values, before):
        whole = (2, chips * extra, width)
        return call(
            functools.partial(product_kernel, cap, block, masks),
            bf16(*whole),
            [VMEM, VMEM if before.shape == whole else ANY] + [VMEM] * len(masks),
            (values, before, *(recvs[m] for m in masks)),
        )

    given = products(1, tuple(range(chips // 2)), borrowed, pick)
    given = products(1, tuple(range(chips // 2, chips)), borrowed, given)
    other = cross(given, "fluid", 1)
    held = products(0, tuple(range(chips)), mine, outside)
    fs0, fs1 = call(ends_kernel, (bf16(3, rows, width),) * 2, [VMEM] * 3, (held, other, pick))
    f0, f1 = swap(fs0, "fluid", 0), swap(fs1, "fluid", 1)
    forcing = call(forcing_kernel, f32(3, planes, rows, width), [VMEM] * 3 + [ANY], (held, other, pick, fs1))
    tops = reg_count // 8
    columns = 8 * FOLD
    span = (planes + 1) * rows // FOLD * width
    sum_rows = 2 * tops * (columns // width)
    inner, fpack, sums = call(
        inner_kernel,
        (f32(3, planes, rows, width), f32(rows, width), f32(tops, columns)),
        [VMEM] * 10,
        (forcing, velocity, nux, nuy, nuyd, nuz, nuzd, rim, regions, outside),
        (
            pltpu.VMEM((tops * FOLD, span), jnp.bfloat16),
            pltpu.VMEM((tops * FOLD, span), jnp.bfloat16),
            pltpu.VMEM((columns, span), jnp.bfloat16),
        ),
    )
    masks = tuple(range(1, walls))
    heights = [sum_rows] + [sum_rows + rows + 16 * (mask - 1) for mask in masks]
    own, *parts = call(
        functools.partial(edge_kernel, groups, masks),
        tuple(bf16(height, width) for height in heights),
        [VMEM] * 7,
        (f0, f1, nux, velocity, regions, sums, fpack),
    )
    arrived = [cross(part, "wall", mask) for part, mask in zip(parts, masks)]
    adjoint, sens = call(
        functools.partial(final_kernel, sizes),
        (f32(3, planes, rows, width), f32(1, REG_DEV)),
        [VMEM] * (6 + len(arrived)),
        (inner, f0, f1, nux, rims, own, *arrived),
        (
            pltpu.VMEM((3, planes, rows, width), jnp.float32),
            pltpu.VMEM((1, REG_DEV), jnp.float32),
            pltpu.SemaphoreType.DMA((4,)),
            pltpu.SemaphoreType.DMA,
        ),
        out_specs=(HBM, HBM),
        flops=10 * grid,
        moved=24 * grid,
    )
    return velocity_next, adjoint, sens.reshape(REG_DEV)


def solution(mesh):
    in_specs = (
        P(None, "fluid", None, "wall"),
        P("fluid", None, "wall"),
        P("fluid", "wall", None, None, None),
        P("fluid", "wall", None, None, None),
        P("fluid", "wall", None),
        P("fluid", "wall", None, None),
    )
    out_specs = (
        P(None, "fluid", None, "wall"),
        P(None, "fluid", None, "wall"),
        P(("fluid", "wall")),
    )
    return jax.shard_map(body, mesh=mesh, in_specs=in_specs, out_specs=out_specs, check_vma=False)
```

```python
import functools

import jax
import jax.numpy as jnp
from jax import lax
from jax.experimental import pallas as pl
from jax.experimental.pallas import tpu as pltpu
from jax.sharding import PartitionSpec as P

REG_DEV = 16

time_step = 0.12
nu_floor = 0.1
nu_spread = 0.9
relax_sq = 4.0
sens_scale = 0.03

VMEM = pl.BlockSpec(memory_space=pltpu.VMEM)
SMEM = pl.BlockSpec(memory_space=pltpu.SMEM)
ANY = pl.BlockSpec(memory_space=pl.ANY)
HBM = pl.BlockSpec(memory_space=pltpu.HBM)
LIMIT = 24 * 1024 * 1024
HIDES = 100_000_000_000


def call(kernel, outs, ins, operands, scratch=(), flops=1, moved=1, out_specs=None, limit=LIMIT):
    return pl.pallas_call(
        kernel,
        out_shape=outs,
        in_specs=ins,
        out_specs=out_specs if out_specs is not None else jax.tree.map(lambda _: VMEM, outs),
        scratch_shapes=list(scratch),
        compiler_params=pltpu.CompilerParams(vmem_limit_bytes=limit),
        cost_estimate=pl.CostEstimate(flops=flops, bytes_accessed=moved, transcendentals=0),
    )(*operands)


def f32(*shape):
    return jax.ShapeDtypeStruct(shape, jnp.float32)


def bf16(*shape):
    return jax.ShapeDtypeStruct(shape, jnp.bfloat16)


def swap(block, axis, turn):
    groups, walls = lax.axis_size("fluid"), lax.axis_size("wall")

    def partner(f, w):
        at, count = (f, groups) if axis == "fluid" else (w, walls)
        other = at + 1 if (at + turn) % 2 == 0 else at - 1
        if axis == "fluid":
            return (other, w) if 0 <= other < count else (f, w ^ 1)
        return (f, other) if 0 <= other < count else (f ^ 1, w)

    pairs = []
    for f in range(groups):
        for w in range(walls):
            to_f, to_w = partner(f, w)
            pairs.append((f * walls + w, to_f * walls + to_w))
    return lax.ppermute(block, ("fluid", "wall"), pairs)


def cross(block, axis, mask):
    return lax.ppermute(block, axis, [(i, i ^ mask) for i in range(lax.axis_size(axis))])


def from_neighbours(index, count, first, second):
    even = index % 2 == 0
    above = jnp.where(even, first, second)
    below = jnp.where(even, second, first)
    above = jnp.where(index == count - 1, jnp.zeros_like(above), above)
    below = jnp.where(index == 0, jnp.zeros_like(below), below)
    return below, above


def pack_edges(packed, plane, m, lane):
    width = lane.shape[1]
    here = (lane == 2 * m) | (lane == (2 * m + width - 1) % width)
    return jnp.where(here, pltpu.roll(plane, 2 * m, 1), packed)


def mix_edges(below, above, lane, shift=2):
    return jnp.where(lane % 2 == 0, above, pltpu.roll(below, shift, 1))


def edge_of(mixed, m):
    width = mixed.shape[1]
    return pltpu.roll(mixed, (2 * width - (2 * m + 1)) % width, 1)


def viscosity(jumps):
    shear_sq = jumps[0] * jumps[0] + jumps[1] * jumps[1] + jumps[2] * jumps[2]
    root = lax.rsqrt(1.0 + relax_sq * shear_sq)
    return nu_floor + nu_spread * (root * lax.rsqrt(root))


def iotas(rows, width):
    shape = (rows, width)
    return lax.broadcasted_iota(jnp.int32, shape, 0), lax.broadcasted_iota(jnp.int32, shape, 1)


def faces_kernel(flow_ref, first_ref, second_ref, sems):
    last = flow_ref.shape[1] - 1
    odd = lax.axis_index("fluid") % 2
    copies = [
        pltpu.make_async_copy(flow_ref.at[c, plane], out_ref.at[c], sems.at[i, c])
        for i, (plane, out_ref) in enumerate(((last - last * odd, first_ref), (last * odd, second_ref)))
        for c in range(flow_ref.shape[0])
    ]
    for copy in copies:
        copy.start()
    for copy in copies:
        copy.wait()


def edges_kernel(groups, flow_ref, regions_ref, x0_ref, x1_ref, edges_ref):
    fields, planes, rows, width = flow_ref.shape
    _, lane = iotas(rows, width)
    outer = jnp.zeros((rows, width), jnp.float32)
    second, beside = outer, outer
    for c in range(fields):
        for x in range(planes):
            m, plane = c * planes + x, flow_ref[c, x]
            outer = pack_edges(outer, plane, m, lane)
            here = (lane == 2 * m) | (lane == (2 * m - 3) % width)
            second = jnp.where(here, pltpu.roll(plane, (2 * m - 1) % width, 1), second)
        for side, plane in enumerate(from_neighbours(lax.axis_index("fluid"), groups, x0_ref[c], x1_ref[c])):
            beside = pack_edges(beside, plane, 2 * c + side, lane)
    for x in range(planes):
        beside = pack_edges(beside, regions_ref[x].astype(jnp.float32), 2 * fields + x, lane)
    edges_ref[0], edges_ref[1], edges_ref[2] = outer, second, beside


def outside_edges(walls, planes, halo, second, beside, inside, rim_nu):
    rows, width = halo.shape
    row, lane = iotas(rows, width)
    x, field = (lane // 2) % planes, (lane // 2) // planes

    def spread(nu):
        nu = jnp.where(field == 0, nu, 0.0)
        return nu + pltpu.roll(nu, 2 * planes, 1) + pltpu.roll(nu, 4 * planes, 1)

    def nu_of(jump):
        return spread(viscosity([jump] + [pltpu.roll(jump, width - 2 * c * planes, 1) for c in (1, 2)]))

    over_x, under_x = pltpu.roll(halo, width - 2, 1), pltpu.roll(halo, 2, 1)
    for c in range(4):
        low = pltpu.roll(beside, (2 * c * planes - 4 * c) % width, 1)
        high = pltpu.roll(beside, (2 * (c * planes + planes - 1) - 4 * c - 2) % width, 1)
        under_x = jnp.where((x == 0) & (field == c), low, under_x)
        over_x = jnp.where((x == planes - 1) & (field == c), high, over_x)
    over_y = jnp.where(row == rows - 1, 0.0, pltpu.roll(halo, rows - 1, 0))
    under_y = jnp.where(row == 0, 0.0, pltpu.roll(halo, 1, 0))
    total = spread(rim_nu) * (inside - halo)
    for other in (over_x, under_x, over_y, under_y, second):
        total += nu_of(other - halo) * (other - halo)
    above = lane % 2 == 0
    gradient_x = pltpu.roll(0.5 * (over_x - under_x), width - 6 * planes, 1)
    gradient_y = pltpu.roll(0.5 * (over_y - under_y), width - 4 * planes, 1)
    gradient_z = pltpu.roll(0.5 * jnp.where(above, second - inside, inside - second), width - 2 * planes, 1)
    gradient = jnp.where(field == 0, gradient_x, jnp.where(field == 1, gradient_y, gradient_z))
    value = halo + time_step * (total - gradient)
    value = jnp.where(field == 3, pltpu.roll(beside, 6 * planes - 16, 1), value)
    me = lax.axis_index("wall")
    exists = jnp.where(above, jnp.where(me < walls - 1, 1, 0), jnp.where(me > 0, 1, 0)) == 1
    return jnp.where(exists & (field < 4), value, 0.0)


def group_kernel(cap, dest_ref, tiles_ref, meas_ref, flow_ref, *refs):
    chips = len(refs) - 12
    sends, halo_refs = refs[:chips], refs[chips : chips + 2]
    (list_ref, held_ref, seen_ref, count_ref, slot_ref, rows_ref,
     list_sem, seen_sem, in_sems, face_sems) = refs[chips + 2 :]
    count_tiles, width, _ = tiles_ref.shape
    groups = 2 * chips
    slots = groups * cap
    extra = rows_ref.shape[0] // groups
    depth = cap * width
    me = lax.axis_index("fluid")
    listed = pltpu.make_async_copy(dest_ref, list_ref, list_sem)
    listed.start()
    piece = count_tiles // in_sems.shape[0]

    def load(p):
        part = pl.ds(p * piece, piece)
        return pltpu.make_async_copy(tiles_ref.at[part], held_ref.at[part], in_sems.at[p])

    for p in range(in_sems.shape[0]):
        load(p).start()
    seen = pltpu.make_async_copy(meas_ref, seen_ref, seen_sem)
    seen.start()
    last = flow_ref.shape[1] - 1
    fields = flow_ref.shape[0]
    faces = [
        pltpu.make_async_copy(flow_ref.at[c, plane], halo_refs[i].at[c], face_sems.at[i * fields + c])
        for i, plane in enumerate((last * (1 - me % 2), last * (me % 2)))
        for c in range(fields)
    ]
    for face in faces:
        face.start()

    def clear(b, carry):
        count_ref[b] = 0
        for k in range(cap):
            slot_ref[b * cap + k] = -1
        return carry

    lax.fori_loop(0, groups, clear, 0)
    _, tile_lane = iotas(8, count_tiles)
    listed.wait()

    def place(t, slot_of):
        b = list_ref[t]
        k = count_ref[b]
        count_ref[b] = k + 1
        slot_ref[b * cap + k] = t
        return jnp.where(tile_lane == t, b * cap + k, slot_of)

    slot_of = lax.fori_loop(
        0, count_tiles, place, jnp.full((8, count_tiles), -1, jnp.int32), unroll=True
    )
    seen.wait()
    row = lax.broadcasted_iota(jnp.int32, (groups * extra, count_tiles), 0)
    within = row % extra
    row_slot = (row // extra) * cap + within // 3
    used = within < cap * 3
    total = jnp.zeros((groups * extra, width), jnp.float32)
    for c in range(3):
        pick = (row_slot == slot_of[0:1, :]) & used & (within % 3 == c)
        total += jnp.dot(
            pick.astype(jnp.float32).astype(jnp.bfloat16), seen_ref[c], preferred_element_type=jnp.float32
        )
    rows_ref[...] = total.astype(jnp.bfloat16)

    for p in range(in_sems.shape[0]):
        load(p).wait()

    for m in list(range(1, chips)) + [0]:
        for j in range(2):
            b = me ^ (2 * m + j)
            for k in range(cap):
                t = slot_ref[b * cap + k]
                at = (j, slice(k * width, (k + 1) * width))
                if slots > count_tiles:
                    sends[m][at] = jnp.where(t >= 0, held_ref[jnp.maximum(t, 0)], jnp.zeros((width, width), jnp.bfloat16))
                else:
                    sends[m][at] = held_ref[t]
    for m in range(chips):
        for j in range(2):
            b = me ^ (2 * m + j)
            sends[m][j, depth:, :] = rows_ref[pl.ds(pl.multiple_of(b * extra, extra), extra), :]
    for face in faces:
        face.wait()


def forward_kernel(
    sizes, cap, cells_ref, flow_ref, x0_ref, x1_ref, z0_ref, z1_ref, edges_ref,
    out_ref, next_ref, nux_ref, nuy_ref, nuz_ref, nuy0_ref, rim_ref, mine_ref, lent_ref, cells_of_ref,
    list_ref, padded_ref, taken_ref, list_sem, out_sems,
):
    _, planes, rows, width = flow_ref.shape
    groups, walls = sizes
    chips, extra, _ = mine_ref.shape
    listed = pltpu.make_async_copy(cells_ref, list_ref, list_sem)
    listed.start()
    row, lane = iotas(rows, width)
    halo = mix_edges(*from_neighbours(lax.axis_index("wall"), walls, z0_ref[0], z1_ref[0]), lane)
    inside = pltpu.roll(edges_ref[0], 1, 1)
    jump = halo - inside
    rim_nu = viscosity([jump] + [pltpu.roll(jump, width - 2 * c * planes, 1) for c in (1, 2)])
    rim_nu = jnp.where(lane < 2 * planes, rim_nu, 0.0)
    rim_ref[...] = rim_nu
    for c in range(4):
        low, high = from_neighbours(lax.axis_index("fluid"), groups, x0_ref[c], x1_ref[c])
        padded_ref[c, 0] = low
        padded_ref[c, planes + 1] = high
        padded_ref[c, 1 : planes + 1] = flow_ref[c]
    nux_ref[0] = viscosity([padded_ref[c, 1] - padded_ref[c, 0] for c in range(3)])

    def plane(x, carry):
        here = [padded_ref[c, x + 1] for c in range(4)]
        over = [padded_ref[c, x + 2] for c in range(4)]
        under = [padded_ref[c, x] for c in range(4)]
        total = [None] * 3
        pressure = [None] * 3

        def add(axis, nu_up, nu_down):
            for c in range(3):
                flux = nu_up * (over[c] - here[c]) - nu_down * (here[c] - under[c])
                total[c] = flux if total[c] is None else total[c] + flux
            pressure[axis] = 0.5 * (over[3] - under[3])

        nu_up = viscosity([over[c] - here[c] for c in range(3)])
        nux_ref[x + 1] = nu_up
        add(0, nu_up, nux_ref[x])
        over = [jnp.where(row == rows - 1, 0.0, pltpu.roll(here[c], rows - 1, 0)) for c in range(4)]
        under = [jnp.where(row == 0, 0.0, pltpu.roll(here[c], 1, 0)) for c in range(4)]
        nu_up = viscosity([over[c] - here[c] for c in range(3)])
        nu_first = viscosity([here[c][:1] for c in range(3)])
        nuy_ref[x] = nu_up
        nuy0_ref[pl.ds(x, 1), :] = nu_first
        add(1, nu_up, jnp.where(row == 0, nu_first, pltpu.roll(nu_up, 1, 0)))
        rim = [edge_of(halo, c * planes + x) for c in range(4)]
        over = [jnp.where(lane == width - 1, rim[c], pltpu.roll(here[c], width - 1, 1)) for c in range(4)]
        under = [jnp.where(lane == 0, rim[c], pltpu.roll(here[c], 1, 1)) for c in range(4)]
        nu_up = viscosity([over[c] - here[c] for c in range(3)])
        nuz_ref[x] = nu_up
        add(2, nu_up, jnp.where(lane == 0, edge_of(rim_nu, x), pltpu.roll(nu_up, 1, 1)))
        for c in range(3):
            value = here[c] + time_step * (total[c] - pressure[c])
            next_ref[c, x] = value
        return carry

    pieces = out_sems.shape[0]
    step = planes // pieces

    def store(i):
        part = pl.ds(i * step, step)
        return pltpu.make_async_copy(next_ref.at[:, part], out_ref.at[:, part], out_sems.at[i])

    for i in range(pieces):
        lax.fori_loop(i * step, (i + 1) * step, plane, 0, unroll=True)
        store(i).start()

    taken_ref[...] = jnp.zeros_like(taken_ref)
    listed.wait()
    _, slot_lane = iotas(8, groups * extra)
    cell_of = jnp.full((8, groups * extra), -1, jnp.int32)
    odd = lax.axis_index("fluid") % 2
    for b in range(groups):
        part = (odd if b % 2 == 0 else 1 - odd) * chips + b // 2
        for k in range(cap):
            cell = list_ref[k, b]
            x, y = lax.div(cell, rows), lax.rem(cell, rows)
            first = part * extra + 3 * k
            for c in range(3):
                taken_ref[pl.ds(first + c, 1), :] = next_ref[c, x, pl.ds(y, 1), :]
            cell_of = jnp.where((slot_lane >= first) & (slot_lane < first + 3), cell, cell_of)
    cells_of_ref[...] = cell_of
    taken = taken_ref[...].astype(jnp.bfloat16).reshape((2,) + mine_ref.shape)
    mine_ref[...] = taken[0]
    lent_ref[...] = taken[1]
    for i in range(pieces):
        store(i).wait()


def pick_kernel(
    sizes, cells_of_ref, z0_ref, z1_ref, edges_ref, rim_ref, nuy_ref, nuz_ref, nuy0_ref,
    outside_ref, rims_ref, pick_ref, nuyd_ref, nuzd_ref,
):
    _, rows, width = edges_ref.shape
    groups, walls = sizes
    _, lines, slot_rows = pick_ref.shape
    planes = lines // rows
    extra = slot_rows // groups
    _, lane = iotas(rows, width)
    halo, second, beside = (
        mix_edges(*from_neighbours(lax.axis_index("wall"), walls, z0_ref[i], z1_ref[i]), lane, shift)
        for i, shift in enumerate((2, 4, 2))
    )
    inside = pltpu.roll(edges_ref[0], 1, 1)
    rim_nu = rim_ref[...]
    outside_ref[...] = outside_edges(walls, planes, halo, second, beside, inside, rim_nu)
    rims_ref[...] = time_step * (rim_nu + pltpu.roll(rim_nu, 2 * planes, 1) + pltpu.roll(rim_nu, 4 * planes, 1))
    line, slot_lane = iotas(lines, slot_rows)
    hit = line == cells_of_ref[0:1, :]
    part = (slot_lane % extra) % 3
    for c in range(3):
        pick_ref[c] = (hit & (part == c)).astype(jnp.float32).astype(jnp.bfloat16)
    row, _ = iotas(rows, width)
    for x in range(planes):
        nuyd_ref[x] = jnp.where(row == 0, nuy0_ref[x : x + 1, :], pltpu.roll(nuy_ref[x], 1, 0))
        nuzd_ref[x] = jnp.where(lane == 0, edge_of(rim_nu, x), pltpu.roll(nuz_ref[x], 1, 1))


def product_kernel(cap, block, masks, more, values_ref, before_ref, *refs):
    chips, extra, width = values_ref.shape
    recvs, out_ref = refs[:-1], refs[-1]
    depth = cap * width
    row, lane = iotas(extra, depth)
    own = row // 3 == lane // width
    here = lax.axis_index("fluid") // 2
    if more:
        out_ref[...] = before_ref[...]
    for m, recv_ref in zip(masks, recvs):
        source = here ^ m
        at = pl.ds(pl.multiple_of(source * extra, extra), extra)
        weights = recv_ref[block, pl.ds(0, depth), :]
        predicted = lax.dot_general(
            values_ref[source], weights, (((1,), (1,)), ((), ())), preferred_element_type=jnp.float32
        )
        seen = recv_ref[block, pl.ds(depth, extra), :].astype(jnp.float32)
        misfit = jnp.where(own, predicted - jnp.concatenate([seen] * cap, axis=1), 0.0).astype(jnp.bfloat16)
        contrib = jnp.dot(misfit, weights, preferred_element_type=jnp.float32)
        high = contrib.astype(jnp.bfloat16)
        out_ref[0, at, :] = high
        out_ref[1, at, :] = (contrib - high.astype(jnp.float32)).astype(jnp.bfloat16)


def shares(mine_ref, other_ref):
    return jnp.concatenate([ref[part] for part in range(2) for ref in (mine_ref, other_ref)], axis=0)


def forcing_rows(c, part, pick_ref, rows):
    pick = pick_ref[c, part, :]
    return jnp.dot(jnp.concatenate([pick, pick], axis=1), rows, preferred_element_type=jnp.float32)


def ends_kernel(mine_ref, other_ref, pick_ref, first_ref, second_ref):
    _, rows, _ = first_ref.shape
    lines = pick_ref.shape[1]
    even = lax.axis_index("fluid") % 2 == 0
    both = shares(mine_ref, other_ref)
    for c in range(3):
        low = forcing_rows(c, slice(0, rows), pick_ref, both)
        high = forcing_rows(c, slice(lines - rows, lines), pick_ref, both)
        first_ref[c] = jnp.where(even, high, low).astype(jnp.bfloat16)
        second_ref[c] = jnp.where(even, low, high).astype(jnp.bfloat16)


def forcing_kernel(mine_ref, other_ref, pick_ref, after_ref, forcing_ref):
    both = shares(mine_ref, other_ref)
    for c in range(3):
        forcing_ref[c] = forcing_rows(c, slice(None), pick_ref, both).reshape(forcing_ref.shape[1:])


FOLD = 16


def region_rows(values, ids, tops):
    def folded(plane):
        return jnp.concatenate([plane[y : y + FOLD] for y in range(0, plane.shape[0], FOLD)], axis=1)

    values, ids = folded(values), folded(ids)
    top, low = (ids // 8).astype(jnp.float32).astype(jnp.bfloat16), (ids % 8).astype(jnp.float32).astype(jnp.bfloat16)
    main = values.astype(jnp.bfloat16)
    rest = (values - main.astype(jnp.float32)).astype(jnp.bfloat16)
    zero = jnp.zeros_like(main)
    one = jnp.ones_like(main)
    hits = [top == jnp.bfloat16(h) for h in range(tops)]
    return (
        jnp.concatenate([jnp.where(hit, main, zero) for hit in hits], axis=0),
        jnp.concatenate([jnp.where(hit, rest, zero) for hit in hits], axis=0),
        jnp.concatenate([jnp.where(low == jnp.bfloat16(l), one, zero) for l in range(8)], axis=0),
    )


def region_sums(main, rest, ones):
    over_lanes = (((1,), (1,)), ((), ()))
    total = lax.dot_general(main, ones, over_lanes, preferred_element_type=jnp.float32)
    total += lax.dot_general(rest, ones, over_lanes, preferred_element_type=jnp.float32)
    row, column = iotas(*total.shape)
    total = jnp.where(row % FOLD == column % FOLD, total, 0.0)
    return jnp.sum(total.reshape(total.shape[0] // FOLD, FOLD, total.shape[1]), axis=1)


def inner_kernel(
    forcing_ref, next_ref, nux_ref, nuy_ref, nuyd_ref, nuz_ref, nuzd_ref, rim_ref, regions_ref, outside_ref,
    adjoint_ref, fpack_ref, sums_ref, main_ref, rest_ref, ones_ref,
):
    _, planes, rows, width = forcing_ref.shape
    row, lane = iotas(rows, width)
    rim_nu = rim_ref[...]
    tops = sums_ref.shape[0]

    def add_up(x, values, ids):
        span = rows // FOLD * width
        at = pl.ds(pl.multiple_of(x * span, span), span)
        for part_ref, part in zip((main_ref, rest_ref, ones_ref), region_rows(values, ids, tops)):
            part_ref[:, at] = part

    def plane(x, fpack):
        nus = (nux_ref[x + 1], nux_ref[x], nuy_ref[x], nuyd_ref[x], nuz_ref[x], nuzd_ref[x])
        next_up, next_down = jnp.minimum(x + 1, planes - 1), jnp.maximum(x - 1, 0)
        at_top, at_bottom = x == planes - 1, x == 0
        product = None
        for c in range(3):
            here = forcing_ref[c, x]
            over = jnp.where(at_top, 0.0, forcing_ref[c, next_up])
            under = jnp.where(at_bottom, 0.0, forcing_ref[c, next_down])
            total = nus[0] * (over - here) - nus[1] * (here - under)
            over = jnp.where(row == rows - 1, 0.0, pltpu.roll(here, rows - 1, 0))
            under = jnp.where(row == 0, 0.0, pltpu.roll(here, 1, 0))
            total += nus[2] * (over - here) - nus[3] * (here - under)
            over = jnp.where(lane == width - 1, 0.0, pltpu.roll(here, width - 1, 1))
            under = jnp.where(lane == 0, 0.0, pltpu.roll(here, 1, 1))
            total += nus[4] * (over - here) - nus[5] * (here - under)
            value = here + time_step * total
            adjoint_ref[c, x] = value
            part = value * next_ref[c, x]
            product = part if product is None else product + part
            fpack = pack_edges(fpack, here, c * planes + x, lane)
        add_up(x, product, regions_ref[x])
        return fpack

    fpack = lax.fori_loop(0, planes, plane, jnp.zeros((rows, width), jnp.float32), unroll=4)
    fpack_ref[...] = fpack
    mixed = outside_ref[...]
    reach = pltpu.roll(fpack, 1, 1) * mixed
    reach = reach + pltpu.roll(reach, width - 2 * planes, 1) + pltpu.roll(reach, width - 4 * planes, 1)
    reach = time_step * reach * rim_nu
    add_up(planes, reach, pltpu.roll(mixed, (width - 6 * planes) % width, 1).astype(jnp.int32))
    sums_ref[...] = region_sums(main_ref[...], rest_ref[...], ones_ref[...])


def edge_kernel(groups, masks, x0_ref, x1_ref, nux_ref, next_ref, regions_ref, sums_ref, fpack_ref, *outs):
    _, planes, rows, width = next_ref.shape
    tops, columns = sums_ref.shape
    low, high = 0.0, 0.0
    for c in range(3):
        below, above = beside_of(c, groups, x0_ref, x1_ref)
        low += below * next_ref[c, 0]
        high += above * next_ref[c, planes - 1]
    ends = [
        region_rows(time_step * nux_ref[0] * low, regions_ref[0], tops),
        region_rows(time_step * nux_ref[planes] * high, regions_ref[planes - 1], tops),
    ]
    total = sums_ref[...] + region_sums(*(jnp.concatenate(both, axis=1) for both in zip(*ends)))
    total = jnp.concatenate([total[:, at : at + width] for at in range(0, columns, width)], axis=0)
    high = total.astype(jnp.bfloat16)
    total = jnp.concatenate([high, (total - high.astype(jnp.float32)).astype(jnp.bfloat16)], axis=0)
    height = total.shape[0]
    for mask, out_ref in zip((0,) + masks, outs):
        out_ref[:height, :] = total
        if mask:
            out_ref[height : height + rows, :] = fpack_ref[...].astype(jnp.bfloat16)
            if out_ref.shape[0] > height + rows:
                out_ref[height + rows :, :] = jnp.zeros((out_ref.shape[0] - height - rows, width), jnp.bfloat16)


def beside_of(c, groups, x0_ref, x1_ref):
    return from_neighbours(
        lax.axis_index("fluid"), groups, x0_ref[c].astype(jnp.float32), x1_ref[c].astype(jnp.float32)
    )


def final_kernel(sizes, inner_ref, x0_ref, x1_ref, nux_ref, rims_ref, own_ref, *refs):
    groups, walls = sizes
    arrived, (adjoint_ref, sens_ref, value_ref, owned_ref, sems, owned_sem) = refs[:-6], refs[-6:]
    _, planes, rows, width = inner_ref.shape
    per = own_ref.shape[0]
    _, lane = iotas(rows, width)
    me = lax.axis_index("wall")

    def sums_of(ref):
        parts = ref[:per, :].astype(jnp.float32)
        return parts[: per // 2] + parts[per // 2 :]

    total = sums_of(own_ref)
    below = jnp.zeros((rows, width), jnp.float32)
    above = jnp.zeros((rows, width), jnp.float32)
    for mask, ref in zip(range(1, walls), arrived):
        total = total + sums_of(ref)
        if mask & (mask + 1) == 0:
            edges = ref[per : per + rows, :].astype(jnp.float32)
            above = jnp.where((me ^ mask) == me + 1, edges, above)
            below = jnp.where((me ^ mask) == me - 1, edges, below)
    mixed = mix_edges(below, above, lane)
    edge_flux = mixed * rims_ref[...]
    on_edge = (lane == 0) | (lane == width - 1)

    beside = [beside_of(c, groups, x0_ref, x1_ref) for c in range(3)]
    step = planes // sems.shape[0]

    def store(i):
        part = pl.ds(i * step, step)
        return pltpu.make_async_copy(value_ref.at[:, part], adjoint_ref.at[:, part], sems.at[i])

    for i in range(sems.shape[0]):
        for x in range(i * step, (i + 1) * step):
            for c in range(3):
                value = inner_ref[c, x] + jnp.where(on_edge, edge_of(edge_flux, c * planes + x), 0.0)
                if x == 0:
                    value += time_step * nux_ref[0] * beside[c][0]
                if x == planes - 1:
                    value += time_step * nux_ref[planes] * beside[c][1]
                value_ref[c, x] = value
        store(i).start()
    parts = width // FOLD
    tops = REG_DEV * walls // 8
    owned = REG_DEV // 8
    top, _ = iotas(tops, width)
    region, lane = iotas(REG_DEV, width)
    sens = jnp.zeros((8, REG_DEV), jnp.float32)
    for i in range(8 // parts):
        for h in range(owned):
            mine = jnp.where(top == me * owned + h, total[i * tops : (i + 1) * tops], 0.0)
            gather = (region == h * 8 + i * parts + lane // FOLD).astype(jnp.float32)
            sens += lax.dot_general(
                jnp.broadcast_to(jnp.sum(mine, axis=0, keepdims=True), (8, width)), gather, (((1,), (1,)), ((), ())),
                precision=lax.Precision.HIGHEST, preferred_element_type=jnp.float32,
            )
    owned_ref[...] = sens_scale * sens[:1]
    owned_copy = pltpu.make_async_copy(owned_ref, sens_ref, owned_sem)
    owned_copy.start()
    for i in range(sems.shape[0]):
        store(i).wait()
    owned_copy.wait()


def body(flow_state, regions, obs_tiles, measured, tile_dest, cell_list):
    groups, walls = lax.axis_size("fluid"), lax.axis_size("wall")
    sizes = (groups, walls)
    _, planes, rows, width = flow_state.shape
    count_tiles = obs_tiles.shape[2]
    cap = cell_list.shape[3]
    extra = -(-cap * 3 // 16) * 16
    reg_count = REG_DEV * walls
    cells = groups * cap
    grid = planes * rows * width

    chips = groups // 2
    height = cap * width + extra
    *sends, xs0, xs1 = call(
        functools.partial(group_kernel, cap),
        (bf16(2, height, width),) * chips + (f32(4, rows, width),) * 2,
        [HBM] * 4,
        tuple(
            pltpu.with_memory_space_constraint(operand, pltpu.HBM)
            for operand in (tile_dest[0, 0], obs_tiles[0, 0], jnp.transpose(measured[0, 0], (1, 0, 2)), flow_state)
        ),
        (
            pltpu.SMEM((count_tiles,), jnp.int32),
            pltpu.VMEM((count_tiles, width, width), jnp.bfloat16),
            pltpu.VMEM((3, count_tiles, width), jnp.bfloat16),
            pltpu.SMEM((groups,), jnp.int32),
            pltpu.SMEM((cells,), jnp.int32),
            pltpu.VMEM((groups * extra, width), jnp.bfloat16),
            pltpu.SemaphoreType.DMA,
            pltpu.SemaphoreType.DMA,
            pltpu.SemaphoreType.DMA((4,)),
            pltpu.SemaphoreType.DMA((8,)),
        ),
        out_specs=(VMEM,) * (chips + 2),
    )
    x0, x1 = swap(xs0, "fluid", 0), swap(xs1, "fluid", 1)
    recvs = [sends[0]] + [cross(sends[m], "fluid", 2 * m) for m in range(1, chips)]
    zs = call(
        functools.partial(edges_kernel, groups),
        f32(3, rows, width),
        [VMEM] * 4,
        (flow_state, regions, x0, x1),
        flops=HIDES,
    )
    z0, z1 = swap(zs, "wall", 0), swap(zs, "wall", 1)
    slot_rows = groups * extra
    velocity_next, velocity, nux, nuy, nuz, nuy0, rim, mine, lent, cells_of = call(
        functools.partial(forward_kernel, sizes, cap),
        (f32(3, planes, rows, width),) * 2
        + (f32(planes + 1, rows, width), f32(planes, rows, width), f32(planes, rows, width))
        + (f32(planes, width), f32(rows, width))
        + (bf16(chips, extra, width),) * 2
        + (jax.ShapeDtypeStruct((8, slot_rows), jnp.int32),),
        [ANY] + [VMEM] * 6,
        (cell_list[0, 0].T, flow_state, x0, x1, z0, z1, zs),
        (
            pltpu.SMEM((cap, groups), jnp.int32),
            pltpu.VMEM((4, planes + 2, rows, width), jnp.float32),
            pltpu.VMEM((slot_rows, width), jnp.float32),
            pltpu.SemaphoreType.DMA,
            pltpu.SemaphoreType.DMA((4,)),
        ),
        out_specs=(HBM,) + (VMEM,) * 9,
    )
    borrowed = cross(lent, "fluid", 1)
    outside, rims, pick, nuyd, nuzd = call(
        functools.partial(pick_kernel, sizes),
        (f32(rows, width), f32(rows, width), bf16(3, planes * rows, slot_rows)) + (f32(planes, rows, width),) * 2,
        [VMEM] * 8,
        (cells_of, z0, z1, zs, rim, nuy, nuz, nuy0),
    )

    def products(block, masks, values, before, more=False):
        whole = (2, chips * extra, width)
        return call(
            functools.partial(product_kernel, cap, block, masks, more),
            bf16(*whole),
            [VMEM, VMEM if more else ANY] + [VMEM] * len(masks),
            (values, before, *(recvs[m] for m in masks)),
        )

    held = products(0, tuple(range(chips // 2)), mine, pick)
    given = products(1, tuple(range(chips // 2)), borrowed, held)
    given = products(1, tuple(range(chips // 2, chips)), borrowed, given, True)
    other = cross(given, "fluid", 1)
    held = products(0, tuple(range(chips // 2, chips)), mine, held, True)
    fs0, fs1 = call(ends_kernel, (bf16(3, rows, width),) * 2, [VMEM] * 3, (held, other, pick))
    f0, f1 = swap(fs0, "fluid", 0), swap(fs1, "fluid", 1)
    forcing = call(forcing_kernel, f32(3, planes, rows, width), [VMEM] * 3 + [ANY], (held, other, pick, fs1))
    tops = reg_count // 8
    columns = 8 * FOLD
    span = (planes + 1) * rows // FOLD * width
    sum_rows = 2 * tops * (columns // width)
    inner, fpack, sums = call(
        inner_kernel,
        (f32(3, planes, rows, width), f32(rows, width), f32(tops, columns)),
        [VMEM] * 10,
        (forcing, velocity, nux, nuy, nuyd, nuz, nuzd, rim, regions, outside),
        (
            pltpu.VMEM((tops * FOLD, span), jnp.bfloat16),
            pltpu.VMEM((tops * FOLD, span), jnp.bfloat16),
            pltpu.VMEM((columns, span), jnp.bfloat16),
        ),
    )
    masks = tuple(range(1, walls))
    heights = [sum_rows] + [sum_rows + rows + 16 * (mask - 1) for mask in masks]
    own, *parts = call(
        functools.partial(edge_kernel, groups, masks),
        tuple(bf16(height, width) for height in heights),
        [VMEM] * 7,
        (f0, f1, nux, velocity, regions, sums, fpack),
    )
    arrived = [cross(part, "wall", mask) for part, mask in zip(parts, masks)]
    adjoint, sens = call(
        functools.partial(final_kernel, sizes),
        (f32(3, planes, rows, width), f32(1, REG_DEV)),
        [VMEM] * (6 + len(arrived)),
        (inner, f0, f1, nux, rims, own, *arrived),
        (
            pltpu.VMEM((3, planes, rows, width), jnp.float32),
            pltpu.VMEM((1, REG_DEV), jnp.float32),
            pltpu.SemaphoreType.DMA((4,)),
            pltpu.SemaphoreType.DMA,
        ),
        out_specs=(HBM, HBM),
        flops=10 * grid,
        moved=24 * grid,
    )
    return velocity_next, adjoint, sens.reshape(REG_DEV)


def solution(mesh):
    in_specs = (
        P(None, "fluid", None, "wall"),
        P("fluid", None, "wall"),
        P("fluid", "wall", None, None, None),
        P("fluid", "wall", None, None, None),
        P("fluid", "wall", None),
        P("fluid", "wall", None, None),
    )
    out_specs = (
        P(None, "fluid", None, "wall"),
        P(None, "fluid", None, "wall"),
        P(("fluid", "wall")),
    )
    return jax.shard_map(body, mesh=mesh, in_specs=in_specs, out_specs=out_specs, check_vma=False)
```
